32 devices in a mesh: section: 2 (over y), dp: 4 (over z), head: 4 (over x, core).
Axes of the slice: x: 2, y: 2, z: 4, core: 2. Of those that a mesh axis runs over, the one named last changes fastest.
Arguments:
- tokens: bfloat16 [8, 384, 2048], P('dp'), may hold values from -6 to 6
- lengths: int32 [8, 3], P('dp'), may hold values from 1 to 288, 384 in all within a row
- cotangent: bfloat16 [8, 384, 2048], P('dp'), may hold values from -6 to 6
- attn_in: bfloat16 [2, 3, 2048, 2048], P('section', None, None, 'head'), may hold values from -0.125 to 0.125
- beta_weight: bfloat16 [2, 2048, 16], P('section', None, 'head'), may hold values from -0.125 to 0.125
- conv_weight: float32 [2, 3, 4, 2048], P('section', None, None, 'head'), may hold values from -3 to 3
- o_gain: float32 [2, 128], P('section'), may hold values from 0.5 to 1.5
- attn_out: bfloat16 [2, 2048, 2048], P('section', 'head'), may hold values from -0.125 to 0.125
- mlp_in: bfloat16 [2, 2, 2048, 5632], P('section', None, None, 'head'), may hold values from -0.125 to 0.125
- mlp_out: bfloat16 [2, 5632, 2048], P('section', 'head'), may hold values from -0.078125 to 0.078125
- norm_gains: float32 [2, 2, 2048], P('section'), may hold values from 0.5 to 1.5
Outputs:
- grad_tokens: float32 [8, 384, 2048], P('dp', 'head', 'section')
- grad_attn_in: float32 [2, 3, 2048, 2048], P('section', None, 'dp', 'head')
- grad_beta_weight: float32 [2, 2048, 16], P('section', 'dp', 'head')
- grad_conv_weight: float32 [2, 3, 4, 2048], P('section', None, None, 'head')
- grad_o_gain: float32 [2, 128], P('section')
- grad_attn_out: float32 [2, 2048, 2048], P('section', 'head', 'dp')
- grad_mlp_in: float32 [2, 2, 2048, 5632], P('section', None, 'dp', 'head')
- grad_mlp_out: float32 [2, 5632, 2048], P('section', 'head', 'dp')
- grad_norm_gains: float32 [2, 2, 2048], P('section')
The draws below stay inside these ranges and needn't reach their ends.
Inputs may be any that keep to these rules, and one draw needn't show every extreme that they name: Each row holds the lengths of the 3 sequences packed into one micro-batch; they sum to 384.
All inputs are finite; a program needn't handle non-finite values.
Results may differ from the reference program's by a relative error of at most 0.038.
Values may be sent and summed in bfloat16 or wider, within the bound.
No kernel may reach another device: no remote copies, remote signals or barrier semaphores. Data moves between devices by JAX's collectives and lax.ppermute only.
A program may use at most 320 MiB of HBM per device.

```python
import math
import jax
import jax.numpy as jnp
import numpy as np
from jax import lax

D = 2048
HEADS = 16
HEAD_DIM = 128
FF = 5632
CONV = 4
SPAN = 64
SEQS = 3
TOK_MB = 384
ROWS = 8


def steps_of(rng, dims, split, smallest, largest):
    level, own = 1.0, jax.random.fold_in(rng, 6)
    for position, shards_of in split:
        heights = jnp.exp(jax.random.uniform(jax.random.fold_in(own, position), (shards_of,), jnp.float32, smallest / len(split), largest / len(split)))
        level = level * jnp.repeat(heights, dims[position] // shards_of).reshape([-1 if axis == position else 1 for axis in range(len(dims))])
    return level


def profile(amount, total, most, slope):
    loads = [(1 << 20) // math.isqrt(standing ** slope) + 1 for standing in range(2, amount + 1)]
    spare, counts = total - most - (amount - 1), [1] * (amount - 1)
    while spare > 0:
        movable = [i for i in range(amount - 1) if counts[i] < most]
        mass, budget = sum([loads[i] for i in movable]), spare
        for i in movable:
            addition = min(most - counts[i], max(1, budget * loads[i] // mass), spare)
            counts[i] = counts[i] + addition
            spare = spare - addition
    return np.array([most] + counts)


def uneven(key, count, total, limit, slope):
    if count == 2:
        one = jax.random.randint(key, (), max(1, total - limit), min(limit, total - 1) + 1)
        return jnp.stack([one, total - one])
    tallies = jnp.asarray(profile(count, total, limit, slope), jnp.int32)
    pairs = (count - 1) // 2
    donor, sink = tallies[1:1 + 2 * pairs:2], tallies[2:2 + 2 * pairs:2]
    margin = jnp.minimum(donor - 1, limit - sink)
    shifted = jax.random.randint(jax.random.fold_in(key, 1), (pairs,), 0, 1 << 20) % (margin + 1)
    tallies = tallies.at[1:1 + 2 * pairs:2].set(donor - shifted).at[2:2 + 2 * pairs:2].set(sink + shifted)
    return tallies[jax.random.permutation(jax.random.fold_in(key, 2), count)]


def bell_draw(stream_key, shape, spread, limit, split=(), kind=jnp.bfloat16):
    drawn = spread * jax.random.normal(stream_key, shape, jnp.float32)
    if split:
        drawn = drawn * steps_of(stream_key, shape, split, -0.22, 0.18)
    return jnp.clip(drawn, -limit, limit).astype(kind)


def setup_inputs(seed: int = 0) -> dict:
    key_list = jax.random.split(jax.random.key(seed), 12)
    tokens = bell_draw(key_list[0], (ROWS, TOK_MB, D), 1.0, 6.0, ((0, 4),))
    lengths = jax.vmap(lambda own: uneven(own, SEQS, TOK_MB, TOK_MB - TOK_MB // 4, 0))(jax.random.split(key_list[1], ROWS)).reshape((ROWS, SEQS)).astype(jnp.int32)
    cotangent = bell_draw(key_list[2], (ROWS, TOK_MB, D), 1.0, 6.0, ((0, 4),))
    attn_in = bell_draw(key_list[3], (2, 3, D, D), D ** -0.5, 0.125, ((0, 2), (3, 4)))
    beta_weight = bell_draw(key_list[4], (2, D, HEADS), D ** -0.5, 0.125, ((0, 2), (2, 4)))
    conv_weight = bell_draw(key_list[5], (2, 3, CONV, D), 0.5, 3.0, ((0, 2), (3, 4)), jnp.float32)
    o_gain = jnp.clip(1.0 + 0.1 * jax.random.normal(key_list[6], (2, HEAD_DIM), jnp.float32), 0.5, 1.5)
    attn_out = bell_draw(key_list[7], (2, D, D), D ** -0.5, 0.125, ((0, 2), (1, 4)))
    mlp_in = bell_draw(key_list[8], (2, 2, D, FF), D ** -0.5, 0.125, ((0, 2), (3, 4)))
    mlp_out = bell_draw(key_list[9], (2, FF, D), FF ** -0.5, 0.078125, ((0, 2), (1, 4)))
    norm_gains = jnp.clip(1.0 + 0.1 * jax.random.normal(key_list[10], (2, 2, D), jnp.float32), 0.5, 1.5)
    return {"tokens": tokens, "lengths": lengths, "cotangent": cotangent, "attn_in": attn_in, "beta_weight": beta_weight, "conv_weight": conv_weight, "o_gain": o_gain, "attn_out": attn_out, "mlp_in": mlp_in, "mlp_out": mlp_out, "norm_gains": norm_gains}


HIGHEST = lax.Precision.HIGHEST
EPS = 1e-06
OUT_FLOOR = 0.0001

@jax.custom_vjp
def low(v):
    return lax.optimization_barrier(v.astype(jnp.bfloat16)).astype(jnp.float32)

@jax.custom_vjp
def low_back(v):
    return v

def low_keep(v):
    return (low(v), None)

def low_pass(kept, grad):
    return (grad,)

def back_keep(v):
    return (v, None)

def back_low(kept, grad):
    return (low(grad),)
low.defvjp(low_keep, low_pass)
low_back.defvjp(back_keep, back_low)

def rmsnorm(values):
    return values * lax.rsqrt(lax.optimization_barrier(jnp.mean(values * values, axis=-1, keepdims=True)) + EPS)

def segment_ids(lengths, count):
    ends = jnp.cumsum(lengths.astype(jnp.int32)).astype(jnp.int32)
    places = jnp.arange(count, dtype=jnp.int32)
    return lax.optimization_barrier(jnp.sum((places[:, None] >= ends[None, :]).astype(jnp.int32), axis=1, dtype=jnp.int32)).astype(jnp.int32)

def delayed(values, tap):
    if tap == 0:
        return values
    padding = jnp.zeros((tap,) + values.shape[1:], values.dtype)
    return jnp.concatenate([padding, values[:values.shape[0] - tap]], axis=0)

def tap_masks(segment):
    masks = []
    for tap in range(CONV):
        if tap == 0:
            masks.append(jnp.ones((segment.shape[0], 1), jnp.float32))
        else:
            earlier = jnp.concatenate([jnp.full((tap,), -1, jnp.int32), segment[:segment.shape[0] - tap].astype(jnp.int32)], axis=0)
            masks.append((earlier == segment).astype(jnp.float32)[:, None])
    return masks

def delta_block(state, inputs):
    query, key, value, gate, segment, previous = inputs
    size = segment.shape[0]
    same = (segment[:, None] == segment[None, :]).astype(jnp.float32)
    carry = (segment == previous).astype(jnp.float32)
    identity = jnp.eye(size, dtype=jnp.float32)
    strict = jnp.tril(jnp.ones((size, size), jnp.float32), -1)
    inner = jnp.einsum('hik,hjk->hij', key, key, precision=HIGHEST)
    system = identity + gate[:, :, None] * inner * (same * strict)
    recalled = jnp.einsum('hvk,hik->hiv', state, key, precision=HIGHEST)
    target = gate[:, :, None] * (value - carry[None, :, None] * recalled)
    fresh = jax.scipy.linalg.solve_triangular(system, target, lower=True)
    scores = jnp.einsum('hik,hjk->hij', query, key, precision=HIGHEST) * (same * (strict + identity))
    output = carry[None, :, None] * jnp.einsum('hvk,hik->hiv', state, query, precision=HIGHEST)
    output = output + jnp.einsum('hij,hjv->hiv', scores, fresh, precision=HIGHEST)
    keep = (segment == segment[size - 1]).astype(jnp.float32)
    state = carry[size - 1] * state + jnp.einsum('hiv,hik->hvk', fresh * keep[None, :, None], key, precision=HIGHEST)
    return (state, output)

def mixer(query_in, key_in, value_in, logit, conv_taps, head_gain, segment):
    count = query_in.shape[0]
    heads = query_in.shape[1] // HEAD_DIM
    masks = tap_masks(segment)

    def convolve(values, which):
        total = jnp.zeros_like(values)
        for tap in range(CONV):
            total = total + conv_taps[which, tap][None, :] * delayed(values, tap) * masks[tap]
        return jax.nn.silu(total).reshape(count, heads, HEAD_DIM)
    query = convolve(query_in, 0)
    key = convolve(key_in, 1)
    value = convolve(value_in, 2)
    query = query * lax.rsqrt(lax.optimization_barrier(jnp.sum(query * query, axis=-1, keepdims=True)) + EPS) * HEAD_DIM ** (-0.5)
    key = key * lax.rsqrt(lax.optimization_barrier(jnp.sum(key * key, axis=-1, keepdims=True)) + EPS)
    gate = jax.nn.sigmoid(logit)
    blocks = count // SPAN

    def blocked(values):
        return values.reshape(blocks, SPAN, heads, HEAD_DIM).transpose(0, 2, 1, 3)
    gates = gate.reshape(blocks, SPAN, heads).transpose(0, 2, 1)
    seg_blocks = segment.astype(jnp.int32).reshape(blocks, SPAN)
    previous = jnp.concatenate([jnp.full((1,), -1, jnp.int32), seg_blocks[:blocks - 1, SPAN - 1].astype(jnp.int32)], axis=0)
    initial = jnp.zeros((heads, HEAD_DIM, HEAD_DIM), jnp.float32)
    final_state, outputs = lax.scan(jax.checkpoint(delta_block), initial, (blocked(query), blocked(key), blocked(value), gates, seg_blocks, previous))
    mixed = outputs.transpose(0, 2, 1, 3).reshape(count, heads, HEAD_DIM)
    mixed = mixed * lax.rsqrt(jnp.maximum(lax.optimization_barrier(jnp.mean(mixed * mixed, axis=-1, keepdims=True)), OUT_FLOOR)) * head_gain
    return mixed.reshape(count, heads * HEAD_DIM)

def dense(left, right):
    return jnp.dot(left, right, precision=HIGHEST)

def layer(inputs, weights, segment):
    attn_in, beta_weight, conv_weight, o_gain, attn_out, mlp_in, mlp_out, norm_gains = weights
    normed = low(rmsnorm(inputs) * norm_gains[0])
    query_in = low_back(dense(normed, attn_in[0]))
    key_in = low_back(dense(normed, attn_in[1]))
    value_in = low_back(dense(normed, attn_in[2]))
    logit = low_back(dense(normed, beta_weight))
    mixed = low(mixer(query_in, key_in, value_in, logit, conv_weight, o_gain, segment))
    middle = inputs + low_back(dense(mixed, attn_out))
    normed_mid = low(rmsnorm(middle) * norm_gains[1])
    gate_in = low_back(dense(normed_mid, mlp_in[0]))
    up_in = low_back(dense(normed_mid, mlp_in[1]))
    hidden = low(jax.nn.silu(gate_in) * up_in)
    return middle + low_back(dense(hidden, mlp_out))

def network(inputs, params, segment):
    first = layer(inputs, tuple((weight[0] for weight in params)), segment)
    moved = low(low_back(first))
    return layer(moved, tuple((weight[1] for weight in params)), segment)

def reference(tokens, lengths, cotangent, attn_in, beta_weight, conv_weight, o_gain, attn_out, mlp_in, mlp_out, norm_gains):
    params = tuple((weight.astype(jnp.float32) for weight in (attn_in, beta_weight, conv_weight, o_gain, attn_out, mlp_in, mlp_out, norm_gains)))
    segments = jax.vmap(lambda row: segment_ids(row, TOK_MB))(lengths.astype(jnp.int32)).astype(jnp.int32)

    def whole(inputs, weights):
        block = jax.checkpoint(lambda pair: network(pair[0], weights, pair[1]))
        return lax.map(block, (inputs, segments))
    outputs, pull = jax.vjp(whole, tokens.astype(jnp.float32), params)
    grad_in, grads = pull(cotangent.astype(jnp.float32))
    return (grad_in, grads[0], grads[1], grads[2], grads[3], grads[4], grads[5], grads[6], grads[7])
```

```python
import functools

import jax
import jax.numpy as jnp
from jax import lax
from jax.experimental import pallas as pl
from jax.experimental.pallas import tpu as pltpu
from jax.sharding import PartitionSpec as P

HEAD_DIM = 128
CONV = 4
TOK_MB = 384
BLOCK = 128
BLOCKS = TOK_MB // BLOCK
EPS = 1e-06
OUT_FLOOR = 0.0001
F32 = jnp.float32
BF16 = jnp.bfloat16
BASE = 4


def mm(left, right):
    return lax.dot_general(
        left.astype(BF16), right.astype(BF16), (((1,), (0,)), ((), ())), preferred_element_type=F32
    )


def mm_t(left, right):
    return lax.dot_general(
        left.astype(BF16), right.astype(BF16), (((1,), (1,)), ((), ())), preferred_element_type=F32
    )


def t_mm(left, right):
    return lax.dot_general(
        left.astype(BF16), right.astype(BF16), (((0,), (0,)), ((), ())), preferred_element_type=F32
    )


def rows_of(b):
    return slice(b * BLOCK, (b + 1) * BLOCK)


def stream(x, taps, masks):
    pre = taps[0:1] * x
    for tap in range(1, CONV):
        pre = pre + taps[tap : tap + 1] * (pltpu.roll(x, tap, 0) * masks[tap - 1])
    gate = jax.nn.sigmoid(pre)
    return pre, gate, pre * gate


def unit_inverses(systems):
    size = systems[0].shape[0]
    row = lax.broadcasted_iota(jnp.int32, (size, size), 0)
    col = lax.broadcasted_iota(jnp.int32, (size, size), 1)
    eye = (row == col).astype(F32)
    near = (row // BASE == col // BASE).astype(F32)
    first = [-a * near for a in systems]
    power = 1
    total = [eye + n for n in first]
    second = [mm(n, n) for n in first]
    third = [mm(n, s) for n, s in zip(first, second)]
    total = [t + s + r for t, s, r in zip(total, second, third)]
    step = BASE
    while step < size:
        span = 2 * step
        off = ((row // span == col // span) & (row // step != col // step)).astype(F32)
        inner = [mm(a * off, t) for a, t in zip(systems, total)]
        outer = [mm(t, i) for t, i in zip(total, inner)]
        total = [t - o for t, o in zip(total, outer)]
        step = span
    return total


def forward_kernel(heads_here, save, qkv_ref, logit_ref, taps_ref, gain_ref, masks_ref, seg_col_ref, seg_row_ref, mixed_ref, *saved):
    step = pl.program_id(0)
    masks = [masks_ref[i] for i in range(CONV - 1)]
    logits = logit_ref[...]
    lane = lax.broadcasted_iota(jnp.int32, logits.shape, 1)
    row = lax.broadcasted_iota(jnp.int32, (BLOCK, BLOCK), 0)
    col = lax.broadcasted_iota(jnp.int32, (BLOCK, BLOCK), 1)
    strict = col < row
    lower = col <= row
    same = {}
    for b in range(BLOCKS):
        for c in range(b + 1):
            same[b, c] = seg_col_ref[rows_of(b), :] == seg_row_ref[:, rows_of(c)]
    queries, keys, values, betas = [], [], [], []
    for h in range(heads_here):
        cols = slice(h * HEAD_DIM, (h + 1) * HEAD_DIM)
        taps = [taps_ref[j, :, cols] for j in range(3)]
        _, _, query = stream(qkv_ref[0, :, cols], taps[0], masks)
        _, _, key = stream(qkv_ref[1, :, cols], taps[1], masks)
        _, _, value = stream(qkv_ref[2, :, cols], taps[2], masks)
        query = query * lax.rsqrt(jnp.sum(query * query, axis=-1, keepdims=True) + EPS) * HEAD_DIM**-0.5
        key = key * lax.rsqrt(jnp.sum(key * key, axis=-1, keepdims=True) + EPS)
        logit = jnp.sum(jnp.where(lane == step * heads_here + h, logits, 0.0), axis=1, keepdims=True)
        beta = jax.nn.sigmoid(logit)
        queries.append(query.astype(BF16))
        keys.append(key.astype(BF16))
        values.append(value * beta)
        betas.append(beta)
    attend, system = {}, {}
    for h in range(heads_here):
        for b in range(BLOCKS):
            for c in range(b + 1):
                inner = mm_t(keys[h][rows_of(b)], keys[h][rows_of(c)])
                keep = same[b, c] & strict if b == c else same[b, c]
                system[h, b, c] = jnp.where(keep, inner * betas[h][rows_of(b)], 0.0)
                scores = mm_t(queries[h][rows_of(b)], keys[h][rows_of(c)])
                keep = same[b, c] & lower if b == c else same[b, c]
                attend[h, b, c] = jnp.where(keep, scores, 0.0).astype(BF16)
    index = [(h, b) for h in range(heads_here) for b in range(BLOCKS)]
    inverse = dict(zip(index, unit_inverses([system[h, b, b] for h, b in index])))
    inverse = {k: v.astype(BF16) for k, v in inverse.items()}
    system = {k: v.astype(BF16) for k, v in system.items()}
    fresh = {}
    for b in range(BLOCKS):
        for h in range(heads_here):
            target = values[h][rows_of(b)]
            for c in range(b):
                target = target - mm(system[h, b, c], fresh[h, c])
            fresh[h, b] = mm(inverse[h, b], target).astype(BF16)
    for h in range(heads_here):
        cols = slice(h * HEAD_DIM, (h + 1) * HEAD_DIM)
        for b in range(BLOCKS):
            out = mm(attend[h, b, 0], fresh[h, 0])
            for c in range(1, b + 1):
                out = out + mm(attend[h, b, c], fresh[h, c])
            mean = jnp.mean(out * out, axis=-1, keepdims=True)
            mixed_ref[rows_of(b), cols] = (
                out * lax.rsqrt(jnp.maximum(mean, OUT_FLOOR)) * gain_ref[...]
            ).astype(BF16)
            if save:
                system_ref, attend_ref, inverse_ref, fresh_ref, out_ref = saved
                out_ref[rows_of(b), cols] = out
                fresh_ref[rows_of(b), cols] = fresh[h, b]
                inverse_ref[h, b] = inverse[h, b]
                for c in range(b + 1):
                    attend_ref[h, rows_of(b), rows_of(c)] = attend[h, b, c]
                    if c < b:
                        system_ref[h, rows_of(b), rows_of(c)] = system[h, b, c]


def mix_forward(qkv, logit, taps, gain, masks, seg_col, seg_row, save, per=1):
    heads = logit.shape[1]
    width = per * HEAD_DIM
    full = lambda shape: pl.BlockSpec(shape, lambda h: (0,) * len(shape))
    out_shape = [jax.ShapeDtypeStruct((TOK_MB, heads * HEAD_DIM), BF16)]
    out_specs = [pl.BlockSpec((TOK_MB, width), lambda h: (0, h))]
    if save:
        out_shape += [
            jax.ShapeDtypeStruct((heads, TOK_MB, TOK_MB), BF16),
            jax.ShapeDtypeStruct((heads, TOK_MB, TOK_MB), BF16),
            jax.ShapeDtypeStruct((heads, BLOCKS, BLOCK, BLOCK), BF16),
            jax.ShapeDtypeStruct((TOK_MB, heads * HEAD_DIM), BF16),
            jax.ShapeDtypeStruct((TOK_MB, heads * HEAD_DIM), F32),
        ]
        out_specs += [
            pl.BlockSpec((per, TOK_MB, TOK_MB), lambda h: (h, 0, 0)),
            pl.BlockSpec((per, TOK_MB, TOK_MB), lambda h: (h, 0, 0)),
            pl.BlockSpec((per, BLOCKS, BLOCK, BLOCK), lambda h: (h, 0, 0, 0)),
            pl.BlockSpec((TOK_MB, width), lambda h: (0, h)),
            pl.BlockSpec((TOK_MB, width), lambda h: (0, h)),
        ]
    return pl.pallas_call(
        functools.partial(forward_kernel, per, save),
        grid=(heads // per,),
        in_specs=[
            pl.BlockSpec((3, TOK_MB, width), lambda h: (0, 0, h)),
            full(logit.shape),
            pl.BlockSpec((3, CONV, width), lambda h: (0, 0, h)),
            full(gain.shape),
            full(masks.shape),
            full(seg_col.shape),
            full(seg_row.shape),
        ],
        out_specs=out_specs,
        out_shape=out_shape,
        compiler_params=pltpu.CompilerParams(vmem_limit_bytes=48 * 1024 * 1024),
        cost_estimate=pl.CostEstimate(flops=heads * 10**9, bytes_accessed=heads * 10**6, transcendentals=0),
    )(qkv, logit, taps, gain, masks, seg_col, seg_row)


def stream_back(grad, x, pre, gate, taps, masks, taps_out, j, cols):
    grad_pre = grad * gate * (1.0 + pre * (1.0 - gate))
    grad_x = taps[0:1] * grad_pre
    taps_out[j, 0:1, cols] = jnp.sum(grad_pre * x, axis=0, keepdims=True)
    for tap in range(1, CONV):
        masked = grad_pre * masks[tap - 1]
        grad_x = grad_x + taps[tap : tap + 1] * pltpu.roll(masked, TOK_MB - tap, 0)
        taps_out[j, tap : tap + 1, cols] = jnp.sum(masked * pltpu.roll(x, tap, 0), axis=0, keepdims=True)
    return grad_x


def backward_kernel(heads_here, qkv_ref, logit_ref, taps_ref, gain_ref, masks_ref, seg_col_ref, seg_row_ref,
                    system_ref, attend_ref, inverse_ref, fresh_ref, out_ref, grad_ref,
                    grad_qkv_ref, grad_logit_ref, grad_taps_ref, grad_gain_ref):
    step = pl.program_id(0)

    @pl.when(step == 0)
    def _():
        grad_logit_ref[...] = jnp.zeros(grad_logit_ref.shape, F32)
        grad_gain_ref[...] = jnp.zeros(grad_gain_ref.shape, F32)

    masks = [masks_ref[i] for i in range(CONV - 1)]
    logits = logit_ref[...]
    lane = lax.broadcasted_iota(jnp.int32, logits.shape, 1)
    wide = lax.broadcasted_iota(jnp.int32, (TOK_MB, HEAD_DIM), 1)
    row = lax.broadcasted_iota(jnp.int32, (BLOCK, BLOCK), 0)
    col = lax.broadcasted_iota(jnp.int32, (BLOCK, BLOCK), 1)
    strict = col < row
    lower = col <= row
    same = {}
    for b in range(BLOCKS):
        for c in range(b + 1):
            same[b, c] = seg_col_ref[rows_of(b), :] == seg_row_ref[:, rows_of(c)]
    for h in range(heads_here):
        cols = slice(h * HEAD_DIM, (h + 1) * HEAD_DIM)
        taps = [taps_ref[j, :, cols] for j in range(3)]
        inputs = [qkv_ref[j, :, cols] for j in range(3)]
        pre_q, gate_q, conv_q = stream(inputs[0], taps[0], masks)
        pre_k, gate_k, conv_k = stream(inputs[1], taps[1], masks)
        pre_v, gate_v, value = stream(inputs[2], taps[2], masks)
        scale_q = lax.rsqrt(jnp.sum(conv_q * conv_q, axis=-1, keepdims=True) + EPS)
        scale_k = lax.rsqrt(jnp.sum(conv_k * conv_k, axis=-1, keepdims=True) + EPS)
        unit_q = conv_q * scale_q
        key = conv_k * scale_k
        query = (unit_q * HEAD_DIM**-0.5).astype(BF16)
        key_b = key.astype(BF16)
        logit = jnp.sum(jnp.where(lane == step * heads_here + h, logits, 0.0), axis=1, keepdims=True)
        beta = jax.nn.sigmoid(logit)

        out = out_ref[:, cols]
        grad_mixed = grad_ref[:, cols]
        mean = jnp.mean(out * out, axis=-1, keepdims=True)
        scale = lax.rsqrt(jnp.maximum(mean, OUT_FLOOR))
        unit = out * scale
        grad_gain_ref[...] += jnp.sum((grad_mixed * unit).reshape(TOK_MB // 8, 8, HEAD_DIM), axis=0)
        grad_unit = grad_mixed * gain_ref[...]
        through = jnp.where(mean > OUT_FLOOR, 1.0, jnp.where(mean == OUT_FLOOR, 0.5, 0.0))
        grad_out = scale * (
            grad_unit - unit * (through * jnp.mean(grad_unit * unit, axis=-1, keepdims=True))
        )
        grad_out = grad_out.astype(BF16)
        fresh = [fresh_ref[rows_of(b), cols] for b in range(BLOCKS)]
        d_out = [grad_out[rows_of(b)] for b in range(BLOCKS)]
        d_fresh = [None] * BLOCKS
        for c in range(BLOCKS):
            total = t_mm(attend_ref[h, rows_of(c), rows_of(c)], d_out[c])
            for b in range(c + 1, BLOCKS):
                total = total + t_mm(attend_ref[h, rows_of(b), rows_of(c)], d_out[b])
            d_fresh[c] = total
        d_target = [None] * BLOCKS
        for b in reversed(range(BLOCKS)):
            d_target[b] = t_mm(inverse_ref[h, b], d_fresh[b])
            for c in range(b):
                d_fresh[c] = d_fresh[c] - t_mm(system_ref[h, rows_of(b), rows_of(c)], d_target[b])
        d_target_b = [d.astype(BF16) for d in d_target]
        grad_query = []
        inner = []
        grad_key = [None] * BLOCKS
        key_blocks = [key_b[rows_of(b)] for b in range(BLOCKS)]
        for b in range(BLOCKS):
            dq = None
            da = None
            beta_row = beta[rows_of(b)]
            for c in range(b + 1):
                d_attend = mm_t(d_out[b], fresh[c])
                keep = same[b, c] & lower if b == c else same[b, c]
                d_attend = jnp.where(keep, d_attend, 0.0).astype(BF16)
                d_system = mm_t(d_target_b[b], fresh[c])
                keep = same[b, c] & strict if b == c else same[b, c]
                d_system = jnp.where(keep, -d_system, 0.0)
                part = mm(d_attend, key_blocks[c])
                dq = part if dq is None else dq + part
                part = mm(d_system, key_blocks[c])
                da = part if da is None else da + part
                part = t_mm(d_attend, query[rows_of(b)]) + t_mm(d_system * beta_row, key_blocks[b])
                grad_key[c] = part if grad_key[c] is None else grad_key[c] + part
            grad_query.append(dq)
            inner.append(da)
        inner = jnp.concatenate(inner, axis=0)
        grad_query = jnp.concatenate(grad_query, axis=0)
        grad_key = jnp.concatenate(grad_key, axis=0) + beta * inner
        d_target = jnp.concatenate(d_target, axis=0)
        grad_beta = jnp.sum(inner * key + d_target * value, axis=-1, keepdims=True)
        grad_logit = grad_beta * beta * (1.0 - beta)
        grad_logit_ref[...] += jnp.where(wide == step * heads_here + h, grad_logit, 0.0)
        grad_value = beta * d_target
        grad_conv_q = (HEAD_DIM**-0.5 * scale_q) * (
            grad_query - unit_q * jnp.sum(grad_query * unit_q, axis=-1, keepdims=True)
        )
        grad_conv_k = scale_k * (grad_key - key * jnp.sum(grad_key * key, axis=-1, keepdims=True))
        for j, (grad, pre, gate) in enumerate(
            ((grad_conv_q, pre_q, gate_q), (grad_conv_k, pre_k, gate_k), (grad_value, pre_v, gate_v))
        ):
            grad_x = stream_back(grad, inputs[j], pre, gate, taps[j], masks, grad_taps_ref, j, cols)
            grad_qkv_ref[j, :, cols] = grad_x.astype(BF16)


def mix_backward(qkv, logit, taps, gain, masks, seg_col, seg_row, saved, grad_mixed, per=1):
    heads = logit.shape[1]
    width = per * HEAD_DIM
    full = lambda shape: pl.BlockSpec(shape, lambda h: (0,) * len(shape))
    rows = pl.BlockSpec((TOK_MB, width), lambda h: (0, h))
    return pl.pallas_call(
        functools.partial(backward_kernel, per),
        grid=(heads // per,),
        in_specs=[
            pl.BlockSpec((3, TOK_MB, width), lambda h: (0, 0, h)),
            full(logit.shape),
            pl.BlockSpec((3, CONV, width), lambda h: (0, 0, h)),
            full(gain.shape),
            full(masks.shape),
            full(seg_col.shape),
            full(seg_row.shape),
            pl.BlockSpec((per, TOK_MB, TOK_MB), lambda h: (h, 0, 0)),
            pl.BlockSpec((per, TOK_MB, TOK_MB), lambda h: (h, 0, 0)),
            pl.BlockSpec((per, BLOCKS, BLOCK, BLOCK), lambda h: (h, 0, 0, 0)),
            rows,
            rows,
            rows,
        ],
        out_specs=[
            pl.BlockSpec((3, TOK_MB, width), lambda h: (0, 0, h)),
            full((TOK_MB, HEAD_DIM)),
            pl.BlockSpec((3, CONV, width), lambda h: (0, 0, h)),
            full((8, HEAD_DIM)),
        ],
        out_shape=[
            jax.ShapeDtypeStruct((3, TOK_MB, heads * HEAD_DIM), BF16),
            jax.ShapeDtypeStruct((TOK_MB, HEAD_DIM), F32),
            jax.ShapeDtypeStruct((3, CONV, heads * HEAD_DIM), F32),
            jax.ShapeDtypeStruct((8, HEAD_DIM), F32),
        ],
        compiler_params=pltpu.CompilerParams(vmem_limit_bytes=48 * 1024 * 1024),
        cost_estimate=pl.CostEstimate(flops=heads * 10**9, bytes_accessed=heads * 2 * 10**6, transcendentals=0),
    )(qkv, logit, taps, gain, masks, seg_col, seg_row, *saved, grad_mixed)


def tap_masks(segment):
    masks = []
    for tap in range(1, CONV):
        earlier = jnp.concatenate([jnp.full((tap,), -1, jnp.int32), segment[: TOK_MB - tap]], axis=0)
        masks.append(jnp.broadcast_to((earlier == segment).astype(F32)[:, None], (TOK_MB, HEAD_DIM)))
    return jnp.stack(masks)


def narrow(values):
    return values.astype(BF16)


def product(left, right):
    return jnp.dot(left, right, preferred_element_type=F32)


def product_left(left, right):
    return lax.dot_general(left, right, (((0,), (0,)), ((), ())), preferred_element_type=F32)


def product_right(left, right):
    return lax.dot_general(left, right, (((1,), (1,)), ((), ())), preferred_element_type=F32)


def rms_parts(values):
    scale = lax.rsqrt(jnp.mean(values * values, axis=-1, keepdims=True) + EPS)
    return (values * scale, scale)


def norm_back(grad_normed, normed, scale, gain):
    grad_scaled = grad_normed * gain
    return scale * (grad_scaled - normed * jnp.mean(grad_scaled * normed, axis=-1, keepdims=True))


def segment_ids(lengths, count):
    ends = jnp.cumsum(lengths)
    places = jnp.arange(count, dtype=jnp.int32)
    return jnp.sum((places[:, None] >= ends[None, :]).astype(jnp.int32), axis=1, dtype=jnp.int32)


def flipped(values, axis, bit):
    return lax.ppermute(values, axis, [(i, i ^ bit) for i in range(lax.axis_size(axis))])


def shifted(values, axis, distance):
    devices = range(lax.axis_size(axis))
    return lax.ppermute(values, axis, [(i, i + distance) for i in devices if i + distance in devices])


def bits_of(axis):
    size = lax.axis_size(axis)
    bits = [1 << k for k in range(size.bit_length() - 1)]
    assert 1 << len(bits) == size
    return bits


def summed(values, axes):
    for axis in axes:
        for bit in bits_of(axis):
            values = values + flipped(values, axis, bit)
    return values


def gather(shard):
    me = lax.axis_index("head")
    parts = shard
    for place, bit in enumerate(reversed(bits_of("head"))):
        other = flipped(parts, "head", bit)
        low = (me & bit) == 0
        parts = jnp.stack([jnp.where(low, parts, other), jnp.where(low, other, parts)], axis=place)
    return parts.reshape(-1, shard.shape[-1])


def scatter(partial):
    me = lax.axis_index("head")
    bits = bits_of("head")
    parts = narrow(partial).reshape([2] * len(bits) + [-1, partial.shape[-1]])
    for place, bit in enumerate(bits):
        axis = len(bits) - 1 - place
        side = (me // bit) % 2
        mine = lax.dynamic_index_in_dim(parts, side, axis, keepdims=False)
        other = lax.dynamic_index_in_dim(parts, 1 - side, axis, keepdims=False)
        total = mine.astype(F32) + flipped(other, "head", bit).astype(F32)
        parts = narrow(total)
    return total


def per_device(
    tokens,
    lengths,
    cotangent,
    attn_in,
    beta_weight,
    conv_weight,
    o_gain,
    attn_out,
    mlp_in,
    mlp_out,
    norm_gains,
):
    section = lax.axis_index("section")
    sections = lax.axis_size("section")
    member = lax.axis_index("head")
    micro = tokens.shape[0]
    width = tokens.shape[2]
    heads = beta_weight.shape[2]
    share = TOK_MB // lax.axis_size("head")
    projections = attn_in[0]
    gate_proj = beta_weight[0]
    taps = conv_weight[0]
    head_gain = o_gain
    merge_weight = attn_out[0]
    expand = mlp_in[0]
    contract_weight = mlp_out[0]
    gains = norm_gains[0]
    every = range(micro)
    segments = [segment_ids(lengths[m], TOK_MB) for m in every]
    masks = [(tap_masks(s), s[:, None], s[None, :]) for s in segments]
    own_rows = lambda values: lax.dynamic_slice_in_dim(values, member * share, share, 0).astype(F32)
    tokens_own = [own_rows(tokens[m]) for m in every]
    cotangent_own = [own_rows(cotangent[m]) for m in every]

    def forward(x, m, save):
        unit, scale = rms_parts(x)
        normed = gather(narrow(unit * gains[0]))
        qkv = jnp.stack([product(normed, projections[j]) for j in range(3)])
        logit = product(normed, gate_proj)
        mixed, *saved = mix_forward(qkv, logit, taps, head_gain, *masks[m], save, heads)
        middle = x + scatter(product(mixed, merge_weight))
        unit_mid, scale_mid = rms_parts(middle)
        normed_mid = gather(narrow(unit_mid * gains[1]))
        gate_in = product(normed_mid, expand[0])
        up_in = product(normed_mid, expand[1])
        hidden = narrow(jax.nn.silu(gate_in) * up_in)
        result = middle + scatter(product(hidden, contract_weight))
        kept = (unit, scale, normed, qkv, logit, mixed, saved, unit_mid, scale_mid, normed_mid, gate_in, up_in, hidden)
        return result, kept

    def backward(incoming, m, kept):
        unit, scale, normed, qkv, logit, mixed, saved, unit_mid, scale_mid, normed_mid, gate_in, up_in, hidden = kept
        grad_out = gather(narrow(incoming))
        sigmoid_gate = jax.nn.sigmoid(gate_in)
        silu_gate = gate_in * sigmoid_gate
        grad_hidden = product_right(grad_out, contract_weight)
        grad_gate = narrow(grad_hidden * up_in * sigmoid_gate * (1.0 + gate_in * (1.0 - sigmoid_gate)))
        grad_up = narrow(grad_hidden * silu_gate)
        grad_mid = scatter(product_right(grad_gate, expand[0]) + product_right(grad_up, expand[1]))
        grad_middle = incoming + norm_back(grad_mid, unit_mid, scale_mid, gains[1])
        gain_two = jnp.sum(grad_mid * unit_mid, axis=0)
        grad_branch = gather(narrow(grad_middle))
        grad_mixed = product_right(grad_branch, merge_weight)
        grad_qkv, grad_logit, grad_taps, grad_head_gain = mix_backward(
            qkv, logit, taps, head_gain, *masks[m], saved, grad_mixed, 2 if heads % 2 == 0 else 1
        )
        grad_logit = narrow(grad_logit[:, :heads])
        grad_norm = product_right(grad_logit, gate_proj)
        for j in range(3):
            grad_norm = grad_norm + product_right(grad_qkv[j], projections[j])
        grad_norm = scatter(grad_norm)
        grad_inputs = grad_middle + norm_back(grad_norm, unit, scale, gains[0])
        gain_one = jnp.sum(grad_norm * unit, axis=0)
        big = (normed, grad_qkv, grad_logit, mixed, grad_branch, normed_mid, grad_gate, grad_up, hidden, grad_out)
        small = (grad_taps, jnp.sum(grad_head_gain, axis=0), jnp.stack([gain_one, gain_two]))
        return grad_inputs, big, small

    inputs = tokens_own
    for turn in range(sections):
        results = [forward(inputs[m], m, turn == sections - 1) for m in every]
        if turn < sections - 1:
            arrived = [shifted(narrow(result), "section", 1).astype(F32) for result, _ in results]
            inputs = [jnp.where(section == 0, tokens_own[m], arrived[m]) for m in every]
    kept = [k for _, k in results]
    incoming = cotangent_own
    for turn in range(sections):
        results = [backward(incoming[m], m, kept[m]) for m in every]
        if turn < sections - 1:
            arrived = [shifted(narrow(result[0]), "section", -1).astype(F32) for result in results]
            incoming = [jnp.where(section == sections - 1, cotangent_own[m], arrived[m]) for m in every]
    rows_out = jnp.stack([result[0] for result in results])
    half = width // sections
    moved = shifted(narrow(rows_out[:, :, half:]), "section", 1).astype(F32)
    grad_tokens = jnp.where(section == 0, rows_out[:, :, :half], moved)

    def joined(place, axis=0):
        return jnp.concatenate([result[1][place] for result in results], axis=axis)

    normed, grad_qkv, grad_logit = joined(0), joined(1, 1), joined(2)
    mixed, grad_branch, normed_mid = joined(3), joined(4), joined(5)
    grad_gate, grad_up, hidden, grad_out = joined(6), joined(7), joined(8), joined(9)

    def spread(value, axis):
        return lax.psum_scatter(narrow(value), "dp", scatter_dimension=axis, tiled=True).astype(F32)

    grad_expand = spread(jnp.stack([product_left(normed_mid, grad_gate), product_left(normed_mid, grad_up)]), 1)
    grad_contract = spread(product_left(hidden, grad_out), 1)
    grad_merge = spread(product_left(mixed, grad_branch), 1)
    grad_project = spread(jnp.stack([product_left(normed, grad_qkv[j]) for j in range(3)]), 1)
    grad_beta = spread(product_left(normed, grad_logit), 0)
    grad_taps, grad_head_gain, grad_gains = (
        sum(result[2][place] for result in results) for place in range(3)
    )
    grad_gains = summed(jnp.concatenate([grad_gains.reshape(-1), grad_head_gain]), ("dp", "head"))
    grad_gains, grad_head_gain = grad_gains[: 2 * width].reshape(2, width), grad_gains[2 * width :]
    grad_taps = summed(grad_taps, ("dp",))
    return (
        grad_tokens,
        grad_project[None],
        grad_beta[None],
        grad_taps[None],
        grad_head_gain[None],
        grad_merge[None],
        grad_expand[None],
        grad_contract[None],
        grad_gains[None],
    )


def solution(mesh):
    return jax.shard_map(
        per_device,
        mesh=mesh,
        in_specs=(
            P("dp", None, None),
            P("dp", None),
            P("dp", None, None),
            P("section", None, None, "head"),
            P("section", None, "head"),
            P("section", None, None, "head"),
            P("section", None),
            P("section", "head", None),
            P("section", None, None, "head"),
            P("section", "head", None),
            P("section", None, None),
        ),
        out_specs=(
            P("dp", "head", "section"),
            P("section", None, "dp", "head"),
            P("section", "dp", "head"),
            P("section", None, None, "head"),
            P("section", None),
            P("section", "head", "dp"),
            P("section", None, "dp", "head"),
            P("section", "head", "dp"),
            P("section", None, None),
        ),
        check_vma=False,
    )
```

```python
import functools

import jax
import jax.numpy as jnp
from jax import lax
from jax.experimental import pallas as pl
from jax.experimental.pallas import tpu as pltpu
from jax.sharding import PartitionSpec as P

HEAD_DIM = 128
CONV = 4
TOK_MB = 384
BLOCK = 128
BLOCKS = TOK_MB // BLOCK
EPS = 1e-06
OUT_FLOOR = 0.0001
F32 = jnp.float32
BF16 = jnp.bfloat16
BASE = 4


def mm(left, right):
    return lax.dot_general(
        left.astype(BF16), right.astype(BF16), (((1,), (0,)), ((), ())), preferred_element_type=F32
    )


def mm_t(left, right):
    return lax.dot_general(
        left.astype(BF16), right.astype(BF16), (((1,), (1,)), ((), ())), preferred_element_type=F32
    )


def t_mm(left, right):
    return lax.dot_general(
        left.astype(BF16), right.astype(BF16), (((0,), (0,)), ((), ())), preferred_element_type=F32
    )


def rows_of(b):
    return slice(b * BLOCK, (b + 1) * BLOCK)


def stream(x, taps, masks):
    pre = taps[0:1] * x
    for tap in range(1, CONV):
        pre = pre + taps[tap : tap + 1] * (pltpu.roll(x, tap, 0) * masks[tap - 1])
    gate = jax.nn.sigmoid(pre)
    return pre, gate, pre * gate


def unit_inverses(systems):
    size = systems[0].shape[0]
    row = lax.broadcasted_iota(jnp.int32, (size, size), 0)
    col = lax.broadcasted_iota(jnp.int32, (size, size), 1)
    eye = (row == col).astype(F32)
    near = (row // BASE == col // BASE).astype(F32)
    first = [-a * near for a in systems]
    power = 1
    total = [eye + n for n in first]
    second = [mm(n, n) for n in first]
    third = [mm(n, s) for n, s in zip(first, second)]
    total = [t + s + r for t, s, r in zip(total, second, third)]
    step = BASE
    while step < size:
        span = 2 * step
        off = ((row // span == col // span) & (row // step != col // step)).astype(F32)
        inner = [mm(a * off, t) for a, t in zip(systems, total)]
        outer = [mm(t, i) for t, i in zip(total, inner)]
        total = [t - o for t, o in zip(total, outer)]
        step = span
    return total


def forward_kernel(heads_here, save, qkv_ref, logit_ref, taps_ref, gain_ref, masks_ref, seg_col_ref, seg_row_ref, mixed_ref, *saved):
    step = pl.program_id(0)
    masks = [masks_ref[i] for i in range(CONV - 1)]
    logits = logit_ref[...]
    lane = lax.broadcasted_iota(jnp.int32, logits.shape, 1)
    row = lax.broadcasted_iota(jnp.int32, (BLOCK, BLOCK), 0)
    col = lax.broadcasted_iota(jnp.int32, (BLOCK, BLOCK), 1)
    strict = col < row
    lower = col <= row
    same = {}
    for b in range(BLOCKS):
        for c in range(b + 1):
            same[b, c] = seg_col_ref[rows_of(b), :] == seg_row_ref[:, rows_of(c)]
    queries, keys, values, betas = [], [], [], []
    for h in range(heads_here):
        cols = slice(h * HEAD_DIM, (h + 1) * HEAD_DIM)
        taps = [taps_ref[j, :, cols] for j in range(3)]
        _, _, query = stream(qkv_ref[0, :, cols], taps[0], masks)
        _, _, key = stream(qkv_ref[1, :, cols], taps[1], masks)
        _, _, value = stream(qkv_ref[2, :, cols], taps[2], masks)
        query = query * lax.rsqrt(jnp.sum(query * query, axis=-1, keepdims=True) + EPS) * HEAD_DIM**-0.5
        key = key * lax.rsqrt(jnp.sum(key * key, axis=-1, keepdims=True) + EPS)
        logit = jnp.sum(jnp.where(lane == step * heads_here + h, logits, 0.0), axis=1, keepdims=True)
        beta = jax.nn.sigmoid(logit)
        queries.append(query.astype(BF16))
        keys.append(key.astype(BF16))
        values.append(value * beta)
        betas.append(beta)
    attend, system = {}, {}
    for h in range(heads_here):
        for b in range(BLOCKS):
            for c in range(b + 1):
                inner = mm_t(keys[h][rows_of(b)], keys[h][rows_of(c)])
                keep = same[b, c] & strict if b == c else same[b, c]
                system[h, b, c] = jnp.where(keep, inner * betas[h][rows_of(b)], 0.0)
                scores = mm_t(queries[h][rows_of(b)], keys[h][rows_of(c)])
                keep = same[b, c] & lower if b == c else same[b, c]
                attend[h, b, c] = jnp.where(keep, scores, 0.0).astype(BF16)
    index = [(h, b) for h in range(heads_here) for b in range(BLOCKS)]
    inverse = dict(zip(index, unit_inverses([system[h, b, b] for h, b in index])))
    inverse = {k: v.astype(BF16) for k, v in inverse.items()}
    system = {k: v.astype(BF16) for k, v in system.items()}
    fresh = {}
    for b in range(BLOCKS):
        for h in range(heads_here):
            target = values[h][rows_of(b)]
            for c in range(b):
                target = target - mm(system[h, b, c], fresh[h, c])
            fresh[h, b] = mm(inverse[h, b], target).astype(BF16)
    for h in range(heads_here):
        cols = slice(h * HEAD_DIM, (h + 1) * HEAD_DIM)
        for b in range(BLOCKS):
            out = mm(attend[h, b, 0], fresh[h, 0])
            for c in range(1, b + 1):
                out = out + mm(attend[h, b, c], fresh[h, c])
            mean = jnp.mean(out * out, axis=-1, keepdims=True)
            mixed_ref[rows_of(b), cols] = (
                out * lax.rsqrt(jnp.maximum(mean, OUT_FLOOR)) * gain_ref[...]
            ).astype(BF16)
            if save:
                system_ref, attend_ref, inverse_ref, fresh_ref, out_ref = saved
                out_ref[rows_of(b), cols] = out
                fresh_ref[rows_of(b), cols] = fresh[h, b]
                inverse_ref[h, b] = inverse[h, b]
                for c in range(b + 1):
                    attend_ref[h, rows_of(b), rows_of(c)] = attend[h, b, c]
                    if c < b:
                        system_ref[h, rows_of(b), rows_of(c)] = system[h, b, c]


def mix_forward(qkv, logit, taps, gain, masks, seg_col, seg_row, save, per=1):
    heads = logit.shape[1]
    width = per * HEAD_DIM
    full = lambda shape: pl.BlockSpec(shape, lambda h: (0,) * len(shape))
    out_shape = [jax.ShapeDtypeStruct((TOK_MB, heads * HEAD_DIM), BF16)]
    out_specs = [pl.BlockSpec((TOK_MB, width), lambda h: (0, h))]
    if save:
        out_shape += [
            jax.ShapeDtypeStruct((heads, TOK_MB, TOK_MB), BF16),
            jax.ShapeDtypeStruct((heads, TOK_MB, TOK_MB), BF16),
            jax.ShapeDtypeStruct((heads, BLOCKS, BLOCK, BLOCK), BF16),
            jax.ShapeDtypeStruct((TOK_MB, heads * HEAD_DIM), BF16),
            jax.ShapeDtypeStruct((TOK_MB, heads * HEAD_DIM), F32),
        ]
        out_specs += [
            pl.BlockSpec((per, TOK_MB, TOK_MB), lambda h: (h, 0, 0)),
            pl.BlockSpec((per, TOK_MB, TOK_MB), lambda h: (h, 0, 0)),
            pl.BlockSpec((per, BLOCKS, BLOCK, BLOCK), lambda h: (h, 0, 0, 0)),
            pl.BlockSpec((TOK_MB, width), lambda h: (0, h)),
            pl.BlockSpec((TOK_MB, width), lambda h: (0, h)),
        ]
    return pl.pallas_call(
        functools.partial(forward_kernel, per, save),
        grid=(heads // per,),
        in_specs=[
            pl.BlockSpec((3, TOK_MB, width), lambda h: (0, 0, h)),
            full(logit.shape),
            pl.BlockSpec((3, CONV, width), lambda h: (0, 0, h)),
            full(gain.shape),
            full(masks.shape),
            full(seg_col.shape),
            full(seg_row.shape),
        ],
        out_specs=out_specs,
        out_shape=out_shape,
        compiler_params=pltpu.CompilerParams(vmem_limit_bytes=48 * 1024 * 1024),
        cost_estimate=pl.CostEstimate(flops=heads * 10**9, bytes_accessed=heads * 10**6, transcendentals=0),
    )(qkv, logit, taps, gain, masks, seg_col, seg_row)


def stream_back(grad, x, pre, gate, taps, masks, taps_out, j, cols):
    grad_pre = grad * gate * (1.0 + pre * (1.0 - gate))
    grad_x = taps[0:1] * grad_pre
    taps_out[j, 0:1, cols] = jnp.sum(grad_pre * x, axis=0, keepdims=True)
    for tap in range(1, CONV):
        masked = grad_pre * masks[tap - 1]
        grad_x = grad_x + taps[tap : tap + 1] * pltpu.roll(masked, TOK_MB - tap, 0)
        taps_out[j, tap : tap + 1, cols] = jnp.sum(masked * pltpu.roll(x, tap, 0), axis=0, keepdims=True)
    return grad_x


def backward_kernel(heads_here, qkv_ref, logit_ref, taps_ref, gain_ref, masks_ref, seg_col_ref, seg_row_ref,
                    system_ref, attend_ref, inverse_ref, fresh_ref, out_ref, grad_ref,
                    grad_qkv_ref, grad_logit_ref, grad_taps_ref, grad_gain_ref):
    step = pl.program_id(0)

    @pl.when(step == 0)
    def _():
        grad_logit_ref[...] = jnp.zeros(grad_logit_ref.shape, F32)
        grad_gain_ref[...] = jnp.zeros(grad_gain_ref.shape, F32)

    masks = [masks_ref[i] for i in range(CONV - 1)]
    logits = logit_ref[...]
    lane = lax.broadcasted_iota(jnp.int32, logits.shape, 1)
    wide = lax.broadcasted_iota(jnp.int32, (TOK_MB, HEAD_DIM), 1)
    row = lax.broadcasted_iota(jnp.int32, (BLOCK, BLOCK), 0)
    col = lax.broadcasted_iota(jnp.int32, (BLOCK, BLOCK), 1)
    strict = col < row
    lower = col <= row
    same = {}
    for b in range(BLOCKS):
        for c in range(b + 1):
            same[b, c] = seg_col_ref[rows_of(b), :] == seg_row_ref[:, rows_of(c)]
    for h in range(heads_here):
        cols = slice(h * HEAD_DIM, (h + 1) * HEAD_DIM)
        taps = [taps_ref[j, :, cols] for j in range(3)]
        inputs = [qkv_ref[j, :, cols] for j in range(3)]
        pre_q, gate_q, conv_q = stream(inputs[0], taps[0], masks)
        pre_k, gate_k, conv_k = stream(inputs[1], taps[1], masks)
        pre_v, gate_v, value = stream(inputs[2], taps[2], masks)
        scale_q = lax.rsqrt(jnp.sum(conv_q * conv_q, axis=-1, keepdims=True) + EPS)
        scale_k = lax.rsqrt(jnp.sum(conv_k * conv_k, axis=-1, keepdims=True) + EPS)
        unit_q = conv_q * scale_q
        key = conv_k * scale_k
        query = (unit_q * HEAD_DIM**-0.5).astype(BF16)
        key_b = key.astype(BF16)
        logit = jnp.sum(jnp.where(lane == step * heads_here + h, logits, 0.0), axis=1, keepdims=True)
        beta = jax.nn.sigmoid(logit)

        out = out_ref[:, cols]
        grad_mixed = grad_ref[:, cols]
        mean = jnp.mean(out * out, axis=-1, keepdims=True)
        scale = lax.rsqrt(jnp.maximum(mean, OUT_FLOOR))
        unit = out * scale
        grad_gain_ref[...] += jnp.sum((grad_mixed * unit).reshape(TOK_MB // 8, 8, HEAD_DIM), axis=0)
        grad_unit = grad_mixed * gain_ref[...]
        through = jnp.where(mean > OUT_FLOOR, 1.0, jnp.where(mean == OUT_FLOOR, 0.5, 0.0))
        grad_out = scale * (
            grad_unit - unit * (through * jnp.mean(grad_unit * unit, axis=-1, keepdims=True))
        )
        grad_out = grad_out.astype(BF16)
        fresh = [fresh_ref[rows_of(b), cols] for b in range(BLOCKS)]
        d_out = [grad_out[rows_of(b)] for b in range(BLOCKS)]
        d_fresh = [None] * BLOCKS
        for c in range(BLOCKS):
            total = t_mm(attend_ref[h, rows_of(c), rows_of(c)], d_out[c])
            for b in range(c + 1, BLOCKS):
                total = total + t_mm(attend_ref[h, rows_of(b), rows_of(c)], d_out[b])
            d_fresh[c] = total
        d_target = [None] * BLOCKS
        for b in reversed(range(BLOCKS)):
            d_target[b] = t_mm(inverse_ref[h, b], d_fresh[b])
            for c in range(b):
                d_fresh[c] = d_fresh[c] - t_mm(system_ref[h, rows_of(b), rows_of(c)], d_target[b])
        d_target_b = [d.astype(BF16) for d in d_target]
        grad_query = []
        inner = []
        grad_key = [None] * BLOCKS
        key_blocks = [key_b[rows_of(b)] for b in range(BLOCKS)]
        for b in range(BLOCKS):
            dq = None
            da = None
            beta_row = beta[rows_of(b)]
            for c in range(b + 1):
                d_attend = mm_t(d_out[b], fresh[c])
                keep = same[b, c] & lower if b == c else same[b, c]
                d_attend = jnp.where(keep, d_attend, 0.0).astype(BF16)
                d_system = mm_t(d_target_b[b], fresh[c])
                keep = same[b, c] & strict if b == c else same[b, c]
                d_system = jnp.where(keep, -d_system, 0.0)
                part = mm(d_attend, key_blocks[c])
                dq = part if dq is None else dq + part
                part = mm(d_system, key_blocks[c])
                da = part if da is None else da + part
                part = t_mm(d_attend, query[rows_of(b)]) + t_mm(d_system * beta_row, key_blocks[b])
                grad_key[c] = part if grad_key[c] is None else grad_key[c] + part
            grad_query.append(dq)
            inner.append(da)
        inner = jnp.concatenate(inner, axis=0)
        grad_query = jnp.concatenate(grad_query, axis=0)
        grad_key = jnp.concatenate(grad_key, axis=0) + beta * inner
        d_target = jnp.concatenate(d_target, axis=0)
        grad_beta = jnp.sum(inner * key + d_target * value, axis=-1, keepdims=True)
        grad_logit = grad_beta * beta * (1.0 - beta)
        grad_logit_ref[...] += jnp.where(wide == step * heads_here + h, grad_logit, 0.0)
        grad_value = beta * d_target
        grad_conv_q = (HEAD_DIM**-0.5 * scale_q) * (
            grad_query - unit_q * jnp.sum(grad_query * unit_q, axis=-1, keepdims=True)
        )
        grad_conv_k = scale_k * (grad_key - key * jnp.sum(grad_key * key, axis=-1, keepdims=True))
        for j, (grad, pre, gate) in enumerate(
            ((grad_conv_q, pre_q, gate_q), (grad_conv_k, pre_k, gate_k), (grad_value, pre_v, gate_v))
        ):
            grad_x = stream_back(grad, inputs[j], pre, gate, taps[j], masks, grad_taps_ref, j, cols)
            grad_qkv_ref[j, :, cols] = grad_x.astype(BF16)


def mix_backward(qkv, logit, taps, gain, masks, seg_col, seg_row, saved, grad_mixed, per=1):
    heads = logit.shape[1]
    width = per * HEAD_DIM
    full = lambda shape: pl.BlockSpec(shape, lambda h: (0,) * len(shape))
    rows = pl.BlockSpec((TOK_MB, width), lambda h: (0, h))
    return pl.pallas_call(
        functools.partial(backward_kernel, per),
        grid=(heads // per,),
        in_specs=[
            pl.BlockSpec((3, TOK_MB, width), lambda h: (0, 0, h)),
            full(logit.shape),
            pl.BlockSpec((3, CONV, width), lambda h: (0, 0, h)),
            full(gain.shape),
            full(masks.shape),
            full(seg_col.shape),
            full(seg_row.shape),
            pl.BlockSpec((per, TOK_MB, TOK_MB), lambda h: (h, 0, 0)),
            pl.BlockSpec((per, TOK_MB, TOK_MB), lambda h: (h, 0, 0)),
            pl.BlockSpec((per, BLOCKS, BLOCK, BLOCK), lambda h: (h, 0, 0, 0)),
            rows,
            rows,
            rows,
        ],
        out_specs=[
            pl.BlockSpec((3, TOK_MB, width), lambda h: (0, 0, h)),
            full((TOK_MB, HEAD_DIM)),
            pl.BlockSpec((3, CONV, width), lambda h: (0, 0, h)),
            full((8, HEAD_DIM)),
        ],
        out_shape=[
            jax.ShapeDtypeStruct((3, TOK_MB, heads * HEAD_DIM), BF16),
            jax.ShapeDtypeStruct((TOK_MB, HEAD_DIM), F32),
            jax.ShapeDtypeStruct((3, CONV, heads * HEAD_DIM), F32),
            jax.ShapeDtypeStruct((8, HEAD_DIM), F32),
        ],
        compiler_params=pltpu.CompilerParams(vmem_limit_bytes=48 * 1024 * 1024),
        cost_estimate=pl.CostEstimate(flops=heads * 10**9, bytes_accessed=heads * 2 * 10**6, transcendentals=0),
    )(qkv, logit, taps, gain, masks, seg_col, seg_row, *saved, grad_mixed)


def tap_masks(segment):
    masks = []
    for tap in range(1, CONV):
        earlier = jnp.concatenate([jnp.full((tap,), -1, jnp.int32), segment[: TOK_MB - tap]], axis=0)
        masks.append(jnp.broadcast_to((earlier == segment).astype(F32)[:, None], (TOK_MB, HEAD_DIM)))
    return jnp.stack(masks)


def narrow(values):
    return values.astype(BF16)


def product(left, right):
    return jnp.dot(left, right, preferred_element_type=F32)


def product_left(left, right):
    return lax.dot_general(left, right, (((0,), (0,)), ((), ())), preferred_element_type=F32)


def product_right(left, right):
    return lax.dot_general(left, right, (((1,), (1,)), ((), ())), preferred_element_type=F32)


def rms_parts(values):
    scale = lax.rsqrt(jnp.mean(values * values, axis=-1, keepdims=True) + EPS)
    return (values * scale, scale)


def norm_back(grad_normed, normed, scale, gain):
    grad_scaled = grad_normed * gain
    return scale * (grad_scaled - normed * jnp.mean(grad_scaled * normed, axis=-1, keepdims=True))


def segment_ids(lengths, count):
    ends = jnp.cumsum(lengths)
    places = jnp.arange(count, dtype=jnp.int32)
    return jnp.sum((places[:, None] >= ends[None, :]).astype(jnp.int32), axis=1, dtype=jnp.int32)


def flipped(values, axis, bit):
    return lax.ppermute(values, axis, [(i, i ^ bit) for i in range(lax.axis_size(axis))])


def shifted(values, axis, distance):
    devices = range(lax.axis_size(axis))
    return lax.ppermute(values, axis, [(i, i + distance) for i in devices if i + distance in devices])


def bits_of(axis):
    size = lax.axis_size(axis)
    bits = [1 << k for k in range(size.bit_length() - 1)]
    assert 1 << len(bits) == size
    return bits


def summed(values, axes):
    for axis in axes:
        for bit in bits_of(axis):
            values = values + flipped(values, axis, bit)
    return values


def gather(shard):
    me = lax.axis_index("head")
    parts = shard
    for place, bit in enumerate(reversed(bits_of("head"))):
        other = flipped(parts, "head", bit)
        low = (me & bit) == 0
        parts = jnp.stack([jnp.where(low, parts, other), jnp.where(low, other, parts)], axis=place)
    return parts.reshape(-1, shard.shape[-1])


def scatter(partial):
    me = lax.axis_index("head")
    bits = bits_of("head")
    parts = narrow(partial).reshape([2] * len(bits) + [-1, partial.shape[-1]])
    for place, bit in enumerate(bits):
        axis = len(bits) - 1 - place
        side = (me // bit) % 2
        mine = lax.dynamic_index_in_dim(parts, side, axis, keepdims=False)
        other = lax.dynamic_index_in_dim(parts, 1 - side, axis, keepdims=False)
        total = mine.astype(F32) + flipped(other, "head", bit).astype(F32)
        parts = narrow(total)
    return total


def line_scatter(parts, axes):
    count = lax.axis_size("dp")
    me = lax.axis_index("dp")

    def block(part, axis, index):
        size = part.shape[axis] // count
        index = jnp.clip(index, 0, count - 1)
        return lax.dynamic_slice_in_dim(part, index * size, size, axis).astype(F32)

    up = [0.0] * len(parts)
    down = [0.0] * len(parts)
    for step in range(1, count):
        up = [narrow(block(p, a, count - step + me) + u) for p, a, u in zip(parts, axes, up)]
        down = [narrow(block(p, a, step - count + me) + d) for p, a, d in zip(parts, axes, down)]
        rising = [(i, i + 1) for i in range(count - 1) if i < step]
        up = [lax.ppermute(u, "dp", rising).astype(F32) for u in up]
        falling = [(count - 1 - i, count - 2 - i) for i in range(count - 1) if i < step]
        down = [lax.ppermute(d, "dp", falling).astype(F32) for d in down]
    return [block(p, a, me) + u + d for p, a, u, d in zip(parts, axes, up, down)]


def per_device(
    tokens,
    lengths,
    cotangent,
    attn_in,
    beta_weight,
    conv_weight,
    o_gain,
    attn_out,
    mlp_in,
    mlp_out,
    norm_gains,
):
    section = lax.axis_index("section")
    sections = lax.axis_size("section")
    member = lax.axis_index("head")
    micro = tokens.shape[0]
    width = tokens.shape[2]
    heads = beta_weight.shape[2]
    share = TOK_MB // lax.axis_size("head")
    projections = attn_in[0]
    gate_proj = beta_weight[0]
    taps = conv_weight[0]
    head_gain = o_gain
    merge_weight = attn_out[0]
    expand = mlp_in[0]
    contract_weight = mlp_out[0]
    gains = norm_gains[0]
    every = range(micro)
    segments = [segment_ids(lengths[m], TOK_MB) for m in every]
    masks = [(tap_masks(s), s[:, None], s[None, :]) for s in segments]
    own_rows = lambda values: lax.dynamic_slice_in_dim(values, member * share, share, 0).astype(F32)
    tokens_own = [own_rows(tokens[m]) for m in every]
    cotangent_own = [own_rows(cotangent[m]) for m in every]

    def forward(x, mine):
        unit, scale = rms_parts(x)
        normed = gather(narrow(unit * gains[0]))
        qkv = jnp.stack([product(normed, projections[j]) for j in range(3)])
        logit = product(normed, gate_proj)
        mixed, *saved = mix_forward(qkv, logit, taps, head_gain, *mine, True, heads)
        middle = x + scatter(product(mixed, merge_weight))
        unit_mid, scale_mid = rms_parts(middle)
        normed_mid = gather(narrow(unit_mid * gains[1]))
        gate_in = product(normed_mid, expand[0])
        up_in = product(normed_mid, expand[1])
        hidden = narrow(jax.nn.silu(gate_in) * up_in)
        result = middle + scatter(product(hidden, contract_weight))
        kept = (unit, scale, normed, qkv, logit, mixed, saved, unit_mid, scale_mid, normed_mid, gate_in, up_in, hidden)
        return result, kept

    def backward(incoming, mine, kept, early=None):
        unit, scale, normed, qkv, logit, mixed, saved, unit_mid, scale_mid, normed_mid, gate_in, up_in, hidden = kept
        grad_out = gather(narrow(incoming))
        sigmoid_gate = jax.nn.sigmoid(gate_in)
        silu_gate = gate_in * sigmoid_gate
        grad_hidden = product_right(grad_out, contract_weight)
        grad_gate = narrow(grad_hidden * up_in * sigmoid_gate * (1.0 + gate_in * (1.0 - sigmoid_gate)))
        grad_up = narrow(grad_hidden * silu_gate)
        grad_mid = scatter(product_right(grad_gate, expand[0]) + product_right(grad_up, expand[1]))
        grad_middle = incoming + norm_back(grad_mid, unit_mid, scale_mid, gains[1])
        spread_early = None
        if early is not None:
            spread_early = early(normed_mid, grad_gate, grad_up, hidden, grad_out)
            grad_middle, spread_early = lax.optimization_barrier((grad_middle, spread_early))
        gain_two = jnp.sum(grad_mid * unit_mid, axis=0)
        grad_branch = gather(narrow(grad_middle))
        grad_mixed = product_right(grad_branch, merge_weight)
        grad_qkv, grad_logit, grad_taps, grad_head_gain = mix_backward(
            qkv, logit, taps, head_gain, *mine, saved, grad_mixed, 2 if heads % 2 == 0 else 1
        )
        grad_logit = narrow(grad_logit[:, :heads])
        grad_norm = product_right(grad_logit, gate_proj)
        for j in range(3):
            grad_norm = grad_norm + product_right(grad_qkv[j], projections[j])
        grad_norm = scatter(grad_norm)
        grad_inputs = grad_middle + norm_back(grad_norm, unit, scale, gains[0])
        gain_one = jnp.sum(grad_norm * unit, axis=0)
        big = (normed, grad_qkv, grad_logit, mixed, grad_branch, normed_mid, grad_gate, grad_up, hidden, grad_out)
        if early is not None:
            big = big[:5] + spread_early
        small = (grad_taps, jnp.sum(grad_head_gain, axis=0), jnp.stack([gain_one, gain_two]))
        return grad_inputs, big, small

    last = sections - 1
    zero = jnp.zeros((share, width), F32)
    steps = micro + last
    kept = []
    arrived = zero
    for step in range(steps):
        first = tokens_own[min(step, micro - 1)]
        inputs = jnp.where(section == 0, first, arrived)
        mine = [jnp.where(section == 0, a, b) for a, b in zip(masks[min(step, micro - 1)], masks[max(step - last, 0)])]
        result, saved = forward(inputs, mine)
        kept.append((saved, mine))
        if step < steps - 1:
            arrived = shifted(narrow(result), "section", 1).astype(F32)
    def joined(own, place, axis=0):
        picked = [terms[i][0][place] for i in range(last, micro)]
        picked.append(jnp.where(section < last, own, terms[micro][0][place]))
        return jnp.concatenate(picked, axis=axis)

    def mlp_terms(*own):
        normed_mid, grad_gate, grad_up, hidden, grad_out = (
            joined(own[place], 5 + place) for place in range(5)
        )
        grad_expand = jnp.stack([product_left(normed_mid, grad_gate), product_left(normed_mid, grad_up)])
        return narrow(grad_expand), narrow(product_left(hidden, grad_out))

    arrived = zero
    terms = [None] * steps
    finals = [None] * micro
    for step in reversed(range(steps)):
        place = step - last
        top = cotangent_own[place] if place >= 0 else zero
        incoming = jnp.where(section == last, top, arrived if step < micro else zero)
        saved, mine = kept[step]
        result, big, small = backward(incoming, mine, saved, mlp_terms if step == 0 else None)
        terms[step] = (big, small)
        if step < micro:
            finals[step] = result
        if step > 0:
            arrived = shifted(narrow(result), "section", -1).astype(F32)
    rows_out = jnp.stack(finals)
    half = width // sections
    moved = shifted(narrow(rows_out[:, :, half:]), "section", 1).astype(F32)
    grad_tokens = jnp.where(section == 0, rows_out[:, :, :half], moved)

    own = terms[0][0]
    normed, grad_qkv, grad_logit = joined(own[0], 0), joined(own[1], 1, 1), joined(own[2], 2)
    mixed, grad_branch = joined(own[3], 3), joined(own[4], 4)
    early = line_scatter([own[5], own[6]], [1, 1])
    grad_project = narrow(jnp.stack([product_left(normed, grad_qkv[j]) for j in range(3)]))
    late = [grad_project, narrow(product_left(mixed, grad_branch)), narrow(product_left(normed, grad_logit))]
    late, early = lax.optimization_barrier((late, early))
    grad_expand, grad_contract = early
    grad_project, grad_merge, grad_beta = line_scatter(late, [1, 1, 0])
    grad_taps, grad_head_gain, grad_gains = (
        sum(term[1][place] for term in terms) for place in range(3)
    )
    grad_gains = summed(jnp.concatenate([grad_gains.reshape(-1), grad_head_gain]), ("dp", "head"))
    grad_gains, grad_head_gain = grad_gains[: 2 * width].reshape(2, width), grad_gains[2 * width :]
    grad_taps = summed(grad_taps, ("dp",))
    return (
        grad_tokens,
        grad_project[None],
        grad_beta[None],
        grad_taps[None],
        grad_head_gain[None],
        grad_merge[None],
        grad_expand[None],
        grad_contract[None],
        grad_gains[None],
    )


def solution(mesh):
    return jax.shard_map(
        per_device,
        mesh=mesh,
        in_specs=(
            P("dp", None, None),
            P("dp", None),
            P("dp", None, None),
            P("section", None, None, "head"),
            P("section", None, "head"),
            P("section", None, None, "head"),
            P("section", None),
            P("section", "head", None),
            P("section", None, None, "head"),
            P("section", "head", None),
            P("section", None, None),
        ),
        out_specs=(
            P("dp", "head", "section"),
            P("section", None, "dp", "head"),
            P("section", "dp", "head"),
            P("section", None, None, "head"),
            P("section", None),
            P("section", "head", "dp"),
            P("section", None, "dp", "head"),
            P("section", "head", "dp"),
            P("section", None, None),
        ),
        check_vma=False,
    )
```

```python
import functools

import jax
import jax.numpy as jnp
from jax import lax
from jax.experimental import pallas as pl
from jax.experimental.pallas import tpu as pltpu
from jax.sharding import PartitionSpec as P

HEAD_DIM = 128
CONV = 4
TOK_MB = 384
BLOCK = 128
BLOCKS = TOK_MB // BLOCK
EPS = 1e-06
OUT_FLOOR = 0.0001
F32 = jnp.float32
BF16 = jnp.bfloat16
BASE = 4


def mm(left, right):
    return lax.dot_general(
        left.astype(BF16), right.astype(BF16), (((1,), (0,)), ((), ())), preferred_element_type=F32
    )


def mm_t(left, right):
    return lax.dot_general(
        left.astype(BF16), right.astype(BF16), (((1,), (1,)), ((), ())), preferred_element_type=F32
    )


def t_mm(left, right):
    return lax.dot_general(
        left.astype(BF16), right.astype(BF16), (((0,), (0,)), ((), ())), preferred_element_type=F32
    )


def rows_of(b):
    return slice(b * BLOCK, (b + 1) * BLOCK)


def stream(x, taps, masks):
    pre = taps[0:1] * x
    for tap in range(1, CONV):
        pre = pre + taps[tap : tap + 1] * (pltpu.roll(x, tap, 0) * masks[tap - 1])
    gate = jax.nn.sigmoid(pre)
    return pre, gate, pre * gate


def unit_inverses(systems):
    size = systems[0].shape[0]
    row = lax.broadcasted_iota(jnp.int32, (size, size), 0)
    col = lax.broadcasted_iota(jnp.int32, (size, size), 1)
    eye = (row == col).astype(F32)
    near = (row // BASE == col // BASE).astype(F32)
    first = [-a * near for a in systems]
    power = 1
    total = [eye + n for n in first]
    second = [mm(n, n) for n in first]
    third = [mm(n, s) for n, s in zip(first, second)]
    total = [t + s + r for t, s, r in zip(total, second, third)]
    step = BASE
    while step < size:
        span = 2 * step
        off = ((row // span == col // span) & (row // step != col // step)).astype(F32)
        inner = [mm(a * off, t) for a, t in zip(systems, total)]
        outer = [mm(t, i) for t, i in zip(total, inner)]
        total = [t - o for t, o in zip(total, outer)]
        step = span
    return total


def forward_kernel(heads_here, save, qkv_ref, logit_ref, taps_ref, gain_ref, masks_ref, seg_col_ref, seg_row_ref, mixed_ref, *saved):
    step = pl.program_id(0)
    masks = [masks_ref[i] for i in range(CONV - 1)]
    logits = logit_ref[...]
    lane = lax.broadcasted_iota(jnp.int32, logits.shape, 1)
    row = lax.broadcasted_iota(jnp.int32, (BLOCK, BLOCK), 0)
    col = lax.broadcasted_iota(jnp.int32, (BLOCK, BLOCK), 1)
    strict = col < row
    lower = col <= row
    same = {}
    for b in range(BLOCKS):
        for c in range(b + 1):
            same[b, c] = seg_col_ref[rows_of(b), :] == seg_row_ref[:, rows_of(c)]
    queries, keys, values, betas = [], [], [], []
    for h in range(heads_here):
        cols = slice(h * HEAD_DIM, (h + 1) * HEAD_DIM)
        taps = [taps_ref[j, :, cols] for j in range(3)]
        _, _, query = stream(qkv_ref[0, :, cols], taps[0], masks)
        _, _, key = stream(qkv_ref[1, :, cols], taps[1], masks)
        _, _, value = stream(qkv_ref[2, :, cols], taps[2], masks)
        query = query * lax.rsqrt(jnp.sum(query * query, axis=-1, keepdims=True) + EPS) * HEAD_DIM**-0.5
        key = key * lax.rsqrt(jnp.sum(key * key, axis=-1, keepdims=True) + EPS)
        logit = jnp.sum(jnp.where(lane == step * heads_here + h, logits, 0.0), axis=1, keepdims=True)
        beta = jax.nn.sigmoid(logit)
        queries.append(query.astype(BF16))
        keys.append(key.astype(BF16))
        values.append(value * beta)
        betas.append(beta)
    attend, system = {}, {}
    for h in range(heads_here):
        for b in range(BLOCKS):
            for c in range(b + 1):
                inner = mm_t(keys[h][rows_of(b)], keys[h][rows_of(c)])
                keep = same[b, c] & strict if b == c else same[b, c]
                system[h, b, c] = jnp.where(keep, inner * betas[h][rows_of(b)], 0.0)
                scores = mm_t(queries[h][rows_of(b)], keys[h][rows_of(c)])
                keep = same[b, c] & lower if b == c else same[b, c]
                attend[h, b, c] = jnp.where(keep, scores, 0.0).astype(BF16)
    index = [(h, b) for h in range(heads_here) for b in range(BLOCKS)]
    inverse = dict(zip(index, unit_inverses([system[h, b, b] for h, b in index])))
    inverse = {k: v.astype(BF16) for k, v in inverse.items()}
    system = {k: v.astype(BF16) for k, v in system.items()}
    fresh = {}
    for b in range(BLOCKS):
        for h in range(heads_here):
            target = values[h][rows_of(b)]
            for c in range(b):
                target = target - mm(system[h, b, c], fresh[h, c])
            fresh[h, b] = mm(inverse[h, b], target).astype(BF16)
    for h in range(heads_here):
        cols = slice(h * HEAD_DIM, (h + 1) * HEAD_DIM)
        for b in range(BLOCKS):
            out = mm(attend[h, b, 0], fresh[h, 0])
            for c in range(1, b + 1):
                out = out + mm(attend[h, b, c], fresh[h, c])
            mean = jnp.mean(out * out, axis=-1, keepdims=True)
            mixed_ref[rows_of(b), cols] = (
                out * lax.rsqrt(jnp.maximum(mean, OUT_FLOOR)) * gain_ref[...]
            ).astype(BF16)
            if save:
                system_ref, attend_ref, inverse_ref, fresh_ref, out_ref = saved
                out_ref[rows_of(b), cols] = out
                fresh_ref[rows_of(b), cols] = fresh[h, b]
                inverse_ref[h, b] = inverse[h, b]
                for c in range(b + 1):
                    attend_ref[h, rows_of(b), rows_of(c)] = attend[h, b, c]
                    if c < b:
                        system_ref[h, rows_of(b), rows_of(c)] = system[h, b, c]


def mix_forward(qkv, logit, taps, gain, masks, seg_col, seg_row, save, per=1):
    heads = logit.shape[1]
    width = per * HEAD_DIM
    full = lambda shape: pl.BlockSpec(shape, lambda h: (0,) * len(shape))
    out_shape = [jax.ShapeDtypeStruct((TOK_MB, heads * HEAD_DIM), BF16)]
    out_specs = [pl.BlockSpec((TOK_MB, width), lambda h: (0, h))]
    if save:
        out_shape += [
            jax.ShapeDtypeStruct((heads, TOK_MB, TOK_MB), BF16),
            jax.ShapeDtypeStruct((heads, TOK_MB, TOK_MB), BF16),
            jax.ShapeDtypeStruct((heads, BLOCKS, BLOCK, BLOCK), BF16),
            jax.ShapeDtypeStruct((TOK_MB, heads * HEAD_DIM), BF16),
            jax.ShapeDtypeStruct((TOK_MB, heads * HEAD_DIM), F32),
        ]
        out_specs += [
            pl.BlockSpec((per, TOK_MB, TOK_MB), lambda h: (h, 0, 0)),
            pl.BlockSpec((per, TOK_MB, TOK_MB), lambda h: (h, 0, 0)),
            pl.BlockSpec((per, BLOCKS, BLOCK, BLOCK), lambda h: (h, 0, 0, 0)),
            pl.BlockSpec((TOK_MB, width), lambda h: (0, h)),
            pl.BlockSpec((TOK_MB, width), lambda h: (0, h)),
        ]
    return pl.pallas_call(
        functools.partial(forward_kernel, per, save),
        grid=(heads // per,),
        in_specs=[
            pl.BlockSpec((3, TOK_MB, width), lambda h: (0, 0, h)),
            full(logit.shape),
            pl.BlockSpec((3, CONV, width), lambda h: (0, 0, h)),
            full(gain.shape),
            full(masks.shape),
            full(seg_col.shape),
            full(seg_row.shape),
        ],
        out_specs=out_specs,
        out_shape=out_shape,
        compiler_params=pltpu.CompilerParams(vmem_limit_bytes=48 * 1024 * 1024),
        cost_estimate=pl.CostEstimate(flops=heads * 10**9, bytes_accessed=heads * 10**6, transcendentals=0),
    )(qkv, logit, taps, gain, masks, seg_col, seg_row)


def stream_back(grad, x, pre, gate, taps, masks, taps_out, j, cols):
    grad_pre = grad * gate * (1.0 + pre * (1.0 - gate))
    grad_x = taps[0:1] * grad_pre
    taps_out[j, 0:1, cols] = jnp.sum(grad_pre * x, axis=0, keepdims=True)
    for tap in range(1, CONV):
        masked = grad_pre * masks[tap - 1]
        grad_x = grad_x + taps[tap : tap + 1] * pltpu.roll(masked, TOK_MB - tap, 0)
        taps_out[j, tap : tap + 1, cols] = jnp.sum(masked * pltpu.roll(x, tap, 0), axis=0, keepdims=True)
    return grad_x


def backward_kernel(heads_here, qkv_ref, logit_ref, taps_ref, gain_ref, masks_ref, seg_col_ref, seg_row_ref,
                    system_ref, attend_ref, inverse_ref, fresh_ref, out_ref, grad_ref,
                    grad_qkv_ref, grad_logit_ref, grad_taps_ref, grad_gain_ref):
    step = pl.program_id(0)

    @pl.when(step == 0)
    def _():
        grad_logit_ref[...] = jnp.zeros(grad_logit_ref.shape, F32)
        grad_gain_ref[...] = jnp.zeros(grad_gain_ref.shape, F32)

    masks = [masks_ref[i] for i in range(CONV - 1)]
    logits = logit_ref[...]
    lane = lax.broadcasted_iota(jnp.int32, logits.shape, 1)
    wide = lax.broadcasted_iota(jnp.int32, (TOK_MB, HEAD_DIM), 1)
    row = lax.broadcasted_iota(jnp.int32, (BLOCK, BLOCK), 0)
    col = lax.broadcasted_iota(jnp.int32, (BLOCK, BLOCK), 1)
    strict = col < row
    lower = col <= row
    same = {}
    for b in range(BLOCKS):
        for c in range(b + 1):
            same[b, c] = seg_col_ref[rows_of(b), :] == seg_row_ref[:, rows_of(c)]
    for h in range(heads_here):
        cols = slice(h * HEAD_DIM, (h + 1) * HEAD_DIM)
        taps = [taps_ref[j, :, cols] for j in range(3)]
        inputs = [qkv_ref[j, :, cols] for j in range(3)]
        pre_q, gate_q, conv_q = stream(inputs[0], taps[0], masks)
        pre_k, gate_k, conv_k = stream(inputs[1], taps[1], masks)
        pre_v, gate_v, value = stream(inputs[2], taps[2], masks)
        scale_q = lax.rsqrt(jnp.sum(conv_q * conv_q, axis=-1, keepdims=True) + EPS)
        scale_k = lax.rsqrt(jnp.sum(conv_k * conv_k, axis=-1, keepdims=True) + EPS)
        unit_q = conv_q * scale_q
        key = conv_k * scale_k
        query = (unit_q * HEAD_DIM**-0.5).astype(BF16)
        key_b = key.astype(BF16)
        logit = jnp.sum(jnp.where(lane == step * heads_here + h, logits, 0.0), axis=1, keepdims=True)
        beta = jax.nn.sigmoid(logit)

        out = out_ref[:, cols]
        grad_mixed = grad_ref[:, cols]
        mean = jnp.mean(out * out, axis=-1, keepdims=True)
        scale = lax.rsqrt(jnp.maximum(mean, OUT_FLOOR))
        unit = out * scale
        grad_gain_ref[...] += jnp.sum((grad_mixed * unit).reshape(TOK_MB // 8, 8, HEAD_DIM), axis=0)
        grad_unit = grad_mixed * gain_ref[...]
        through = jnp.where(mean > OUT_FLOOR, 1.0, jnp.where(mean == OUT_FLOOR, 0.5, 0.0))
        grad_out = scale * (
            grad_unit - unit * (through * jnp.mean(grad_unit * unit, axis=-1, keepdims=True))
        )
        grad_out = grad_out.astype(BF16)
        fresh = [fresh_ref[rows_of(b), cols] for b in range(BLOCKS)]
        d_out = [grad_out[rows_of(b)] for b in range(BLOCKS)]
        d_fresh = [None] * BLOCKS
        for c in range(BLOCKS):
            total = t_mm(attend_ref[h, rows_of(c), rows_of(c)], d_out[c])
            for b in range(c + 1, BLOCKS):
                total = total + t_mm(attend_ref[h, rows_of(b), rows_of(c)], d_out[b])
            d_fresh[c] = total
        d_target = [None] * BLOCKS
        for b in reversed(range(BLOCKS)):
            d_target[b] = t_mm(inverse_ref[h, b], d_fresh[b])
            for c in range(b):
                d_fresh[c] = d_fresh[c] - t_mm(system_ref[h, rows_of(b), rows_of(c)], d_target[b])
        d_target_b = [d.astype(BF16) for d in d_target]
        grad_query = []
        inner = []
        grad_key = [None] * BLOCKS
        key_blocks = [key_b[rows_of(b)] for b in range(BLOCKS)]
        for b in range(BLOCKS):
            dq = None
            da = None
            beta_row = beta[rows_of(b)]
            for c in range(b + 1):
                d_attend = mm_t(d_out[b], fresh[c])
                keep = same[b, c] & lower if b == c else same[b, c]
                d_attend = jnp.where(keep, d_attend, 0.0).astype(BF16)
                d_system = mm_t(d_target_b[b], fresh[c])
                keep = same[b, c] & strict if b == c else same[b, c]
                d_system = jnp.where(keep, -d_system, 0.0)
                part = mm(d_attend, key_blocks[c])
                dq = part if dq is None else dq + part
                part = mm(d_system, key_blocks[c])
                da = part if da is None else da + part
                part = t_mm(d_attend, query[rows_of(b)]) + t_mm(d_system * beta_row, key_blocks[b])
                grad_key[c] = part if grad_key[c] is None else grad_key[c] + part
            grad_query.append(dq)
            inner.append(da)
        inner = jnp.concatenate(inner, axis=0)
        grad_query = jnp.concatenate(grad_query, axis=0)
        grad_key = jnp.concatenate(grad_key, axis=0) + beta * inner
        d_target = jnp.concatenate(d_target, axis=0)
        grad_beta = jnp.sum(inner * key + d_target * value, axis=-1, keepdims=True)
        grad_logit = grad_beta * beta * (1.0 - beta)
        grad_logit_ref[...] += jnp.where(wide == step * heads_here + h, grad_logit, 0.0)
        grad_value = beta * d_target
        grad_conv_q = (HEAD_DIM**-0.5 * scale_q) * (
            grad_query - unit_q * jnp.sum(grad_query * unit_q, axis=-1, keepdims=True)
        )
        grad_conv_k = scale_k * (grad_key - key * jnp.sum(grad_key * key, axis=-1, keepdims=True))
        for j, (grad, pre, gate) in enumerate(
            ((grad_conv_q, pre_q, gate_q), (grad_conv_k, pre_k, gate_k), (grad_value, pre_v, gate_v))
        ):
            grad_x = stream_back(grad, inputs[j], pre, gate, taps[j], masks, grad_taps_ref, j, cols)
            grad_qkv_ref[j, :, cols] = grad_x.astype(BF16)


def mix_backward(qkv, logit, taps, gain, masks, seg_col, seg_row, saved, grad_mixed, per=1):
    heads = logit.shape[1]
    width = per * HEAD_DIM
    full = lambda shape: pl.BlockSpec(shape, lambda h: (0,) * len(shape))
    rows = pl.BlockSpec((TOK_MB, width), lambda h: (0, h))
    return pl.pallas_call(
        functools.partial(backward_kernel, per),
        grid=(heads // per,),
        in_specs=[
            pl.BlockSpec((3, TOK_MB, width), lambda h: (0, 0, h)),
            full(logit.shape),
            pl.BlockSpec((3, CONV, width), lambda h: (0, 0, h)),
            full(gain.shape),
            full(masks.shape),
            full(seg_col.shape),
            full(seg_row.shape),
            pl.BlockSpec((per, TOK_MB, TOK_MB), lambda h: (h, 0, 0)),
            pl.BlockSpec((per, TOK_MB, TOK_MB), lambda h: (h, 0, 0)),
            pl.BlockSpec((per, BLOCKS, BLOCK, BLOCK), lambda h: (h, 0, 0, 0)),
            rows,
            rows,
            rows,
        ],
        out_specs=[
            pl.BlockSpec((3, TOK_MB, width), lambda h: (0, 0, h)),
            full((TOK_MB, HEAD_DIM)),
            pl.BlockSpec((3, CONV, width), lambda h: (0, 0, h)),
            full((8, HEAD_DIM)),
        ],
        out_shape=[
            jax.ShapeDtypeStruct((3, TOK_MB, heads * HEAD_DIM), BF16),
            jax.ShapeDtypeStruct((TOK_MB, HEAD_DIM), F32),
            jax.ShapeDtypeStruct((3, CONV, heads * HEAD_DIM), F32),
            jax.ShapeDtypeStruct((8, HEAD_DIM), F32),
        ],
        compiler_params=pltpu.CompilerParams(vmem_limit_bytes=48 * 1024 * 1024),
        cost_estimate=pl.CostEstimate(flops=heads * 10**9, bytes_accessed=heads * 2 * 10**6, transcendentals=0),
    )(qkv, logit, taps, gain, masks, seg_col, seg_row, *saved, grad_mixed)


def tap_masks(segment):
    masks = []
    for tap in range(1, CONV):
        earlier = jnp.concatenate([jnp.full((tap,), -1, jnp.int32), segment[: TOK_MB - tap]], axis=0)
        masks.append(jnp.broadcast_to((earlier == segment).astype(F32)[:, None], (TOK_MB, HEAD_DIM)))
    return jnp.stack(masks)


def narrow(values):
    return values.astype(BF16)


def product(left, right):
    return jnp.dot(left, right, preferred_element_type=F32)


def product_left(left, right):
    return lax.dot_general(left, right, (((0,), (0,)), ((), ())), preferred_element_type=F32)


def product_right(left, right):
    return lax.dot_general(left, right, (((1,), (1,)), ((), ())), preferred_element_type=F32)


def rms_parts(values):
    scale = lax.rsqrt(jnp.mean(values * values, axis=-1, keepdims=True) + EPS)
    return (values * scale, scale)


def norm_back(grad_normed, normed, scale, gain):
    grad_scaled = grad_normed * gain
    return scale * (grad_scaled - normed * jnp.mean(grad_scaled * normed, axis=-1, keepdims=True))


def segment_ids(lengths, count):
    ends = jnp.cumsum(lengths)
    places = jnp.arange(count, dtype=jnp.int32)
    return jnp.sum((places[:, None] >= ends[None, :]).astype(jnp.int32), axis=1, dtype=jnp.int32)


def flipped(values, axis, bit):
    return lax.ppermute(values, axis, [(i, i ^ bit) for i in range(lax.axis_size(axis))])


def shifted(values, axis, distance):
    devices = range(lax.axis_size(axis))
    return lax.ppermute(values, axis, [(i, i + distance) for i in devices if i + distance in devices])


def bits_of(axis):
    size = lax.axis_size(axis)
    bits = [1 << k for k in range(size.bit_length() - 1)]
    assert 1 << len(bits) == size
    return bits


def summed(values, axes):
    for axis in axes:
        for bit in bits_of(axis):
            values = values + flipped(values, axis, bit)
    return values


def gather(shard):
    me = lax.axis_index("head")
    parts = shard
    for place, bit in enumerate(reversed(bits_of("head"))):
        other = flipped(parts, "head", bit)
        low = (me & bit) == 0
        parts = jnp.stack([jnp.where(low, parts, other), jnp.where(low, other, parts)], axis=place)
    return parts.reshape(-1, shard.shape[-1])


def scatter(partial):
    me = lax.axis_index("head")
    bits = bits_of("head")
    parts = narrow(partial).reshape([2] * len(bits) + [-1, partial.shape[-1]])
    for place, bit in enumerate(bits):
        axis = len(bits) - 1 - place
        side = (me // bit) % 2
        mine = lax.dynamic_index_in_dim(parts, side, axis, keepdims=False)
        other = lax.dynamic_index_in_dim(parts, 1 - side, axis, keepdims=False)
        total = mine.astype(F32) + flipped(other, "head", bit).astype(F32)
        parts = narrow(total)
    return total


def swapped(shard):
    count = lax.axis_size("dp")
    me = lax.axis_index("dp")
    rows, width = shard.shape
    blocks = shard.reshape(rows, count, width // count)
    arrived = []
    for distance in range(count):
        block = lax.dynamic_index_in_dim(blocks, (me + distance) % count, 1, keepdims=False)
        if distance:
            block = lax.ppermute(block, "dp", [(i, (i + distance) % count) for i in range(count)])
        arrived.append(block)
    arrived = jnp.stack(arrived)
    ordered = [lax.dynamic_index_in_dim(arrived, (me - q) % count, 0, keepdims=False) for q in range(count)]
    return jnp.concatenate(ordered, axis=1)


def per_device(
    tokens,
    lengths,
    cotangent,
    attn_in,
    beta_weight,
    conv_weight,
    o_gain,
    attn_out,
    mlp_in,
    mlp_out,
    norm_gains,
):
    section = lax.axis_index("section")
    sections = lax.axis_size("section")
    member = lax.axis_index("head")
    micro = tokens.shape[0]
    width = tokens.shape[2]
    heads = beta_weight.shape[2]
    share = TOK_MB // lax.axis_size("head")
    projections = attn_in[0]
    gate_proj = beta_weight[0]
    taps = conv_weight[0]
    head_gain = o_gain
    merge_weight = attn_out[0]
    expand = mlp_in[0]
    contract_weight = mlp_out[0]
    gains = norm_gains[0]
    every = range(micro)
    segments = [segment_ids(lengths[m], TOK_MB) for m in every]
    masks = [(tap_masks(s), s[:, None], s[None, :]) for s in segments]
    own_rows = lambda values: lax.dynamic_slice_in_dim(values, member * share, share, 0).astype(F32)
    tokens_own = [own_rows(tokens[m]) for m in every]
    cotangent_own = [own_rows(cotangent[m]) for m in every]

    def forward(x, mine):
        unit, scale = rms_parts(x)
        normed = gather(narrow(unit * gains[0]))
        qkv = jnp.stack([product(normed, projections[j]) for j in range(3)])
        logit = product(normed, gate_proj)
        mixed, *saved = mix_forward(qkv, logit, taps, head_gain, *mine, True, heads)
        middle = x + scatter(product(mixed, merge_weight))
        unit_mid, scale_mid = rms_parts(middle)
        normed_mid = gather(narrow(unit_mid * gains[1]))
        gate_in = product(normed_mid, expand[0])
        up_in = product(normed_mid, expand[1])
        hidden = narrow(jax.nn.silu(gate_in) * up_in)
        result = middle + scatter(product(hidden, contract_weight))
        kept = (unit, scale, normed, qkv, logit, mixed, saved, unit_mid, scale_mid, normed_mid, gate_in, up_in, hidden)
        return result, kept

    def backward(incoming, mine, kept, early=None):
        unit, scale, normed, qkv, logit, mixed, saved, unit_mid, scale_mid, normed_mid, gate_in, up_in, hidden = kept
        grad_out = gather(narrow(incoming))
        sigmoid_gate = jax.nn.sigmoid(gate_in)
        silu_gate = gate_in * sigmoid_gate
        grad_hidden = product_right(grad_out, contract_weight)
        grad_gate = narrow(grad_hidden * up_in * sigmoid_gate * (1.0 + gate_in * (1.0 - sigmoid_gate)))
        grad_up = narrow(grad_hidden * silu_gate)
        grad_mid = scatter(product_right(grad_gate, expand[0]) + product_right(grad_up, expand[1]))
        grad_middle = incoming + norm_back(grad_mid, unit_mid, scale_mid, gains[1])
        spread_early = None
        if early is not None:
            spread_early = early(normed_mid, grad_gate, grad_up)
            grad_middle, spread_early = lax.optimization_barrier((grad_middle, spread_early))
        gain_two = jnp.sum(grad_mid * unit_mid, axis=0)
        grad_branch = gather(narrow(grad_middle))
        grad_mixed = product_right(grad_branch, merge_weight)
        grad_qkv, grad_logit, grad_taps, grad_head_gain = mix_backward(
            qkv, logit, taps, head_gain, *mine, saved, grad_mixed, 2 if heads % 2 == 0 else 1
        )
        grad_logit = narrow(grad_logit[:, :heads])
        grad_norm = product_right(grad_logit, gate_proj)
        for j in range(3):
            grad_norm = grad_norm + product_right(grad_qkv[j], projections[j])
        grad_norm = scatter(grad_norm)
        grad_inputs = grad_middle + norm_back(grad_norm, unit, scale, gains[0])
        gain_one = jnp.sum(grad_norm * unit, axis=0)
        big = (normed, grad_qkv, grad_logit, narrow(incoming), narrow(grad_middle))
        big += (normed_mid, grad_gate, grad_up) if early is None else (spread_early,)
        small = (grad_taps, jnp.sum(grad_head_gain, axis=0), jnp.stack([gain_one, gain_two]))
        return grad_inputs, big, small

    last = sections - 1
    zero = jnp.zeros((share, width), F32)
    steps = micro + last
    kept = []
    arrived = zero
    for step in range(steps):
        first = tokens_own[min(step, micro - 1)]
        inputs = jnp.where(section == 0, first, arrived)
        mine = [jnp.where(section == 0, a, b) for a, b in zip(masks[min(step, micro - 1)], masks[max(step - last, 0)])]
        result, saved = forward(inputs, mine)
        kept.append((saved, mine))
        if step < steps - 1:
            arrived = shifted(narrow(result), "section", 1).astype(F32)
    def picked(values, own=None):
        chosen = [values[i] for i in range(last, micro)]
        for i in range(last):
            first = values[i] if own is None else own
            chosen.append(jnp.where(section <= i, first, values[i + micro]))
        return chosen

    def joined(own, place, axis=0):
        return jnp.concatenate(picked([term and term[0][place] for term in terms], own), axis=axis)

    def mlp_terms(*own):
        normed_mid, grad_gate, grad_up = (joined(own[place], 5 + place) for place in range(3))
        return narrow(jnp.stack([product_left(normed_mid, grad_gate), product_left(normed_mid, grad_up)]))

    def every_row(values):
        return [lax.all_gather(value, "dp", axis=0) for value in picked(values)]

    hidden_rows = every_row([saved[-1] for saved, _ in kept])
    mixed_rows = every_row([saved[5] for saved, _ in kept])

    arrived = zero
    terms = [None] * steps
    finals = [None] * micro
    for step in reversed(range(steps)):
        place = step - last
        top = cotangent_own[place] if place >= 0 else zero
        incoming = jnp.where(section == last, top, arrived if step < micro else zero)
        saved, mine = kept[step]
        if step < len(hidden_rows):
            turn = len(hidden_rows) - 1 - step
            incoming, hidden_rows[turn], mixed_rows[turn] = lax.optimization_barrier(
                (incoming, hidden_rows[turn], mixed_rows[turn])
            )
        result, big, small = backward(incoming, mine, saved, mlp_terms if step == 0 else None)
        terms[step] = (big, small)
        if step < micro:
            finals[step] = result
        if step > 0:
            arrived = shifted(narrow(result), "section", -1).astype(F32)
    rows_out = jnp.stack(finals)
    half = width // sections
    moved = shifted(narrow(rows_out[:, :, half:]), "section", 1).astype(F32)
    grad_tokens = jnp.where(section == 0, rows_out[:, :, :half], moved)

    def spread(value, axis):
        return lax.psum_scatter(value, "dp", scatter_dimension=axis, tiled=True)

    own = terms[0][0]
    early = spread(own[5], 1)
    normed, grad_qkv, grad_logit = joined(own[0], 0), joined(own[1], 1, 1), joined(own[2], 2)
    grad_project = narrow(jnp.stack([product_left(normed, grad_qkv[j]) for j in range(3)]))
    grad_beta = product_left(normed, grad_logit)
    grad_project, early = lax.optimization_barrier((grad_project, early))
    grad_expand = early.astype(F32)
    grad_project = spread(grad_project, 1).astype(F32)

    def from_rows(rows, place):
        total = 0.0
        for left, right in zip(rows, picked([term[0][place] for term in terms])):
            right = gather(swapped(right)).reshape(TOK_MB, left.shape[0], -1)
            total = total + lax.dot_general(
                left, right, (((0, 1), (1, 0)), ((), ())), preferred_element_type=F32
            )
        return total

    grad_contract = from_rows(hidden_rows, 3)
    grad_merge = from_rows(mixed_rows, 4)
    grad_taps, grad_head_gain, grad_gains = (
        sum(term[1][place] for term in terms) for place in range(3)
    )
    grad_gains = summed(jnp.concatenate([grad_gains.reshape(-1), grad_head_gain]), ("dp", "head"))
    grad_gains, grad_head_gain = grad_gains[: 2 * width].reshape(2, width), grad_gains[2 * width :]
    flat = summed(jnp.concatenate([grad_taps.reshape(-1), grad_beta.reshape(-1)]), ("dp",))
    grad_taps, grad_beta = flat[: grad_taps.size].reshape(grad_taps.shape), flat[grad_taps.size :]
    rows = width // lax.axis_size("dp")
    grad_beta = lax.dynamic_slice_in_dim(grad_beta.reshape(width, heads), lax.axis_index("dp") * rows, rows, 0)
    return (
        grad_tokens,
        grad_project[None],
        grad_beta[None],
        grad_taps[None],
        grad_head_gain[None],
        grad_merge[None],
        grad_expand[None],
        grad_contract[None],
        grad_gains[None],
    )


def solution(mesh):
    return jax.shard_map(
        per_device,
        mesh=mesh,
        in_specs=(
            P("dp", None, None),
            P("dp", None),
            P("dp", None, None),
            P("section", None, None, "head"),
            P("section", None, "head"),
            P("section", None, None, "head"),
            P("section", None),
            P("section", "head", None),
            P("section", None, None, "head"),
            P("section", "head", None),
            P("section", None, None),
        ),
        out_specs=(
            P("dp", "head", "section"),
            P("section", None, "dp", "head"),
            P("section", "dp", "head"),
            P("section", None, None, "head"),
            P("section", None),
            P("section", "head", "dp"),
            P("section", None, "dp", "head"),
            P("section", "head", "dp"),
            P("section", None, None),
        ),
        check_vma=False,
    )
```

```python
import functools

import jax
import jax.numpy as jnp
from jax import lax
from jax.experimental import pallas as pl
from jax.experimental.pallas import tpu as pltpu
from jax.sharding import PartitionSpec as P

HEAD_DIM = 128
CONV = 4
TOK_MB = 384
BLOCK = 128
BLOCKS = TOK_MB // BLOCK
EPS = 1e-06
OUT_FLOOR = 0.0001
F32 = jnp.float32
BF16 = jnp.bfloat16
BASE = 4
LANES = 128
TILE = 256
QUARTERS = 4
VMEM_LIMIT = 44 * 1024 * 1024


def mm(left, right):
    return lax.dot_general(
        left.astype(BF16), right.astype(BF16), (((1,), (0,)), ((), ())), preferred_element_type=F32
    )


def mm_t(left, right):
    return lax.dot_general(
        left.astype(BF16), right.astype(BF16), (((1,), (1,)), ((), ())), preferred_element_type=F32
    )


def t_mm(left, right):
    return lax.dot_general(
        left.astype(BF16), right.astype(BF16), (((0,), (0,)), ((), ())), preferred_element_type=F32
    )


def rows_of(b):
    return slice(b * BLOCK, (b + 1) * BLOCK)


def tiles_of(size, tile=TILE):
    return [slice(start, min(start + tile, size)) for start in range(0, size, tile)]


def quarters(size):
    return tiles_of(size, size // QUARTERS)


def relative_order(count):
    order, bit = [0], count // 2
    while bit:
        order = order + [k ^ bit for k in order]
        bit //= 2
    return order


def place_of(me_ref, difference, share):
    return pl.ds(pl.multiple_of((me_ref[0] ^ difference) * share, 16), share)


def stream(x, taps, masks):
    pre = taps[0:1] * x
    for tap in range(1, CONV):
        pre = pre + taps[tap : tap + 1] * (pltpu.roll(x, tap, 0) * masks[tap - 1])
    gate = jax.nn.sigmoid(pre)
    return pre, gate, pre * gate


def unit_inverses(systems):
    size = systems[0].shape[0]
    row = lax.broadcasted_iota(jnp.int32, (size, size), 0)
    col = lax.broadcasted_iota(jnp.int32, (size, size), 1)
    eye = (row == col).astype(F32)
    near = (row // BASE == col // BASE).astype(F32)
    first = [-a * near for a in systems]
    total = [eye + n for n in first]
    second = [mm(n, n) for n in first]
    third = [mm(n, s) for n, s in zip(first, second)]
    total = [t + s + r for t, s, r in zip(total, second, third)]
    step = BASE
    while step < size:
        span = 2 * step
        off = ((row // span == col // span) & (row // step != col // step)).astype(F32)
        inner = [mm(a * off, t) for a, t in zip(systems, total)]
        outer = [mm(t, i) for t, i in zip(total, inner)]
        total = [t - o for t, o in zip(total, outer)]
        step = span
    return total


def block_masks(seg_col_ref, seg_row_ref):
    row = lax.broadcasted_iota(jnp.int32, (BLOCK, BLOCK), 0)
    col = lax.broadcasted_iota(jnp.int32, (BLOCK, BLOCK), 1)
    strict, lower = {}, {}
    for b in range(BLOCKS):
        for c in range(b + 1):
            same = seg_col_ref[rows_of(b), :] == seg_row_ref[:, rows_of(c)]
            strict[b, c] = same & (col < row) if b == c else same
            lower[b, c] = same & (col <= row) if b == c else same
    return strict, lower


class Fetch:

    def __init__(self, pairs, sems, ahead):
        self.copies = [pltpu.make_async_copy(src, dst, sems.at[i]) for i, (src, dst) in enumerate(pairs)]
        self.ahead = ahead
        self.started = 0
        self.start_to(ahead)

    def start_to(self, place):
        while self.started < min(place, len(self.copies)):
            self.copies[self.started].start()
            self.started += 1

    def wait(self, place):
        self.copies[place].wait()
        self.start_to(place + 1 + self.ahead)

    def wait_group(self, group):
        for place in range(QUARTERS):
            self.wait(QUARTERS * group + place)


def attend_kernel(heads, count, me_ref, seg_col_ref, seg_row_ref, masks_ref, taps_ref, gain_ref, *refs):
    shards, refs = refs[:count], refs[count:]
    project_hbm, beta_hbm, merge_hbm = refs[:3]
    qkv_ref, logit_ref, mixed_ref, system_ref, attend_ref, inverse_ref, fresh_ref, out_ref = refs[3:11]
    partials = refs[11 : 11 + count]
    rows_ref, mixed_abs, project_ref, beta_ref, merge_ref, sems = refs[11 + count :]
    order = relative_order(count)
    share = TOK_MB // count
    fetch = Fetch(
        [(project_hbm.at[0, j], project_ref.at[j]) for j in range(3)]
        + [(beta_hbm, beta_ref), (merge_hbm.at[0], merge_ref)],
        sems,
        5,
    )
    for k in range(count):
        rows_ref[k * share : (k + 1) * share, :] = shards[k][...]
    rows = rows_ref[...]

    def spread(ref, value, *lead):
        for k, difference in enumerate(order):
            ref[(*lead, place_of(me_ref, difference, share), slice(None))] = value[k * share : (k + 1) * share]

    for j in range(3):
        fetch.wait(j)
        for cols in tiles_of(heads * HEAD_DIM):
            value = mm(rows, project_ref[j, :, cols])
            for k, difference in enumerate(order):
                qkv_ref[j, place_of(me_ref, difference, share), cols] = value[k * share : (k + 1) * share]
    fetch.wait(3)
    spread(logit_ref, mm(rows, beta_ref[...]))

    masks = [masks_ref[i] for i in range(CONV - 1)]
    strict, lower = block_masks(seg_col_ref, seg_row_ref)
    queries, keys, values, betas = [], [], [], []
    for h in range(heads):
        cols = slice(h * HEAD_DIM, (h + 1) * HEAD_DIM)
        taps = [taps_ref[0, j, :, cols] for j in range(3)]
        _, _, query = stream(qkv_ref[0, :, cols], taps[0], masks)
        _, _, key = stream(qkv_ref[1, :, cols], taps[1], masks)
        _, _, value = stream(qkv_ref[2, :, cols], taps[2], masks)
        query = query * lax.rsqrt(jnp.sum(query * query, axis=-1, keepdims=True) + EPS) * HEAD_DIM**-0.5
        key = key * lax.rsqrt(jnp.sum(key * key, axis=-1, keepdims=True) + EPS)
        beta = jax.nn.sigmoid(logit_ref[:, h : h + 1])
        queries.append(query.astype(BF16))
        keys.append(key.astype(BF16))
        values.append(value * beta)
        betas.append(beta)
    attend, system = {}, {}
    for h in range(heads):
        for b in range(BLOCKS):
            for c in range(b + 1):
                inner = mm_t(keys[h][rows_of(b)], keys[h][rows_of(c)])
                system[h, b, c] = jnp.where(strict[b, c], inner * betas[h][rows_of(b)], 0.0)
                scores = mm_t(queries[h][rows_of(b)], keys[h][rows_of(c)])
                attend[h, b, c] = jnp.where(lower[b, c], scores, 0.0).astype(BF16)
                attend_ref[h, rows_of(b), rows_of(c)] = attend[h, b, c]
                if c < b:
                    system[h, b, c] = system[h, b, c].astype(BF16)
                    system_ref[h, rows_of(b), rows_of(c)] = system[h, b, c]
    index = [(h, b) for h in range(heads) for b in range(BLOCKS)]
    inverse = dict(zip(index, unit_inverses([system[h, b, b] for h, b in index])))
    for h, b in index:
        inverse[h, b] = inverse[h, b].astype(BF16)
        inverse_ref[h, b] = inverse[h, b]
    fresh = {}
    for b in range(BLOCKS):
        for h in range(heads):
            target = values[h][rows_of(b)]
            for c in range(b):
                target = target - mm(system[h, b, c], fresh[h, c])
            fresh[h, b] = mm(inverse[h, b], target).astype(BF16)
            fresh_ref[rows_of(b), h * HEAD_DIM : (h + 1) * HEAD_DIM] = fresh[h, b]
    for h in range(heads):
        cols = slice(h * HEAD_DIM, (h + 1) * HEAD_DIM)
        for b in range(BLOCKS):
            out = mm(attend[h, b, 0], fresh[h, 0])
            for c in range(1, b + 1):
                out = out + mm(attend[h, b, c], fresh[h, c])
            mean = jnp.mean(out * out, axis=-1, keepdims=True)
            out_ref[rows_of(b), cols] = out
            mixed_abs[rows_of(b), cols] = (
                out * lax.rsqrt(jnp.maximum(mean, OUT_FLOOR)) * gain_ref[...]
            ).astype(BF16)
    for k, difference in enumerate(order):
        mixed_ref[k * share : (k + 1) * share, :] = mixed_abs[place_of(me_ref, difference, share), :]
    fetch.wait(4)
    write_partials(partials, merge_ref.shape[1], share, lambda cols: mm(mixed_ref[...], merge_ref[:, cols]))


def write_partials(partials, width, share, product):
    for cols in tiles_of(width):
        value = product(cols)
        for k, ref in enumerate(partials):
            ref[:, cols] = value[k * share : (k + 1) * share].astype(ref.dtype)


def partial_shapes(count, width):
    share = TOK_MB // count
    return [jax.ShapeDtypeStruct((share, width), F32 if k < count // 2 else BF16) for k in range(count)]


def call(kernel, operands, hbm, out_shape, scratch_shapes):
    vmem = pl.BlockSpec(memory_space=pltpu.VMEM)
    return pl.pallas_call(
        kernel,
        in_specs=[pl.BlockSpec(memory_space=pltpu.SMEM)]
        + [vmem] * (len(operands) - 1)
        + [pl.BlockSpec(memory_space=pl.ANY)] * len(hbm),
        out_specs=[vmem] * len(out_shape),
        out_shape=out_shape,
        scratch_shapes=scratch_shapes,
        compiler_params=pltpu.CompilerParams(vmem_limit_bytes=VMEM_LIMIT),
        cost_estimate=pl.CostEstimate(flops=10**6, bytes_accessed=10**5, transcendentals=0),
    )(*operands, *hbm)


def attend_forward(me, mine, shards, taps, gain, project, beta_weight, merge):
    masks, seg_col, seg_row = mine
    heads = merge.shape[1] // HEAD_DIM
    width = heads * HEAD_DIM
    model = merge.shape[2]
    count = len(shards)
    out = [
        jax.ShapeDtypeStruct((3, TOK_MB, width), F32),
        jax.ShapeDtypeStruct((TOK_MB, LANES), F32),
        jax.ShapeDtypeStruct((TOK_MB, width), BF16),
        jax.ShapeDtypeStruct((heads, TOK_MB, TOK_MB), BF16),
        jax.ShapeDtypeStruct((heads, TOK_MB, TOK_MB), BF16),
        jax.ShapeDtypeStruct((heads, BLOCKS, BLOCK, BLOCK), BF16),
        jax.ShapeDtypeStruct((TOK_MB, width), BF16),
        jax.ShapeDtypeStruct((TOK_MB, width), F32),
    ] + partial_shapes(count, model)
    results = call(
        functools.partial(attend_kernel, heads, count),
        (me, seg_col, seg_row, masks, taps, gain, *shards),
        (project, beta_weight, merge),
        out,
        [
            pltpu.VMEM((TOK_MB, model), BF16),
            pltpu.VMEM((TOK_MB, width), BF16),
            pltpu.VMEM(project.shape[1:], BF16),
            pltpu.VMEM(beta_weight.shape, BF16),
            pltpu.VMEM(merge.shape[1:], BF16),
            pltpu.SemaphoreType.DMA((5,)),
        ],
    )
    return results[:8], results[8:]


def expand_kernel(count, me_ref, *refs):
    shards, refs = refs[:count], refs[count:]
    expand_hbm, contract_hbm, hidden_ref, silu_ref, slope_ref = refs[:5]
    partials = refs[5 : 5 + count]
    rows_ref, gate_ref, expand_ref, contract_ref, sems = refs[5 + count :]
    share = TOK_MB // count
    tiles = tiles_of(hidden_ref.shape[1])
    fetch = Fetch(
        [(expand_hbm.at[0, j, s, :], expand_ref.at[j, s, :]) for j in range(2) for s in quarters(expand_ref.shape[1])]
        + [(contract_hbm.at[0, s, :], contract_ref.at[s, :]) for s in quarters(contract_ref.shape[0])],
        sems,
        QUARTERS,
    )
    for k in range(count):
        rows_ref[k * share : (k + 1) * share, :] = shards[k][...]
    fetch.wait_group(0)
    for t in tiles:
        gate_ref[:, t] = mm(rows_ref[...], expand_ref[0, :, t])
    fetch.wait_group(1)
    for t in tiles:
        up_in = mm(rows_ref[...], expand_ref[1, :, t])
        gate_in = gate_ref[:, t]
        gate = jax.nn.sigmoid(gate_in)
        silu = gate_in * gate
        hidden_ref[:, t] = (silu * up_in).astype(BF16)
        silu_ref[:, t] = silu.astype(BF16)
        slope_ref[:, t] = (up_in * gate * (1.0 + gate_in * (1.0 - gate))).astype(BF16)
    fetch.wait_group(2)
    write_partials(partials, rows_ref.shape[1], share, lambda cols: mm(hidden_ref[...], contract_ref[:, cols]))


def expand_forward(me, shards, expand, contract):
    count = len(shards)
    model, units = expand.shape[2:]
    kept = jax.ShapeDtypeStruct((TOK_MB, units), BF16)
    results = call(
        functools.partial(expand_kernel, count),
        (me, *shards),
        (expand, contract),
        [kept, kept, kept] + partial_shapes(count, model),
        [
            pltpu.VMEM((TOK_MB, model), BF16),
            pltpu.VMEM((TOK_MB, units), F32),
            pltpu.VMEM(expand.shape[1:], BF16),
            pltpu.VMEM(contract.shape[1:], BF16),
            pltpu.SemaphoreType.DMA((3 * QUARTERS,)),
        ],
    )
    return results[:3], results[3:]


def expand_back_kernel(count, me_ref, silu_ref, slope_ref, *refs):
    shards, refs = refs[:count], refs[count:]
    expand_hbm, contract_hbm, gate_ref, up_ref = refs[:4]
    partials = refs[4 : 4 + count]
    rows_ref, expand_ref, contract_ref, sems = refs[4 + count :]
    share = TOK_MB // count
    tiles = tiles_of(gate_ref.shape[1])
    spans = tiles_of(rows_ref.shape[1], 2 * TILE)
    fetch = Fetch(
        [(contract_hbm.at[0, s, :], contract_ref.at[s, :]) for s in quarters(contract_ref.shape[0])]
        + [(expand_hbm.at[0, j, s, :], expand_ref.at[j, s, :]) for s in spans for j in range(2)],
        sems,
        4,
    )
    for k in range(count):
        rows_ref[k * share : (k + 1) * share, :] = shards[k][...]
    fetch.wait_group(0)
    for t in tiles:
        grad_hidden = mm_t(rows_ref[...], contract_ref[t, :])
        gate_ref[:, t] = (grad_hidden * slope_ref[:, t].astype(F32)).astype(BF16)
        up_ref[:, t] = (grad_hidden * silu_ref[:, t].astype(F32)).astype(BF16)
    for i, span in enumerate(spans):
        for j in range(2):
            fetch.wait(QUARTERS + 2 * i + j)
        for s in tiles_of(span.stop - span.start):
            s = slice(span.start + s.start, span.start + s.stop)
            value = mm_t(gate_ref[...], expand_ref[0, s, :]) + mm_t(up_ref[...], expand_ref[1, s, :])
            for k, ref in enumerate(partials):
                ref[:, s] = value[k * share : (k + 1) * share].astype(ref.dtype)


def expand_backward(me, shards, silu, slope, expand, contract):
    count = len(shards)
    model, units = expand.shape[2:]
    kept = jax.ShapeDtypeStruct((TOK_MB, units), BF16)
    results = call(
        functools.partial(expand_back_kernel, count),
        (me, silu, slope, *shards),
        (expand, contract),
        [kept, kept] + partial_shapes(count, model),
        [
            pltpu.VMEM((TOK_MB, model), BF16),
            pltpu.VMEM(expand.shape[1:], BF16),
            pltpu.VMEM(contract.shape[1:], BF16),
            pltpu.SemaphoreType.DMA((QUARTERS + 2 * len(tiles_of(model, 2 * TILE)),)),
        ],
    )
    return results[:2], results[2:]


def stream_back(grad, x, pre, gate, taps, masks, taps_out, j, cols):
    grad_pre = grad * gate * (1.0 + pre * (1.0 - gate))
    grad_x = taps[0:1] * grad_pre
    taps_out[j, 0:1, cols] = jnp.sum(grad_pre * x, axis=0, keepdims=True)
    for tap in range(1, CONV):
        masked = grad_pre * masks[tap - 1]
        grad_x = grad_x + taps[tap : tap + 1] * pltpu.roll(masked, TOK_MB - tap, 0)
        taps_out[j, tap : tap + 1, cols] = jnp.sum(masked * pltpu.roll(x, tap, 0), axis=0, keepdims=True)
    return grad_x


def attend_back_kernel(heads, count, me_ref, seg_col_ref, seg_row_ref, masks_ref, taps_ref, gain_ref,
                       qkv_ref, logit_ref, system_ref, attend_ref, inverse_ref, fresh_ref, out_ref, *refs):
    shards, refs = refs[:count], refs[count:]
    project_hbm, beta_hbm, merge_hbm = refs[:3]
    grad_qkv_ref, grad_logit_ref, grad_taps_ref, grad_gain_ref = refs[3:7]
    partials = refs[7 : 7 + count]
    rows_ref, grad_mixed_ref, grad_abs_ref, logit_abs_ref, project_ref, beta_ref, merge_ref, sems = refs[7 + count :]
    order = relative_order(count)
    share = TOK_MB // count
    model = rows_ref.shape[1]
    width = heads * HEAD_DIM
    fetch = Fetch(
        [(merge_hbm.at[0], merge_ref), (beta_hbm, beta_ref)]
        + [(project_hbm.at[0, j], project_ref.at[j]) for j in range(3)],
        sems,
        0,
    )
    fetch.start_to(5)
    for k in range(count):
        rows_ref[k * share : (k + 1) * share, :] = shards[k][...]
    fetch.wait(0)
    for cols in tiles_of(heads * HEAD_DIM):
        value = mm_t(rows_ref[...], merge_ref[cols, :])
        for k, difference in enumerate(order):
            grad_mixed_ref[place_of(me_ref, difference, share), cols] = value[k * share : (k + 1) * share]

    masks = [masks_ref[i] for i in range(CONV - 1)]
    strict, lower = block_masks(seg_col_ref, seg_row_ref)
    lane = lax.broadcasted_iota(jnp.int32, (TOK_MB, LANES), 1)
    everyone = range(heads)
    columns = [slice(h * HEAD_DIM, (h + 1) * HEAD_DIM) for h in everyone]
    grad_gain = jnp.zeros((8, HEAD_DIM), F32)
    grad_outs, queries, keys, values, betas, convs = [], [], [], [], [], []
    for h in everyone:
        cols = columns[h]
        taps = [taps_ref[0, j, :, cols] for j in range(3)]
        _, _, conv_q = stream(qkv_ref[0, :, cols], taps[0], masks)
        _, _, conv_k = stream(qkv_ref[1, :, cols], taps[1], masks)
        scale_q = lax.rsqrt(jnp.sum(conv_q * conv_q, axis=-1, keepdims=True) + EPS)
        scale_k = lax.rsqrt(jnp.sum(conv_k * conv_k, axis=-1, keepdims=True) + EPS)
        queries.append((conv_q * (scale_q * HEAD_DIM**-0.5)).astype(BF16))
        keys.append((conv_k * scale_k).astype(BF16))
        betas.append(jax.nn.sigmoid(logit_ref[:, h : h + 1]))
        out = out_ref[:, cols]
        grad_mixed = grad_mixed_ref[:, cols]
        mean = jnp.mean(out * out, axis=-1, keepdims=True)
        scale = lax.rsqrt(jnp.maximum(mean, OUT_FLOOR))
        unit = out * scale
        grad_gain = grad_gain + jnp.sum((grad_mixed * unit).reshape(TOK_MB // 8, 8, HEAD_DIM), axis=0)
        grad_unit = grad_mixed * gain_ref[...]
        through = jnp.where(mean > OUT_FLOOR, 1.0, jnp.where(mean == OUT_FLOOR, 0.5, 0.0))
        grad_out = scale * (
            grad_unit - unit * (through * jnp.mean(grad_unit * unit, axis=-1, keepdims=True))
        )
        grad_outs.append(grad_out.astype(BF16))
    grad_gain_ref[...] = grad_gain
    fresh = {(h, b): fresh_ref[rows_of(b), columns[h]] for h in everyone for b in range(BLOCKS)}
    d_out = {(h, b): grad_outs[h][rows_of(b)] for h in everyone for b in range(BLOCKS)}
    key_blocks = {(h, b): keys[h][rows_of(b)] for h in everyone for b in range(BLOCKS)}
    d_fresh, d_target, d_target_b = {}, {}, {}
    for c in range(BLOCKS):
        for h in everyone:
            total = t_mm(attend_ref[h, rows_of(c), rows_of(c)], d_out[h, c])
            for b in range(c + 1, BLOCKS):
                total = total + t_mm(attend_ref[h, rows_of(b), rows_of(c)], d_out[h, b])
            d_fresh[h, c] = total
    for b in reversed(range(BLOCKS)):
        for h in everyone:
            d_target[h, b] = t_mm(inverse_ref[h, b], d_fresh[h, b])
            d_target_b[h, b] = d_target[h, b].astype(BF16)
        for h in everyone:
            for c in range(b):
                d_fresh[h, c] = d_fresh[h, c] - t_mm(system_ref[h, rows_of(b), rows_of(c)], d_target_b[h, b])
    grad_query, inner, grad_key = {}, {}, {}
    for b in range(BLOCKS):
        for c in range(b + 1):
            for h in everyone:
                d_attend = jnp.where(lower[b, c], mm_t(d_out[h, b], fresh[h, c]), 0.0).astype(BF16)
                d_system = jnp.where(strict[b, c], -mm_t(d_target_b[h, b], fresh[h, c]), 0.0)
                for store, place, part in (
                    (grad_query, b, mm(d_attend, key_blocks[h, c])),
                    (inner, b, mm(d_system, key_blocks[h, c])),
                    (grad_key, c, t_mm(d_attend, queries[h][rows_of(b)])
                     + t_mm(d_system * betas[h][rows_of(b)], key_blocks[h, b])),
                ):
                    store[h, place] = store[h, place] + part if (h, place) in store else part

    def whole(store, h):
        return jnp.concatenate([store[h, b] for b in range(BLOCKS)], axis=0)

    grad_logits = jnp.zeros((TOK_MB, LANES), F32)
    for h in everyone:
        cols = columns[h]
        beta = betas[h]
        taps = [taps_ref[0, j, :, cols] for j in range(3)]
        inputs = [qkv_ref[j, :, cols] for j in range(3)]
        pre_q, gate_q, conv_q = stream(inputs[0], taps[0], masks)
        pre_k, gate_k, conv_k = stream(inputs[1], taps[1], masks)
        pre_v, gate_v, value = stream(inputs[2], taps[2], masks)
        scale_q = lax.rsqrt(jnp.sum(conv_q * conv_q, axis=-1, keepdims=True) + EPS)
        scale_k = lax.rsqrt(jnp.sum(conv_k * conv_k, axis=-1, keepdims=True) + EPS)
        unit_q, key = conv_q * scale_q, conv_k * scale_k
        within = whole(inner, h)
        target = whole(d_target, h)
        grad_q = whole(grad_query, h)
        grad_k = whole(grad_key, h) + beta * within
        grad_beta = jnp.sum(within * key + target * value, axis=-1, keepdims=True)
        grad_logits = jnp.where(lane == h, grad_beta * beta * (1.0 - beta), grad_logits)
        grad_conv_q = (HEAD_DIM**-0.5 * scale_q) * (
            grad_q - unit_q * jnp.sum(grad_q * unit_q, axis=-1, keepdims=True)
        )
        grad_conv_k = scale_k * (grad_k - key * jnp.sum(grad_k * key, axis=-1, keepdims=True))
        for j, (grad, pre, gate) in enumerate(
            ((grad_conv_q, pre_q, gate_q), (grad_conv_k, pre_k, gate_k), (beta * target, pre_v, gate_v))
        ):
            grad_x = stream_back(grad, inputs[j], pre, gate, taps[j], masks, grad_taps_ref, j, cols)
            grad_abs_ref[j, :, cols] = grad_x.astype(BF16)
    logit_abs_ref[...] = grad_logits.astype(BF16)
    for k, difference in enumerate(order):
        here = slice(k * share, (k + 1) * share)
        there = place_of(me_ref, difference, share)
        grad_logit_ref[here, :] = logit_abs_ref[there, :]
        for j in range(3):
            grad_qkv_ref[here, j * width : (j + 1) * width] = grad_abs_ref[j, there, :]
    for place in range(1, 5):
        fetch.wait(place)
    for span in tiles_of(model):
        value = mm_t(grad_logit_ref[...], beta_ref[span, :])
        for j in range(3):
            value = value + mm_t(grad_qkv_ref[:, j * width : (j + 1) * width], project_ref[j, span, :])
        for k, ref in enumerate(partials):
            ref[:, span] = value[k * share : (k + 1) * share].astype(ref.dtype)


def attend_backward(me, mine, shards, kept, taps, gain, project, beta_weight, merge):
    masks, seg_col, seg_row = mine
    heads = merge.shape[1] // HEAD_DIM
    width = heads * HEAD_DIM
    model = merge.shape[2]
    count = len(shards)
    qkv, logit, _, system, attend, inverse, fresh, out = kept
    results = call(
        functools.partial(attend_back_kernel, heads, count),
        (me, seg_col, seg_row, masks, taps, gain, qkv, logit, system, attend, inverse, fresh, out, *shards),
        (project, beta_weight, merge),
        [
            jax.ShapeDtypeStruct((TOK_MB, 3 * width), BF16),
            jax.ShapeDtypeStruct((TOK_MB, LANES), BF16),
            jax.ShapeDtypeStruct((3, CONV, width), F32),
            jax.ShapeDtypeStruct((8, HEAD_DIM), F32),
        ]
        + partial_shapes(count, model),
        [
            pltpu.VMEM((TOK_MB, model), BF16),
            pltpu.VMEM((TOK_MB, width), F32),
            pltpu.VMEM((3, TOK_MB, width), BF16),
            pltpu.VMEM((TOK_MB, LANES), BF16),
            pltpu.VMEM(project.shape[1:], BF16),
            pltpu.VMEM(beta_weight.shape, BF16),
            pltpu.VMEM(merge.shape[1:], BF16),
            pltpu.SemaphoreType.DMA((5,)),
        ],
    )
    return results[:4], results[4:]


def tap_masks(segment):
    masks = []
    for tap in range(1, CONV):
        earlier = jnp.concatenate([jnp.full((tap,), -1, jnp.int32), segment[: TOK_MB - tap]], axis=0)
        masks.append(jnp.broadcast_to((earlier == segment).astype(F32)[:, None], (TOK_MB, HEAD_DIM)))
    return jnp.stack(masks)


def narrow(values):
    return values.astype(BF16)


def product(left, right):
    return jnp.dot(left, right, preferred_element_type=F32)


def product_left(left, right):
    return lax.dot_general(left, right, (((0,), (0,)), ((), ())), preferred_element_type=F32)


def product_right(left, right):
    return lax.dot_general(left, right, (((1,), (1,)), ((), ())), preferred_element_type=F32)


def rms_parts(values):
    scale = lax.rsqrt(jnp.mean(values * values, axis=-1, keepdims=True) + EPS)
    return (values * scale, scale)


def norm_back(grad_normed, normed, scale, gain):
    grad_scaled = grad_normed * gain
    return scale * (grad_scaled - normed * jnp.mean(grad_scaled * normed, axis=-1, keepdims=True))


def segment_ids(lengths, count):
    ends = jnp.cumsum(lengths)
    places = jnp.arange(count, dtype=jnp.int32)
    return jnp.sum((places[:, None] >= ends[None, :]).astype(jnp.int32), axis=1, dtype=jnp.int32)


def flipped(values, axis, bit):
    return lax.ppermute(values, axis, [(i, i ^ bit) for i in range(lax.axis_size(axis))])


def shifted(values, axis, distance):
    devices = range(lax.axis_size(axis))
    return lax.ppermute(values, axis, [(i, i + distance) for i in devices if i + distance in devices])


def bits_of(axis):
    size = lax.axis_size(axis)
    bits = [1 << k for k in range(size.bit_length() - 1)]
    assert 1 << len(bits) == size
    return bits


def summed(values, axes):
    for axis in axes:
        for bit in bits_of(axis):
            values = values + flipped(values, axis, bit)
    return values


def gather(shard):
    parts = [shard]
    for bit in reversed(bits_of("head")):
        parts = parts + [flipped(part, "head", bit) for part in parts]
    return parts


def scatter(parts):
    for bit in bits_of("head"):
        half = len(parts) // 2
        arrived = [flipped(narrow(part), "head", bit) for part in parts[half:]]
        parts = [part.astype(F32) + other.astype(F32) for part, other in zip(parts[:half], arrived)]
    return parts[0]


def swapped(shard):
    count = lax.axis_size("dp")
    me = lax.axis_index("dp")
    rows, width = shard.shape
    blocks = shard.reshape(rows, count, width // count)
    arrived = []
    for distance in range(count):
        block = lax.dynamic_index_in_dim(blocks, (me + distance) % count, 1, keepdims=False)
        if distance:
            block = lax.ppermute(block, "dp", [(i, (i + distance) % count) for i in range(count)])
        arrived.append(block)
    arrived = jnp.stack(arrived)
    ordered = [lax.dynamic_index_in_dim(arrived, (me - q) % count, 0, keepdims=False) for q in range(count)]
    return jnp.concatenate(ordered, axis=1)


def per_device(
    tokens,
    lengths,
    cotangent,
    attn_in,
    beta_weight,
    conv_weight,
    o_gain,
    attn_out,
    mlp_in,
    mlp_out,
    norm_gains,
):
    section = lax.axis_index("section")
    sections = lax.axis_size("section")
    member = lax.axis_index("head")
    micro = tokens.shape[0]
    width = tokens.shape[2]
    heads = beta_weight.shape[2]
    share = TOK_MB // lax.axis_size("head")
    me = member[None]
    beta_wide = jnp.pad(beta_weight[0], ((0, 0), (0, LANES - heads)))
    gains = norm_gains[0]
    every = range(micro)
    segments = [segment_ids(lengths[m], TOK_MB) for m in every]
    masks = [(tap_masks(s), s[:, None], s[None, :]) for s in segments]
    own_rows = lambda values: lax.dynamic_slice_in_dim(values, member * share, share, 0).astype(F32)
    tokens_own = [own_rows(tokens[m]) for m in every]
    cotangent_own = [own_rows(cotangent[m]) for m in every]

    def forward(x, mine):
        unit, scale = rms_parts(x)
        normed = gather(narrow(unit * gains[0]))
        kept, partials = attend_forward(me, mine, normed, conv_weight, o_gain, attn_in, beta_wide, attn_out)
        middle = x + scatter(partials)
        unit_mid, scale_mid = rms_parts(middle)
        normed_mid = gather(narrow(unit_mid * gains[1]))
        (hidden, silu, slope), partials = expand_forward(me, normed_mid, mlp_in, mlp_out)
        result = middle + scatter(partials)
        return result, (unit, scale, normed, kept, unit_mid, scale_mid, normed_mid, hidden, silu, slope)

    def backward(incoming, mine, saved, early=None):
        unit, scale, normed, kept, unit_mid, scale_mid, normed_mid, _, silu, slope = saved
        (grad_gate, grad_up), partials = expand_backward(
            me, gather(narrow(incoming)), silu, slope, mlp_in, mlp_out
        )
        grad_mid = scatter(partials)
        grad_middle = incoming + norm_back(grad_mid, unit_mid, scale_mid, gains[1])
        big = (normed_mid, grad_gate, grad_up)
        if early is not None:
            big = early(*big)
            grad_middle, big = lax.optimization_barrier((grad_middle, big))
        gain_two = jnp.sum(grad_mid * unit_mid, axis=0)
        (grad_qkv, grad_logit, grad_taps, grad_head_gain), partials = attend_backward(
            me, mine, gather(narrow(grad_middle)), kept, conv_weight, o_gain, attn_in, beta_wide, attn_out
        )
        grad_norm = scatter(partials)
        grad_inputs = grad_middle + norm_back(grad_norm, unit, scale, gains[0])
        gain_one = jnp.sum(grad_norm * unit, axis=0)
        big = (normed, grad_qkv, grad_logit, narrow(incoming), narrow(grad_middle)) + big
        small = (grad_taps, jnp.sum(grad_head_gain, axis=0), jnp.stack([gain_one, gain_two]))
        return grad_inputs, big, small

    last = sections - 1
    zero = jnp.zeros((share, width), F32)
    steps = micro + last
    kept = []
    arrived = zero
    for step in range(steps):
        first = tokens_own[min(step, micro - 1)]
        inputs = jnp.where(section == 0, first, arrived)
        mine = [jnp.where(section == 0, a, b) for a, b in zip(masks[min(step, micro - 1)], masks[max(step - last, 0)])]
        result, saved = forward(inputs, mine)
        kept.append((saved, mine))
        if step < steps - 1:
            arrived = shifted(narrow(result), "section", 1).astype(F32)
    def picked(values, own=None):
        chosen = [values[i] for i in range(last, micro)]
        for i in range(last):
            first = values[i] if own is None else own
            chosen.append(jax.tree.map(lambda a, b: jnp.where(section <= i, a, b), first, values[i + micro]))
        return chosen

    def joined(own, place):
        chosen = picked([term and term[0][place] for term in terms], own)
        if isinstance(own, list):
            chosen = [part for parts in chosen for part in parts]
        return jnp.concatenate(chosen, axis=0)

    def mlp_terms(*own):
        normed_mid, grad_gate, grad_up = (joined(own[place], 5 + place) for place in range(3))
        return narrow(product_left(normed_mid, grad_gate)), narrow(product_left(normed_mid, grad_up))

    def every_row(values):
        return [lax.all_gather(value, "dp", axis=0) for value in picked(values)]

    hidden_rows = every_row([saved[7] for saved, _ in kept])
    mixed_rows = every_row([saved[3][2] for saved, _ in kept])

    arrived = zero
    terms = [None] * steps
    finals = [None] * micro
    for step in reversed(range(steps)):
        place = step - last
        top = cotangent_own[place] if place >= 0 else zero
        incoming = jnp.where(section == last, top, arrived if step < micro else zero)
        saved, mine = kept[step]
        if step < len(hidden_rows):
            turn = len(hidden_rows) - 1 - step
            incoming, hidden_rows[turn], mixed_rows[turn] = lax.optimization_barrier(
                (incoming, hidden_rows[turn], mixed_rows[turn])
            )
        result, big, small = backward(incoming, mine, saved, mlp_terms if step == 0 else None)
        terms[step] = (big, small)
        if step < micro:
            finals[step] = result
        if step > 0:
            arrived = shifted(narrow(result), "section", -1).astype(F32)
    rows_out = jnp.stack(finals)
    half = width // sections
    moved = shifted(narrow(rows_out[:, :, half:]), "section", 1).astype(F32)
    grad_tokens = jnp.where(section == 0, rows_out[:, :, :half], moved)

    def spread(value, axis):
        return lax.psum_scatter(value, "dp", scatter_dimension=axis, tiled=True)

    own = terms[0][0]
    early = [spread(part, 0) for part in own[5:]]
    normed, grad_qkv, grad_logit = (joined(own[place], place) for place in range(3))
    grad_project = narrow(product_left(normed, grad_qkv))
    grad_beta = product_left(normed, grad_logit)[:, :heads]
    grad_project, early = lax.optimization_barrier((grad_project, early))
    grad_expand = jnp.stack(early).astype(F32)
    grad_project = jnp.stack(jnp.split(spread(grad_project, 0), 3, axis=1)).astype(F32)

    def from_rows(rows, place):
        total = 0.0
        for left, right in zip(rows, picked([term[0][place] for term in terms])):
            right = jnp.concatenate(gather(swapped(right)), axis=0).reshape(TOK_MB, left.shape[0], -1)
            total = total + lax.dot_general(
                left, right, (((0, 1), (1, 0)), ((), ())), preferred_element_type=F32
            )
        return total

    grad_contract = from_rows(hidden_rows, 3)
    grad_merge = from_rows(mixed_rows, 4)
    grad_taps, grad_head_gain, grad_gains = (
        sum(term[1][place] for term in terms) for place in range(3)
    )
    grad_gains = summed(jnp.concatenate([grad_gains.reshape(-1), grad_head_gain]), ("dp", "head"))
    grad_gains, grad_head_gain = grad_gains[: 2 * width].reshape(2, width), grad_gains[2 * width :]
    flat = summed(jnp.concatenate([grad_taps.reshape(-1), grad_beta.reshape(-1)]), ("dp",))
    grad_taps, grad_beta = flat[: grad_taps.size].reshape(grad_taps.shape), flat[grad_taps.size :]
    rows = width // lax.axis_size("dp")
    grad_beta = lax.dynamic_slice_in_dim(grad_beta.reshape(width, heads), lax.axis_index("dp") * rows, rows, 0)
    return (
        grad_tokens,
        grad_project[None],
        grad_beta[None],
        grad_taps[None],
        grad_head_gain[None],
        grad_merge[None],
        grad_expand[None],
        grad_contract[None],
        grad_gains[None],
    )


def solution(mesh):
    return jax.shard_map(
        per_device,
        mesh=mesh,
        in_specs=(
            P("dp", None, None),
            P("dp", None),
            P("dp", None, None),
            P("section", None, None, "head"),
            P("section", None, "head"),
            P("section", None, None, "head"),
            P("section", None),
            P("section", "head", None),
            P("section", None, None, "head"),
            P("section", "head", None),
            P("section", None, None),
        ),
        out_specs=(
            P("dp", "head", "section"),
            P("section", None, "dp", "head"),
            P("section", "dp", "head"),
            P("section", None, None, "head"),
            P("section", None),
            P("section", "head", "dp"),
            P("section", None, "dp", "head"),
            P("section", "head", "dp"),
            P("section", None, None),
        ),
        check_vma=False,
    )
```

```python
import functools

import jax
import jax.numpy as jnp
from jax import lax
from jax.experimental import pallas as pl
from jax.experimental.pallas import tpu as pltpu
from jax.sharding import PartitionSpec as P

HEAD_DIM = 128
CONV = 4
TOK_MB = 384
BLOCK = 128
BLOCKS = TOK_MB // BLOCK
EPS = 1e-06
OUT_FLOOR = 0.0001
F32 = jnp.float32
BF16 = jnp.bfloat16
BASE = 4
LANES = 128
TILE = 256
QUARTERS = 4
VMEM_LIMIT = 44 * 1024 * 1024


def mm(left, right):
    return lax.dot_general(
        left.astype(BF16), right.astype(BF16), (((1,), (0,)), ((), ())), preferred_element_type=F32
    )


def mm_t(left, right):
    return lax.dot_general(
        left.astype(BF16), right.astype(BF16), (((1,), (1,)), ((), ())), preferred_element_type=F32
    )


def t_mm(left, right):
    return lax.dot_general(
        left.astype(BF16), right.astype(BF16), (((0,), (0,)), ((), ())), preferred_element_type=F32
    )


def rows_of(b):
    return slice(b * BLOCK, (b + 1) * BLOCK)


def tiles_of(size, tile=TILE):
    return [slice(start, min(start + tile, size)) for start in range(0, size, tile)]


def quarters(size):
    return tiles_of(size, size // QUARTERS)


def relative_order(count):
    order, bit = [0], count // 2
    while bit:
        order = order + [k ^ bit for k in order]
        bit //= 2
    return order


def place_of(me_ref, difference, share):
    return pl.ds(pl.multiple_of((me_ref[0] ^ difference) * share, 16), share)


def stream(x, taps, masks):
    pre = taps[0:1] * x
    for tap in range(1, CONV):
        pre = pre + taps[tap : tap + 1] * (pltpu.roll(x, tap, 0) * masks[tap - 1])
    gate = jax.nn.sigmoid(pre)
    return pre, gate, pre * gate


def unit_inverses(systems):
    size = systems[0].shape[0]
    row = lax.broadcasted_iota(jnp.int32, (size, size), 0)
    col = lax.broadcasted_iota(jnp.int32, (size, size), 1)
    eye = (row == col).astype(F32)
    near = (row // BASE == col // BASE).astype(F32)
    first = [-a * near for a in systems]
    total = [eye + n for n in first]
    second = [mm(n, n) for n in first]
    third = [mm(n, s) for n, s in zip(first, second)]
    total = [t + s + r for t, s, r in zip(total, second, third)]
    step = BASE
    while step < size:
        span = 2 * step
        off = ((row // span == col // span) & (row // step != col // step)).astype(F32)
        inner = [mm(a * off, t) for a, t in zip(systems, total)]
        outer = [mm(t, i) for t, i in zip(total, inner)]
        total = [t - o for t, o in zip(total, outer)]
        step = span
    return total


def block_masks(seg_col_ref, seg_row_ref):
    row = lax.broadcasted_iota(jnp.int32, (BLOCK, BLOCK), 0)
    col = lax.broadcasted_iota(jnp.int32, (BLOCK, BLOCK), 1)
    strict, lower = {}, {}
    for b in range(BLOCKS):
        for c in range(b + 1):
            same = seg_col_ref[rows_of(b), :] == seg_row_ref[:, rows_of(c)]
            strict[b, c] = same & (col < row) if b == c else same
            lower[b, c] = same & (col <= row) if b == c else same
    return strict, lower


class Fetch:

    def __init__(self, pairs, sems, ahead):
        self.copies = [pltpu.make_async_copy(src, dst, sems.at[i]) for i, (src, dst) in enumerate(pairs)]
        self.ahead = ahead
        self.started = 0
        self.start_to(ahead)

    def start_to(self, place):
        while self.started < min(place, len(self.copies)):
            self.copies[self.started].start()
            self.started += 1

    def wait(self, place):
        self.copies[place].wait()
        self.start_to(place + 1 + self.ahead)

    def wait_group(self, group):
        for place in range(QUARTERS):
            self.wait(QUARTERS * group + place)


def attend_kernel(heads, count, me_ref, seg_col_ref, seg_row_ref, masks_ref, taps_ref, gain_ref, *refs):
    shards, refs = refs[:count], refs[count:]
    project_hbm, beta_hbm, merge_hbm = refs[:3]
    qkv_ref, logit_ref, mixed_ref, system_ref, attend_ref, inverse_ref, fresh_ref, out_ref = refs[3:11]
    partials = refs[11 : 11 + count]
    rows_ref, mixed_abs, project_ref, beta_ref, merge_ref, sems = refs[11 + count :]
    order = relative_order(count)
    share = TOK_MB // count
    fetch = Fetch(
        [(project_hbm.at[0, j], project_ref.at[j]) for j in range(3)]
        + [(beta_hbm, beta_ref), (merge_hbm.at[0], merge_ref)],
        sems,
        5,
    )
    for k in range(count):
        rows_ref[k * share : (k + 1) * share, :] = shards[k][...]
    rows = rows_ref[...]

    def spread(ref, value, *lead):
        for k, difference in enumerate(order):
            ref[(*lead, place_of(me_ref, difference, share), slice(None))] = value[k * share : (k + 1) * share]

    for j in range(3):
        fetch.wait(j)
        for cols in tiles_of(heads * HEAD_DIM):
            value = mm(rows, project_ref[j, :, cols])
            for k, difference in enumerate(order):
                qkv_ref[j, place_of(me_ref, difference, share), cols] = value[k * share : (k + 1) * share]
    fetch.wait(3)
    spread(logit_ref, mm(rows, beta_ref[...]))

    masks = [masks_ref[i] for i in range(CONV - 1)]
    strict, lower = block_masks(seg_col_ref, seg_row_ref)
    queries, keys, values, betas = [], [], [], []
    for h in range(heads):
        cols = slice(h * HEAD_DIM, (h + 1) * HEAD_DIM)
        taps = [taps_ref[0, j, :, cols] for j in range(3)]
        _, _, query = stream(qkv_ref[0, :, cols], taps[0], masks)
        _, _, key = stream(qkv_ref[1, :, cols], taps[1], masks)
        _, _, value = stream(qkv_ref[2, :, cols], taps[2], masks)
        query = query * lax.rsqrt(jnp.sum(query * query, axis=-1, keepdims=True) + EPS) * HEAD_DIM**-0.5
        key = key * lax.rsqrt(jnp.sum(key * key, axis=-1, keepdims=True) + EPS)
        beta = jax.nn.sigmoid(logit_ref[:, h : h + 1])
        queries.append(query.astype(BF16))
        keys.append(key.astype(BF16))
        values.append(value * beta)
        betas.append(beta)
    attend, system = {}, {}
    for h in range(heads):
        for b in range(BLOCKS):
            for c in range(b + 1):
                inner = mm_t(keys[h][rows_of(b)], keys[h][rows_of(c)])
                system[h, b, c] = jnp.where(strict[b, c], inner * betas[h][rows_of(b)], 0.0)
                scores = mm_t(queries[h][rows_of(b)], keys[h][rows_of(c)])
                attend[h, b, c] = jnp.where(lower[b, c], scores, 0.0).astype(BF16)
                attend_ref[h, rows_of(b), rows_of(c)] = attend[h, b, c]
                if c < b:
                    system[h, b, c] = system[h, b, c].astype(BF16)
                    system_ref[h, rows_of(b), rows_of(c)] = system[h, b, c]
    index = [(h, b) for h in range(heads) for b in range(BLOCKS)]
    inverse = dict(zip(index, unit_inverses([system[h, b, b] for h, b in index])))
    for h, b in index:
        inverse[h, b] = inverse[h, b].astype(BF16)
        inverse_ref[h, b] = inverse[h, b]
    fresh = {}
    for b in range(BLOCKS):
        for h in range(heads):
            target = values[h][rows_of(b)]
            for c in range(b):
                target = target - mm(system[h, b, c], fresh[h, c])
            fresh[h, b] = mm(inverse[h, b], target).astype(BF16)
            fresh_ref[rows_of(b), h * HEAD_DIM : (h + 1) * HEAD_DIM] = fresh[h, b]
    for h in range(heads):
        cols = slice(h * HEAD_DIM, (h + 1) * HEAD_DIM)
        for b in range(BLOCKS):
            out = mm(attend[h, b, 0], fresh[h, 0])
            for c in range(1, b + 1):
                out = out + mm(attend[h, b, c], fresh[h, c])
            mean = jnp.mean(out * out, axis=-1, keepdims=True)
            out_ref[rows_of(b), cols] = out
            mixed_abs[rows_of(b), cols] = (
                out * lax.rsqrt(jnp.maximum(mean, OUT_FLOOR)) * gain_ref[...]
            ).astype(BF16)
    for k, difference in enumerate(order):
        mixed_ref[k * share : (k + 1) * share, :] = mixed_abs[place_of(me_ref, difference, share), :]
    fetch.wait(4)
    write_partials(partials, merge_ref.shape[1], share, lambda cols: mm(mixed_ref[...], merge_ref[:, cols]))


def write_partials(partials, width, share, product):
    for cols in tiles_of(width):
        value = product(cols)
        for k, ref in enumerate(partials):
            ref[:, cols] = value[k * share : (k + 1) * share].astype(ref.dtype)


def partial_shapes(count, width):
    share = TOK_MB // count
    return [jax.ShapeDtypeStruct((share, width), F32 if k < count // 2 else BF16) for k in range(count)]


def call(kernel, operands, hbm, out_shape, scratch_shapes):
    vmem = pl.BlockSpec(memory_space=pltpu.VMEM)
    return pl.pallas_call(
        kernel,
        in_specs=[pl.BlockSpec(memory_space=pltpu.SMEM)]
        + [vmem] * (len(operands) - 1)
        + [pl.BlockSpec(memory_space=pl.ANY)] * len(hbm),
        out_specs=[vmem] * len(out_shape),
        out_shape=out_shape,
        scratch_shapes=scratch_shapes,
        compiler_params=pltpu.CompilerParams(vmem_limit_bytes=VMEM_LIMIT),
        cost_estimate=pl.CostEstimate(flops=10**6, bytes_accessed=10**5, transcendentals=0),
    )(*operands, *hbm)


def attend_forward(me, mine, shards, taps, gain, project, beta_weight, merge):
    masks, seg_col, seg_row = mine
    heads = merge.shape[1] // HEAD_DIM
    width = heads * HEAD_DIM
    model = merge.shape[2]
    count = len(shards)
    out = [
        jax.ShapeDtypeStruct((3, TOK_MB, width), F32),
        jax.ShapeDtypeStruct((TOK_MB, LANES), F32),
        jax.ShapeDtypeStruct((TOK_MB, width), BF16),
        jax.ShapeDtypeStruct((heads, TOK_MB, TOK_MB), BF16),
        jax.ShapeDtypeStruct((heads, TOK_MB, TOK_MB), BF16),
        jax.ShapeDtypeStruct((heads, BLOCKS, BLOCK, BLOCK), BF16),
        jax.ShapeDtypeStruct((TOK_MB, width), BF16),
        jax.ShapeDtypeStruct((TOK_MB, width), F32),
    ] + partial_shapes(count, model)
    results = call(
        functools.partial(attend_kernel, heads, count),
        (me, seg_col, seg_row, masks, taps, gain, *shards),
        (project, beta_weight, merge),
        out,
        [
            pltpu.VMEM((TOK_MB, model), BF16),
            pltpu.VMEM((TOK_MB, width), BF16),
            pltpu.VMEM(project.shape[1:], BF16),
            pltpu.VMEM(beta_weight.shape, BF16),
            pltpu.VMEM(merge.shape[1:], BF16),
            pltpu.SemaphoreType.DMA((5,)),
        ],
    )
    return results[:8], results[8:]


def expand_kernel(count, me_ref, *refs):
    shards, refs = refs[:count], refs[count:]
    expand_hbm, contract_hbm, hidden_ref, silu_ref, slope_ref = refs[:5]
    partials = refs[5 : 5 + count]
    rows_ref, gate_ref, expand_ref, contract_ref, sems = refs[5 + count :]
    share = TOK_MB // count
    tiles = tiles_of(hidden_ref.shape[1])
    fetch = Fetch(
        [(expand_hbm.at[0, j, s, :], expand_ref.at[j, s, :]) for j in range(2) for s in quarters(expand_ref.shape[1])]
        + [(contract_hbm.at[0, s, :], contract_ref.at[s, :]) for s in quarters(contract_ref.shape[0])],
        sems,
        QUARTERS,
    )
    for k in range(count):
        rows_ref[k * share : (k + 1) * share, :] = shards[k][...]
    fetch.wait_group(0)
    for t in tiles:
        gate_ref[:, t] = mm(rows_ref[...], expand_ref[0, :, t])
    fetch.wait_group(1)
    for t in tiles:
        up_in = mm(rows_ref[...], expand_ref[1, :, t])
        gate_in = gate_ref[:, t]
        gate = jax.nn.sigmoid(gate_in)
        silu = gate_in * gate
        hidden_ref[:, t] = (silu * up_in).astype(BF16)
        silu_ref[:, t] = silu.astype(BF16)
        slope_ref[:, t] = (up_in * gate * (1.0 + gate_in * (1.0 - gate))).astype(BF16)
    fetch.wait_group(2)
    write_partials(partials, rows_ref.shape[1], share, lambda cols: mm(hidden_ref[...], contract_ref[:, cols]))


def expand_forward(me, shards, expand, contract):
    count = len(shards)
    model, units = expand.shape[2:]
    kept = jax.ShapeDtypeStruct((TOK_MB, units), BF16)
    results = call(
        functools.partial(expand_kernel, count),
        (me, *shards),
        (expand, contract),
        [kept, kept, kept] + partial_shapes(count, model),
        [
            pltpu.VMEM((TOK_MB, model), BF16),
            pltpu.VMEM((TOK_MB, units), F32),
            pltpu.VMEM(expand.shape[1:], BF16),
            pltpu.VMEM(contract.shape[1:], BF16),
            pltpu.SemaphoreType.DMA((3 * QUARTERS,)),
        ],
    )
    return results[:3], results[3:]


def expand_back_kernel(count, me_ref, silu_ref, slope_ref, *refs):
    shards, refs = refs[:count], refs[count:]
    expand_hbm, contract_hbm, gate_ref, up_ref = refs[:4]
    partials = refs[4 : 4 + count]
    rows_ref, expand_ref, contract_ref, sems = refs[4 + count :]
    share = TOK_MB // count
    tiles = tiles_of(gate_ref.shape[1])
    spans = tiles_of(rows_ref.shape[1], 2 * TILE)
    fetch = Fetch(
        [(contract_hbm.at[0, s, :], contract_ref.at[s, :]) for s in quarters(contract_ref.shape[0])]
        + [(expand_hbm.at[0, j, s, :], expand_ref.at[j, s, :]) for s in spans for j in range(2)],
        sems,
        4,
    )
    for k in range(count):
        rows_ref[k * share : (k + 1) * share, :] = shards[k][...]
    fetch.wait_group(0)
    for t in tiles:
        grad_hidden = mm_t(rows_ref[...], contract_ref[t, :])
        gate_ref[:, t] = (grad_hidden * slope_ref[:, t].astype(F32)).astype(BF16)
        up_ref[:, t] = (grad_hidden * silu_ref[:, t].astype(F32)).astype(BF16)
    for i, span in enumerate(spans):
        for j in range(2):
            fetch.wait(QUARTERS + 2 * i + j)
        for s in tiles_of(span.stop - span.start):
            s = slice(span.start + s.start, span.start + s.stop)
            value = mm_t(gate_ref[...], expand_ref[0, s, :]) + mm_t(up_ref[...], expand_ref[1, s, :])
            for k, ref in enumerate(partials):
                ref[:, s] = value[k * share : (k + 1) * share].astype(ref.dtype)


def expand_backward(me, shards, silu, slope, expand, contract):
    count = len(shards)
    model, units = expand.shape[2:]
    kept = jax.ShapeDtypeStruct((TOK_MB, units), BF16)
    results = call(
        functools.partial(expand_back_kernel, count),
        (me, silu, slope, *shards),
        (expand, contract),
        [kept, kept] + partial_shapes(count, model),
        [
            pltpu.VMEM((TOK_MB, model), BF16),
            pltpu.VMEM(expand.shape[1:], BF16),
            pltpu.VMEM(contract.shape[1:], BF16),
            pltpu.SemaphoreType.DMA((QUARTERS + 2 * len(tiles_of(model, 2 * TILE)),)),
        ],
    )
    return results[:2], results[2:]


def stream_back(grad, x, pre, gate, taps, masks, taps_out, j, cols):
    grad_pre = grad * gate * (1.0 + pre * (1.0 - gate))
    grad_x = taps[0:1] * grad_pre
    taps_out[j, 0:1, cols] = jnp.sum(grad_pre * x, axis=0, keepdims=True)
    for tap in range(1, CONV):
        masked = grad_pre * masks[tap - 1]
        grad_x = grad_x + taps[tap : tap + 1] * pltpu.roll(masked, TOK_MB - tap, 0)
        taps_out[j, tap : tap + 1, cols] = jnp.sum(masked * pltpu.roll(x, tap, 0), axis=0, keepdims=True)
    return grad_x


def attend_back_kernel(heads, count, me_ref, seg_col_ref, seg_row_ref, masks_ref, taps_ref, gain_ref,
                       qkv_ref, logit_ref, system_ref, attend_ref, inverse_ref, fresh_ref, out_ref, *refs):
    shards, refs = refs[:count], refs[count:]
    project_hbm, beta_hbm, merge_hbm = refs[:3]
    grad_qkv_ref, grad_logit_ref, grad_taps_ref, grad_gain_ref = refs[3:7]
    partials = refs[7 : 7 + count]
    rows_ref, grad_mixed_ref, grad_abs_ref, logit_abs_ref, project_ref, beta_ref, merge_ref, sems = refs[7 + count :]
    order = relative_order(count)
    share = TOK_MB // count
    model = rows_ref.shape[1]
    width = heads * HEAD_DIM
    fetch = Fetch(
        [(merge_hbm.at[0], merge_ref), (beta_hbm, beta_ref)]
        + [(project_hbm.at[0, j], project_ref.at[j]) for j in range(3)],
        sems,
        0,
    )
    fetch.start_to(5)
    for k in range(count):
        rows_ref[k * share : (k + 1) * share, :] = shards[k][...]
    fetch.wait(0)
    for cols in tiles_of(heads * HEAD_DIM):
        value = mm_t(rows_ref[...], merge_ref[cols, :])
        for k, difference in enumerate(order):
            grad_mixed_ref[place_of(me_ref, difference, share), cols] = value[k * share : (k + 1) * share]

    masks = [masks_ref[i] for i in range(CONV - 1)]
    strict, lower = block_masks(seg_col_ref, seg_row_ref)
    lane = lax.broadcasted_iota(jnp.int32, (TOK_MB, LANES), 1)
    everyone = range(heads)
    columns = [slice(h * HEAD_DIM, (h + 1) * HEAD_DIM) for h in everyone]
    grad_gain = jnp.zeros((8, HEAD_DIM), F32)
    grad_outs, queries, keys, values, betas, convs = [], [], [], [], [], []
    for h in everyone:
        cols = columns[h]
        taps = [taps_ref[0, j, :, cols] for j in range(3)]
        _, _, conv_q = stream(qkv_ref[0, :, cols], taps[0], masks)
        _, _, conv_k = stream(qkv_ref[1, :, cols], taps[1], masks)
        scale_q = lax.rsqrt(jnp.sum(conv_q * conv_q, axis=-1, keepdims=True) + EPS)
        scale_k = lax.rsqrt(jnp.sum(conv_k * conv_k, axis=-1, keepdims=True) + EPS)
        queries.append((conv_q * (scale_q * HEAD_DIM**-0.5)).astype(BF16))
        keys.append((conv_k * scale_k).astype(BF16))
        betas.append(jax.nn.sigmoid(logit_ref[:, h : h + 1]))
        out = out_ref[:, cols]
        grad_mixed = grad_mixed_ref[:, cols]
        mean = jnp.mean(out * out, axis=-1, keepdims=True)
        scale = lax.rsqrt(jnp.maximum(mean, OUT_FLOOR))
        unit = out * scale
        grad_gain = grad_gain + jnp.sum((grad_mixed * unit).reshape(TOK_MB // 8, 8, HEAD_DIM), axis=0)
        grad_unit = grad_mixed * gain_ref[...]
        through = jnp.where(mean > OUT_FLOOR, 1.0, jnp.where(mean == OUT_FLOOR, 0.5, 0.0))
        grad_out = scale * (
            grad_unit - unit * (through * jnp.mean(grad_unit * unit, axis=-1, keepdims=True))
        )
        grad_outs.append(grad_out.astype(BF16))
    grad_gain_ref[...] = grad_gain
    fresh = {(h, b): fresh_ref[rows_of(b), columns[h]] for h in everyone for b in range(BLOCKS)}
    d_out = {(h, b): grad_outs[h][rows_of(b)] for h in everyone for b in range(BLOCKS)}
    key_blocks = {(h, b): keys[h][rows_of(b)] for h in everyone for b in range(BLOCKS)}
    d_fresh, d_target, d_target_b = {}, {}, {}
    for c in range(BLOCKS):
        for h in everyone:
            total = t_mm(attend_ref[h, rows_of(c), rows_of(c)], d_out[h, c])
            for b in range(c + 1, BLOCKS):
                total = total + t_mm(attend_ref[h, rows_of(b), rows_of(c)], d_out[h, b])
            d_fresh[h, c] = total
    for b in reversed(range(BLOCKS)):
        for h in everyone:
            d_target[h, b] = t_mm(inverse_ref[h, b], d_fresh[h, b])
            d_target_b[h, b] = d_target[h, b].astype(BF16)
        for h in everyone:
            for c in range(b):
                d_fresh[h, c] = d_fresh[h, c] - t_mm(system_ref[h, rows_of(b), rows_of(c)], d_target_b[h, b])
    grad_query, inner, grad_key = {}, {}, {}
    for b in range(BLOCKS):
        for c in range(b + 1):
            for h in everyone:
                d_attend = jnp.where(lower[b, c], mm_t(d_out[h, b], fresh[h, c]), 0.0).astype(BF16)
                d_system = jnp.where(strict[b, c], -mm_t(d_target_b[h, b], fresh[h, c]), 0.0)
                for store, place, part in (
                    (grad_query, b, mm(d_attend, key_blocks[h, c])),
                    (inner, b, mm(d_system, key_blocks[h, c])),
                    (grad_key, c, t_mm(d_attend, queries[h][rows_of(b)])
                     + t_mm(d_system * betas[h][rows_of(b)], key_blocks[h, b])),
                ):
                    store[h, place] = store[h, place] + part if (h, place) in store else part

    def whole(store, h):
        return jnp.concatenate([store[h, b] for b in range(BLOCKS)], axis=0)

    grad_logits = jnp.zeros((TOK_MB, LANES), F32)
    for h in everyone:
        cols = columns[h]
        beta = betas[h]
        taps = [taps_ref[0, j, :, cols] for j in range(3)]
        inputs = [qkv_ref[j, :, cols] for j in range(3)]
        pre_q, gate_q, conv_q = stream(inputs[0], taps[0], masks)
        pre_k, gate_k, conv_k = stream(inputs[1], taps[1], masks)
        pre_v, gate_v, value = stream(inputs[2], taps[2], masks)
        scale_q = lax.rsqrt(jnp.sum(conv_q * conv_q, axis=-1, keepdims=True) + EPS)
        scale_k = lax.rsqrt(jnp.sum(conv_k * conv_k, axis=-1, keepdims=True) + EPS)
        unit_q, key = conv_q * scale_q, conv_k * scale_k
        within = whole(inner, h)
        target = whole(d_target, h)
        grad_q = whole(grad_query, h)
        grad_k = whole(grad_key, h) + beta * within
        grad_beta = jnp.sum(within * key + target * value, axis=-1, keepdims=True)
        grad_logits = jnp.where(lane == h, grad_beta * beta * (1.0 - beta), grad_logits)
        grad_conv_q = (HEAD_DIM**-0.5 * scale_q) * (
            grad_q - unit_q * jnp.sum(grad_q * unit_q, axis=-1, keepdims=True)
        )
        grad_conv_k = scale_k * (grad_k - key * jnp.sum(grad_k * key, axis=-1, keepdims=True))
        for j, (grad, pre, gate) in enumerate(
            ((grad_conv_q, pre_q, gate_q), (grad_conv_k, pre_k, gate_k), (beta * target, pre_v, gate_v))
        ):
            grad_x = stream_back(grad, inputs[j], pre, gate, taps[j], masks, grad_taps_ref, j, cols)
            grad_abs_ref[j, :, cols] = grad_x.astype(BF16)
    logit_abs_ref[...] = grad_logits.astype(BF16)
    for k, difference in enumerate(order):
        here = slice(k * share, (k + 1) * share)
        there = place_of(me_ref, difference, share)
        grad_logit_ref[here, :] = logit_abs_ref[there, :]
        for j in range(3):
            grad_qkv_ref[here, j * width : (j + 1) * width] = grad_abs_ref[j, there, :]
    for place in range(1, 5):
        fetch.wait(place)
    for span in tiles_of(model):
        value = mm_t(grad_logit_ref[...], beta_ref[span, :])
        for j in range(3):
            value = value + mm_t(grad_qkv_ref[:, j * width : (j + 1) * width], project_ref[j, span, :])
        for k, ref in enumerate(partials):
            ref[:, span] = value[k * share : (k + 1) * share].astype(ref.dtype)


def attend_backward(me, mine, shards, kept, taps, gain, project, beta_weight, merge):
    masks, seg_col, seg_row = mine
    heads = merge.shape[1] // HEAD_DIM
    width = heads * HEAD_DIM
    model = merge.shape[2]
    count = len(shards)
    qkv, logit, _, system, attend, inverse, fresh, out = kept
    results = call(
        functools.partial(attend_back_kernel, heads, count),
        (me, seg_col, seg_row, masks, taps, gain, qkv, logit, system, attend, inverse, fresh, out, *shards),
        (project, beta_weight, merge),
        [
            jax.ShapeDtypeStruct((TOK_MB, 3 * width), BF16),
            jax.ShapeDtypeStruct((TOK_MB, LANES), BF16),
            jax.ShapeDtypeStruct((3, CONV, width), F32),
            jax.ShapeDtypeStruct((8, HEAD_DIM), F32),
        ]
        + partial_shapes(count, model),
        [
            pltpu.VMEM((TOK_MB, model), BF16),
            pltpu.VMEM((TOK_MB, width), F32),
            pltpu.VMEM((3, TOK_MB, width), BF16),
            pltpu.VMEM((TOK_MB, LANES), BF16),
            pltpu.VMEM(project.shape[1:], BF16),
            pltpu.VMEM(beta_weight.shape, BF16),
            pltpu.VMEM(merge.shape[1:], BF16),
            pltpu.SemaphoreType.DMA((5,)),
        ],
    )
    return results[:4], results[4:]


def tap_masks(segment):
    masks = []
    for tap in range(1, CONV):
        earlier = jnp.concatenate([jnp.full((tap,), -1, jnp.int32), segment[: TOK_MB - tap]], axis=0)
        masks.append(jnp.broadcast_to((earlier == segment).astype(F32)[:, None], (TOK_MB, HEAD_DIM)))
    return jnp.stack(masks)


def narrow(values):
    return values.astype(BF16)


def product(left, right):
    return jnp.dot(left, right, preferred_element_type=F32)


def product_left(left, right):
    return lax.dot_general(left, right, (((0,), (0,)), ((), ())), preferred_element_type=F32)


def product_right(left, right):
    return lax.dot_general(left, right, (((1,), (1,)), ((), ())), preferred_element_type=F32)


def rms_parts(values):
    scale = lax.rsqrt(jnp.mean(values * values, axis=-1, keepdims=True) + EPS)
    return (values * scale, scale)


def norm_back(grad_normed, normed, scale, gain):
    grad_scaled = grad_normed * gain
    return scale * (grad_scaled - normed * jnp.mean(grad_scaled * normed, axis=-1, keepdims=True))


def segment_ids(lengths, count):
    ends = jnp.cumsum(lengths)
    places = jnp.arange(count, dtype=jnp.int32)
    return jnp.sum((places[:, None] >= ends[None, :]).astype(jnp.int32), axis=1, dtype=jnp.int32)


def flipped(values, axis, bit):
    return lax.ppermute(values, axis, [(i, i ^ bit) for i in range(lax.axis_size(axis))])


def shifted(values, axis, distance):
    devices = range(lax.axis_size(axis))
    return lax.ppermute(values, axis, [(i, i + distance) for i in devices if i + distance in devices])


def bits_of(axis):
    size = lax.axis_size(axis)
    bits = [1 << k for k in range(size.bit_length() - 1)]
    assert 1 << len(bits) == size
    return bits


def summed(values, axes):
    for axis in axes:
        for bit in bits_of(axis):
            values = values + flipped(values, axis, bit)
    return values


def gather(shard):
    parts = [shard]
    for bit in reversed(bits_of("head")):
        parts = parts + [flipped(part, "head", bit) for part in parts]
    return parts


def scatter(parts):
    for bit in bits_of("head"):
        half = len(parts) // 2
        arrived = [flipped(narrow(part), "head", bit) for part in parts[half:]]
        parts = [part.astype(F32) + other.astype(F32) for part, other in zip(parts[:half], arrived)]
    return parts[0]


def swapped(shard):
    count = lax.axis_size("dp")
    me = lax.axis_index("dp")
    rows, width = shard.shape
    blocks = shard.reshape(rows, count, width // count)
    arrived = []
    for distance in range(count):
        block = lax.dynamic_index_in_dim(blocks, (me + distance) % count, 1, keepdims=False)
        if distance:
            block = lax.ppermute(block, "dp", [(i, (i + distance) % count) for i in range(count)])
        arrived.append(block)
    arrived = jnp.stack(arrived)
    ordered = [lax.dynamic_index_in_dim(arrived, (me - q) % count, 0, keepdims=False) for q in range(count)]
    return jnp.concatenate(ordered, axis=1)


def per_device(
    tokens,
    lengths,
    cotangent,
    attn_in,
    beta_weight,
    conv_weight,
    o_gain,
    attn_out,
    mlp_in,
    mlp_out,
    norm_gains,
):
    section = lax.axis_index("section")
    sections = lax.axis_size("section")
    member = lax.axis_index("head")
    micro = tokens.shape[0]
    width = tokens.shape[2]
    heads = beta_weight.shape[2]
    share = TOK_MB // lax.axis_size("head")
    me = member[None]
    beta_wide = jnp.pad(beta_weight[0], ((0, 0), (0, LANES - heads)))
    gains = norm_gains[0]
    every = range(micro)
    segments = [segment_ids(lengths[m], TOK_MB) for m in every]
    masks = [(tap_masks(s), s[:, None], s[None, :]) for s in segments]
    own_rows = lambda values: lax.dynamic_slice_in_dim(values, member * share, share, 0).astype(F32)
    tokens_own = [own_rows(tokens[m]) for m in every]
    cotangent_own = [own_rows(cotangent[m]) for m in every]

    def forward(x, mine):
        unit, scale = rms_parts(x)
        normed = gather(narrow(unit * gains[0]))
        kept, partials = attend_forward(me, mine, normed, conv_weight, o_gain, attn_in, beta_wide, attn_out)
        middle = x + scatter(partials)
        unit_mid, scale_mid = rms_parts(middle)
        normed_mid = gather(narrow(unit_mid * gains[1]))
        (hidden, silu, slope), partials = expand_forward(me, normed_mid, mlp_in, mlp_out)
        result = middle + scatter(partials)
        return result, (unit, scale, normed, kept, unit_mid, scale_mid, normed_mid, hidden, silu, slope)

    def backward_mlp(incoming, saved):
        unit_mid, scale_mid, silu, slope = saved[4], saved[5], saved[8], saved[9]
        grads, partials = expand_backward(me, gather(narrow(incoming)), silu, slope, mlp_in, mlp_out)
        grad_mid = scatter(partials)
        grad_middle = incoming + norm_back(grad_mid, unit_mid, scale_mid, gains[1])
        return grad_middle, grads, jnp.sum(grad_mid * unit_mid, axis=0)

    def backward_mix(grad_middle, gain_two, mine, saved):
        unit, scale, _, kept = saved[:4]
        (grad_qkv, grad_logit, grad_taps, grad_head_gain), partials = attend_backward(
            me, mine, gather(narrow(grad_middle)), kept, conv_weight, o_gain, attn_in, beta_wide, attn_out
        )
        grad_norm = scatter(partials)
        grad_inputs = grad_middle + norm_back(grad_norm, unit, scale, gains[0])
        gain_one = jnp.sum(grad_norm * unit, axis=0)
        small = (grad_taps, jnp.sum(grad_head_gain, axis=0), jnp.stack([gain_one, gain_two]))
        return grad_inputs, grad_qkv, grad_logit, small

    def forward_turn(inputs):
        results = [forward(inputs[m], masks[m]) for m in every]
        return [result for result, _ in results], [saved for _, saved in results]

    last = sections - 1
    inputs = tokens_own
    for turn in range(sections):
        outputs, kept = forward_turn(inputs)
        if turn < last:
            arrived = [shifted(narrow(value), "section", 1).astype(F32) for value in outputs]
            inputs = [jnp.where(section == 0, tokens_own[m], arrived[m]) for m in every]

    def every_row(values):
        return [lax.all_gather(value, "dp", axis=0) for value in values]

    hidden_rows = every_row([saved[7] for saved in kept])
    mixed_rows = every_row([saved[3][2] for saved in kept])

    incoming = cotangent_own
    for turn in range(sections):
        if turn == last:
            incoming, hidden_rows, mixed_rows = lax.optimization_barrier((incoming, hidden_rows, mixed_rows))
        halves = [backward_mlp(incoming[m], kept[m]) for m in every]
        middles = [half[0] for half in halves]
        if turn == last:
            normed_mid = jnp.concatenate([part for saved in kept for part in saved[6]], axis=0)
            expands = [
                narrow(product_left(normed_mid, jnp.concatenate([half[1][j] for half in halves], axis=0)))
                for j in range(2)
            ]
            middles, expands = lax.optimization_barrier((middles, expands))
        results = [backward_mix(middles[m], halves[m][2], masks[m], kept[m]) for m in every]
        finals = [result[0] for result in results]
        if turn < last:
            arrived = [shifted(narrow(value), "section", -1).astype(F32) for value in finals]
            incoming = [jnp.where(section == last, cotangent_own[m], arrived[m]) for m in every]
    rows_out = jnp.stack(finals)
    half = width // sections
    moved = shifted(narrow(rows_out[:, :, half:]), "section", 1).astype(F32)
    grad_tokens = jnp.where(section == 0, rows_out[:, :, :half], moved)

    def spread(value, axis):
        return lax.psum_scatter(value, "dp", scatter_dimension=axis, tiled=True)

    early = [spread(part, 0) for part in expands]
    normed = jnp.concatenate([part for saved in kept for part in saved[2]], axis=0)
    grad_qkv = jnp.concatenate([result[1] for result in results], axis=0)
    grad_logit = jnp.concatenate([result[2] for result in results], axis=0)
    grad_project = narrow(product_left(normed, grad_qkv))
    grad_beta = product_left(normed, grad_logit)[:, :heads]

    def from_rows(rows, shards):
        total = 0.0
        for left, right in zip(rows, shards):
            right = jnp.concatenate(gather(swapped(right)), axis=0).reshape(TOK_MB, left.shape[0], -1)
            total = total + lax.dot_general(
                left, right, (((0, 1), (1, 0)), ((), ())), preferred_element_type=F32
            )
        return total

    grad_contract = from_rows(hidden_rows, [narrow(value) for value in incoming])
    grad_merge = from_rows(mixed_rows, [narrow(value) for value in middles])
    grad_taps, grad_head_gain, grad_gains = (
        sum(result[3][place] for result in results) for place in range(3)
    )
    grad_gains = summed(jnp.concatenate([grad_gains.reshape(-1), grad_head_gain]), ("dp", "head"))
    grad_gains, grad_head_gain = grad_gains[: 2 * width].reshape(2, width), grad_gains[2 * width :]
    flat = summed(jnp.concatenate([grad_taps.reshape(-1), grad_beta.reshape(-1)]), ("dp",))
    grad_taps, grad_beta = flat[: grad_taps.size].reshape(grad_taps.shape), flat[grad_taps.size :]
    rows = width // lax.axis_size("dp")
    grad_beta = lax.dynamic_slice_in_dim(grad_beta.reshape(width, heads), lax.axis_index("dp") * rows, rows, 0)
    done = (grad_tokens, grad_contract, grad_merge, grad_beta, grad_taps, grad_head_gain, grad_gains, early)
    grad_project, done = lax.optimization_barrier((grad_project, done))
    grad_tokens, grad_contract, grad_merge, grad_beta, grad_taps, grad_head_gain, grad_gains, early = done
    grad_expand = jnp.stack(early).astype(F32)
    grad_project = jnp.stack(jnp.split(spread(grad_project, 0), 3, axis=1)).astype(F32)
    return (
        grad_tokens,
        grad_project[None],
        grad_beta[None],
        grad_taps[None],
        grad_head_gain[None],
        grad_merge[None],
        grad_expand[None],
        grad_contract[None],
        grad_gains[None],
    )


def solution(mesh):
    return jax.shard_map(
        per_device,
        mesh=mesh,
        in_specs=(
            P("dp", None, None),
            P("dp", None),
            P("dp", None, None),
            P("section", None, None, "head"),
            P("section", None, "head"),
            P("section", None, None, "head"),
            P("section", None),
            P("section", "head", None),
            P("section", None, None, "head"),
            P("section", "head", None),
            P("section", None, None),
        ),
        out_specs=(
            P("dp", "head", "section"),
            P("section", None, "dp", "head"),
            P("section", "dp", "head"),
            P("section", None, None, "head"),
            P("section", None),
            P("section", "head", "dp"),
            P("section", None, "dp", "head"),
            P("section", "head", "dp"),
            P("section", None, None),
        ),
        check_vma=False,
    )
```

```python
import functools

import jax
import jax.numpy as jnp
from jax import lax
from jax.experimental import pallas as pl
from jax.experimental.pallas import tpu as pltpu
from jax.sharding import PartitionSpec as P

HEAD_DIM = 128
CONV = 4
TOK_MB = 384
BLOCK = 128
BLOCKS = TOK_MB // BLOCK
EPS = 1e-06
OUT_FLOOR = 0.0001
F32 = jnp.float32
BF16 = jnp.bfloat16
BASE = 4
LANES = 128
TILE = 256
QUARTERS = 4
VMEM_LIMIT = 44 * 1024 * 1024


def mm(left, right):
    return lax.dot_general(
        left.astype(BF16), right.astype(BF16), (((1,), (0,)), ((), ())), preferred_element_type=F32
    )


def mm_t(left, right):
    return lax.dot_general(
        left.astype(BF16), right.astype(BF16), (((1,), (1,)), ((), ())), preferred_element_type=F32
    )


def t_mm(left, right):
    return lax.dot_general(
        left.astype(BF16), right.astype(BF16), (((0,), (0,)), ((), ())), preferred_element_type=F32
    )


def rows_of(b):
    return slice(b * BLOCK, (b + 1) * BLOCK)


def tiles_of(size, tile=TILE):
    return [slice(start, min(start + tile, size)) for start in range(0, size, tile)]


def quarters(size):
    return tiles_of(size, size // QUARTERS)


def relative_order(count):
    order, bit = [0], count // 2
    while bit:
        order = order + [k ^ bit for k in order]
        bit //= 2
    return order


def place_of(me_ref, difference, share):
    return pl.ds(pl.multiple_of((me_ref[0] ^ difference) * share, 16), share)


def stream(x, taps, masks):
    pre = taps[0:1] * x
    for tap in range(1, CONV):
        pre = pre + taps[tap : tap + 1] * (pltpu.roll(x, tap, 0) * masks[tap - 1])
    gate = jax.nn.sigmoid(pre)
    return pre, gate, pre * gate


def unit_inverses(systems):
    size = systems[0].shape[0]
    row = lax.broadcasted_iota(jnp.int32, (size, size), 0)
    col = lax.broadcasted_iota(jnp.int32, (size, size), 1)
    eye = (row == col).astype(F32)
    near = (row // BASE == col // BASE).astype(F32)
    first = [-a * near for a in systems]
    total = [eye + n for n in first]
    second = [mm(n, n) for n in first]
    third = [mm(n, s) for n, s in zip(first, second)]
    total = [t + s + r for t, s, r in zip(total, second, third)]
    step = BASE
    while step < size:
        span = 2 * step
        off = ((row // span == col // span) & (row // step != col // step)).astype(F32)
        inner = [mm(a * off, t) for a, t in zip(systems, total)]
        outer = [mm(t, i) for t, i in zip(total, inner)]
        total = [t - o for t, o in zip(total, outer)]
        step = span
    return total


def block_masks(seg_col_ref, seg_row_ref):
    row = lax.broadcasted_iota(jnp.int32, (BLOCK, BLOCK), 0)
    col = lax.broadcasted_iota(jnp.int32, (BLOCK, BLOCK), 1)
    strict, lower = {}, {}
    for b in range(BLOCKS):
        for c in range(b + 1):
            same = seg_col_ref[rows_of(b), :] == seg_row_ref[:, rows_of(c)]
            strict[b, c] = same & (col < row) if b == c else same
            lower[b, c] = same & (col <= row) if b == c else same
    return strict, lower


class Fetch:

    def __init__(self, pairs, sems, ahead):
        self.copies = [pltpu.make_async_copy(src, dst, sems.at[i]) for i, (src, dst) in enumerate(pairs)]
        self.ahead = ahead
        self.started = 0
        self.start_to(ahead)

    def start_to(self, place):
        while self.started < min(place, len(self.copies)):
            self.copies[self.started].start()
            self.started += 1

    def wait(self, place):
        self.copies[place].wait()
        self.start_to(place + 1 + self.ahead)

    def wait_group(self, group):
        for place in range(QUARTERS):
            self.wait(QUARTERS * group + place)


def attend_kernel(heads, count, save, me_ref, seg_col_ref, seg_row_ref, masks_ref, taps_ref, gain_ref, *refs):
    shards, refs = refs[:count], refs[count:]
    project_hbm, beta_hbm, merge_hbm = refs[:3]
    partials, refs = refs[3 : 3 + count], refs[3 + count :]
    rows_ref, qkv_ref, logit_ref, mixed_ref, refs = *refs[:4], refs[4:]
    if save:
        system_ref, attend_ref, inverse_ref, fresh_ref, out_ref, refs = *refs[:5], refs[5:]
    mixed_abs, project_ref, beta_ref, merge_ref, sems = refs
    order = relative_order(count)
    share = TOK_MB // count
    fetch = Fetch(
        [(project_hbm.at[0, j], project_ref.at[j]) for j in range(3)]
        + [(beta_hbm, beta_ref), (merge_hbm.at[0], merge_ref)],
        sems,
        5,
    )
    for k in range(count):
        rows_ref[k * share : (k + 1) * share, :] = shards[k][...]
    rows = rows_ref[...]

    def spread(ref, value, *lead):
        for k, difference in enumerate(order):
            ref[(*lead, place_of(me_ref, difference, share), slice(None))] = value[k * share : (k + 1) * share]

    for j in range(3):
        fetch.wait(j)
        for cols in tiles_of(heads * HEAD_DIM):
            value = mm(rows, project_ref[j, :, cols])
            for k, difference in enumerate(order):
                qkv_ref[j, place_of(me_ref, difference, share), cols] = value[k * share : (k + 1) * share]
    fetch.wait(3)
    spread(logit_ref, mm(rows, beta_ref[...]))

    masks = [masks_ref[i] for i in range(CONV - 1)]
    strict, lower = block_masks(seg_col_ref, seg_row_ref)
    queries, keys, values, betas = [], [], [], []
    for h in range(heads):
        cols = slice(h * HEAD_DIM, (h + 1) * HEAD_DIM)
        taps = [taps_ref[0, j, :, cols] for j in range(3)]
        _, _, query = stream(qkv_ref[0, :, cols], taps[0], masks)
        _, _, key = stream(qkv_ref[1, :, cols], taps[1], masks)
        _, _, value = stream(qkv_ref[2, :, cols], taps[2], masks)
        query = query * lax.rsqrt(jnp.sum(query * query, axis=-1, keepdims=True) + EPS) * HEAD_DIM**-0.5
        key = key * lax.rsqrt(jnp.sum(key * key, axis=-1, keepdims=True) + EPS)
        beta = jax.nn.sigmoid(logit_ref[:, h : h + 1])
        queries.append(query.astype(BF16))
        keys.append(key.astype(BF16))
        values.append(value * beta)
        betas.append(beta)
    attend, system = {}, {}
    for h in range(heads):
        for b in range(BLOCKS):
            for c in range(b + 1):
                inner = mm_t(keys[h][rows_of(b)], keys[h][rows_of(c)])
                system[h, b, c] = jnp.where(strict[b, c], inner * betas[h][rows_of(b)], 0.0)
                scores = mm_t(queries[h][rows_of(b)], keys[h][rows_of(c)])
                attend[h, b, c] = jnp.where(lower[b, c], scores, 0.0).astype(BF16)
                if c < b:
                    system[h, b, c] = system[h, b, c].astype(BF16)
                if save:
                    attend_ref[h, rows_of(b), rows_of(c)] = attend[h, b, c]
                    if c < b:
                        system_ref[h, rows_of(b), rows_of(c)] = system[h, b, c]
    index = [(h, b) for h in range(heads) for b in range(BLOCKS)]
    inverse = dict(zip(index, unit_inverses([system[h, b, b] for h, b in index])))
    for h, b in index:
        inverse[h, b] = inverse[h, b].astype(BF16)
        if save:
            inverse_ref[h, b] = inverse[h, b]
    fresh = {}
    for b in range(BLOCKS):
        for h in range(heads):
            target = values[h][rows_of(b)]
            for c in range(b):
                target = target - mm(system[h, b, c], fresh[h, c])
            fresh[h, b] = mm(inverse[h, b], target).astype(BF16)
            if save:
                fresh_ref[rows_of(b), h * HEAD_DIM : (h + 1) * HEAD_DIM] = fresh[h, b]
    for h in range(heads):
        cols = slice(h * HEAD_DIM, (h + 1) * HEAD_DIM)
        for b in range(BLOCKS):
            out = mm(attend[h, b, 0], fresh[h, 0])
            for c in range(1, b + 1):
                out = out + mm(attend[h, b, c], fresh[h, c])
            mean = jnp.mean(out * out, axis=-1, keepdims=True)
            if save:
                out_ref[rows_of(b), cols] = out
            mixed_abs[rows_of(b), cols] = (
                out * lax.rsqrt(jnp.maximum(mean, OUT_FLOOR)) * gain_ref[...]
            ).astype(BF16)
    for k, difference in enumerate(order):
        mixed_ref[k * share : (k + 1) * share, :] = mixed_abs[place_of(me_ref, difference, share), :]
    fetch.wait(4)
    write_partials(partials, merge_ref.shape[1], share, lambda cols: mm(mixed_ref[...], merge_ref[:, cols]))


def write_partials(partials, width, share, product):
    for cols in tiles_of(width):
        value = product(cols)
        for k, ref in enumerate(partials):
            ref[:, cols] = value[k * share : (k + 1) * share].astype(ref.dtype)


def partial_shapes(count, width):
    share = TOK_MB // count
    return [jax.ShapeDtypeStruct((share, width), F32 if k < count // 2 else BF16) for k in range(count)]


def call(kernel, operands, hbm, out_shape, scratch_shapes):
    vmem = pl.BlockSpec(memory_space=pltpu.VMEM)
    return pl.pallas_call(
        kernel,
        in_specs=[pl.BlockSpec(memory_space=pltpu.SMEM)]
        + [vmem] * (len(operands) - 1)
        + [pl.BlockSpec(memory_space=pl.ANY)] * len(hbm),
        out_specs=[vmem] * len(out_shape),
        out_shape=out_shape,
        scratch_shapes=scratch_shapes,
        compiler_params=pltpu.CompilerParams(vmem_limit_bytes=VMEM_LIMIT),
        cost_estimate=pl.CostEstimate(flops=10**6, bytes_accessed=10**5, transcendentals=0),
    )(*operands, *hbm)


def as_scratch(shapes):
    return [pltpu.VMEM(shape.shape, shape.dtype) for shape in shapes]


def attend_forward(me, mine, shards, taps, gain, project, beta_weight, merge, save):
    masks, seg_col, seg_row = mine
    heads = merge.shape[1] // HEAD_DIM
    width = heads * HEAD_DIM
    model = merge.shape[2]
    count = len(shards)
    kept = [
        jax.ShapeDtypeStruct((TOK_MB, model), BF16),
        jax.ShapeDtypeStruct((3, TOK_MB, width), F32),
        jax.ShapeDtypeStruct((TOK_MB, LANES), F32),
        jax.ShapeDtypeStruct((TOK_MB, width), BF16),
    ]
    more = [
        jax.ShapeDtypeStruct((heads, TOK_MB, TOK_MB), BF16),
        jax.ShapeDtypeStruct((heads, TOK_MB, TOK_MB), BF16),
        jax.ShapeDtypeStruct((heads, BLOCKS, BLOCK, BLOCK), BF16),
        jax.ShapeDtypeStruct((TOK_MB, width), BF16),
        jax.ShapeDtypeStruct((TOK_MB, width), F32),
    ]
    results = call(
        functools.partial(attend_kernel, heads, count, save),
        (me, seg_col, seg_row, masks, taps, gain, *shards),
        (project, beta_weight, merge),
        partial_shapes(count, model) + (kept + more if save else []),
        ([] if save else as_scratch(kept))
        + [
            pltpu.VMEM((TOK_MB, width), BF16),
            pltpu.VMEM(project.shape[1:], BF16),
            pltpu.VMEM(beta_weight.shape, BF16),
            pltpu.VMEM(merge.shape[1:], BF16),
            pltpu.SemaphoreType.DMA((5,)),
        ],
    )
    return results[count:], results[:count]


def expand_kernel(count, save, me_ref, *refs):
    shards, refs = refs[:count], refs[count:]
    expand_hbm, contract_hbm = refs[:2]
    partials, refs = refs[2 : 2 + count], refs[2 + count :]
    rows_ref, hidden_ref, refs = *refs[:2], refs[2:]
    if save:
        silu_ref, slope_ref, refs = *refs[:2], refs[2:]
    gate_ref, expand_ref, contract_ref, sems = refs
    share = TOK_MB // count
    tiles = tiles_of(hidden_ref.shape[1])
    fetch = Fetch(
        [(expand_hbm.at[0, j, s, :], expand_ref.at[j, s, :]) for j in range(2) for s in quarters(expand_ref.shape[1])]
        + [(contract_hbm.at[0, s, :], contract_ref.at[s, :]) for s in quarters(contract_ref.shape[0])],
        sems,
        QUARTERS,
    )
    for k in range(count):
        rows_ref[k * share : (k + 1) * share, :] = shards[k][...]
    fetch.wait_group(0)
    for t in tiles:
        gate_ref[:, t] = mm(rows_ref[...], expand_ref[0, :, t])
    fetch.wait_group(1)
    for t in tiles:
        up_in = mm(rows_ref[...], expand_ref[1, :, t])
        gate_in = gate_ref[:, t]
        gate = jax.nn.sigmoid(gate_in)
        silu = gate_in * gate
        hidden_ref[:, t] = (silu * up_in).astype(BF16)
        if save:
            silu_ref[:, t] = silu.astype(BF16)
            slope_ref[:, t] = (up_in * gate * (1.0 + gate_in * (1.0 - gate))).astype(BF16)
    fetch.wait_group(2)
    write_partials(partials, rows_ref.shape[1], share, lambda cols: mm(hidden_ref[...], contract_ref[:, cols]))


def expand_forward(me, shards, expand, contract, save):
    count = len(shards)
    model, units = expand.shape[2:]
    kept = [jax.ShapeDtypeStruct((TOK_MB, model), BF16)] + [jax.ShapeDtypeStruct((TOK_MB, units), BF16)] * 3
    results = call(
        functools.partial(expand_kernel, count, save),
        (me, *shards),
        (expand, contract),
        partial_shapes(count, model) + (kept if save else []),
        ([] if save else as_scratch(kept[:2]))
        + [
            pltpu.VMEM((TOK_MB, units), F32),
            pltpu.VMEM(expand.shape[1:], BF16),
            pltpu.VMEM(contract.shape[1:], BF16),
            pltpu.SemaphoreType.DMA((3 * QUARTERS,)),
        ],
    )
    return results[count:], results[:count]


def expand_back_kernel(count, me_ref, silu_ref, slope_ref, *refs):
    shards, refs = refs[:count], refs[count:]
    expand_hbm, contract_hbm, gate_ref, up_ref = refs[:4]
    partials = refs[4 : 4 + count]
    rows_ref, expand_ref, contract_ref, sems = refs[4 + count :]
    share = TOK_MB // count
    tiles = tiles_of(gate_ref.shape[1])
    spans = tiles_of(rows_ref.shape[1], 2 * TILE)
    fetch = Fetch(
        [(contract_hbm.at[0, s, :], contract_ref.at[s, :]) for s in quarters(contract_ref.shape[0])]
        + [(expand_hbm.at[0, j, s, :], expand_ref.at[j, s, :]) for s in spans for j in range(2)],
        sems,
        4,
    )
    for k in range(count):
        rows_ref[k * share : (k + 1) * share, :] = shards[k][...]
    fetch.wait_group(0)
    for t in tiles:
        grad_hidden = mm_t(rows_ref[...], contract_ref[t, :])
        gate_ref[:, t] = (grad_hidden * slope_ref[:, t].astype(F32)).astype(BF16)
        up_ref[:, t] = (grad_hidden * silu_ref[:, t].astype(F32)).astype(BF16)
    for i, span in enumerate(spans):
        for j in range(2):
            fetch.wait(QUARTERS + 2 * i + j)
        for s in tiles_of(span.stop - span.start):
            s = slice(span.start + s.start, span.start + s.stop)
            value = mm_t(gate_ref[...], expand_ref[0, s, :]) + mm_t(up_ref[...], expand_ref[1, s, :])
            for k, ref in enumerate(partials):
                ref[:, s] = value[k * share : (k + 1) * share].astype(ref.dtype)


def expand_backward(me, shards, silu, slope, expand, contract):
    count = len(shards)
    model, units = expand.shape[2:]
    kept = jax.ShapeDtypeStruct((TOK_MB, units), BF16)
    results = call(
        functools.partial(expand_back_kernel, count),
        (me, silu, slope, *shards),
        (expand, contract),
        [kept, kept] + partial_shapes(count, model),
        [
            pltpu.VMEM((TOK_MB, model), BF16),
            pltpu.VMEM(expand.shape[1:], BF16),
            pltpu.VMEM(contract.shape[1:], BF16),
            pltpu.SemaphoreType.DMA((QUARTERS + 2 * len(tiles_of(model, 2 * TILE)),)),
        ],
    )
    return results[:2], results[2:]


def stream_back(grad, x, pre, gate, taps, masks, taps_out, j, cols):
    grad_pre = grad * gate * (1.0 + pre * (1.0 - gate))
    grad_x = taps[0:1] * grad_pre
    taps_out[j, 0:1, cols] = jnp.sum(grad_pre * x, axis=0, keepdims=True)
    for tap in range(1, CONV):
        masked = grad_pre * masks[tap - 1]
        grad_x = grad_x + taps[tap : tap + 1] * pltpu.roll(masked, TOK_MB - tap, 0)
        taps_out[j, tap : tap + 1, cols] = jnp.sum(masked * pltpu.roll(x, tap, 0), axis=0, keepdims=True)
    return grad_x


def attend_back_kernel(heads, count, me_ref, seg_col_ref, seg_row_ref, masks_ref, taps_ref, gain_ref,
                       qkv_ref, logit_ref, system_ref, attend_ref, inverse_ref, fresh_ref, out_ref, *refs):
    shards, refs = refs[:count], refs[count:]
    project_hbm, beta_hbm, merge_hbm = refs[:3]
    grad_qkv_ref, grad_logit_ref, grad_taps_ref, grad_gain_ref = refs[3:7]
    partials = refs[7 : 7 + count]
    rows_ref, grad_mixed_ref, grad_abs_ref, logit_abs_ref, project_ref, beta_ref, merge_ref, sems = refs[7 + count :]
    order = relative_order(count)
    share = TOK_MB // count
    model = rows_ref.shape[1]
    width = heads * HEAD_DIM
    fetch = Fetch(
        [(merge_hbm.at[0], merge_ref), (beta_hbm, beta_ref)]
        + [(project_hbm.at[0, j], project_ref.at[j]) for j in range(3)],
        sems,
        0,
    )
    fetch.start_to(5)
    for k in range(count):
        rows_ref[k * share : (k + 1) * share, :] = shards[k][...]
    fetch.wait(0)
    for cols in tiles_of(heads * HEAD_DIM):
        value = mm_t(rows_ref[...], merge_ref[cols, :])
        for k, difference in enumerate(order):
            grad_mixed_ref[place_of(me_ref, difference, share), cols] = value[k * share : (k + 1) * share]

    masks = [masks_ref[i] for i in range(CONV - 1)]
    strict, lower = block_masks(seg_col_ref, seg_row_ref)
    lane = lax.broadcasted_iota(jnp.int32, (TOK_MB, LANES), 1)
    everyone = range(heads)
    columns = [slice(h * HEAD_DIM, (h + 1) * HEAD_DIM) for h in everyone]
    grad_gain = jnp.zeros((8, HEAD_DIM), F32)
    grad_outs, queries, keys, values, betas, convs = [], [], [], [], [], []
    for h in everyone:
        cols = columns[h]
        taps = [taps_ref[0, j, :, cols] for j in range(3)]
        _, _, conv_q = stream(qkv_ref[0, :, cols], taps[0], masks)
        _, _, conv_k = stream(qkv_ref[1, :, cols], taps[1], masks)
        scale_q = lax.rsqrt(jnp.sum(conv_q * conv_q, axis=-1, keepdims=True) + EPS)
        scale_k = lax.rsqrt(jnp.sum(conv_k * conv_k, axis=-1, keepdims=True) + EPS)
        queries.append((conv_q * (scale_q * HEAD_DIM**-0.5)).astype(BF16))
        keys.append((conv_k * scale_k).astype(BF16))
        betas.append(jax.nn.sigmoid(logit_ref[:, h : h + 1]))
        out = out_ref[:, cols]
        grad_mixed = grad_mixed_ref[:, cols]
        mean = jnp.mean(out * out, axis=-1, keepdims=True)
        scale = lax.rsqrt(jnp.maximum(mean, OUT_FLOOR))
        unit = out * scale
        grad_gain = grad_gain + jnp.sum((grad_mixed * unit).reshape(TOK_MB // 8, 8, HEAD_DIM), axis=0)
        grad_unit = grad_mixed * gain_ref[...]
        through = jnp.where(mean > OUT_FLOOR, 1.0, jnp.where(mean == OUT_FLOOR, 0.5, 0.0))
        grad_out = scale * (
            grad_unit - unit * (through * jnp.mean(grad_unit * unit, axis=-1, keepdims=True))
        )
        grad_outs.append(grad_out.astype(BF16))
    grad_gain_ref[...] = grad_gain
    fresh = {(h, b): fresh_ref[rows_of(b), columns[h]] for h in everyone for b in range(BLOCKS)}
    d_out = {(h, b): grad_outs[h][rows_of(b)] for h in everyone for b in range(BLOCKS)}
    key_blocks = {(h, b): keys[h][rows_of(b)] for h in everyone for b in range(BLOCKS)}
    d_fresh, d_target, d_target_b = {}, {}, {}
    for c in range(BLOCKS):
        for h in everyone:
            total = t_mm(attend_ref[h, rows_of(c), rows_of(c)], d_out[h, c])
            for b in range(c + 1, BLOCKS):
                total = total + t_mm(attend_ref[h, rows_of(b), rows_of(c)], d_out[h, b])
            d_fresh[h, c] = total
    for b in reversed(range(BLOCKS)):
        for h in everyone:
            d_target[h, b] = t_mm(inverse_ref[h, b], d_fresh[h, b])
            d_target_b[h, b] = d_target[h, b].astype(BF16)
        for h in everyone:
            for c in range(b):
                d_fresh[h, c] = d_fresh[h, c] - t_mm(system_ref[h, rows_of(b), rows_of(c)], d_target_b[h, b])
    grad_query, inner, grad_key = {}, {}, {}
    for b in range(BLOCKS):
        for c in range(b + 1):
            for h in everyone:
                d_attend = jnp.where(lower[b, c], mm_t(d_out[h, b], fresh[h, c]), 0.0).astype(BF16)
                d_system = jnp.where(strict[b, c], -mm_t(d_target_b[h, b], fresh[h, c]), 0.0)
                for store, place, part in (
                    (grad_query, b, mm(d_attend, key_blocks[h, c])),
                    (inner, b, mm(d_system, key_blocks[h, c])),
                    (grad_key, c, t_mm(d_attend, queries[h][rows_of(b)])
                     + t_mm(d_system * betas[h][rows_of(b)], key_blocks[h, b])),
                ):
                    store[h, place] = store[h, place] + part if (h, place) in store else part

    def whole(store, h):
        return jnp.concatenate([store[h, b] for b in range(BLOCKS)], axis=0)

    grad_logits = jnp.zeros((TOK_MB, LANES), F32)
    for h in everyone:
        cols = columns[h]
        beta = betas[h]
        taps = [taps_ref[0, j, :, cols] for j in range(3)]
        inputs = [qkv_ref[j, :, cols] for j in range(3)]
        pre_q, gate_q, conv_q = stream(inputs[0], taps[0], masks)
        pre_k, gate_k, conv_k = stream(inputs[1], taps[1], masks)
        pre_v, gate_v, value = stream(inputs[2], taps[2], masks)
        scale_q = lax.rsqrt(jnp.sum(conv_q * conv_q, axis=-1, keepdims=True) + EPS)
        scale_k = lax.rsqrt(jnp.sum(conv_k * conv_k, axis=-1, keepdims=True) + EPS)
        unit_q, key = conv_q * scale_q, conv_k * scale_k
        within = whole(inner, h)
        target = whole(d_target, h)
        grad_q = whole(grad_query, h)
        grad_k = whole(grad_key, h) + beta * within
        grad_beta = jnp.sum(within * key + target * value, axis=-1, keepdims=True)
        grad_logits = jnp.where(lane == h, grad_beta * beta * (1.0 - beta), grad_logits)
        grad_conv_q = (HEAD_DIM**-0.5 * scale_q) * (
            grad_q - unit_q * jnp.sum(grad_q * unit_q, axis=-1, keepdims=True)
        )
        grad_conv_k = scale_k * (grad_k - key * jnp.sum(grad_k * key, axis=-1, keepdims=True))
        for j, (grad, pre, gate) in enumerate(
            ((grad_conv_q, pre_q, gate_q), (grad_conv_k, pre_k, gate_k), (beta * target, pre_v, gate_v))
        ):
            grad_x = stream_back(grad, inputs[j], pre, gate, taps[j], masks, grad_taps_ref, j, cols)
            grad_abs_ref[j, :, cols] = grad_x.astype(BF16)
    logit_abs_ref[...] = grad_logits.astype(BF16)
    for k, difference in enumerate(order):
        here = slice(k * share, (k + 1) * share)
        there = place_of(me_ref, difference, share)
        grad_logit_ref[here, :] = logit_abs_ref[there, :]
        for j in range(3):
            grad_qkv_ref[here, j * width : (j + 1) * width] = grad_abs_ref[j, there, :]
    for place in range(1, 5):
        fetch.wait(place)
    for span in tiles_of(model):
        value = mm_t(grad_logit_ref[...], beta_ref[span, :])
        for j in range(3):
            value = value + mm_t(grad_qkv_ref[:, j * width : (j + 1) * width], project_ref[j, span, :])
        for k, ref in enumerate(partials):
            ref[:, span] = value[k * share : (k + 1) * share].astype(ref.dtype)


def attend_backward(me, mine, shards, kept, taps, gain, project, beta_weight, merge):
    masks, seg_col, seg_row = mine
    heads = merge.shape[1] // HEAD_DIM
    width = heads * HEAD_DIM
    model = merge.shape[2]
    count = len(shards)
    _, qkv, logit, _, system, attend, inverse, fresh, out = kept
    results = call(
        functools.partial(attend_back_kernel, heads, count),
        (me, seg_col, seg_row, masks, taps, gain, qkv, logit, system, attend, inverse, fresh, out, *shards),
        (project, beta_weight, merge),
        [
            jax.ShapeDtypeStruct((TOK_MB, 3 * width), BF16),
            jax.ShapeDtypeStruct((TOK_MB, LANES), BF16),
            jax.ShapeDtypeStruct((3, CONV, width), F32),
            jax.ShapeDtypeStruct((8, HEAD_DIM), F32),
        ]
        + partial_shapes(count, model),
        [
            pltpu.VMEM((TOK_MB, model), BF16),
            pltpu.VMEM((TOK_MB, width), F32),
            pltpu.VMEM((3, TOK_MB, width), BF16),
            pltpu.VMEM((TOK_MB, LANES), BF16),
            pltpu.VMEM(project.shape[1:], BF16),
            pltpu.VMEM(beta_weight.shape, BF16),
            pltpu.VMEM(merge.shape[1:], BF16),
            pltpu.SemaphoreType.DMA((5,)),
        ],
    )
    return results[:4], results[4:]


def tap_masks(segment):
    masks = []
    for tap in range(1, CONV):
        earlier = jnp.concatenate([jnp.full((tap,), -1, jnp.int32), segment[: TOK_MB - tap]], axis=0)
        masks.append(jnp.broadcast_to((earlier == segment).astype(F32)[:, None], (TOK_MB, HEAD_DIM)))
    return jnp.stack(masks)


def narrow(values):
    return values.astype(BF16)


def product(left, right):
    return jnp.dot(left, right, preferred_element_type=F32)


def product_left(left, right):
    return lax.dot_general(left, right, (((0,), (0,)), ((), ())), preferred_element_type=F32)


def product_right(left, right):
    return lax.dot_general(left, right, (((1,), (1,)), ((), ())), preferred_element_type=F32)


def rms_parts(values):
    scale = lax.rsqrt(jnp.mean(values * values, axis=-1, keepdims=True) + EPS)
    return (values * scale, scale)


def norm_back(grad_normed, normed, scale, gain):
    grad_scaled = grad_normed * gain
    return scale * (grad_scaled - normed * jnp.mean(grad_scaled * normed, axis=-1, keepdims=True))


def segment_ids(lengths, count):
    ends = jnp.cumsum(lengths)
    places = jnp.arange(count, dtype=jnp.int32)
    return jnp.sum((places[:, None] >= ends[None, :]).astype(jnp.int32), axis=1, dtype=jnp.int32)


def flipped(values, axis, bit):
    return lax.ppermute(values, axis, [(i, i ^ bit) for i in range(lax.axis_size(axis))])


def shifted(values, axis, distance):
    devices = range(lax.axis_size(axis))
    return lax.ppermute(values, axis, [(i, i + distance) for i in devices if i + distance in devices])


def bits_of(axis):
    size = lax.axis_size(axis)
    bits = [1 << k for k in range(size.bit_length() - 1)]
    assert 1 << len(bits) == size
    return bits


def summed(values, axes):
    for axis in axes:
        for bit in bits_of(axis):
            values = values + flipped(values, axis, bit)
    return values


def gather(shard):
    parts = [shard]
    for bit in reversed(bits_of("head")):
        parts = parts + [flipped(part, "head", bit) for part in parts]
    return parts


def added(parts, arrived):
    return [part.astype(F32) + other.astype(F32) for part, other in zip(parts, arrived)]


def scatter_near(parts):
    half = len(parts) // 2
    return added(parts[:half], [flipped(part, "head", 1) for part in parts[half:]])


def scatter_far(parts):
    for bit in bits_of("head")[1:]:
        half = len(parts) // 2
        parts = added(parts[:half], [flipped(narrow(part), "head", bit) for part in parts[half:]])
    return parts[0]


def in_turn(kernel, shards):
    results, near = [], None
    for parts in shards:
        if near is not None:
            (parts, near) = lax.optimization_barrier((parts, near))
            results[-1] = (results[-1][0], near)
        kept, partials = kernel(len(results), parts)
        near = scatter_near(partials)
        results.append((kept, near))
    return [kept for kept, _ in results], [scatter_far(near) for _, near in results]


def gather_in_turn(shards):
    gathered = []
    for shard in shards:
        if gathered:
            shard, gathered[-1][1] = lax.optimization_barrier((shard, gathered[-1][1]))
        gathered.append(gather(shard))
    return gathered


def swapped(shards):
    count = lax.axis_size("dp")
    me = lax.axis_index("dp")
    values = jnp.stack(shards)
    wide = values.shape[-1] // count
    arrived = []
    for distance in range(count):
        block = lax.dynamic_slice_in_dim(values, ((me + distance) % count) * wide, wide, 2)
        if distance:
            block = lax.ppermute(block, "dp", [(i, (i + distance) % count) for i in range(count)])
        arrived.append(block)
    arrived = jnp.stack(arrived)
    ordered = [lax.dynamic_index_in_dim(arrived, (me - q) % count, 0, keepdims=False) for q in range(count)]
    return jnp.stack(ordered, axis=1)


def per_device(
    tokens,
    lengths,
    cotangent,
    attn_in,
    beta_weight,
    conv_weight,
    o_gain,
    attn_out,
    mlp_in,
    mlp_out,
    norm_gains,
):
    section = lax.axis_index("section")
    sections = lax.axis_size("section")
    member = lax.axis_index("head")
    micro = tokens.shape[0]
    width = tokens.shape[2]
    heads = beta_weight.shape[2]
    share = TOK_MB // lax.axis_size("head")
    me = member[None]
    beta_wide = jnp.pad(beta_weight[0], ((0, 0), (0, LANES - heads)))
    gains = norm_gains[0]
    every = range(micro)
    segments = [segment_ids(lengths[m], TOK_MB) for m in every]
    masks = [(tap_masks(s), s[:, None], s[None, :]) for s in segments]
    own_rows = lambda values: lax.dynamic_slice_in_dim(values, member * share, share, 0).astype(F32)
    tokens_own = [own_rows(tokens[m]) for m in every]
    cotangent_own = [own_rows(cotangent[m]) for m in every]

    def forward_turn(inputs, save):
        parts = [rms_parts(x) for x in inputs]
        normed = gather_in_turn([narrow(unit * gains[0]) for unit, _ in parts])
        kept, sums = in_turn(
            lambda m, rows: attend_forward(
                me, masks[m], rows, conv_weight, o_gain, attn_in, beta_wide, attn_out, save
            ),
            normed,
        )
        middles = [x + total for x, total in zip(inputs, sums)]
        parts_mid = [rms_parts(middle) for middle in middles]
        normed_mid = [gather(narrow(unit * gains[1])) for unit, _ in parts_mid]
        kept_mid, sums = in_turn(lambda m, rows: expand_forward(me, rows, mlp_in, mlp_out, save), normed_mid)
        outputs = [middle + total for middle, total in zip(middles, sums)]
        return outputs, (parts, kept, parts_mid, kept_mid)

    def backward_expand(incoming, saved):
        _, _, parts_mid, kept_mid = saved
        grads, sums = in_turn(
            lambda m, rows: expand_backward(me, rows, *kept_mid[m][2:], mlp_in, mlp_out),
            gather_in_turn([narrow(value) for value in incoming]),
        )
        middles = [value + norm_back(sums[m], *parts_mid[m], gains[1]) for m, value in enumerate(incoming)]
        return middles, grads, sum(jnp.sum(sums[m] * parts_mid[m][0], axis=0) for m in every)

    def backward_attend(middles, saved):
        parts, kept, _, _ = saved
        grads, sums = in_turn(
            lambda m, rows: attend_backward(
                me, masks[m], rows, kept[m], conv_weight, o_gain, attn_in, beta_wide, attn_out
            ),
            gather_in_turn([narrow(value) for value in middles]),
        )
        finals = [value + norm_back(sums[m], *parts[m], gains[0]) for m, value in enumerate(middles)]
        return finals, grads, sum(jnp.sum(sums[m] * parts[m][0], axis=0) for m in every)

    def all_rows(values):
        return jnp.concatenate(values, axis=0)

    last = sections - 1
    inputs = tokens_own
    for turn in range(sections):
        outputs, saved = forward_turn(inputs, turn == last)
        if turn < last:
            arrived = [shifted(narrow(value), "section", 1).astype(F32) for value in outputs]
            inputs = [jnp.where(section == 0, tokens_own[m], arrived[m]) for m in every]

    hidden_rows = [lax.all_gather(values[1], "dp", axis=0, tiled=True) for values in saved[3]]
    mixed_rows = [lax.all_gather(values[3], "dp", axis=0, tiled=True) for values in saved[1]]

    incoming = cotangent_own
    for turn in range(sections):
        if turn == last:
            incoming, hidden_rows, mixed_rows = lax.optimization_barrier((incoming, hidden_rows, mixed_rows))
        middles, grads, gain_two = backward_expand(incoming, saved)
        if turn == last:
            swapped_out = swapped([narrow(value) for value in incoming])
            normed_mid = all_rows([values[0] for values in saved[3]])
            expands = [narrow(product_left(normed_mid, all_rows([grad[j] for grad in grads]))) for j in range(2)]
            middles, expands, swapped_out = lax.optimization_barrier((middles, expands, swapped_out))
        finals, grads, gain_one = backward_attend(middles, saved)
        if turn < last:
            arrived = [shifted(narrow(value), "section", -1).astype(F32) for value in finals]
            incoming = [jnp.where(section == last, cotangent_own[m], arrived[m]) for m in every]
    rows_out = jnp.stack(finals)
    half = width // sections
    moved = shifted(narrow(rows_out[:, :, half:]), "section", 1).astype(F32)
    grad_tokens = jnp.where(section == 0, rows_out[:, :, :half], moved)

    def spread(value, axis):
        return lax.psum_scatter(value, "dp", scatter_dimension=axis, tiled=True)

    early = [spread(part, 0) for part in expands]
    normed = all_rows([values[0] for values in saved[1]])
    grad_project = narrow(product_left(normed, all_rows([grad[0] for grad in grads])))
    grad_beta = product_left(normed, all_rows([grad[1] for grad in grads]))[:, :heads]
    grad_taps, grad_head_gain = (sum(grad[place] for grad in grads) for place in (2, 3))
    grad_head_gain = jnp.sum(grad_head_gain, axis=0)

    def from_rows(rows, columns):
        total = 0.0
        columns = jnp.concatenate(gather(columns), axis=2)
        for left, right in zip(rows, columns):
            total = total + product_left(left, right.reshape(left.shape[0], -1))
        return total

    grad_contract = from_rows(hidden_rows, swapped_out)
    grad_merge = from_rows(mixed_rows, swapped([narrow(value) for value in middles]))
    flat = jnp.concatenate([gain_one, gain_two, grad_head_gain])
    flat = summed(flat, ("dp", "head"))
    grad_gains, grad_head_gain = flat[: 2 * width].reshape(2, width), flat[2 * width :]
    flat = summed(jnp.concatenate([grad_taps.reshape(-1), grad_beta.reshape(-1)]), ("dp",))
    grad_taps, grad_beta = flat[: grad_taps.size].reshape(grad_taps.shape), flat[grad_taps.size :]
    rows = width // lax.axis_size("dp")
    grad_beta = lax.dynamic_slice_in_dim(grad_beta.reshape(width, heads), lax.axis_index("dp") * rows, rows, 0)
    done = (grad_tokens, grad_contract, grad_merge, grad_beta, grad_taps, grad_head_gain, grad_gains, early)
    grad_project, done = lax.optimization_barrier((grad_project, done))
    grad_tokens, grad_contract, grad_merge, grad_beta, grad_taps, grad_head_gain, grad_gains, early = done
    grad_expand = jnp.stack(early).astype(F32)
    grad_project = jnp.stack(jnp.split(spread(grad_project, 0), 3, axis=1)).astype(F32)
    return (
        grad_tokens,
        grad_project[None],
        grad_beta[None],
        grad_taps[None],
        grad_head_gain[None],
        grad_merge[None],
        grad_expand[None],
        grad_contract[None],
        grad_gains[None],
    )


def solution(mesh):
    return jax.shard_map(
        per_device,
        mesh=mesh,
        in_specs=(
            P("dp", None, None),
            P("dp", None),
            P("dp", None, None),
            P("section", None, None, "head"),
            P("section", None, "head"),
            P("section", None, None, "head"),
            P("section", None),
            P("section", "head", None),
            P("section", None, None, "head"),
            P("section", "head", None),
            P("section", None, None),
        ),
        out_specs=(
            P("dp", "head", "section"),
            P("section", None, "dp", "head"),
            P("section", "dp", "head"),
            P("section", None, None, "head"),
            P("section", None),
            P("section", "head", "dp"),
            P("section", None, "dp", "head"),
            P("section", "head", "dp"),
            P("section", None, None),
        ),
        check_vma=False,
    )
```

```python
import functools

import jax
import jax.numpy as jnp
from jax import lax
from jax.experimental import pallas as pl
from jax.experimental.pallas import tpu as pltpu
from jax.sharding import PartitionSpec as P

HEAD_DIM = 128
CONV = 4
TOK_MB = 384
BLOCK = 128
BLOCKS = TOK_MB // BLOCK
EPS = 1e-06
OUT_FLOOR = 0.0001
F32 = jnp.float32
BF16 = jnp.bfloat16
BASE = 4
LANES = 128
TILE = 256
QUARTERS = 4
ATTEND_KEPT = 9
VMEM_LIMIT = 50 * 1024 * 1024


def mm(left, right):
    return lax.dot_general(
        left.astype(BF16), right.astype(BF16), (((1,), (0,)), ((), ())), preferred_element_type=F32
    )


def mm_t(left, right):
    return lax.dot_general(
        left.astype(BF16), right.astype(BF16), (((1,), (1,)), ((), ())), preferred_element_type=F32
    )


def t_mm(left, right):
    return lax.dot_general(
        left.astype(BF16), right.astype(BF16), (((0,), (0,)), ((), ())), preferred_element_type=F32
    )


def rows_of(b):
    return slice(b * BLOCK, (b + 1) * BLOCK)


def tiles_of(size, tile=TILE):
    return [slice(start, min(start + tile, size)) for start in range(0, size, tile)]


def quarters(size):
    return tiles_of(size, size // QUARTERS)


def relative_order(count):
    order, bit = [0], count // 2
    while bit:
        order = order + [k ^ bit for k in order]
        bit //= 2
    return order


def place_of(me_ref, difference, share):
    return pl.ds(pl.multiple_of((me_ref[0] ^ difference) * share, 16), share)


def stream(x, taps, masks):
    pre = taps[0:1] * x
    for tap in range(1, CONV):
        pre = pre + taps[tap : tap + 1] * (pltpu.roll(x, tap, 0) * masks[tap - 1])
    gate = jax.nn.sigmoid(pre)
    return pre, gate, pre * gate


def unit_inverses(systems):
    size = systems[0].shape[0]
    row = lax.broadcasted_iota(jnp.int32, (size, size), 0)
    col = lax.broadcasted_iota(jnp.int32, (size, size), 1)
    eye = (row == col).astype(F32)
    near = (row // BASE == col // BASE).astype(F32)
    first = [-a * near for a in systems]
    total = [eye + n for n in first]
    second = [mm(n, n) for n in first]
    third = [mm(n, s) for n, s in zip(first, second)]
    total = [t + s + r for t, s, r in zip(total, second, third)]
    step = BASE
    while step < size:
        span = 2 * step
        off = ((row // span == col // span) & (row // step != col // step)).astype(F32)
        inner = [mm(a * off, t) for a, t in zip(systems, total)]
        outer = [mm(t, i) for t, i in zip(total, inner)]
        total = [t - o for t, o in zip(total, outer)]
        step = span
    return total


def block_masks(seg_col_ref, seg_row_ref):
    row = lax.broadcasted_iota(jnp.int32, (BLOCK, BLOCK), 0)
    col = lax.broadcasted_iota(jnp.int32, (BLOCK, BLOCK), 1)
    strict, lower = {}, {}
    for b in range(BLOCKS):
        for c in range(b + 1):
            same = seg_col_ref[rows_of(b), :] == seg_row_ref[:, rows_of(c)]
            strict[b, c] = same & (col < row) if b == c else same
            lower[b, c] = same & (col <= row) if b == c else same
    return strict, lower


class Fetch:

    def __init__(self, pairs, sems, ahead):
        self.copies = [pltpu.make_async_copy(src, dst, sems.at[i]) for i, (src, dst) in enumerate(pairs)]
        self.ahead = ahead
        self.started = 0
        self.start_to(ahead)

    def start_to(self, place):
        while self.started < min(place, len(self.copies)):
            self.copies[self.started].start()
            self.started += 1

    def wait(self, place):
        self.copies[place].wait()
        self.start_to(place + 1 + self.ahead)

    def wait_group(self, group):
        for place in range(QUARTERS):
            self.wait(QUARTERS * group + place)


class Push:

    def __init__(self, sems):
        self.sems = sems
        self.copies = []

    def start(self, source, target):
        copy = pltpu.make_async_copy(source, target, self.sems.at[len(self.copies)])
        copy.start()
        self.copies.append(copy)

    def wait(self):
        for copy in self.copies:
            copy.wait()


def attend_kernel(heads, count, save, me_ref, seg_col_ref, seg_row_ref, masks_ref, taps_ref, gain_ref, *refs):
    shards, refs = refs[:count], refs[count:]
    project_hbm, beta_hbm, merge_hbm = refs[:3]
    partials, refs = refs[3 : 3 + count], refs[3 + count :]
    targets, refs = (refs[:ATTEND_KEPT], refs[ATTEND_KEPT:]) if save else ([], refs)
    kept_refs, refs = refs[:ATTEND_KEPT], refs[ATTEND_KEPT:]
    rows_ref, qkv_ref, logit_ref, mixed_ref, system_ref, attend_ref, inverse_ref, fresh_ref, out_ref = kept_refs
    mixed_abs, project_ref, beta_ref, merge_ref, sems, push_sems = refs
    push = Push(push_sems)

    def ready(*places):
        if save:
            for place in places:
                push.start(kept_refs[place], targets[place])

    order = relative_order(count)
    share = TOK_MB // count
    fetch = Fetch(
        [(project_hbm.at[0, j], project_ref.at[j]) for j in range(3)]
        + [(beta_hbm, beta_ref), (merge_hbm.at[0], merge_ref)],
        sems,
        5,
    )
    for k in range(count):
        rows_ref[k * share : (k + 1) * share, :] = shards[k][...]
    rows = rows_ref[...]
    ready(0)

    def spread(ref, value, *lead):
        for k, difference in enumerate(order):
            ref[(*lead, place_of(me_ref, difference, share), slice(None))] = value[k * share : (k + 1) * share]

    for j in range(3):
        fetch.wait(j)
        for cols in tiles_of(heads * HEAD_DIM):
            value = mm(rows, project_ref[j, :, cols])
            for k, difference in enumerate(order):
                qkv_ref[j, place_of(me_ref, difference, share), cols] = value[k * share : (k + 1) * share]
    fetch.wait(3)
    spread(logit_ref, mm(rows, beta_ref[...]))
    ready(1, 2)

    masks = [masks_ref[i] for i in range(CONV - 1)]
    strict, lower = block_masks(seg_col_ref, seg_row_ref)
    queries, keys, values, betas = [], [], [], []
    for h in range(heads):
        cols = slice(h * HEAD_DIM, (h + 1) * HEAD_DIM)
        taps = [taps_ref[0, j, :, cols] for j in range(3)]
        _, _, query = stream(qkv_ref[0, :, cols], taps[0], masks)
        _, _, key = stream(qkv_ref[1, :, cols], taps[1], masks)
        _, _, value = stream(qkv_ref[2, :, cols], taps[2], masks)
        query = query * lax.rsqrt(jnp.sum(query * query, axis=-1, keepdims=True) + EPS) * HEAD_DIM**-0.5
        key = key * lax.rsqrt(jnp.sum(key * key, axis=-1, keepdims=True) + EPS)
        beta = jax.nn.sigmoid(logit_ref[:, h : h + 1])
        queries.append(query.astype(BF16))
        keys.append(key.astype(BF16))
        values.append(value * beta)
        betas.append(beta)
    attend, system = {}, {}
    for h in range(heads):
        for b in range(BLOCKS):
            for c in range(b + 1):
                inner = mm_t(keys[h][rows_of(b)], keys[h][rows_of(c)])
                system[h, b, c] = jnp.where(strict[b, c], inner * betas[h][rows_of(b)], 0.0)
                scores = mm_t(queries[h][rows_of(b)], keys[h][rows_of(c)])
                attend[h, b, c] = jnp.where(lower[b, c], scores, 0.0).astype(BF16)
                if c < b:
                    system[h, b, c] = system[h, b, c].astype(BF16)
                if save:
                    attend_ref[h, rows_of(b), rows_of(c)] = attend[h, b, c]
                    if c < b:
                        system_ref[h, rows_of(b), rows_of(c)] = system[h, b, c]
    index = [(h, b) for h in range(heads) for b in range(BLOCKS)]
    inverse = dict(zip(index, unit_inverses([system[h, b, b] for h, b in index])))
    for h, b in index:
        inverse[h, b] = inverse[h, b].astype(BF16)
        if save:
            inverse_ref[h, b] = inverse[h, b]
    ready(4, 5, 6)
    fresh = {}
    for b in range(BLOCKS):
        for h in range(heads):
            target = values[h][rows_of(b)]
            for c in range(b):
                target = target - mm(system[h, b, c], fresh[h, c])
            fresh[h, b] = mm(inverse[h, b], target).astype(BF16)
            if save:
                fresh_ref[rows_of(b), h * HEAD_DIM : (h + 1) * HEAD_DIM] = fresh[h, b]
    for h in range(heads):
        cols = slice(h * HEAD_DIM, (h + 1) * HEAD_DIM)
        for b in range(BLOCKS):
            out = mm(attend[h, b, 0], fresh[h, 0])
            for c in range(1, b + 1):
                out = out + mm(attend[h, b, c], fresh[h, c])
            mean = jnp.mean(out * out, axis=-1, keepdims=True)
            if save:
                out_ref[rows_of(b), cols] = out
            mixed_abs[rows_of(b), cols] = (
                out * lax.rsqrt(jnp.maximum(mean, OUT_FLOOR)) * gain_ref[...]
            ).astype(BF16)
    for k, difference in enumerate(order):
        mixed_ref[k * share : (k + 1) * share, :] = mixed_abs[place_of(me_ref, difference, share), :]
    ready(3, 7, 8)
    fetch.wait(4)
    write_partials(partials, merge_ref.shape[1], share, lambda cols: mm(mixed_ref[...], merge_ref[:, cols]))
    push.wait()


def write_partials(partials, width, share, product):
    for cols in tiles_of(width):
        value = product(cols)
        for k, ref in enumerate(partials):
            ref[:, cols] = value[k * share : (k + 1) * share].astype(ref.dtype)


def partial_shapes(count, width):
    share = TOK_MB // count
    return [jax.ShapeDtypeStruct((share, width), F32 if k < count // 2 else BF16) for k in range(count)]


def call(kernel, operands, hbm, out_shape, hbm_shape, scratch_shapes):
    vmem = pl.BlockSpec(memory_space=pltpu.VMEM)
    far = pl.BlockSpec(memory_space=pltpu.HBM)
    return pl.pallas_call(
        kernel,
        in_specs=[pl.BlockSpec(memory_space=pltpu.SMEM)] + [vmem] * (len(operands) - 1) + [far] * len(hbm),
        out_specs=[vmem] * len(out_shape) + [far] * len(hbm_shape),
        out_shape=out_shape + hbm_shape,
        scratch_shapes=scratch_shapes,
        compiler_params=pltpu.CompilerParams(vmem_limit_bytes=VMEM_LIMIT),
        cost_estimate=pl.CostEstimate(flops=2 * 10**9, bytes_accessed=10**5, transcendentals=0),
    )(*operands, *hbm)


def as_scratch(shapes):
    return [pltpu.VMEM(shape.shape, shape.dtype) for shape in shapes]


def attend_forward(me, mine, shards, taps, gain, project, beta_weight, merge, save):
    masks, seg_col, seg_row = mine
    heads = merge.shape[1] // HEAD_DIM
    width = heads * HEAD_DIM
    model = merge.shape[2]
    count = len(shards)
    kept = [
        jax.ShapeDtypeStruct((TOK_MB, model), BF16),
        jax.ShapeDtypeStruct((3, TOK_MB, width), F32),
        jax.ShapeDtypeStruct((TOK_MB, LANES), F32),
        jax.ShapeDtypeStruct((TOK_MB, width), BF16),
        jax.ShapeDtypeStruct((heads, TOK_MB, TOK_MB), BF16),
        jax.ShapeDtypeStruct((heads, TOK_MB, TOK_MB), BF16),
        jax.ShapeDtypeStruct((heads, BLOCKS, BLOCK, BLOCK), BF16),
        jax.ShapeDtypeStruct((TOK_MB, width), BF16),
        jax.ShapeDtypeStruct((TOK_MB, width), F32),
    ]
    results = call(
        functools.partial(attend_kernel, heads, count, save),
        (me, seg_col, seg_row, masks, taps, gain, *shards),
        (project, beta_weight, merge),
        partial_shapes(count, model),
        kept if save else [],
        as_scratch(kept)
        + [
            pltpu.VMEM((TOK_MB, width), BF16),
            pltpu.VMEM(project.shape[1:], BF16),
            pltpu.VMEM(beta_weight.shape, BF16),
            pltpu.VMEM(merge.shape[1:], BF16),
            pltpu.SemaphoreType.DMA((5,)),
            pltpu.SemaphoreType.DMA((ATTEND_KEPT,)),
        ],
    )
    return results[count:], results[:count]


def expand_kernel(count, save, me_ref, *refs):
    shards, refs = refs[:count], refs[count:]
    share = TOK_MB // count
    if save:
        expand_hbm, *targets = refs[:5]
        rows_ref, hidden_ref, silu_ref, slope_ref, gate_ref, expand_ref, sems, push_sems = refs[5:]
        push = Push(push_sems)
        contract_copies = []
    else:
        expand_hbm, contract_hbm, *partials = refs[: 2 + count]
        rows_ref, hidden_ref, gate_ref, expand_ref, contract_ref, sems = refs[2 + count :]
        contract_copies = [(contract_hbm.at[0, s, :], contract_ref.at[s, :]) for s in quarters(contract_ref.shape[0])]
    tiles = tiles_of(hidden_ref.shape[1])
    fetch = Fetch(
        [(expand_hbm.at[0, j, s, :], expand_ref.at[j, s, :]) for j in range(2) for s in quarters(expand_ref.shape[1])]
        + contract_copies,
        sems,
        QUARTERS,
    )
    for k in range(count):
        rows_ref[k * share : (k + 1) * share, :] = shards[k][...]
    if save:
        push.start(rows_ref, targets[0])
    fetch.wait_group(0)
    for t in tiles:
        gate_ref[:, t] = mm(rows_ref[...], expand_ref[0, :, t])
    fetch.wait_group(1)
    for t in tiles:
        up_in = mm(rows_ref[...], expand_ref[1, :, t])
        gate_in = gate_ref[:, t]
        gate = jax.nn.sigmoid(gate_in)
        silu = gate_in * gate
        hidden_ref[:, t] = (silu * up_in).astype(BF16)
        if save:
            silu_ref[:, t] = silu.astype(BF16)
            slope_ref[:, t] = (up_in * gate * (1.0 + gate_in * (1.0 - gate))).astype(BF16)
    if save:
        for source, target in zip((hidden_ref, silu_ref, slope_ref), targets[1:]):
            push.start(source, target)
        push.wait()
    else:
        fetch.wait_group(2)
        write_partials(partials, rows_ref.shape[1], share, lambda cols: mm(hidden_ref[...], contract_ref[:, cols]))


def expand_forward(me, shards, expand, contract, save):
    count = len(shards)
    model, units = expand.shape[2:]
    kept = [jax.ShapeDtypeStruct((TOK_MB, model), BF16)] + [jax.ShapeDtypeStruct((TOK_MB, units), BF16)] * 3
    results = call(
        functools.partial(expand_kernel, count, save),
        (me, *shards),
        (expand,) if save else (expand, contract),
        [] if save else partial_shapes(count, model),
        kept if save else [],
        as_scratch(kept if save else kept[:2])
        + [pltpu.VMEM((TOK_MB, units), F32), pltpu.VMEM(expand.shape[1:], BF16)]
        + ([] if save else [pltpu.VMEM(contract.shape[1:], BF16)])
        + [pltpu.SemaphoreType.DMA(((2 if save else 3) * QUARTERS,))]
        + ([pltpu.SemaphoreType.DMA((4,))] if save else []),
    )
    return (results, None) if save else (None, results)


def padded(units):
    return -(-units // LANES) * LANES


def expand_back_kernel(count, me_ref, *refs):
    shards, refs = refs[:count], refs[count:]
    silu_hbm, slope_hbm, expand_hbm, contract_hbm = refs[:4]
    partials, refs = refs[4 : 4 + count], refs[4 + count :]
    both_hbm, rows_ref, silu_ref, slope_ref, both_ref, expand_ref, contract_ref, sems, push_sems = refs
    push = Push(push_sems)
    share = TOK_MB // count
    units = silu_ref.shape[1]
    second = padded(units)
    spans = tiles_of(rows_ref.shape[1], 2 * TILE)
    fetch = Fetch(
        [(contract_hbm.at[0, s, :], contract_ref.at[s, :]) for s in quarters(contract_ref.shape[0])]
        + [(slope_hbm, slope_ref), (silu_hbm, silu_ref)]
        + [(expand_hbm.at[0, j, s, :], expand_ref.at[j, s, :]) for s in spans for j in range(2)],
        sems,
        QUARTERS + 2,
    )
    for k in range(count):
        rows_ref[k * share : (k + 1) * share, :] = shards[k][...]
    if second > units:
        both_ref[...] = jnp.zeros(both_ref.shape, BF16)
    fetch.wait_group(0)
    fetch.wait(QUARTERS)
    fetch.wait(QUARTERS + 1)
    for t in tiles_of(units):
        grad_hidden = mm_t(rows_ref[...], contract_ref[t, :])
        both_ref[:, t] = (grad_hidden * slope_ref[:, t].astype(F32)).astype(BF16)
        both_ref[:, second + t.start : second + t.stop] = (
            grad_hidden * silu_ref[:, t].astype(F32)
        ).astype(BF16)
    push.start(both_ref, both_hbm)
    for i, span in enumerate(spans):
        for j in range(2):
            fetch.wait(QUARTERS + 2 + 2 * i + j)
        for s in tiles_of(span.stop - span.start):
            s = slice(span.start + s.start, span.start + s.stop)
            value = mm_t(both_ref[:, :units], expand_ref[0, s, :])
            value = value + mm_t(both_ref[:, second : second + units], expand_ref[1, s, :])
            for k, ref in enumerate(partials):
                ref[:, s] = value[k * share : (k + 1) * share].astype(ref.dtype)
    push.wait()


def expand_backward(me, shards, silu, slope, expand, contract):
    count = len(shards)
    model, units = expand.shape[2:]
    both = jax.ShapeDtypeStruct((TOK_MB, 2 * padded(units)), BF16)
    results = call(
        functools.partial(expand_back_kernel, count),
        (me, *shards),
        (silu, slope, expand, contract),
        partial_shapes(count, model),
        [both],
        [pltpu.VMEM((TOK_MB, model), BF16)]
        + as_scratch([silu, slope, both])
        + [
            pltpu.VMEM(expand.shape[1:], BF16),
            pltpu.VMEM(contract.shape[1:], BF16),
            pltpu.SemaphoreType.DMA((QUARTERS + 2 + 2 * len(tiles_of(model, 2 * TILE)),)),
            pltpu.SemaphoreType.DMA((1,)),
        ],
    )
    return results[count], results[:count]


def stream_back(grad, x, pre, gate, taps, masks, taps_out, j, cols):
    grad_pre = grad * gate * (1.0 + pre * (1.0 - gate))
    grad_x = taps[0:1] * grad_pre
    taps_out[j, 0:1, cols] = jnp.sum(grad_pre * x, axis=0, keepdims=True)
    for tap in range(1, CONV):
        masked = grad_pre * masks[tap - 1]
        grad_x = grad_x + taps[tap : tap + 1] * pltpu.roll(masked, TOK_MB - tap, 0)
        taps_out[j, tap : tap + 1, cols] = jnp.sum(masked * pltpu.roll(x, tap, 0), axis=0, keepdims=True)
    return grad_x


def attend_back_kernel(heads, count, me_ref, seg_col_ref, seg_row_ref, masks_ref, taps_ref, gain_ref, *refs):
    shards, refs = refs[:count], refs[count:]
    sources, refs = refs[: ATTEND_KEPT - 2], refs[ATTEND_KEPT - 2 :]
    project_hbm, beta_hbm, merge_hbm = refs[:3]
    partials, refs = refs[3 : 3 + count], refs[3 + count :]
    grad_taps_ref, grad_gain_ref, grad_qkv_hbm, grad_logit_hbm = refs[:4]
    kept_refs, refs = refs[4 : 2 + ATTEND_KEPT], refs[2 + ATTEND_KEPT :]
    qkv_ref, logit_ref, system_ref, attend_ref, inverse_ref, fresh_ref, out_ref = kept_refs
    rows_ref, grad_mixed_ref, grad_abs_ref, logit_abs_ref, grad_qkv_ref, grad_logit_ref, *refs = refs
    project_ref, beta_ref, merge_ref, sems, push_sems = refs
    push = Push(push_sems)
    order = relative_order(count)
    share = TOK_MB // count
    model = rows_ref.shape[1]
    width = heads * HEAD_DIM
    fetch = Fetch(
        [(merge_hbm.at[0], merge_ref)]
        + list(zip(sources, kept_refs))
        + [(beta_hbm, beta_ref)]
        + [(project_hbm.at[0, j], project_ref.at[j]) for j in range(3)],
        sems,
        ATTEND_KEPT,
    )
    for k in range(count):
        rows_ref[k * share : (k + 1) * share, :] = shards[k][...]
    fetch.wait(0)
    for cols in tiles_of(heads * HEAD_DIM):
        value = mm_t(rows_ref[...], merge_ref[cols, :])
        for k, difference in enumerate(order):
            grad_mixed_ref[place_of(me_ref, difference, share), cols] = value[k * share : (k + 1) * share]

    for place in range(1, ATTEND_KEPT - 1):
        fetch.wait(place)
    masks = [masks_ref[i] for i in range(CONV - 1)]
    strict, lower = block_masks(seg_col_ref, seg_row_ref)
    lane = lax.broadcasted_iota(jnp.int32, (TOK_MB, LANES), 1)
    everyone = range(heads)
    columns = [slice(h * HEAD_DIM, (h + 1) * HEAD_DIM) for h in everyone]
    grad_gain = jnp.zeros((8, HEAD_DIM), F32)
    grad_outs, queries, keys, values, betas, convs = [], [], [], [], [], []
    for h in everyone:
        cols = columns[h]
        taps = [taps_ref[0, j, :, cols] for j in range(3)]
        _, _, conv_q = stream(qkv_ref[0, :, cols], taps[0], masks)
        _, _, conv_k = stream(qkv_ref[1, :, cols], taps[1], masks)
        scale_q = lax.rsqrt(jnp.sum(conv_q * conv_q, axis=-1, keepdims=True) + EPS)
        scale_k = lax.rsqrt(jnp.sum(conv_k * conv_k, axis=-1, keepdims=True) + EPS)
        queries.append((conv_q * (scale_q * HEAD_DIM**-0.5)).astype(BF16))
        keys.append((conv_k * scale_k).astype(BF16))
        betas.append(jax.nn.sigmoid(logit_ref[:, h : h + 1]))
        out = out_ref[:, cols]
        grad_mixed = grad_mixed_ref[:, cols]
        mean = jnp.mean(out * out, axis=-1, keepdims=True)
        scale = lax.rsqrt(jnp.maximum(mean, OUT_FLOOR))
        unit = out * scale
        grad_gain = grad_gain + jnp.sum((grad_mixed * unit).reshape(TOK_MB // 8, 8, HEAD_DIM), axis=0)
        grad_unit = grad_mixed * gain_ref[...]
        through = jnp.where(mean > OUT_FLOOR, 1.0, jnp.where(mean == OUT_FLOOR, 0.5, 0.0))
        grad_out = scale * (
            grad_unit - unit * (through * jnp.mean(grad_unit * unit, axis=-1, keepdims=True))
        )
        grad_outs.append(grad_out.astype(BF16))
    grad_gain_ref[...] = grad_gain
    fresh = {(h, b): fresh_ref[rows_of(b), columns[h]] for h in everyone for b in range(BLOCKS)}
    d_out = {(h, b): grad_outs[h][rows_of(b)] for h in everyone for b in range(BLOCKS)}
    key_blocks = {(h, b): keys[h][rows_of(b)] for h in everyone for b in range(BLOCKS)}
    d_fresh, d_target, d_target_b = {}, {}, {}
    for c in range(BLOCKS):
        for h in everyone:
            total = t_mm(attend_ref[h, rows_of(c), rows_of(c)], d_out[h, c])
            for b in range(c + 1, BLOCKS):
                total = total + t_mm(attend_ref[h, rows_of(b), rows_of(c)], d_out[h, b])
            d_fresh[h, c] = total
    for b in reversed(range(BLOCKS)):
        for h in everyone:
            d_target[h, b] = t_mm(inverse_ref[h, b], d_fresh[h, b])
            d_target_b[h, b] = d_target[h, b].astype(BF16)
        for h in everyone:
            for c in range(b):
                d_fresh[h, c] = d_fresh[h, c] - t_mm(system_ref[h, rows_of(b), rows_of(c)], d_target_b[h, b])
    grad_query, inner, grad_key = {}, {}, {}
    for b in range(BLOCKS):
        for c in range(b + 1):
            for h in everyone:
                d_attend = jnp.where(lower[b, c], mm_t(d_out[h, b], fresh[h, c]), 0.0).astype(BF16)
                d_system = jnp.where(strict[b, c], -mm_t(d_target_b[h, b], fresh[h, c]), 0.0)
                for store, place, part in (
                    (grad_query, b, mm(d_attend, key_blocks[h, c])),
                    (inner, b, mm(d_system, key_blocks[h, c])),
                    (grad_key, c, t_mm(d_attend, queries[h][rows_of(b)])
                     + t_mm(d_system * betas[h][rows_of(b)], key_blocks[h, b])),
                ):
                    store[h, place] = store[h, place] + part if (h, place) in store else part

    def whole(store, h):
        return jnp.concatenate([store[h, b] for b in range(BLOCKS)], axis=0)

    grad_logits = jnp.zeros((TOK_MB, LANES), F32)
    for h in everyone:
        cols = columns[h]
        beta = betas[h]
        taps = [taps_ref[0, j, :, cols] for j in range(3)]
        inputs = [qkv_ref[j, :, cols] for j in range(3)]
        pre_q, gate_q, conv_q = stream(inputs[0], taps[0], masks)
        pre_k, gate_k, conv_k = stream(inputs[1], taps[1], masks)
        pre_v, gate_v, value = stream(inputs[2], taps[2], masks)
        scale_q = lax.rsqrt(jnp.sum(conv_q * conv_q, axis=-1, keepdims=True) + EPS)
        scale_k = lax.rsqrt(jnp.sum(conv_k * conv_k, axis=-1, keepdims=True) + EPS)
        unit_q, key = conv_q * scale_q, conv_k * scale_k
        within = whole(inner, h)
        target = whole(d_target, h)
        grad_q = whole(grad_query, h)
        grad_k = whole(grad_key, h) + beta * within
        grad_beta = jnp.sum(within * key + target * value, axis=-1, keepdims=True)
        grad_logits = jnp.where(lane == h, grad_beta * beta * (1.0 - beta), grad_logits)
        grad_conv_q = (HEAD_DIM**-0.5 * scale_q) * (
            grad_q - unit_q * jnp.sum(grad_q * unit_q, axis=-1, keepdims=True)
        )
        grad_conv_k = scale_k * (grad_k - key * jnp.sum(grad_k * key, axis=-1, keepdims=True))
        for j, (grad, pre, gate) in enumerate(
            ((grad_conv_q, pre_q, gate_q), (grad_conv_k, pre_k, gate_k), (beta * target, pre_v, gate_v))
        ):
            grad_x = stream_back(grad, inputs[j], pre, gate, taps[j], masks, grad_taps_ref, j, cols)
            grad_abs_ref[j, :, cols] = grad_x.astype(BF16)
    logit_abs_ref[...] = grad_logits.astype(BF16)
    for k, difference in enumerate(order):
        here = slice(k * share, (k + 1) * share)
        there = place_of(me_ref, difference, share)
        grad_logit_ref[here, :] = logit_abs_ref[there, :]
        for j in range(3):
            grad_qkv_ref[here, j * width : (j + 1) * width] = grad_abs_ref[j, there, :]
    push.start(grad_qkv_ref, grad_qkv_hbm)
    push.start(grad_logit_ref, grad_logit_hbm)
    for place in range(ATTEND_KEPT - 1, ATTEND_KEPT + 3):
        fetch.wait(place)
    for span in tiles_of(model):
        value = mm_t(grad_logit_ref[...], beta_ref[span, :])
        for j in range(3):
            value = value + mm_t(grad_qkv_ref[:, j * width : (j + 1) * width], project_ref[j, span, :])
        for k, ref in enumerate(partials):
            ref[:, span] = value[k * share : (k + 1) * share].astype(ref.dtype)
    push.wait()


def attend_backward(me, mine, shards, kept, taps, gain, project, beta_weight, merge):
    masks, seg_col, seg_row = mine
    heads = merge.shape[1] // HEAD_DIM
    width = heads * HEAD_DIM
    model = merge.shape[2]
    count = len(shards)
    kept = kept[1:3] + kept[4:]
    grads = [jax.ShapeDtypeStruct((TOK_MB, 3 * width), BF16), jax.ShapeDtypeStruct((TOK_MB, LANES), BF16)]
    results = call(
        functools.partial(attend_back_kernel, heads, count),
        (me, seg_col, seg_row, masks, taps, gain, *shards),
        (*kept, project, beta_weight, merge),
        partial_shapes(count, model)
        + [
            jax.ShapeDtypeStruct((3, CONV, width), F32),
            jax.ShapeDtypeStruct((8, HEAD_DIM), F32),
        ],
        grads,
        as_scratch(kept)
        + [
            pltpu.VMEM((TOK_MB, model), BF16),
            pltpu.VMEM((TOK_MB, width), F32),
            pltpu.VMEM((3, TOK_MB, width), BF16),
            pltpu.VMEM((TOK_MB, LANES), BF16),
        ]
        + as_scratch(grads)
        + [
            pltpu.VMEM(project.shape[1:], BF16),
            pltpu.VMEM(beta_weight.shape, BF16),
            pltpu.VMEM(merge.shape[1:], BF16),
            pltpu.SemaphoreType.DMA((ATTEND_KEPT + 3,)),
            pltpu.SemaphoreType.DMA((2,)),
        ],
    )
    return results[count + 2 :] + results[count : count + 2], results[:count]


def small_call(kernel, operands, out_shape):
    vmem = pl.BlockSpec(memory_space=pltpu.VMEM)
    return pl.pallas_call(
        kernel,
        in_specs=[vmem] * len(operands),
        out_specs=[vmem] * len(out_shape),
        out_shape=out_shape,
        compiler_params=pltpu.CompilerParams(vmem_limit_bytes=16 * 1024 * 1024),
        cost_estimate=pl.CostEstimate(flops=10**9, bytes_accessed=10**5, transcendentals=0),
    )(*operands)


def norm_kernel(gain_ref, x_ref, *refs):
    *more, total_ref, normed_ref = refs
    total = x_ref[...].astype(F32)
    for ref in more:
        total = total + ref[...].astype(F32)
    scale = lax.rsqrt(jnp.mean(total * total, axis=-1, keepdims=True) + EPS)
    total_ref[...] = total
    normed_ref[...] = (total * scale * gain_ref[...]).astype(BF16)


def norm_of_sum(gain, *terms):
    shape = terms[0].shape
    return small_call(
        norm_kernel, (gain, *terms), [jax.ShapeDtypeStruct(shape, F32), jax.ShapeDtypeStruct(shape, BF16)]
    )


def norm_back_kernel(gain_ref, base_ref, x_ref, near_ref, far_ref, grad_ref, narrow_ref, gain_out):
    grad_normed = near_ref[...].astype(F32) + far_ref[...].astype(F32)
    x = x_ref[...].astype(F32)
    scale = lax.rsqrt(jnp.mean(x * x, axis=-1, keepdims=True) + EPS)
    unit = x * scale
    grad_scaled = grad_normed * gain_ref[...]
    grad = base_ref[...].astype(F32) + scale * (
        grad_scaled - unit * jnp.mean(grad_scaled * unit, axis=-1, keepdims=True)
    )
    grad_ref[...] = grad
    narrow_ref[...] = grad.astype(BF16)
    rows, width = x.shape
    gain_out[...] = jnp.sum((grad_normed * unit).reshape(rows // 8, 8, width), axis=0)


def norm_backward(gain, base, x, near, far):
    shape = x.shape
    return small_call(
        norm_back_kernel,
        (gain, base, x, near, far),
        [
            jax.ShapeDtypeStruct(shape, F32),
            jax.ShapeDtypeStruct(shape, BF16),
            jax.ShapeDtypeStruct((8, shape[1]), F32),
        ],
    )


def tap_masks(segment):
    masks = []
    for tap in range(1, CONV):
        earlier = jnp.concatenate([jnp.full((tap,), -1, jnp.int32), segment[: TOK_MB - tap]], axis=0)
        masks.append(jnp.broadcast_to((earlier == segment).astype(F32)[:, None], (TOK_MB, HEAD_DIM)))
    return jnp.stack(masks)


def narrow(values):
    return values.astype(BF16)


def product(left, right):
    return jnp.dot(left, right, preferred_element_type=F32)


def product_left(left, right):
    return lax.dot_general(left, right, (((0,), (0,)), ((), ())), preferred_element_type=F32)


def product_right(left, right):
    return lax.dot_general(left, right, (((1,), (1,)), ((), ())), preferred_element_type=F32)


def segment_ids(lengths, count):
    ends = jnp.cumsum(lengths)
    places = jnp.arange(count, dtype=jnp.int32)
    return jnp.sum((places[:, None] >= ends[None, :]).astype(jnp.int32), axis=1, dtype=jnp.int32)


def flipped(values, axis, bit):
    return lax.ppermute(values, axis, [(i, i ^ bit) for i in range(lax.axis_size(axis))])


def shifted(values, axis, distance):
    devices = range(lax.axis_size(axis))
    return lax.ppermute(values, axis, [(i, i + distance) for i in devices if i + distance in devices])


def bits_of(axis):
    size = lax.axis_size(axis)
    bits = [1 << k for k in range(size.bit_length() - 1)]
    assert 1 << len(bits) == size
    return bits


def summed(values, axes):
    for axis in axes:
        for bit in bits_of(axis):
            values = values + flipped(values, axis, bit)
    return values


class Order:

    def __init__(self):
        self.last = None

    def flipped(self, values, bit):
        if bit > 1:
            if self.last is not None:
                values, _ = lax.optimization_barrier((values, self.last))
            self.last = flipped(values, "head", bit)
            return self.last
        return flipped(values, "head", bit)


def gather_far(shard, order):
    parts = [shard]
    for bit in reversed(bits_of("head")[1:]):
        parts = parts + [order.flipped(part, bit) for part in parts]
    return parts


def gather_near(parts):
    return parts + [flipped(part, "head", 1) for part in parts]


def gather(shard, order):
    return gather_near(gather_far(shard, order))


def added(parts, arrived):
    return [part.astype(F32) + other.astype(F32) for part, other in zip(parts, arrived)]


def scatter_near(parts):
    half = len(parts) // 2
    return added(parts[:half], [flipped(part, "head", 1) for part in parts[half:]])


def scatter_far(parts, order):
    for bit in bits_of("head")[1:]:
        half = len(parts) // 2
        arrived = [order.flipped(narrow(part), bit) for part in parts[half:]]
        if half == 1:
            return parts[0], arrived[0]
        parts = added(parts[:half], arrived)


def after(values, earlier):
    return lax.optimization_barrier((values, earlier))[0]


def together(*values):
    return lax.optimization_barrier(values)


def in_turn(kernel, order, shards=None, rows=None, finish=None):
    if rows is None:
        fars = [gather_far(shard, order) for shard in shards]
    kept, sums, near = [], [], None
    for m in range(len(rows or fars)):
        parts = gather_near(fars[m]) if rows is None else rows[m]
        if near is not None:
            parts, near = together(parts, near)
            sums.append(scatter_far(near, order))
        keep, partials = kernel(m, parts)
        if sums:
            partials = after(partials, sums[-1][1])
        if rows is None and m + 1 < len(fars):
            fars[m + 1], keep, partials = together(fars[m + 1], keep, partials)
        kept.append(keep)
        if finish is not None and m + 1 == len(rows or fars):
            kept = finish(kept)
            partials = after(partials, kept)
        if partials is not None:
            near = scatter_near(partials)
    if near is not None:
        sums.append(scatter_far(near, order))
    return kept, sums


def in_order(sums, finish):
    results = []
    for m, (near, far) in enumerate(sums):
        if results:
            far, results[-1] = together(far, results[-1])
        results.append(finish(m, near, far))
    return results


def sent(distance, sums, finish):
    arrived = []
    for m, (near, far) in enumerate(sums):
        if arrived:
            far = after(far, arrived[-1])
        arrived.append(shifted(finish(m, near, far), "section", distance))
    return arrived


def swapped(shards):
    count = lax.axis_size("dp")
    me = lax.axis_index("dp")
    values = jnp.stack(shards)
    wide = values.shape[-1] // count
    arrived = []
    for distance in range(count):
        block = lax.dynamic_slice_in_dim(values, ((me + distance) % count) * wide, wide, 2)
        if distance:
            block = lax.ppermute(block, "dp", [(i, (i + distance) % count) for i in range(count)])
        arrived.append(block)
    arrived = jnp.stack(arrived)
    ordered = [lax.dynamic_index_in_dim(arrived, (me - q) % count, 0, keepdims=False) for q in range(count)]
    return jnp.stack(ordered, axis=1)


def per_device(
    tokens,
    lengths,
    cotangent,
    attn_in,
    beta_weight,
    conv_weight,
    o_gain,
    attn_out,
    mlp_in,
    mlp_out,
    norm_gains,
):
    section = lax.axis_index("section")
    sections = lax.axis_size("section")
    member = lax.axis_index("head")
    micro = tokens.shape[0]
    width = tokens.shape[2]
    heads = beta_weight.shape[2]
    share = TOK_MB // lax.axis_size("head")
    me = member[None]
    beta_wide = jnp.pad(beta_weight[0], ((0, 0), (0, LANES - heads)))
    gains = norm_gains[0]
    every = range(micro)
    segments = [segment_ids(lengths[m], TOK_MB) for m in every]
    masks = [(tap_masks(s), s[:, None], s[None, :]) for s in segments]
    order = Order()
    relative = relative_order(lax.axis_size("head"))

    def blocks(values):
        return [lax.dynamic_slice_in_dim(values, (member ^ k) * share, share, 0) for k in relative]

    tokens_own = [blocks(tokens[m])[0] for m in every]
    cotangent_own = [blocks(cotangent[m])[0] for m in every]
    gain_in, gain_mid = gains[0:1], gains[1:2]

    def forward_turn(inputs, save, shards=None, rows=None):
        kept, sums = in_turn(
            lambda m, rows: attend_forward(
                me, masks[m], rows, conv_weight, o_gain, attn_in, beta_wide, attn_out, save
            ),
            order,
            shards,
            rows,
        )
        middles = in_order(sums, lambda m, near, far: norm_of_sum(gain_mid, inputs[m], near, far))
        kept_mid, sums = in_turn(
            lambda m, rows: expand_forward(me, rows, mlp_in, mlp_out, save),
            order,
            [values[1] for values in middles],
        )
        if save:
            return kept, [values[0] for values in middles], kept_mid
        return sent(1, sums, lambda m, near, far: narrow(middles[m][0] + near + far.astype(F32)))

    def backward_expand(incoming, slopes, shards=None, rows=None, finish=None):
        grads, sums = in_turn(
            lambda m, rows: expand_backward(me, rows, *slopes[m], mlp_in, mlp_out), order, shards, rows, finish
        )
        return grads, in_order(sums, lambda m, *terms: norm_backward(gain_mid, incoming[m], middles[m], *terms))

    def backward_attend(grad_middles):
        return in_turn(
            lambda m, rows: attend_backward(
                me, masks[m], rows, kept[m], conv_weight, o_gain, attn_in, beta_wide, attn_out
            ),
            order,
            [values[1] for values in grad_middles],
        )

    def all_rows(values):
        return jnp.concatenate(values, axis=0)

    last = sections - 1
    inputs = tokens_own
    normed_own, normed = None, [blocks(norm_of_sum(gain_in, tokens[m])[1]) for m in every]
    for turn in range(last):
        arrived = forward_turn(inputs, False, normed_own, normed)
        inputs = [jnp.where(section == 0, tokens_own[m], arrived[m]) for m in every]
        normed_own = [norm_of_sum(gain_in, value)[1] for value in inputs]
        normed = None
    kept, middles, kept_mid = forward_turn(inputs, True, normed_own, normed)

    hidden_rows = [lax.all_gather(values[1], "dp", axis=0, tiled=True) for values in kept_mid]
    mixed_rows = [lax.all_gather(values[3], "dp", axis=0, tiled=True) for values in kept]

    slopes = [values[2:] for values in kept_mid]
    incoming = cotangent_own
    rows = [blocks(cotangent[m]) for m in every]
    for turn in range(last):
        _, grad_middles = backward_expand(incoming, slopes, incoming, rows)
        _, sums = backward_attend(grad_middles)
        arrived = sent(
            -1, sums, lambda m, *terms: norm_backward(gain_in, grad_middles[m][0], inputs[m], *terms)[1]
        )
        incoming = [jnp.where(section == last, cotangent_own[m], arrived[m]) for m in every]
        rows = None
    normed_mid = all_rows([values[0] for values in kept_mid])
    slopes[-1], hidden_rows, mixed_rows = together(slopes[-1], hidden_rows, mixed_rows)
    expands, grad_middles = backward_expand(
        incoming, slopes, incoming, rows, lambda grads: narrow(product_left(normed_mid, all_rows(grads)))
    )
    grads, sums = backward_attend(grad_middles)
    finals = [norm_backward(gain_in, grad_middles[m][0], inputs[m], *sums[m]) for m in every]
    gain_one, gain_two = (
        sum(jnp.sum(values[2], axis=0) for values in group) for group in (finals, grad_middles)
    )
    rows_out = jnp.stack([values[0] for values in finals])
    half = width // sections
    moved = shifted(narrow(rows_out[:, :, half:]), "section", 1).astype(F32)
    grad_tokens = jnp.where(section == 0, rows_out[:, :, :half], moved)

    def spread(value, axis):
        return lax.psum_scatter(value, "dp", scatter_dimension=axis, tiled=True)

    early = spread(expands, 0)
    normed = all_rows([values[0] for values in kept])
    grad_project = narrow(product_left(normed, all_rows([grad[0] for grad in grads])))
    grad_beta = product_left(normed, all_rows([grad[1] for grad in grads]))[:, :heads]
    grad_taps, grad_head_gain = (sum(grad[place] for grad in grads) for place in (2, 3))
    grad_head_gain = jnp.sum(grad_head_gain, axis=0)

    columns = swapped(after(incoming, expands) + [values[1] for values in grad_middles])
    columns = jnp.concatenate(gather(columns, order), axis=2)
    columns = [part.reshape(-1, part.shape[-1]) for part in columns]
    grad_contract = sum(product_left(left, right) for left, right in zip(hidden_rows, columns[:micro]))
    grad_merge = sum(product_left(left, right) for left, right in zip(mixed_rows, columns[micro:]))
    flat = jnp.concatenate([gain_one, gain_two, grad_head_gain])
    flat = summed(flat, ("dp", "head"))
    grad_gains, grad_head_gain = flat[: 2 * width].reshape(2, width), flat[2 * width :]
    flat = summed(jnp.concatenate([grad_taps.reshape(-1), grad_beta.reshape(-1)]), ("dp",))
    grad_taps, grad_beta = flat[: grad_taps.size].reshape(grad_taps.shape), flat[grad_taps.size :]
    rows = width // lax.axis_size("dp")
    grad_beta = lax.dynamic_slice_in_dim(grad_beta.reshape(width, heads), lax.axis_index("dp") * rows, rows, 0)
    done = (grad_tokens, grad_contract, grad_merge, grad_beta, grad_taps, grad_head_gain, grad_gains, early)
    grad_project, done = lax.optimization_barrier((grad_project, done))
    grad_tokens, grad_contract, grad_merge, grad_beta, grad_taps, grad_head_gain, grad_gains, early = done
    units = mlp_in.shape[3]
    grad_expand = jnp.stack([part[:, :units] for part in jnp.split(early, 2, axis=1)]).astype(F32)
    grad_project = jnp.stack(jnp.split(spread(grad_project, 0), 3, axis=1)).astype(F32)
    return (
        grad_tokens,
        grad_project[None],
        grad_beta[None],
        grad_taps[None],
        grad_head_gain[None],
        grad_merge[None],
        grad_expand[None],
        grad_contract[None],
        grad_gains[None],
    )


def solution(mesh):
    return jax.shard_map(
        per_device,
        mesh=mesh,
        in_specs=(
            P("dp", None, None),
            P("dp", None),
            P("dp", None, None),
            P("section", None, None, "head"),
            P("section", None, "head"),
            P("section", None, None, "head"),
            P("section", None),
            P("section", "head", None),
            P("section", None, None, "head"),
            P("section", "head", None),
            P("section", None, None),
        ),
        out_specs=(
            P("dp", "head", "section"),
            P("section", None, "dp", "head"),
            P("section", "dp", "head"),
            P("section", None, None, "head"),
            P("section", None),
            P("section", "head", "dp"),
            P("section", None, "dp", "head"),
            P("section", "head", "dp"),
            P("section", None, None),
        ),
        check_vma=False,
    )
```

```python
import functools

import jax
import jax.numpy as jnp
from jax import lax
from jax.experimental import pallas as pl
from jax.experimental.pallas import tpu as pltpu
from jax.sharding import PartitionSpec as P

HEAD_DIM = 128
CONV = 4
TOK_MB = 384
BLOCK = 128
BLOCKS = TOK_MB // BLOCK
EPS = 1e-06
OUT_FLOOR = 0.0001
F32 = jnp.float32
BF16 = jnp.bfloat16
BASE = 4
LANES = 128
TILE = 256
QUARTERS = 4
ATTEND_KEPT = 9
ROW_COPIES = 16
VMEM_LIMIT = 50 * 1024 * 1024


def mm(left, right):
    return lax.dot_general(
        left.astype(BF16), right.astype(BF16), (((1,), (0,)), ((), ())), preferred_element_type=F32
    )


def mm_t(left, right):
    return lax.dot_general(
        left.astype(BF16), right.astype(BF16), (((1,), (1,)), ((), ())), preferred_element_type=F32
    )


def t_mm(left, right):
    return lax.dot_general(
        left.astype(BF16), right.astype(BF16), (((0,), (0,)), ((), ())), preferred_element_type=F32
    )


def rows_of(b):
    return slice(b * BLOCK, (b + 1) * BLOCK)


def tiles_of(size, tile=TILE):
    return [slice(start, min(start + tile, size)) for start in range(0, size, tile)]


def quarters(size):
    return tiles_of(size, size // QUARTERS)


def relative_order(count):
    order, bit = [0], count // 2
    while bit:
        order = order + [k ^ bit for k in order]
        bit //= 2
    return order


def place_of(me_ref, difference, share):
    return pl.ds(pl.multiple_of((me_ref[0] ^ difference) * share, 16), share)


def stream(x, taps, masks):
    pre = taps[0:1] * x
    for tap in range(1, CONV):
        pre = pre + taps[tap : tap + 1] * (pltpu.roll(x, tap, 0) * masks[tap - 1])
    gate = jax.nn.sigmoid(pre)
    return pre, gate, pre * gate


def unit_inverses(systems):
    size = systems[0].shape[0]
    row = lax.broadcasted_iota(jnp.int32, (size, size), 0)
    col = lax.broadcasted_iota(jnp.int32, (size, size), 1)
    eye = (row == col).astype(F32)
    near = (row // BASE == col // BASE).astype(F32)
    first = [-a * near for a in systems]
    total = [eye + n for n in first]
    second = [mm(n, n) for n in first]
    third = [mm(n, s) for n, s in zip(first, second)]
    total = [t + s + r for t, s, r in zip(total, second, third)]
    step = BASE
    while step < size:
        span = 2 * step
        off = ((row // span == col // span) & (row // step != col // step)).astype(F32)
        inner = [mm(a * off, t) for a, t in zip(systems, total)]
        outer = [mm(t, i) for t, i in zip(total, inner)]
        total = [t - o for t, o in zip(total, outer)]
        step = span
    return total


def block_masks(seg_col_ref, seg_row_ref):
    row = lax.broadcasted_iota(jnp.int32, (BLOCK, BLOCK), 0)
    col = lax.broadcasted_iota(jnp.int32, (BLOCK, BLOCK), 1)
    strict, lower = {}, {}
    for b in range(BLOCKS):
        for c in range(b + 1):
            same = seg_col_ref[rows_of(b), :] == seg_row_ref[:, rows_of(c)]
            strict[b, c] = same & (col < row) if b == c else same
            lower[b, c] = same & (col <= row) if b == c else same
    return strict, lower


class Fetch:

    def __init__(self, pairs, sems, ahead):
        self.copies = [pltpu.make_async_copy(src, dst, sems.at[i]) for i, (src, dst) in enumerate(pairs)]
        self.ahead = ahead
        self.started = 0
        self.start_to(ahead)

    def start_to(self, place):
        while self.started < min(place, len(self.copies)):
            self.copies[self.started].start()
            self.started += 1

    def wait(self, place):
        self.copies[place].wait()
        self.start_to(place + 1 + self.ahead)

    def wait_group(self, group):
        for place in range(QUARTERS):
            self.wait(QUARTERS * group + place)


def load_rows(me_ref, shards, rows_ref, count, sems):
    share = TOK_MB // count
    if len(shards) == count:
        for k in range(count):
            rows_ref[k * share : (k + 1) * share, :] = shards[k][...]
        return
    copies = [
        pltpu.make_async_copy(
            shards[0].at[place_of(me_ref, difference, share), :],
            rows_ref.at[k * share : (k + 1) * share, :],
            sems.at[k],
        )
        for k, difference in enumerate(relative_order(count))
    ]
    for copy in copies:
        copy.start()
    for copy in copies:
        copy.wait()


class Push:

    def __init__(self, sems):
        self.sems = sems
        self.copies = []

    def start(self, source, target):
        copy = pltpu.make_async_copy(source, target, self.sems.at[len(self.copies)])
        copy.start()
        self.copies.append(copy)

    def wait(self):
        for copy in self.copies:
            copy.wait()


def attend_kernel(heads, count, save, held, me_ref, seg_col_ref, seg_row_ref, masks_ref, taps_ref, gain_ref, *refs):
    *refs, row_sems = refs
    shards, refs = refs[:held], refs[held:]
    project_hbm, beta_hbm, merge_hbm = refs[:3]
    partials, refs = refs[3 : 3 + count], refs[3 + count :]
    targets, refs = (refs[:ATTEND_KEPT], refs[ATTEND_KEPT:]) if save else ([], refs)
    kept_refs, refs = refs[:ATTEND_KEPT], refs[ATTEND_KEPT:]
    rows_ref, qkv_ref, logit_ref, mixed_ref, system_ref, attend_ref, inverse_ref, fresh_ref, out_ref = kept_refs
    mixed_abs, project_ref, beta_ref, merge_ref, sems, push_sems = refs
    push = Push(push_sems)

    def ready(*places):
        if save:
            for place in places:
                push.start(kept_refs[place], targets[place])

    order = relative_order(count)
    share = TOK_MB // count
    fetch = Fetch(
        [(project_hbm.at[0, j], project_ref.at[j]) for j in range(3)]
        + [(beta_hbm, beta_ref), (merge_hbm.at[0], merge_ref)],
        sems,
        5,
    )
    load_rows(me_ref, shards, rows_ref, count, row_sems)
    rows = rows_ref[...]
    ready(0)

    def spread(ref, value, *lead):
        for k, difference in enumerate(order):
            ref[(*lead, place_of(me_ref, difference, share), slice(None))] = value[k * share : (k + 1) * share]

    for j in range(3):
        fetch.wait(j)
        for cols in tiles_of(heads * HEAD_DIM):
            value = mm(rows, project_ref[j, :, cols])
            for k, difference in enumerate(order):
                qkv_ref[j, place_of(me_ref, difference, share), cols] = value[k * share : (k + 1) * share]
    fetch.wait(3)
    spread(logit_ref, mm(rows, beta_ref[...]))
    ready(1, 2)

    masks = [masks_ref[i] for i in range(CONV - 1)]
    strict, lower = block_masks(seg_col_ref, seg_row_ref)
    queries, keys, values, betas = [], [], [], []
    for h in range(heads):
        cols = slice(h * HEAD_DIM, (h + 1) * HEAD_DIM)
        taps = [taps_ref[0, j, :, cols] for j in range(3)]
        _, _, query = stream(qkv_ref[0, :, cols], taps[0], masks)
        _, _, key = stream(qkv_ref[1, :, cols], taps[1], masks)
        _, _, value = stream(qkv_ref[2, :, cols], taps[2], masks)
        query = query * lax.rsqrt(jnp.sum(query * query, axis=-1, keepdims=True) + EPS) * HEAD_DIM**-0.5
        key = key * lax.rsqrt(jnp.sum(key * key, axis=-1, keepdims=True) + EPS)
        beta = jax.nn.sigmoid(logit_ref[:, h : h + 1])
        queries.append(query.astype(BF16))
        keys.append(key.astype(BF16))
        values.append(value * beta)
        betas.append(beta)
    attend, system = {}, {}
    for h in range(heads):
        for b in range(BLOCKS):
            for c in range(b + 1):
                inner = mm_t(keys[h][rows_of(b)], keys[h][rows_of(c)])
                system[h, b, c] = jnp.where(strict[b, c], inner * betas[h][rows_of(b)], 0.0)
                scores = mm_t(queries[h][rows_of(b)], keys[h][rows_of(c)])
                attend[h, b, c] = jnp.where(lower[b, c], scores, 0.0).astype(BF16)
                if c < b:
                    system[h, b, c] = system[h, b, c].astype(BF16)
                if save:
                    attend_ref[h, rows_of(b), rows_of(c)] = attend[h, b, c]
                    if c < b:
                        system_ref[h, rows_of(b), rows_of(c)] = system[h, b, c]
    index = [(h, b) for h in range(heads) for b in range(BLOCKS)]
    inverse = dict(zip(index, unit_inverses([system[h, b, b] for h, b in index])))
    for h, b in index:
        inverse[h, b] = inverse[h, b].astype(BF16)
        if save:
            inverse_ref[h, b] = inverse[h, b]
    ready(4, 5, 6)
    fresh = {}
    for b in range(BLOCKS):
        for h in range(heads):
            target = values[h][rows_of(b)]
            for c in range(b):
                target = target - mm(system[h, b, c], fresh[h, c])
            fresh[h, b] = mm(inverse[h, b], target).astype(BF16)
            if save:
                fresh_ref[rows_of(b), h * HEAD_DIM : (h + 1) * HEAD_DIM] = fresh[h, b]
    for h in range(heads):
        cols = slice(h * HEAD_DIM, (h + 1) * HEAD_DIM)
        for b in range(BLOCKS):
            out = mm(attend[h, b, 0], fresh[h, 0])
            for c in range(1, b + 1):
                out = out + mm(attend[h, b, c], fresh[h, c])
            mean = jnp.mean(out * out, axis=-1, keepdims=True)
            if save:
                out_ref[rows_of(b), cols] = out
            mixed_abs[rows_of(b), cols] = (
                out * lax.rsqrt(jnp.maximum(mean, OUT_FLOOR)) * gain_ref[...]
            ).astype(BF16)
    for k, difference in enumerate(order):
        mixed_ref[k * share : (k + 1) * share, :] = mixed_abs[place_of(me_ref, difference, share), :]
    ready(3, 7, 8)
    fetch.wait(4)
    write_partials(partials, merge_ref.shape[1], share, lambda cols: mm(mixed_ref[...], merge_ref[:, cols]))
    push.wait()


def write_partials(partials, width, share, product):
    for cols in tiles_of(width):
        value = product(cols)
        for k, ref in enumerate(partials):
            ref[:, cols] = value[k * share : (k + 1) * share].astype(ref.dtype)


def partial_shapes(count, width):
    share = TOK_MB // count
    return [jax.ShapeDtypeStruct((share, width), F32 if k < count // 2 else BF16) for k in range(count)]


def call(kernel, operands, rows, hbm, out_shape, hbm_shape, scratch_shapes, in_place=False):
    vmem = pl.BlockSpec(memory_space=pltpu.VMEM)
    far = pl.BlockSpec(memory_space=pltpu.HBM)
    blocks = isinstance(rows, list)
    rows = rows if blocks else [rows]
    return pl.pallas_call(
        functools.partial(kernel, len(rows)),
        in_specs=[pl.BlockSpec(memory_space=pltpu.SMEM)]
        + [vmem] * (len(operands) - 1)
        + [vmem if blocks else far] * len(rows)
        + [far] * len(hbm),
        out_specs=[vmem] * len(out_shape) + [far] * len(hbm_shape),
        out_shape=out_shape + hbm_shape,
        input_output_aliases=(
            {len(operands) + len(rows) + len(hbm) - 1: len(out_shape) + len(hbm_shape) - 1} if in_place else {}
        ),
        scratch_shapes=scratch_shapes + [pltpu.SemaphoreType.DMA((ROW_COPIES,))],
        compiler_params=pltpu.CompilerParams(vmem_limit_bytes=VMEM_LIMIT),
        cost_estimate=pl.CostEstimate(flops=2 * 10**9, bytes_accessed=10**5, transcendentals=0),
    )(*operands, *rows, *hbm)


def as_scratch(shapes):
    return [pltpu.VMEM(shape.shape, shape.dtype) for shape in shapes]


def attend_forward(me, mine, count, rows, taps, gain, project, beta_weight, merge, save):
    masks, seg_col, seg_row = mine
    heads = merge.shape[1] // HEAD_DIM
    width = heads * HEAD_DIM
    model = merge.shape[2]
    kept = [
        jax.ShapeDtypeStruct((TOK_MB, model), BF16),
        jax.ShapeDtypeStruct((3, TOK_MB, width), F32),
        jax.ShapeDtypeStruct((TOK_MB, LANES), F32),
        jax.ShapeDtypeStruct((TOK_MB, width), BF16),
        jax.ShapeDtypeStruct((heads, TOK_MB, TOK_MB), BF16),
        jax.ShapeDtypeStruct((heads, TOK_MB, TOK_MB), BF16),
        jax.ShapeDtypeStruct((heads, BLOCKS, BLOCK, BLOCK), BF16),
        jax.ShapeDtypeStruct((TOK_MB, width), BF16),
        jax.ShapeDtypeStruct((TOK_MB, width), F32),
    ]
    results = call(
        functools.partial(attend_kernel, heads, count, save),
        (me, seg_col, seg_row, masks, taps, gain),
        rows,
        (project, beta_weight, merge),
        partial_shapes(count, model),
        kept if save else [],
        as_scratch(kept)
        + [
            pltpu.VMEM((TOK_MB, width), BF16),
            pltpu.VMEM(project.shape[1:], BF16),
            pltpu.VMEM(beta_weight.shape, BF16),
            pltpu.VMEM(merge.shape[1:], BF16),
            pltpu.SemaphoreType.DMA((5,)),
            pltpu.SemaphoreType.DMA((ATTEND_KEPT,)),
        ],
    )
    return results[count:], results[:count]


def expand_kernel(count, save, held, me_ref, *refs):
    *refs, row_sems = refs
    shards, refs = refs[:held], refs[held:]
    share = TOK_MB // count
    if save:
        expand_hbm, *targets = refs[:5]
        rows_ref, hidden_ref, silu_ref, slope_ref, gate_ref, expand_ref, sems, push_sems = refs[5:]
        push = Push(push_sems)
        contract_copies = []
    else:
        expand_hbm, contract_hbm, *partials = refs[: 2 + count]
        rows_ref, hidden_ref, gate_ref, expand_ref, contract_ref, sems = refs[2 + count :]
        contract_copies = [(contract_hbm.at[0, s, :], contract_ref.at[s, :]) for s in quarters(contract_ref.shape[0])]
    tiles = tiles_of(hidden_ref.shape[1])
    fetch = Fetch(
        [(expand_hbm.at[0, j, s, :], expand_ref.at[j, s, :]) for j in range(2) for s in quarters(expand_ref.shape[1])]
        + contract_copies,
        sems,
        QUARTERS,
    )
    load_rows(me_ref, shards, rows_ref, count, row_sems)
    if save:
        push.start(rows_ref, targets[0])
    fetch.wait_group(0)
    for t in tiles:
        gate_ref[:, t] = mm(rows_ref[...], expand_ref[0, :, t])
    fetch.wait_group(1)
    for t in tiles:
        up_in = mm(rows_ref[...], expand_ref[1, :, t])
        gate_in = gate_ref[:, t]
        gate = jax.nn.sigmoid(gate_in)
        silu = gate_in * gate
        hidden_ref[:, t] = (silu * up_in).astype(BF16)
        if save:
            silu_ref[:, t] = silu.astype(BF16)
            slope_ref[:, t] = (up_in * gate * (1.0 + gate_in * (1.0 - gate))).astype(BF16)
    if save:
        for source, target in zip((hidden_ref, silu_ref, slope_ref), targets[1:]):
            push.start(source, target)
        push.wait()
    else:
        fetch.wait_group(2)
        write_partials(partials, rows_ref.shape[1], share, lambda cols: mm(hidden_ref[...], contract_ref[:, cols]))


def expand_forward(me, count, rows, expand, contract, save):
    model, units = expand.shape[2:]
    kept = [jax.ShapeDtypeStruct((TOK_MB, model), BF16)] + [jax.ShapeDtypeStruct((TOK_MB, units), BF16)] * 3
    results = call(
        functools.partial(expand_kernel, count, save),
        (me,),
        rows,
        (expand,) if save else (expand, contract),
        [] if save else partial_shapes(count, model),
        kept if save else [],
        as_scratch(kept if save else kept[:2])
        + [pltpu.VMEM((TOK_MB, units), F32), pltpu.VMEM(expand.shape[1:], BF16)]
        + ([] if save else [pltpu.VMEM(contract.shape[1:], BF16)])
        + [pltpu.SemaphoreType.DMA(((2 if save else 3) * QUARTERS,))]
        + ([pltpu.SemaphoreType.DMA((4,))] if save else []),
    )
    return (results, None) if save else (None, results)


def padded(units):
    return -(-units // LANES) * LANES


def expand_back_kernel(count, into, held, me_ref, *refs):
    *refs, row_sems = refs
    shards, refs = refs[:held], refs[held:]
    silu_hbm, slope_hbm, expand_hbm, contract_hbm, *refs = refs
    if into:
        refs = refs[1:]
    partials, refs = refs[:count], refs[count:]
    both_hbm, rows_ref, silu_ref, slope_ref, both_ref, expand_ref, contract_ref, sems, push_sems = refs
    push = Push(push_sems)
    share = TOK_MB // count
    units = silu_ref.shape[1]
    second = padded(units)
    spans = tiles_of(rows_ref.shape[1], 2 * TILE)
    fetch = Fetch(
        [(contract_hbm.at[0, s, :], contract_ref.at[s, :]) for s in quarters(contract_ref.shape[0])]
        + [(slope_hbm, slope_ref), (silu_hbm, silu_ref)]
        + [(expand_hbm.at[0, j, s, :], expand_ref.at[j, s, :]) for s in spans for j in range(2)],
        sems,
        QUARTERS + 2,
    )
    load_rows(me_ref, shards, rows_ref, count, row_sems)
    if second > units:
        both_ref[...] = jnp.zeros(both_ref.shape, BF16)
    fetch.wait_group(0)
    fetch.wait(QUARTERS)
    fetch.wait(QUARTERS + 1)
    for t in tiles_of(units):
        grad_hidden = mm_t(rows_ref[...], contract_ref[t, :])
        both_ref[:, t] = (grad_hidden * slope_ref[:, t].astype(F32)).astype(BF16)
        both_ref[:, second + t.start : second + t.stop] = (
            grad_hidden * silu_ref[:, t].astype(F32)
        ).astype(BF16)
    push.start(both_ref, both_hbm.at[into * TOK_MB : (into + 1) * TOK_MB, :])
    for i, span in enumerate(spans):
        for j in range(2):
            fetch.wait(QUARTERS + 2 + 2 * i + j)
        for s in tiles_of(span.stop - span.start):
            s = slice(span.start + s.start, span.start + s.stop)
            value = mm_t(both_ref[:, :units], expand_ref[0, s, :])
            value = value + mm_t(both_ref[:, second : second + units], expand_ref[1, s, :])
            for k, ref in enumerate(partials):
                ref[:, s] = value[k * share : (k + 1) * share].astype(ref.dtype)
    push.wait()


def expand_backward(me, count, rows, silu, slope, expand, contract, into, micro, joint):
    model, units = expand.shape[2:]
    both = jax.ShapeDtypeStruct((TOK_MB, 2 * padded(units)), BF16)
    results = call(
        functools.partial(expand_back_kernel, count, into),
        (me,),
        rows,
        (silu, slope, expand, contract) + ((joint,) if into else ()),
        partial_shapes(count, model),
        [jax.ShapeDtypeStruct((micro * TOK_MB, both.shape[1]), BF16)],
        [pltpu.VMEM((TOK_MB, model), BF16)]
        + as_scratch([silu, slope, both])
        + [
            pltpu.VMEM(expand.shape[1:], BF16),
            pltpu.VMEM(contract.shape[1:], BF16),
            pltpu.SemaphoreType.DMA((QUARTERS + 2 + 2 * len(tiles_of(model, 2 * TILE)),)),
            pltpu.SemaphoreType.DMA((1,)),
        ],
        into > 0,
    )
    return results[count], results[:count]


def stream_back(grad, x, pre, gate, taps, masks, taps_out, j, cols):
    grad_pre = grad * gate * (1.0 + pre * (1.0 - gate))
    grad_x = taps[0:1] * grad_pre
    taps_out[j, 0:1, cols] = jnp.sum(grad_pre * x, axis=0, keepdims=True)
    for tap in range(1, CONV):
        masked = grad_pre * masks[tap - 1]
        grad_x = grad_x + taps[tap : tap + 1] * pltpu.roll(masked, TOK_MB - tap, 0)
        taps_out[j, tap : tap + 1, cols] = jnp.sum(masked * pltpu.roll(x, tap, 0), axis=0, keepdims=True)
    return grad_x


def attend_back_kernel(heads, count, held, me_ref, seg_col_ref, seg_row_ref, masks_ref, taps_ref, gain_ref, *refs):
    *refs, row_sems = refs
    shards, refs = refs[:held], refs[held:]
    sources, refs = refs[: ATTEND_KEPT - 2], refs[ATTEND_KEPT - 2 :]
    project_hbm, beta_hbm, merge_hbm = refs[:3]
    partials, refs = refs[3 : 3 + count], refs[3 + count :]
    grad_taps_ref, grad_gain_ref, grad_qkv_hbm, grad_logit_hbm = refs[:4]
    kept_refs, refs = refs[4 : 2 + ATTEND_KEPT], refs[2 + ATTEND_KEPT :]
    qkv_ref, logit_ref, system_ref, attend_ref, inverse_ref, fresh_ref, out_ref = kept_refs
    rows_ref, grad_mixed_ref, grad_abs_ref, logit_abs_ref, grad_qkv_ref, grad_logit_ref, *refs = refs
    project_ref, beta_ref, merge_ref, sems, push_sems = refs
    push = Push(push_sems)
    order = relative_order(count)
    share = TOK_MB // count
    model = rows_ref.shape[1]
    width = heads * HEAD_DIM
    fetch = Fetch(
        [(merge_hbm.at[0], merge_ref)]
        + list(zip(sources, kept_refs))
        + [(beta_hbm, beta_ref)]
        + [(project_hbm.at[0, j], project_ref.at[j]) for j in range(3)],
        sems,
        ATTEND_KEPT,
    )
    load_rows(me_ref, shards, rows_ref, count, row_sems)
    fetch.wait(0)
    for cols in tiles_of(heads * HEAD_DIM):
        value = mm_t(rows_ref[...], merge_ref[cols, :])
        for k, difference in enumerate(order):
            grad_mixed_ref[place_of(me_ref, difference, share), cols] = value[k * share : (k + 1) * share]

    for place in range(1, ATTEND_KEPT - 1):
        fetch.wait(place)
    masks = [masks_ref[i] for i in range(CONV - 1)]
    strict, lower = block_masks(seg_col_ref, seg_row_ref)
    lane = lax.broadcasted_iota(jnp.int32, (TOK_MB, LANES), 1)
    everyone = range(heads)
    columns = [slice(h * HEAD_DIM, (h + 1) * HEAD_DIM) for h in everyone]
    grad_gain = jnp.zeros((8, HEAD_DIM), F32)
    grad_outs, queries, keys, values, betas, convs = [], [], [], [], [], []
    for h in everyone:
        cols = columns[h]
        taps = [taps_ref[0, j, :, cols] for j in range(3)]
        _, _, conv_q = stream(qkv_ref[0, :, cols], taps[0], masks)
        _, _, conv_k = stream(qkv_ref[1, :, cols], taps[1], masks)
        scale_q = lax.rsqrt(jnp.sum(conv_q * conv_q, axis=-1, keepdims=True) + EPS)
        scale_k = lax.rsqrt(jnp.sum(conv_k * conv_k, axis=-1, keepdims=True) + EPS)
        queries.append((conv_q * (scale_q * HEAD_DIM**-0.5)).astype(BF16))
        keys.append((conv_k * scale_k).astype(BF16))
        betas.append(jax.nn.sigmoid(logit_ref[:, h : h + 1]))
        out = out_ref[:, cols]
        grad_mixed = grad_mixed_ref[:, cols]
        mean = jnp.mean(out * out, axis=-1, keepdims=True)
        scale = lax.rsqrt(jnp.maximum(mean, OUT_FLOOR))
        unit = out * scale
        grad_gain = grad_gain + jnp.sum((grad_mixed * unit).reshape(TOK_MB // 8, 8, HEAD_DIM), axis=0)
        grad_unit = grad_mixed * gain_ref[...]
        through = jnp.where(mean > OUT_FLOOR, 1.0, jnp.where(mean == OUT_FLOOR, 0.5, 0.0))
        grad_out = scale * (
            grad_unit - unit * (through * jnp.mean(grad_unit * unit, axis=-1, keepdims=True))
        )
        grad_outs.append(grad_out.astype(BF16))
    grad_gain_ref[...] = grad_gain
    fresh = {(h, b): fresh_ref[rows_of(b), columns[h]] for h in everyone for b in range(BLOCKS)}
    d_out = {(h, b): grad_outs[h][rows_of(b)] for h in everyone for b in range(BLOCKS)}
    key_blocks = {(h, b): keys[h][rows_of(b)] for h in everyone for b in range(BLOCKS)}
    d_fresh, d_target, d_target_b = {}, {}, {}
    for c in range(BLOCKS):
        for h in everyone:
            total = t_mm(attend_ref[h, rows_of(c), rows_of(c)], d_out[h, c])
            for b in range(c + 1, BLOCKS):
                total = total + t_mm(attend_ref[h, rows_of(b), rows_of(c)], d_out[h, b])
            d_fresh[h, c] = total
    for b in reversed(range(BLOCKS)):
        for h in everyone:
            d_target[h, b] = t_mm(inverse_ref[h, b], d_fresh[h, b])
            d_target_b[h, b] = d_target[h, b].astype(BF16)
        for h in everyone:
            for c in range(b):
                d_fresh[h, c] = d_fresh[h, c] - t_mm(system_ref[h, rows_of(b), rows_of(c)], d_target_b[h, b])
    grad_query, inner, grad_key = {}, {}, {}
    for b in range(BLOCKS):
        for c in range(b + 1):
            for h in everyone:
                d_attend = jnp.where(lower[b, c], mm_t(d_out[h, b], fresh[h, c]), 0.0).astype(BF16)
                d_system = jnp.where(strict[b, c], -mm_t(d_target_b[h, b], fresh[h, c]), 0.0)
                for store, place, part in (
                    (grad_query, b, mm(d_attend, key_blocks[h, c])),
                    (inner, b, mm(d_system, key_blocks[h, c])),
                    (grad_key, c, t_mm(d_attend, queries[h][rows_of(b)])
                     + t_mm(d_system * betas[h][rows_of(b)], key_blocks[h, b])),
                ):
                    store[h, place] = store[h, place] + part if (h, place) in store else part

    def whole(store, h):
        return jnp.concatenate([store[h, b] for b in range(BLOCKS)], axis=0)

    grad_logits = jnp.zeros((TOK_MB, LANES), F32)
    for h in everyone:
        cols = columns[h]
        beta = betas[h]
        taps = [taps_ref[0, j, :, cols] for j in range(3)]
        inputs = [qkv_ref[j, :, cols] for j in range(3)]
        pre_q, gate_q, conv_q = stream(inputs[0], taps[0], masks)
        pre_k, gate_k, conv_k = stream(inputs[1], taps[1], masks)
        pre_v, gate_v, value = stream(inputs[2], taps[2], masks)
        scale_q = lax.rsqrt(jnp.sum(conv_q * conv_q, axis=-1, keepdims=True) + EPS)
        scale_k = lax.rsqrt(jnp.sum(conv_k * conv_k, axis=-1, keepdims=True) + EPS)
        unit_q, key = conv_q * scale_q, conv_k * scale_k
        within = whole(inner, h)
        target = whole(d_target, h)
        grad_q = whole(grad_query, h)
        grad_k = whole(grad_key, h) + beta * within
        grad_beta = jnp.sum(within * key + target * value, axis=-1, keepdims=True)
        grad_logits = jnp.where(lane == h, grad_beta * beta * (1.0 - beta), grad_logits)
        grad_conv_q = (HEAD_DIM**-0.5 * scale_q) * (
            grad_q - unit_q * jnp.sum(grad_q * unit_q, axis=-1, keepdims=True)
        )
        grad_conv_k = scale_k * (grad_k - key * jnp.sum(grad_k * key, axis=-1, keepdims=True))
        for j, (grad, pre, gate) in enumerate(
            ((grad_conv_q, pre_q, gate_q), (grad_conv_k, pre_k, gate_k), (beta * target, pre_v, gate_v))
        ):
            grad_x = stream_back(grad, inputs[j], pre, gate, taps[j], masks, grad_taps_ref, j, cols)
            grad_abs_ref[j, :, cols] = grad_x.astype(BF16)
    logit_abs_ref[...] = grad_logits.astype(BF16)
    for k, difference in enumerate(order):
        here = slice(k * share, (k + 1) * share)
        there = place_of(me_ref, difference, share)
        grad_logit_ref[here, :] = logit_abs_ref[there, :]
        for j in range(3):
            grad_qkv_ref[here, j * width : (j + 1) * width] = grad_abs_ref[j, there, :]
    push.start(grad_qkv_ref, grad_qkv_hbm)
    push.start(grad_logit_ref, grad_logit_hbm)
    for place in range(ATTEND_KEPT - 1, ATTEND_KEPT + 3):
        fetch.wait(place)
    for span in tiles_of(model):
        value = mm_t(grad_logit_ref[...], beta_ref[span, :])
        for j in range(3):
            value = value + mm_t(grad_qkv_ref[:, j * width : (j + 1) * width], project_ref[j, span, :])
        for k, ref in enumerate(partials):
            ref[:, span] = value[k * share : (k + 1) * share].astype(ref.dtype)
    push.wait()


def attend_backward(me, mine, count, rows, kept, taps, gain, project, beta_weight, merge):
    masks, seg_col, seg_row = mine
    heads = merge.shape[1] // HEAD_DIM
    width = heads * HEAD_DIM
    model = merge.shape[2]
    kept = kept[1:3] + kept[4:]
    grads = [jax.ShapeDtypeStruct((TOK_MB, 3 * width), BF16), jax.ShapeDtypeStruct((TOK_MB, LANES), BF16)]
    results = call(
        functools.partial(attend_back_kernel, heads, count),
        (me, seg_col, seg_row, masks, taps, gain),
        rows,
        (*kept, project, beta_weight, merge),
        partial_shapes(count, model)
        + [
            jax.ShapeDtypeStruct((3, CONV, width), F32),
            jax.ShapeDtypeStruct((8, HEAD_DIM), F32),
        ],
        grads,
        as_scratch(kept)
        + [
            pltpu.VMEM((TOK_MB, model), BF16),
            pltpu.VMEM((TOK_MB, width), F32),
            pltpu.VMEM((3, TOK_MB, width), BF16),
            pltpu.VMEM((TOK_MB, LANES), BF16),
        ]
        + as_scratch(grads)
        + [
            pltpu.VMEM(project.shape[1:], BF16),
            pltpu.VMEM(beta_weight.shape, BF16),
            pltpu.VMEM(merge.shape[1:], BF16),
            pltpu.SemaphoreType.DMA((ATTEND_KEPT + 3,)),
            pltpu.SemaphoreType.DMA((2,)),
        ],
    )
    return results[count + 2 :] + results[count : count + 2], results[:count]


def small_call(kernel, operands, out_shape):
    vmem = pl.BlockSpec(memory_space=pltpu.VMEM)
    return pl.pallas_call(
        kernel,
        in_specs=[vmem] * len(operands),
        out_specs=[vmem] * len(out_shape),
        out_shape=out_shape,
        compiler_params=pltpu.CompilerParams(vmem_limit_bytes=16 * 1024 * 1024),
        cost_estimate=pl.CostEstimate(flops=10**9, bytes_accessed=10**5, transcendentals=0),
    )(*operands)


def total_of(refs):
    total = refs[0][...].astype(F32)
    for ref in refs[1:]:
        total = total + ref[...].astype(F32)
    return total


def norm_kernel(gain_ref, *refs):
    *terms, total_ref, normed_ref = refs
    total = total_of(terms)
    scale = lax.rsqrt(jnp.mean(total * total, axis=-1, keepdims=True) + EPS)
    total_ref[...] = total
    normed_ref[...] = (total * scale * gain_ref[...]).astype(BF16)


def norm_of_sum(gain, *terms):
    shape = terms[0].shape
    return small_call(
        norm_kernel, (gain, *terms), [jax.ShapeDtypeStruct(shape, F32), jax.ShapeDtypeStruct(shape, BF16)]
    )


def first_norm_kernel(m, me_ref, gain_ref, tokens_hbm, normed_ref, own_ref, rows_ref, sem):
    copy = pltpu.make_async_copy(tokens_hbm.at[m], rows_ref, sem)
    copy.start()
    copy.wait()
    share = own_ref.shape[0]
    own_ref[...] = rows_ref[place_of(me_ref, 0, share), :]
    for rows in tiles_of(TOK_MB, BLOCK):
        x = rows_ref[rows, :].astype(F32)
        scale = lax.rsqrt(jnp.mean(x * x, axis=-1, keepdims=True) + EPS)
        normed_ref[rows, :] = (x * scale * gain_ref[...]).astype(BF16)


def first_norm(me, gain, tokens, m, share):
    vmem = pl.BlockSpec(memory_space=pltpu.VMEM)
    width = tokens.shape[2]
    return pl.pallas_call(
        functools.partial(first_norm_kernel, m),
        in_specs=[pl.BlockSpec(memory_space=pltpu.SMEM), vmem, pl.BlockSpec(memory_space=pltpu.HBM)],
        out_specs=[vmem, vmem],
        out_shape=[jax.ShapeDtypeStruct((TOK_MB, width), BF16), jax.ShapeDtypeStruct((share, width), BF16)],
        scratch_shapes=[pltpu.VMEM((TOK_MB, width), BF16), pltpu.SemaphoreType.DMA],
        compiler_params=pltpu.CompilerParams(vmem_limit_bytes=16 * 1024 * 1024),
        cost_estimate=pl.CostEstimate(flops=10**9, bytes_accessed=10**5, transcendentals=0),
    )(me, gain, tokens)


def norm_back_kernel(gain_ref, base_ref, x_ref, *refs):
    *terms, grad_ref, narrow_ref, gain_out = refs
    grad_normed = total_of(terms)
    x = x_ref[...].astype(F32)
    scale = lax.rsqrt(jnp.mean(x * x, axis=-1, keepdims=True) + EPS)
    unit = x * scale
    grad_scaled = grad_normed * gain_ref[...]
    grad = base_ref[...].astype(F32) + scale * (
        grad_scaled - unit * jnp.mean(grad_scaled * unit, axis=-1, keepdims=True)
    )
    grad_ref[...] = grad
    narrow_ref[...] = grad.astype(BF16)
    rows, width = x.shape
    gain_out[...] = jnp.sum((grad_normed * unit).reshape(rows // 8, 8, width), axis=0)


def norm_backward(gain, base, x, *terms):
    shape = x.shape
    return small_call(
        norm_back_kernel,
        (gain, base, x, *terms),
        [
            jax.ShapeDtypeStruct(shape, F32),
            jax.ShapeDtypeStruct(shape, BF16),
            jax.ShapeDtypeStruct((8, shape[1]), F32),
        ],
    )


def tap_masks(segment):
    masks = []
    for tap in range(1, CONV):
        earlier = jnp.concatenate([jnp.full((tap,), -1, jnp.int32), segment[: TOK_MB - tap]], axis=0)
        masks.append(jnp.broadcast_to((earlier == segment).astype(F32)[:, None], (TOK_MB, HEAD_DIM)))
    return jnp.stack(masks)


def narrow(values):
    return values.astype(BF16)


def product(left, right):
    return jnp.dot(left, right, preferred_element_type=F32)


def product_left(left, right):
    return lax.dot_general(left, right, (((0,), (0,)), ((), ())), preferred_element_type=F32)


def product_right(left, right):
    return lax.dot_general(left, right, (((1,), (1,)), ((), ())), preferred_element_type=F32)


def segment_ids(lengths, count):
    ends = jnp.cumsum(lengths)
    places = jnp.arange(count, dtype=jnp.int32)
    return jnp.sum((places[:, None] >= ends[None, :]).astype(jnp.int32), axis=1, dtype=jnp.int32)


def flipped(values, axis, bit):
    return lax.ppermute(values, axis, [(i, i ^ bit) for i in range(lax.axis_size(axis))])


def shifted(values, axis, distance):
    devices = range(lax.axis_size(axis))
    return lax.ppermute(values, axis, [(i, i + distance) for i in devices if i + distance in devices])


def bits_of(axis):
    size = lax.axis_size(axis)
    bits = [1 << k for k in range(size.bit_length() - 1)]
    assert 1 << len(bits) == size
    return bits


def summed(values, axes):
    for axis in axes:
        for bit in bits_of(axis):
            values = values + flipped(values, axis, bit)
    return values


class Order:

    def __init__(self):
        self.last = None

    def flipped(self, values, bit):
        if bit > 1:
            if self.last is not None:
                values, _ = lax.optimization_barrier((values, self.last))
            self.last = flipped(values, "head", bit)
            return self.last
        return flipped(values, "head", bit)


def gather_far(shard, order):
    parts = [shard]
    for bit in reversed(bits_of("head")[1:]):
        parts = parts + [order.flipped(part, bit) for part in parts]
    return parts


def gather_near(parts):
    return parts + [flipped(part, "head", 1) for part in parts]


def gather(shard, order):
    return gather_near(gather_far(shard, order))


def total(terms):
    return sum(term.astype(F32) for term in terms)


def scatter_near(parts):
    half = len(parts) // 2
    return [[part, flipped(other, "head", 1)] for part, other in zip(parts[:half], parts[half:])]


def scatter_far(parts, order):
    for bit in bits_of("head")[1:]:
        half = len(parts) // 2
        arrived = [order.flipped(narrow(total(terms)), bit) for terms in parts[half:]]
        parts = [terms + [other] for terms, other in zip(parts[:half], arrived)]
    return parts[0]


def after(values, earlier):
    return lax.optimization_barrier((values, earlier))[0]


def together(*values):
    return lax.optimization_barrier(values)


def in_turn(kernel, order, shards=None, rows=None, finish=None):
    if rows is None:
        fars = [gather_far(shard, order) for shard in shards]
    kept, sums, near = [], [], None
    for m in range(len(rows or fars)):
        parts = gather_near(fars[m]) if rows is None else rows[m]
        if near is not None:
            half = len(near) // 2
            sent_on = [[total(terms)] for terms in near[half:]]
            parts, sent_on = together(parts, sent_on)
            near = near[:half] + sent_on
            sums.append(scatter_far(near, order))
        keep, partials = kernel(m, parts)
        if sums:
            partials = after(partials, sums[-1][-1])
        if rows is None and m + 1 < len(fars):
            fars[m + 1], keep, partials = together(fars[m + 1], keep, partials)
        kept.append(keep)
        if finish is not None and m + 1 == len(rows or fars):
            kept = finish(kept)
            partials = after(partials, kept)
        if partials is not None:
            near = scatter_near(partials)
    if near is not None:
        sums.append(scatter_far(near, order))
    return kept, sums


def in_order(sums, finish):
    results = []
    for m, (*terms, far) in enumerate(sums):
        if results:
            far, results[-1] = together(far, results[-1])
        results.append(finish(m, *terms, far))
    return results


def sent(distance, sums, finish):
    arrived = []
    for m, (*terms, far) in enumerate(sums):
        if arrived:
            far = after(far, arrived[-1])
        arrived.append(shifted(finish(m, *terms, far), "section", distance))
    return arrived


def swapped(shards):
    count = lax.axis_size("dp")
    me = lax.axis_index("dp")
    values = jnp.stack(shards)
    wide = values.shape[-1] // count
    arrived = []
    for distance in range(count):
        block = lax.dynamic_slice_in_dim(values, ((me + distance) % count) * wide, wide, 2)
        if distance:
            block = lax.ppermute(block, "dp", [(i, (i + distance) % count) for i in range(count)])
        arrived.append(block)
    arrived = jnp.stack(arrived)
    ordered = [lax.dynamic_index_in_dim(arrived, (me - q) % count, 0, keepdims=False) for q in range(count)]
    return jnp.stack(ordered, axis=1)


def per_device(
    tokens,
    lengths,
    cotangent,
    attn_in,
    beta_weight,
    conv_weight,
    o_gain,
    attn_out,
    mlp_in,
    mlp_out,
    norm_gains,
):
    section = lax.axis_index("section")
    sections = lax.axis_size("section")
    member = lax.axis_index("head")
    micro = tokens.shape[0]
    width = tokens.shape[2]
    heads = beta_weight.shape[2]
    share = TOK_MB // lax.axis_size("head")
    me = member[None]
    beta_wide = jnp.pad(beta_weight[0], ((0, 0), (0, LANES - heads)))
    gains = norm_gains[0]
    every = range(micro)
    segments = [segment_ids(lengths[m], TOK_MB) for m in every]
    masks = [(tap_masks(s), s[:, None], s[None, :]) for s in segments]
    order = Order()
    groups = lax.axis_size("head")
    cotangent_own = [
        lax.dynamic_slice(cotangent, (m, member * share, 0), (1, share, width))[0] for m in every
    ]
    gain_in, gain_mid = gains[0:1], gains[1:2]

    def forward_turn(inputs, save, shards=None, rows=None):
        kept, sums = in_turn(
            lambda m, rows: attend_forward(
                me, masks[m], groups, rows, conv_weight, o_gain, attn_in, beta_wide, attn_out, save
            ),
            order,
            shards,
            rows,
        )
        middles = in_order(sums, lambda m, *terms: norm_of_sum(gain_mid, inputs[m], *terms))
        kept_mid, sums = in_turn(
            lambda m, rows: expand_forward(me, groups, rows, mlp_in, mlp_out, save),
            order,
            [values[1] for values in middles],
        )
        if save:
            return kept, [values[0] for values in middles], kept_mid
        return sent(1, sums, lambda m, *terms: narrow(total([middles[m][0], *terms])))

    def backward_expand(incoming, slopes, shards=None, rows=None, finish=None):
        joint = [None]

        def kernel(m, rows):
            joint[0], partials = expand_backward(
                me, groups, rows, *slopes[m], mlp_in, mlp_out, m, micro, joint[0]
            )
            return joint[0], partials

        grads, sums = in_turn(kernel, order, shards, rows, finish)
        return grads, in_order(sums, lambda m, *terms: norm_backward(gain_mid, incoming[m], middles[m], *terms))

    def backward_attend(grad_middles):
        return in_turn(
            lambda m, rows: attend_backward(
                me, masks[m], groups, rows, kept[m], conv_weight, o_gain, attn_in, beta_wide, attn_out
            ),
            order,
            [values[1] for values in grad_middles],
        )

    def all_rows(values):
        return jnp.concatenate(values, axis=0)

    last = sections - 1
    normed, tokens_own = zip(*(first_norm(me, gain_in, tokens, m, share) for m in every))
    inputs, normed_own = tokens_own, None
    for turn in range(last):
        arrived = forward_turn(inputs, False, normed_own, normed)
        inputs = [jnp.where(section == 0, tokens_own[m], arrived[m]) for m in every]
        normed_own = [norm_of_sum(gain_in, value)[1] for value in inputs]
        normed = None
    kept, middles, kept_mid = forward_turn(inputs, True, normed_own, normed)

    hidden_rows = [lax.all_gather(values[1], "dp", axis=0, tiled=True) for values in kept_mid]
    mixed_rows = [lax.all_gather(values[3], "dp", axis=0, tiled=True) for values in kept]

    slopes = [values[2:] for values in kept_mid]
    incoming = cotangent_own
    rows = [cotangent[m] for m in every]
    for turn in range(last):
        _, grad_middles = backward_expand(incoming, slopes, incoming, rows)
        _, sums = backward_attend(grad_middles)
        arrived = sent(
            -1, sums, lambda m, *terms: norm_backward(gain_in, grad_middles[m][0], inputs[m], *terms)[1]
        )
        incoming = [jnp.where(section == last, cotangent_own[m], arrived[m]) for m in every]
        rows = None
    normed_mid = all_rows([values[0] for values in kept_mid])


    def expand_terms(grads):
        nonlocal hidden_rows, mixed_rows
        both, hidden_rows, mixed_rows = together(grads[-1], hidden_rows, mixed_rows)
        columns = swapped(after(incoming, both))
        return together(narrow(product_left(normed_mid, both)), columns)

    (expands, columns_out), grad_middles = backward_expand(incoming, slopes, incoming, rows, expand_terms)
    grads, sums = backward_attend(grad_middles)
    finals = [norm_backward(gain_in, grad_middles[m][0], inputs[m], *sums[m]) for m in every]
    gain_one, gain_two = (
        sum(jnp.sum(values[2], axis=0) for values in group) for group in (finals, grad_middles)
    )
    rows_out = jnp.stack([values[0] for values in finals])
    half = width // sections
    moved = shifted(narrow(rows_out[:, :, half:]), "section", 1).astype(F32)
    grad_tokens = jnp.where(section == 0, rows_out[:, :, :half], moved)

    def spread(value, axis):
        return lax.psum_scatter(value, "dp", scatter_dimension=axis, tiled=True)

    early = spread(expands, 0)
    normed = all_rows([values[0] for values in kept])
    grad_project = narrow(product_left(normed, all_rows([grad[0] for grad in grads])))
    grad_beta = product_left(normed, all_rows([grad[1] for grad in grads]))[:, :heads]
    grad_taps, grad_head_gain = (sum(grad[place] for grad in grads) for place in (2, 3))
    grad_head_gain = jnp.sum(grad_head_gain, axis=0)

    grad_project, early, middles_out = together(grad_project, early, [values[1] for values in grad_middles])
    grad_project, columns_mid = together(grad_project, swapped(middles_out))
    columns = [
        part.reshape(-1, part.shape[-1])
        for arrived in (columns_out, columns_mid)
        for part in jnp.concatenate(gather(arrived, order), axis=2)
    ]
    grad_contract = sum(product_left(left, right) for left, right in zip(hidden_rows, columns[:micro]))
    grad_merge = sum(product_left(left, right) for left, right in zip(mixed_rows, columns[micro:]))
    flat = jnp.concatenate([gain_one, gain_two, grad_head_gain])
    flat = summed(flat, ("dp", "head"))
    grad_gains, grad_head_gain = flat[: 2 * width].reshape(2, width), flat[2 * width :]
    flat = summed(jnp.concatenate([grad_taps.reshape(-1), grad_beta.reshape(-1)]), ("dp",))
    grad_taps, grad_beta = flat[: grad_taps.size].reshape(grad_taps.shape), flat[grad_taps.size :]
    rows = width // lax.axis_size("dp")
    grad_beta = lax.dynamic_slice_in_dim(grad_beta.reshape(width, heads), lax.axis_index("dp") * rows, rows, 0)
    units = mlp_in.shape[3]
    grad_expand = jnp.stack([part[:, :units] for part in jnp.split(early, 2, axis=1)]).astype(F32)
    grad_project = jnp.stack(jnp.split(spread(grad_project, 0), 3, axis=1)).astype(F32)
    return (
        grad_tokens,
        grad_project[None],
        grad_beta[None],
        grad_taps[None],
        grad_head_gain[None],
        grad_merge[None],
        grad_expand[None],
        grad_contract[None],
        grad_gains[None],
    )


def solution(mesh):
    return jax.shard_map(
        per_device,
        mesh=mesh,
        in_specs=(
            P("dp", None, None),
            P("dp", None),
            P("dp", None, None),
            P("section", None, None, "head"),
            P("section", None, "head"),
            P("section", None, None, "head"),
            P("section", None),
            P("section", "head", None),
            P("section", None, None, "head"),
            P("section", "head", None),
            P("section", None, None),
        ),
        out_specs=(
            P("dp", "head", "section"),
            P("section", None, "dp", "head"),
            P("section", "dp", "head"),
            P("section", None, None, "head"),
            P("section", None),
            P("section", "head", "dp"),
            P("section", None, "dp", "head"),
            P("section", "head", "dp"),
            P("section", None, None),
        ),
        check_vma=False,
    )
```

```python
import functools

import jax
import jax.numpy as jnp
from jax import lax
from jax.experimental import pallas as pl
from jax.experimental.pallas import tpu as pltpu
from jax.sharding import PartitionSpec as P

HEAD_DIM = 128
CONV = 4
TOK_MB = 384
BLOCK = 128
BLOCKS = TOK_MB // BLOCK
EPS = 1e-06
OUT_FLOOR = 0.0001
F32 = jnp.float32
BF16 = jnp.bfloat16
BASE = 4
LANES = 128
TILE = 256
QUARTERS = 4
ATTEND_KEPT = 9
ROW_COPIES = 16
KEEP_GRANT, PASS_GRANT, EXPAND_BACK_GRANT, ATTEND_BACK_GRANT = 50, 47, 50, 50


def mm(left, right):
    return lax.dot_general(
        left.astype(BF16), right.astype(BF16), (((1,), (0,)), ((), ())), preferred_element_type=F32
    )


def mm_t(left, right):
    return lax.dot_general(
        left.astype(BF16), right.astype(BF16), (((1,), (1,)), ((), ())), preferred_element_type=F32
    )


def t_mm(left, right):
    return lax.dot_general(
        left.astype(BF16), right.astype(BF16), (((0,), (0,)), ((), ())), preferred_element_type=F32
    )


def rows_of(b):
    return slice(b * BLOCK, (b + 1) * BLOCK)


def tiles_of(size, tile=TILE):
    return [slice(start, min(start + tile, size)) for start in range(0, size, tile)]


def quarters(size):
    return tiles_of(size, size // QUARTERS)


def relative_order(count):
    order, bit = [0], count // 2
    while bit:
        order = order + [k ^ bit for k in order]
        bit //= 2
    return order


def place_of(me_ref, difference, share):
    return pl.ds(pl.multiple_of((me_ref[0] ^ difference) * share, 16), share)


def stream(x, taps, masks):
    pre = taps[0:1] * x
    for tap in range(1, CONV):
        pre = pre + taps[tap : tap + 1] * (pltpu.roll(x, tap, 0) * masks[tap - 1])
    gate = jax.nn.sigmoid(pre)
    return pre, gate, pre * gate


def unit_inverses(systems):
    size = systems[0].shape[0]
    row = lax.broadcasted_iota(jnp.int32, (size, size), 0)
    col = lax.broadcasted_iota(jnp.int32, (size, size), 1)
    eye = (row == col).astype(F32)
    near = (row // BASE == col // BASE).astype(F32)
    first = [-a * near for a in systems]
    total = [eye + n for n in first]
    second = [mm(n, n) for n in first]
    third = [mm(n, s) for n, s in zip(first, second)]
    total = [t + s + r for t, s, r in zip(total, second, third)]
    step = BASE
    while step < size:
        span = 2 * step
        off = ((row // span == col // span) & (row // step != col // step)).astype(F32)
        inner = [mm(a * off, t) for a, t in zip(systems, total)]
        outer = [mm(t, i) for t, i in zip(total, inner)]
        total = [t - o for t, o in zip(total, outer)]
        step = span
    return total


def block_masks(seg_col_ref, seg_row_ref):
    row = lax.broadcasted_iota(jnp.int32, (BLOCK, BLOCK), 0)
    col = lax.broadcasted_iota(jnp.int32, (BLOCK, BLOCK), 1)
    strict, lower = {}, {}
    for b in range(BLOCKS):
        for c in range(b + 1):
            same = seg_col_ref[rows_of(b), :] == seg_row_ref[:, rows_of(c)]
            strict[b, c] = same & (col < row) if b == c else same
            lower[b, c] = same & (col <= row) if b == c else same
    return strict, lower


class Fetch:

    def __init__(self, pairs, sems, ahead):
        self.copies = [pltpu.make_async_copy(src, dst, sems.at[i]) for i, (src, dst) in enumerate(pairs)]
        self.ahead = ahead
        self.started = 0
        self.start_to(ahead)

    def start_to(self, place):
        while self.started < min(place, len(self.copies)):
            self.copies[self.started].start()
            self.started += 1

    def wait(self, place):
        self.copies[place].wait()
        self.start_to(place + 1 + self.ahead)

    def wait_group(self, group):
        for place in range(QUARTERS):
            self.wait(QUARTERS * group + place)


def load_rows(me_ref, shards, rows_ref, count, sems):
    share = TOK_MB // count
    if len(shards) == count:
        for k in range(count):
            rows_ref[k * share : (k + 1) * share, :] = shards[k][...]
        return
    copies = [
        pltpu.make_async_copy(
            shards[0].at[place_of(me_ref, difference, share), :],
            rows_ref.at[k * share : (k + 1) * share, :],
            sems.at[k],
        )
        for k, difference in enumerate(relative_order(count))
    ]
    for copy in copies:
        copy.start()
    for copy in copies:
        copy.wait()


class Push:

    def __init__(self, sems):
        self.sems = sems
        self.copies = []

    def start(self, source, target):
        copy = pltpu.make_async_copy(source, target, self.sems.at[len(self.copies)])
        copy.start()
        self.copies.append(copy)

    def wait(self):
        for copy in self.copies:
            copy.wait()


def attend_kernel(heads, count, save, held, me_ref, seg_col_ref, seg_row_ref, masks_ref, taps_ref, gain_ref, *refs):
    *refs, row_sems = refs
    shards, refs = refs[:held], refs[held:]
    project_hbm, beta_hbm, merge_hbm = refs[:3]
    partials, refs = refs[3 : 3 + count], refs[3 + count :]
    targets, refs = (refs[:ATTEND_KEPT], refs[ATTEND_KEPT:]) if save else ([], refs)
    kept_refs, refs = refs[:ATTEND_KEPT], refs[ATTEND_KEPT:]
    rows_ref, qkv_ref, logit_ref, mixed_ref, system_ref, attend_ref, inverse_ref, fresh_ref, out_ref = kept_refs
    mixed_abs, project_ref, beta_ref, merge_ref, sems, push_sems = refs
    push = Push(push_sems)

    def ready(*places):
        if save:
            for place in places:
                push.start(kept_refs[place], targets[place])

    order = relative_order(count)
    share = TOK_MB // count
    fetch = Fetch(
        [(project_hbm.at[0, j], project_ref.at[j]) for j in range(3)]
        + [(beta_hbm, beta_ref), (merge_hbm.at[0], merge_ref)],
        sems,
        5,
    )
    load_rows(me_ref, shards, rows_ref, count, row_sems)
    rows = rows_ref[...]
    ready(0)

    def spread(ref, value, *lead):
        for k, difference in enumerate(order):
            ref[(*lead, place_of(me_ref, difference, share), slice(None))] = value[k * share : (k + 1) * share]

    for j in range(3):
        fetch.wait(j)
        for cols in tiles_of(heads * HEAD_DIM):
            value = mm(rows, project_ref[j, :, cols])
            for k, difference in enumerate(order):
                qkv_ref[j, place_of(me_ref, difference, share), cols] = value[k * share : (k + 1) * share]
    fetch.wait(3)
    spread(logit_ref, mm(rows, beta_ref[...]))
    ready(1, 2)

    masks = [masks_ref[i] for i in range(CONV - 1)]
    strict, lower = block_masks(seg_col_ref, seg_row_ref)
    queries, keys, values, betas = [], [], [], []
    for h in range(heads):
        cols = slice(h * HEAD_DIM, (h + 1) * HEAD_DIM)
        taps = [taps_ref[0, j, :, cols] for j in range(3)]
        _, _, query = stream(qkv_ref[0, :, cols], taps[0], masks)
        _, _, key = stream(qkv_ref[1, :, cols], taps[1], masks)
        _, _, value = stream(qkv_ref[2, :, cols], taps[2], masks)
        query = query * lax.rsqrt(jnp.sum(query * query, axis=-1, keepdims=True) + EPS) * HEAD_DIM**-0.5
        key = key * lax.rsqrt(jnp.sum(key * key, axis=-1, keepdims=True) + EPS)
        beta = jax.nn.sigmoid(logit_ref[:, h : h + 1])
        queries.append(query.astype(BF16))
        keys.append(key.astype(BF16))
        values.append(value * beta)
        betas.append(beta)
    attend, system = {}, {}
    for h in range(heads):
        for b in range(BLOCKS):
            for c in range(b + 1):
                inner = mm_t(keys[h][rows_of(b)], keys[h][rows_of(c)])
                system[h, b, c] = jnp.where(strict[b, c], inner * betas[h][rows_of(b)], 0.0)
                scores = mm_t(queries[h][rows_of(b)], keys[h][rows_of(c)])
                attend[h, b, c] = jnp.where(lower[b, c], scores, 0.0).astype(BF16)
                if c < b:
                    system[h, b, c] = system[h, b, c].astype(BF16)
                if save:
                    attend_ref[h, rows_of(b), rows_of(c)] = attend[h, b, c]
                    if c < b:
                        system_ref[h, rows_of(b), rows_of(c)] = system[h, b, c]
    index = [(h, b) for h in range(heads) for b in range(BLOCKS)]
    inverse = dict(zip(index, unit_inverses([system[h, b, b] for h, b in index])))
    for h, b in index:
        inverse[h, b] = inverse[h, b].astype(BF16)
        if save:
            inverse_ref[h, b] = inverse[h, b]
    ready(4, 5, 6)
    fresh = {}
    for b in range(BLOCKS):
        for h in range(heads):
            target = values[h][rows_of(b)]
            for c in range(b):
                target = target - mm(system[h, b, c], fresh[h, c])
            fresh[h, b] = mm(inverse[h, b], target).astype(BF16)
            if save:
                fresh_ref[rows_of(b), h * HEAD_DIM : (h + 1) * HEAD_DIM] = fresh[h, b]
    for h in range(heads):
        cols = slice(h * HEAD_DIM, (h + 1) * HEAD_DIM)
        for b in range(BLOCKS):
            out = mm(attend[h, b, 0], fresh[h, 0])
            for c in range(1, b + 1):
                out = out + mm(attend[h, b, c], fresh[h, c])
            mean = jnp.mean(out * out, axis=-1, keepdims=True)
            if save:
                out_ref[rows_of(b), cols] = out
            mixed_abs[rows_of(b), cols] = (
                out * lax.rsqrt(jnp.maximum(mean, OUT_FLOOR)) * gain_ref[...]
            ).astype(BF16)
    for k, difference in enumerate(order):
        mixed_ref[k * share : (k + 1) * share, :] = mixed_abs[place_of(me_ref, difference, share), :]
    ready(3, 7, 8)
    fetch.wait(4)
    write_partials(partials, merge_ref.shape[1], share, lambda cols: mm(mixed_ref[...], merge_ref[:, cols]))
    push.wait()


def write_partials(partials, width, share, product):
    for cols in tiles_of(width):
        value = product(cols)
        for k, ref in enumerate(partials):
            ref[:, cols] = value[k * share : (k + 1) * share].astype(ref.dtype)


def partial_shapes(count, width):
    share = TOK_MB // count
    return [jax.ShapeDtypeStruct((share, width), F32 if k < count // 2 else BF16) for k in range(count)]


def call(kernel, operands, rows, hbm, out_shape, hbm_shape, scratch_shapes, grant, in_place=False):
    vmem = pl.BlockSpec(memory_space=pltpu.VMEM)
    far = pl.BlockSpec(memory_space=pltpu.HBM)
    blocks = isinstance(rows, list)
    rows = rows if blocks else [rows]
    return pl.pallas_call(
        functools.partial(kernel, len(rows)),
        in_specs=[pl.BlockSpec(memory_space=pltpu.SMEM)]
        + [vmem] * (len(operands) - 1)
        + [vmem if blocks else far] * len(rows)
        + [far] * len(hbm),
        out_specs=[vmem] * len(out_shape) + [far] * len(hbm_shape),
        out_shape=out_shape + hbm_shape,
        input_output_aliases=(
            {len(operands) + len(rows) + len(hbm) - 1: len(out_shape) + len(hbm_shape) - 1} if in_place else {}
        ),
        scratch_shapes=scratch_shapes + [pltpu.SemaphoreType.DMA((ROW_COPIES,))],
        compiler_params=pltpu.CompilerParams(vmem_limit_bytes=grant * 1024 * 1024),
        cost_estimate=pl.CostEstimate(flops=2 * 10**9, bytes_accessed=10**5, transcendentals=0),
    )(*operands, *rows, *hbm)


def as_scratch(shapes):
    return [pltpu.VMEM(shape.shape, shape.dtype) for shape in shapes]


def attend_forward(me, mine, count, rows, taps, gain, project, beta_weight, merge, save):
    masks, seg_col, seg_row = mine
    heads = merge.shape[1] // HEAD_DIM
    width = heads * HEAD_DIM
    model = merge.shape[2]
    kept = [
        jax.ShapeDtypeStruct((TOK_MB, model), BF16),
        jax.ShapeDtypeStruct((3, TOK_MB, width), F32),
        jax.ShapeDtypeStruct((TOK_MB, LANES), F32),
        jax.ShapeDtypeStruct((TOK_MB, width), BF16),
        jax.ShapeDtypeStruct((heads, TOK_MB, TOK_MB), BF16),
        jax.ShapeDtypeStruct((heads, TOK_MB, TOK_MB), BF16),
        jax.ShapeDtypeStruct((heads, BLOCKS, BLOCK, BLOCK), BF16),
        jax.ShapeDtypeStruct((TOK_MB, width), BF16),
        jax.ShapeDtypeStruct((TOK_MB, width), F32),
    ]
    results = call(
        functools.partial(attend_kernel, heads, count, save),
        (me, seg_col, seg_row, masks, taps, gain),
        rows,
        (project, beta_weight, merge),
        partial_shapes(count, model),
        kept if save else [],
        as_scratch(kept)
        + [
            pltpu.VMEM((TOK_MB, width), BF16),
            pltpu.VMEM(project.shape[1:], BF16),
            pltpu.VMEM(beta_weight.shape, BF16),
            pltpu.VMEM(merge.shape[1:], BF16),
            pltpu.SemaphoreType.DMA((5,)),
            pltpu.SemaphoreType.DMA((ATTEND_KEPT,)),
        ],
        KEEP_GRANT if save else PASS_GRANT,
    )
    return results[count:], results[:count]


def expand_kernel(count, save, held, me_ref, *refs):
    *refs, row_sems = refs
    shards, refs = refs[:held], refs[held:]
    share = TOK_MB // count
    if save:
        expand_hbm, *targets = refs[:5]
        rows_ref, hidden_ref, silu_ref, slope_ref, gate_ref, expand_ref, sems, push_sems = refs[5:]
        push = Push(push_sems)
        contract_copies = []
    else:
        expand_hbm, contract_hbm, *partials = refs[: 2 + count]
        rows_ref, hidden_ref, gate_ref, expand_ref, contract_ref, sems = refs[2 + count :]
        contract_copies = [(contract_hbm.at[0, s, :], contract_ref.at[s, :]) for s in quarters(contract_ref.shape[0])]
    tiles = tiles_of(hidden_ref.shape[1])
    fetch = Fetch(
        [(expand_hbm.at[0, j, s, :], expand_ref.at[j, s, :]) for j in range(2) for s in quarters(expand_ref.shape[1])]
        + contract_copies,
        sems,
        QUARTERS,
    )
    load_rows(me_ref, shards, rows_ref, count, row_sems)
    if save:
        push.start(rows_ref, targets[0])
    fetch.wait_group(0)
    for t in tiles:
        gate_ref[:, t] = mm(rows_ref[...], expand_ref[0, :, t])
    fetch.wait_group(1)
    for t in tiles:
        up_in = mm(rows_ref[...], expand_ref[1, :, t])
        gate_in = gate_ref[:, t]
        gate = jax.nn.sigmoid(gate_in)
        silu = gate_in * gate
        hidden_ref[:, t] = (silu * up_in).astype(BF16)
        if save:
            silu_ref[:, t] = silu.astype(BF16)
            slope_ref[:, t] = (up_in * gate * (1.0 + gate_in * (1.0 - gate))).astype(BF16)
    if save:
        for source, target in zip((hidden_ref, silu_ref, slope_ref), targets[1:]):
            push.start(source, target)
        push.wait()
    else:
        fetch.wait_group(2)
        write_partials(partials, rows_ref.shape[1], share, lambda cols: mm(hidden_ref[...], contract_ref[:, cols]))


def expand_forward(me, count, rows, expand, contract, save):
    model, units = expand.shape[2:]
    kept = [jax.ShapeDtypeStruct((TOK_MB, model), BF16)] + [jax.ShapeDtypeStruct((TOK_MB, units), BF16)] * 3
    results = call(
        functools.partial(expand_kernel, count, save),
        (me,),
        rows,
        (expand,) if save else (expand, contract),
        [] if save else partial_shapes(count, model),
        kept if save else [],
        as_scratch(kept if save else kept[:2])
        + [pltpu.VMEM((TOK_MB, units), F32), pltpu.VMEM(expand.shape[1:], BF16)]
        + ([] if save else [pltpu.VMEM(contract.shape[1:], BF16)])
        + [pltpu.SemaphoreType.DMA(((2 if save else 3) * QUARTERS,))]
        + ([pltpu.SemaphoreType.DMA((4,))] if save else []),
        KEEP_GRANT if save else PASS_GRANT,
    )
    return (results, None) if save else (None, results)


def padded(units):
    return -(-units // LANES) * LANES


def expand_back_kernel(count, into, held, me_ref, *refs):
    *refs, row_sems = refs
    shards, refs = refs[:held], refs[held:]
    silu_hbm, slope_hbm, expand_hbm, contract_hbm, *refs = refs
    if into:
        refs = refs[1:]
    partials, refs = refs[:count], refs[count:]
    both_hbm, rows_ref, silu_ref, slope_ref, both_ref, expand_ref, contract_ref, sems, push_sems = refs
    push = Push(push_sems)
    share = TOK_MB // count
    units = silu_ref.shape[1]
    second = padded(units)
    spans = tiles_of(rows_ref.shape[1], 2 * TILE)
    fetch = Fetch(
        [(contract_hbm.at[0, s, :], contract_ref.at[s, :]) for s in quarters(contract_ref.shape[0])]
        + [(slope_hbm, slope_ref), (silu_hbm, silu_ref)]
        + [(expand_hbm.at[0, j, s, :], expand_ref.at[j, s, :]) for s in spans for j in range(2)],
        sems,
        QUARTERS + 2,
    )
    load_rows(me_ref, shards, rows_ref, count, row_sems)
    if second > units:
        both_ref[...] = jnp.zeros(both_ref.shape, BF16)
    fetch.wait_group(0)
    fetch.wait(QUARTERS)
    fetch.wait(QUARTERS + 1)
    for t in tiles_of(units):
        grad_hidden = mm_t(rows_ref[...], contract_ref[t, :])
        both_ref[:, t] = (grad_hidden * slope_ref[:, t].astype(F32)).astype(BF16)
        both_ref[:, second + t.start : second + t.stop] = (
            grad_hidden * silu_ref[:, t].astype(F32)
        ).astype(BF16)
    push.start(both_ref, both_hbm.at[into * TOK_MB : (into + 1) * TOK_MB, :])
    for i, span in enumerate(spans):
        for j in range(2):
            fetch.wait(QUARTERS + 2 + 2 * i + j)
        for s in tiles_of(span.stop - span.start):
            s = slice(span.start + s.start, span.start + s.stop)
            value = mm_t(both_ref[:, :units], expand_ref[0, s, :])
            value = value + mm_t(both_ref[:, second : second + units], expand_ref[1, s, :])
            for k, ref in enumerate(partials):
                ref[:, s] = value[k * share : (k + 1) * share].astype(ref.dtype)
    push.wait()


def expand_backward(me, count, rows, silu, slope, expand, contract, into, micro, joint):
    model, units = expand.shape[2:]
    both = jax.ShapeDtypeStruct((TOK_MB, 2 * padded(units)), BF16)
    results = call(
        functools.partial(expand_back_kernel, count, into),
        (me,),
        rows,
        (silu, slope, expand, contract) + ((joint,) if into else ()),
        partial_shapes(count, model),
        [jax.ShapeDtypeStruct((micro * TOK_MB, both.shape[1]), BF16)],
        [pltpu.VMEM((TOK_MB, model), BF16)]
        + as_scratch([silu, slope, both])
        + [
            pltpu.VMEM(expand.shape[1:], BF16),
            pltpu.VMEM(contract.shape[1:], BF16),
            pltpu.SemaphoreType.DMA((QUARTERS + 2 + 2 * len(tiles_of(model, 2 * TILE)),)),
            pltpu.SemaphoreType.DMA((1,)),
        ],
        EXPAND_BACK_GRANT,
        into > 0,
    )
    return results[count], results[:count]


def stream_back(grad, x, pre, gate, taps, masks, taps_out, j, cols):
    grad_pre = grad * gate * (1.0 + pre * (1.0 - gate))
    grad_x = taps[0:1] * grad_pre
    taps_out[j, 0:1, cols] = jnp.sum(grad_pre * x, axis=0, keepdims=True)
    for tap in range(1, CONV):
        masked = grad_pre * masks[tap - 1]
        grad_x = grad_x + taps[tap : tap + 1] * pltpu.roll(masked, TOK_MB - tap, 0)
        taps_out[j, tap : tap + 1, cols] = jnp.sum(masked * pltpu.roll(x, tap, 0), axis=0, keepdims=True)
    return grad_x


def attend_back_kernel(heads, count, held, me_ref, seg_col_ref, seg_row_ref, masks_ref, taps_ref, gain_ref, *refs):
    *refs, row_sems = refs
    shards, refs = refs[:held], refs[held:]
    sources, refs = refs[: ATTEND_KEPT - 2], refs[ATTEND_KEPT - 2 :]
    project_hbm, beta_hbm, merge_hbm = refs[:3]
    partials, refs = refs[3 : 3 + count], refs[3 + count :]
    grad_taps_ref, grad_gain_ref, grad_qkv_hbm, grad_logit_hbm = refs[:4]
    kept_refs, refs = refs[4 : 2 + ATTEND_KEPT], refs[2 + ATTEND_KEPT :]
    qkv_ref, logit_ref, system_ref, attend_ref, inverse_ref, fresh_ref, out_ref = kept_refs
    rows_ref, grad_mixed_ref, grad_abs_ref, logit_abs_ref, grad_qkv_ref, grad_logit_ref, *refs = refs
    project_ref, beta_ref, merge_ref, sems, push_sems = refs
    push = Push(push_sems)
    order = relative_order(count)
    share = TOK_MB // count
    model = rows_ref.shape[1]
    width = heads * HEAD_DIM
    fetch = Fetch(
        [(merge_hbm.at[0], merge_ref)]
        + list(zip(sources, kept_refs))
        + [(beta_hbm, beta_ref)]
        + [(project_hbm.at[0, j], project_ref.at[j]) for j in range(3)],
        sems,
        ATTEND_KEPT,
    )
    load_rows(me_ref, shards, rows_ref, count, row_sems)
    fetch.wait(0)
    for cols in tiles_of(heads * HEAD_DIM):
        value = mm_t(rows_ref[...], merge_ref[cols, :])
        for k, difference in enumerate(order):
            grad_mixed_ref[place_of(me_ref, difference, share), cols] = value[k * share : (k + 1) * share]

    for place in range(1, ATTEND_KEPT - 1):
        fetch.wait(place)
    masks = [masks_ref[i] for i in range(CONV - 1)]
    strict, lower = block_masks(seg_col_ref, seg_row_ref)
    lane = lax.broadcasted_iota(jnp.int32, (TOK_MB, LANES), 1)
    everyone = range(heads)
    columns = [slice(h * HEAD_DIM, (h + 1) * HEAD_DIM) for h in everyone]
    grad_gain = jnp.zeros((8, HEAD_DIM), F32)
    grad_outs, queries, keys, values, betas, convs = [], [], [], [], [], []
    for h in everyone:
        cols = columns[h]
        taps = [taps_ref[0, j, :, cols] for j in range(3)]
        _, _, conv_q = stream(qkv_ref[0, :, cols], taps[0], masks)
        _, _, conv_k = stream(qkv_ref[1, :, cols], taps[1], masks)
        scale_q = lax.rsqrt(jnp.sum(conv_q * conv_q, axis=-1, keepdims=True) + EPS)
        scale_k = lax.rsqrt(jnp.sum(conv_k * conv_k, axis=-1, keepdims=True) + EPS)
        queries.append((conv_q * (scale_q * HEAD_DIM**-0.5)).astype(BF16))
        keys.append((conv_k * scale_k).astype(BF16))
        betas.append(jax.nn.sigmoid(logit_ref[:, h : h + 1]))
        out = out_ref[:, cols]
        grad_mixed = grad_mixed_ref[:, cols]
        mean = jnp.mean(out * out, axis=-1, keepdims=True)
        scale = lax.rsqrt(jnp.maximum(mean, OUT_FLOOR))
        unit = out * scale
        grad_gain = grad_gain + jnp.sum((grad_mixed * unit).reshape(TOK_MB // 8, 8, HEAD_DIM), axis=0)
        grad_unit = grad_mixed * gain_ref[...]
        through = jnp.where(mean > OUT_FLOOR, 1.0, jnp.where(mean == OUT_FLOOR, 0.5, 0.0))
        grad_out = scale * (
            grad_unit - unit * (through * jnp.mean(grad_unit * unit, axis=-1, keepdims=True))
        )
        grad_outs.append(grad_out.astype(BF16))
    grad_gain_ref[...] = grad_gain
    fresh = {(h, b): fresh_ref[rows_of(b), columns[h]] for h in everyone for b in range(BLOCKS)}
    d_out = {(h, b): grad_outs[h][rows_of(b)] for h in everyone for b in range(BLOCKS)}
    key_blocks = {(h, b): keys[h][rows_of(b)] for h in everyone for b in range(BLOCKS)}
    d_fresh, d_target, d_target_b = {}, {}, {}
    for c in range(BLOCKS):
        for h in everyone:
            total = t_mm(attend_ref[h, rows_of(c), rows_of(c)], d_out[h, c])
            for b in range(c + 1, BLOCKS):
                total = total + t_mm(attend_ref[h, rows_of(b), rows_of(c)], d_out[h, b])
            d_fresh[h, c] = total
    for b in reversed(range(BLOCKS)):
        for h in everyone:
            d_target[h, b] = t_mm(inverse_ref[h, b], d_fresh[h, b])
            d_target_b[h, b] = d_target[h, b].astype(BF16)
        for h in everyone:
            for c in range(b):
                d_fresh[h, c] = d_fresh[h, c] - t_mm(system_ref[h, rows_of(b), rows_of(c)], d_target_b[h, b])
    grad_query, inner, grad_key = {}, {}, {}
    for b in range(BLOCKS):
        for c in range(b + 1):
            for h in everyone:
                d_attend = jnp.where(lower[b, c], mm_t(d_out[h, b], fresh[h, c]), 0.0).astype(BF16)
                d_system = jnp.where(strict[b, c], -mm_t(d_target_b[h, b], fresh[h, c]), 0.0)
                for store, place, part in (
                    (grad_query, b, mm(d_attend, key_blocks[h, c])),
                    (inner, b, mm(d_system, key_blocks[h, c])),
                    (grad_key, c, t_mm(d_attend, queries[h][rows_of(b)])
                     + t_mm(d_system * betas[h][rows_of(b)], key_blocks[h, b])),
                ):
                    store[h, place] = store[h, place] + part if (h, place) in store else part

    def whole(store, h):
        return jnp.concatenate([store[h, b] for b in range(BLOCKS)], axis=0)

    grad_logits = jnp.zeros((TOK_MB, LANES), F32)
    for h in everyone:
        cols = columns[h]
        beta = betas[h]
        taps = [taps_ref[0, j, :, cols] for j in range(3)]
        inputs = [qkv_ref[j, :, cols] for j in range(3)]
        pre_q, gate_q, conv_q = stream(inputs[0], taps[0], masks)
        pre_k, gate_k, conv_k = stream(inputs[1], taps[1], masks)
        pre_v, gate_v, value = stream(inputs[2], taps[2], masks)
        scale_q = lax.rsqrt(jnp.sum(conv_q * conv_q, axis=-1, keepdims=True) + EPS)
        scale_k = lax.rsqrt(jnp.sum(conv_k * conv_k, axis=-1, keepdims=True) + EPS)
        unit_q, key = conv_q * scale_q, conv_k * scale_k
        within = whole(inner, h)
        target = whole(d_target, h)
        grad_q = whole(grad_query, h)
        grad_k = whole(grad_key, h) + beta * within
        grad_beta = jnp.sum(within * key + target * value, axis=-1, keepdims=True)
        grad_logits = jnp.where(lane == h, grad_beta * beta * (1.0 - beta), grad_logits)
        grad_conv_q = (HEAD_DIM**-0.5 * scale_q) * (
            grad_q - unit_q * jnp.sum(grad_q * unit_q, axis=-1, keepdims=True)
        )
        grad_conv_k = scale_k * (grad_k - key * jnp.sum(grad_k * key, axis=-1, keepdims=True))
        for j, (grad, pre, gate) in enumerate(
            ((grad_conv_q, pre_q, gate_q), (grad_conv_k, pre_k, gate_k), (beta * target, pre_v, gate_v))
        ):
            grad_x = stream_back(grad, inputs[j], pre, gate, taps[j], masks, grad_taps_ref, j, cols)
            grad_abs_ref[j, :, cols] = grad_x.astype(BF16)
    logit_abs_ref[...] = grad_logits.astype(BF16)
    for k, difference in enumerate(order):
        here = slice(k * share, (k + 1) * share)
        there = place_of(me_ref, difference, share)
        grad_logit_ref[here, :] = logit_abs_ref[there, :]
        for j in range(3):
            grad_qkv_ref[here, j * width : (j + 1) * width] = grad_abs_ref[j, there, :]
    push.start(grad_qkv_ref, grad_qkv_hbm)
    push.start(grad_logit_ref, grad_logit_hbm)
    for place in range(ATTEND_KEPT - 1, ATTEND_KEPT + 3):
        fetch.wait(place)
    for span in tiles_of(model):
        value = mm_t(grad_logit_ref[...], beta_ref[span, :])
        for j in range(3):
            value = value + mm_t(grad_qkv_ref[:, j * width : (j + 1) * width], project_ref[j, span, :])
        for k, ref in enumerate(partials):
            ref[:, span] = value[k * share : (k + 1) * share].astype(ref.dtype)
    push.wait()


def attend_backward(me, mine, count, rows, kept, taps, gain, project, beta_weight, merge):
    masks, seg_col, seg_row = mine
    heads = merge.shape[1] // HEAD_DIM
    width = heads * HEAD_DIM
    model = merge.shape[2]
    kept = kept[1:3] + kept[4:]
    grads = [jax.ShapeDtypeStruct((TOK_MB, 3 * width), BF16), jax.ShapeDtypeStruct((TOK_MB, LANES), BF16)]
    results = call(
        functools.partial(attend_back_kernel, heads, count),
        (me, seg_col, seg_row, masks, taps, gain),
        rows,
        (*kept, project, beta_weight, merge),
        partial_shapes(count, model)
        + [
            jax.ShapeDtypeStruct((3, CONV, width), F32),
            jax.ShapeDtypeStruct((8, HEAD_DIM), F32),
        ],
        grads,
        as_scratch(kept)
        + [
            pltpu.VMEM((TOK_MB, model), BF16),
            pltpu.VMEM((TOK_MB, width), F32),
            pltpu.VMEM((3, TOK_MB, width), BF16),
            pltpu.VMEM((TOK_MB, LANES), BF16),
        ]
        + as_scratch(grads)
        + [
            pltpu.VMEM(project.shape[1:], BF16),
            pltpu.VMEM(beta_weight.shape, BF16),
            pltpu.VMEM(merge.shape[1:], BF16),
            pltpu.SemaphoreType.DMA((ATTEND_KEPT + 3,)),
            pltpu.SemaphoreType.DMA((2,)),
        ],
        ATTEND_BACK_GRANT,
    )
    return results[count + 2 :] + results[count : count + 2], results[:count]


def small_call(kernel, operands, out_shape):
    vmem = pl.BlockSpec(memory_space=pltpu.VMEM)
    return pl.pallas_call(
        kernel,
        in_specs=[vmem] * len(operands),
        out_specs=[vmem] * len(out_shape),
        out_shape=out_shape,
        compiler_params=pltpu.CompilerParams(vmem_limit_bytes=16 * 1024 * 1024),
        cost_estimate=pl.CostEstimate(flops=10**9, bytes_accessed=10**5, transcendentals=0),
    )(*operands)


def total_of(refs):
    total = refs[0][...].astype(F32)
    for ref in refs[1:]:
        total = total + ref[...].astype(F32)
    return total


def norm_kernel(gain_ref, *refs):
    *terms, total_ref, normed_ref = refs
    total = total_of(terms)
    scale = lax.rsqrt(jnp.mean(total * total, axis=-1, keepdims=True) + EPS)
    total_ref[...] = total
    normed_ref[...] = (total * scale * gain_ref[...]).astype(BF16)


def norm_of_sum(gain, *terms):
    shape = terms[0].shape
    return small_call(
        norm_kernel, (gain, *terms), [jax.ShapeDtypeStruct(shape, F32), jax.ShapeDtypeStruct(shape, BF16)]
    )


def first_norm_kernel(m, me_ref, gain_ref, tokens_hbm, normed_ref, own_ref, rows_ref, sem):
    copy = pltpu.make_async_copy(tokens_hbm.at[m], rows_ref, sem)
    copy.start()
    copy.wait()
    share = own_ref.shape[0]
    own_ref[...] = rows_ref[place_of(me_ref, 0, share), :]
    for rows in tiles_of(TOK_MB, BLOCK):
        x = rows_ref[rows, :].astype(F32)
        scale = lax.rsqrt(jnp.mean(x * x, axis=-1, keepdims=True) + EPS)
        normed_ref[rows, :] = (x * scale * gain_ref[...]).astype(BF16)


def first_norm(me, gain, tokens, m, share):
    vmem = pl.BlockSpec(memory_space=pltpu.VMEM)
    width = tokens.shape[2]
    return pl.pallas_call(
        functools.partial(first_norm_kernel, m),
        in_specs=[pl.BlockSpec(memory_space=pltpu.SMEM), vmem, pl.BlockSpec(memory_space=pltpu.HBM)],
        out_specs=[vmem, vmem],
        out_shape=[jax.ShapeDtypeStruct((TOK_MB, width), BF16), jax.ShapeDtypeStruct((share, width), BF16)],
        scratch_shapes=[pltpu.VMEM((TOK_MB, width), BF16), pltpu.SemaphoreType.DMA],
        compiler_params=pltpu.CompilerParams(vmem_limit_bytes=16 * 1024 * 1024),
        cost_estimate=pl.CostEstimate(flops=10**9, bytes_accessed=10**5, transcendentals=0),
    )(me, gain, tokens)


def norm_back_kernel(gain_ref, base_ref, x_ref, *refs):
    *terms, grad_ref, narrow_ref, gain_out = refs
    grad_normed = total_of(terms)
    x = x_ref[...].astype(F32)
    scale = lax.rsqrt(jnp.mean(x * x, axis=-1, keepdims=True) + EPS)
    unit = x * scale
    grad_scaled = grad_normed * gain_ref[...]
    grad = base_ref[...].astype(F32) + scale * (
        grad_scaled - unit * jnp.mean(grad_scaled * unit, axis=-1, keepdims=True)
    )
    grad_ref[...] = grad
    narrow_ref[...] = grad.astype(BF16)
    rows, width = x.shape
    gain_out[...] = jnp.sum((grad_normed * unit).reshape(rows // 8, 8, width), axis=0)


def norm_backward(gain, base, x, *terms):
    shape = x.shape
    return small_call(
        norm_back_kernel,
        (gain, base, x, *terms),
        [
            jax.ShapeDtypeStruct(shape, F32),
            jax.ShapeDtypeStruct(shape, BF16),
            jax.ShapeDtypeStruct((8, shape[1]), F32),
        ],
    )


def tap_masks(segment):
    masks = []
    for tap in range(1, CONV):
        earlier = jnp.concatenate([jnp.full((tap,), -1, jnp.int32), segment[: TOK_MB - tap]], axis=0)
        masks.append(jnp.broadcast_to((earlier == segment).astype(F32)[:, None], (TOK_MB, HEAD_DIM)))
    return jnp.stack(masks)


def narrow(values):
    return values.astype(BF16)


def product(left, right):
    return jnp.dot(left, right, preferred_element_type=F32)


def product_left(left, right):
    return lax.dot_general(left, right, (((0,), (0,)), ((), ())), preferred_element_type=F32)


def product_right(left, right):
    return lax.dot_general(left, right, (((1,), (1,)), ((), ())), preferred_element_type=F32)


def segment_ids(lengths, count):
    ends = jnp.cumsum(lengths)
    places = jnp.arange(count, dtype=jnp.int32)
    return jnp.sum((places[:, None] >= ends[None, :]).astype(jnp.int32), axis=1, dtype=jnp.int32)


def flipped(values, axis, bit):
    return lax.ppermute(values, axis, [(i, i ^ bit) for i in range(lax.axis_size(axis))])


def shifted(values, axis, distance):
    devices = range(lax.axis_size(axis))
    return lax.ppermute(values, axis, [(i, i + distance) for i in devices if i + distance in devices])


def bits_of(axis):
    size = lax.axis_size(axis)
    bits = [1 << k for k in range(size.bit_length() - 1)]
    assert 1 << len(bits) == size
    return bits


def summed(values, axes):
    for axis in axes:
        for bit in bits_of(axis):
            values = values + flipped(values, axis, bit)
    return values


class Order:

    def __init__(self):
        self.last = None

    def flipped(self, values, bit):
        if bit > 1:
            if self.last is not None:
                values, _ = lax.optimization_barrier((values, self.last))
            self.last = flipped(values, "head", bit)
            return self.last
        return flipped(values, "head", bit)


def gather_far(shard, order):
    parts = [shard]
    for bit in reversed(bits_of("head")[1:]):
        parts = parts + [order.flipped(part, bit) for part in parts]
    return parts


def gather_near(parts):
    return parts + [flipped(part, "head", 1) for part in parts]


def gather(shard, order):
    return gather_near(gather_far(shard, order))


def total(terms):
    return sum(term.astype(F32) for term in terms)


def scatter_near(parts):
    half = len(parts) // 2
    return [[part, flipped(other, "head", 1)] for part, other in zip(parts[:half], parts[half:])]


def scatter_far(parts, order):
    for bit in bits_of("head")[1:]:
        half = len(parts) // 2
        arrived = [order.flipped(narrow(total(terms)), bit) for terms in parts[half:]]
        parts = [terms + [other] for terms, other in zip(parts[:half], arrived)]
    return parts[0]


def after(values, earlier):
    return lax.optimization_barrier((values, earlier))[0]


def together(*values):
    return lax.optimization_barrier(values)


def in_turn(kernel, order, shards=None, rows=None, finish=None):
    if rows is None:
        fars = [gather_far(shard, order) for shard in shards]
    kept, sums, near = [], [], None
    for m in range(len(rows or fars)):
        parts = gather_near(fars[m]) if rows is None else rows[m]
        if near is not None:
            half = len(near) // 2
            sent_on = [[total(terms)] for terms in near[half:]]
            parts, sent_on = together(parts, sent_on)
            near = near[:half] + sent_on
            sums.append(scatter_far(near, order))
        keep, partials = kernel(m, parts)
        if sums:
            partials = after(partials, sums[-1][-1])
        if rows is None and m + 1 < len(fars):
            fars[m + 1], keep, partials = together(fars[m + 1], keep, partials)
        kept.append(keep)
        if finish is not None and m + 1 == len(rows or fars):
            kept = finish(kept)
            partials = after(partials, kept)
        if partials is not None:
            near = scatter_near(partials)
    if near is not None:
        sums.append(scatter_far(near, order))
    return kept, sums


def in_order(sums, finish):
    results = []
    for m, (*terms, far) in enumerate(sums):
        if results:
            far, results[-1] = together(far, results[-1])
        results.append(finish(m, *terms, far))
    return results


def sent(distance, sums, finish):
    arrived = []
    for m, (*terms, far) in enumerate(sums):
        if arrived:
            far = after(far, arrived[-1])
        arrived.append(shifted(finish(m, *terms, far), "section", distance))
    return arrived


def swapped(shards):
    count = lax.axis_size("dp")
    me = lax.axis_index("dp")
    values = jnp.stack(shards)
    wide = values.shape[-1] // count
    arrived = []
    for distance in range(count):
        block = lax.dynamic_slice_in_dim(values, ((me + distance) % count) * wide, wide, 2)
        if distance:
            block = lax.ppermute(block, "dp", [(i, (i + distance) % count) for i in range(count)])
        arrived.append(block)
    arrived = jnp.stack(arrived)
    ordered = [lax.dynamic_index_in_dim(arrived, (me - q) % count, 0, keepdims=False) for q in range(count)]
    return jnp.stack(ordered, axis=1)


def per_device(
    tokens,
    lengths,
    cotangent,
    attn_in,
    beta_weight,
    conv_weight,
    o_gain,
    attn_out,
    mlp_in,
    mlp_out,
    norm_gains,
):
    section = lax.axis_index("section")
    sections = lax.axis_size("section")
    member = lax.axis_index("head")
    micro = tokens.shape[0]
    width = tokens.shape[2]
    heads = beta_weight.shape[2]
    share = TOK_MB // lax.axis_size("head")
    me = member[None]
    beta_wide = jnp.pad(beta_weight[0], ((0, 0), (0, LANES - heads)))
    gains = norm_gains[0]
    every = range(micro)
    segments = [segment_ids(lengths[m], TOK_MB) for m in every]
    masks = [(tap_masks(s), s[:, None], s[None, :]) for s in segments]
    order = Order()
    groups = lax.axis_size("head")
    cotangent_own = [
        lax.dynamic_slice(cotangent, (m, member * share, 0), (1, share, width))[0] for m in every
    ]
    gain_in, gain_mid = gains[0:1], gains[1:2]

    def forward_turn(inputs, save, shards=None, rows=None):
        kept, sums = in_turn(
            lambda m, rows: attend_forward(
                me, masks[m], groups, rows, conv_weight, o_gain, attn_in, beta_wide, attn_out, save
            ),
            order,
            shards,
            rows,
        )
        middles = in_order(sums, lambda m, *terms: norm_of_sum(gain_mid, inputs[m], *terms))
        kept_mid, sums = in_turn(
            lambda m, rows: expand_forward(me, groups, rows, mlp_in, mlp_out, save),
            order,
            [values[1] for values in middles],
        )
        if save:
            return kept, [values[0] for values in middles], kept_mid
        return sent(1, sums, lambda m, *terms: narrow(total([middles[m][0], *terms])))

    def backward_expand(incoming, slopes, shards=None, rows=None, finish=None):
        joint = [None]

        def kernel(m, rows):
            joint[0], partials = expand_backward(
                me, groups, rows, *slopes[m], mlp_in, mlp_out, m, micro, joint[0]
            )
            return joint[0], partials

        grads, sums = in_turn(kernel, order, shards, rows, finish)
        return grads, in_order(sums, lambda m, *terms: norm_backward(gain_mid, incoming[m], middles[m], *terms))

    def backward_attend(grad_middles):
        return in_turn(
            lambda m, rows: attend_backward(
                me, masks[m], groups, rows, kept[m], conv_weight, o_gain, attn_in, beta_wide, attn_out
            ),
            order,
            [values[1] for values in grad_middles],
        )

    def all_rows(values):
        return jnp.concatenate(values, axis=0)

    last = sections - 1
    normed, tokens_own = zip(*(first_norm(me, gain_in, tokens, m, share) for m in every))
    inputs, normed_own = tokens_own, None
    for turn in range(last):
        arrived = forward_turn(inputs, False, normed_own, normed)
        inputs = [jnp.where(section == 0, tokens_own[m], arrived[m]) for m in every]
        normed_own = [norm_of_sum(gain_in, value)[1] for value in inputs]
        normed = None
    kept, middles, kept_mid = forward_turn(inputs, True, normed_own, normed)

    hidden_rows = [lax.all_gather(values[1], "dp", axis=0, tiled=True) for values in kept_mid]
    mixed_rows = [lax.all_gather(values[3], "dp", axis=0, tiled=True) for values in kept]

    slopes = [values[2:] for values in kept_mid]
    incoming = cotangent_own
    rows = [cotangent[m] for m in every]
    for turn in range(last):
        _, grad_middles = backward_expand(incoming, slopes, incoming, rows)
        _, sums = backward_attend(grad_middles)
        arrived = sent(
            -1, sums, lambda m, *terms: norm_backward(gain_in, grad_middles[m][0], inputs[m], *terms)[1]
        )
        incoming = [jnp.where(section == last, cotangent_own[m], arrived[m]) for m in every]
        rows = None
    normed_mid = all_rows([values[0] for values in kept_mid])


    def expand_terms(grads):
        nonlocal hidden_rows, mixed_rows
        both, hidden_rows, mixed_rows = together(grads[-1], hidden_rows, mixed_rows)
        columns = swapped(after(incoming, both))
        return together(narrow(product_left(normed_mid, both)), columns)

    (expands, columns_out), grad_middles = backward_expand(incoming, slopes, incoming, rows, expand_terms)
    grads, sums = backward_attend(grad_middles)
    finals = [norm_backward(gain_in, grad_middles[m][0], inputs[m], *sums[m]) for m in every]
    gain_one, gain_two = (
        sum(jnp.sum(values[2], axis=0) for values in group) for group in (finals, grad_middles)
    )
    rows_out = jnp.stack([values[0] for values in finals])
    half = width // sections
    moved = shifted(narrow(rows_out[:, :, half:]), "section", 1).astype(F32)
    grad_tokens = jnp.where(section == 0, rows_out[:, :, :half], moved)

    def spread(value, axis):
        return lax.psum_scatter(value, "dp", scatter_dimension=axis, tiled=True)

    early = spread(expands, 0)
    normed = all_rows([values[0] for values in kept])
    grad_project = narrow(product_left(normed, all_rows([grad[0] for grad in grads])))
    grad_beta = product_left(normed, all_rows([grad[1] for grad in grads]))[:, :heads]
    grad_taps, grad_head_gain = (sum(grad[place] for grad in grads) for place in (2, 3))
    grad_head_gain = jnp.sum(grad_head_gain, axis=0)

    grad_project, early, middles_out = together(grad_project, early, [values[1] for values in grad_middles])
    grad_project, columns_mid = together(grad_project, swapped(middles_out))
    columns = [
        part.reshape(-1, part.shape[-1])
        for arrived in (columns_out, columns_mid)
        for part in jnp.concatenate(gather(arrived, order), axis=2)
    ]
    grad_contract = sum(product_left(left, right) for left, right in zip(hidden_rows, columns[:micro]))
    grad_merge = sum(product_left(left, right) for left, right in zip(mixed_rows, columns[micro:]))
    flat = jnp.concatenate([gain_one, gain_two, grad_head_gain])
    flat = summed(flat, ("dp", "head"))
    grad_gains, grad_head_gain = flat[: 2 * width].reshape(2, width), flat[2 * width :]
    flat = summed(jnp.concatenate([grad_taps.reshape(-1), grad_beta.reshape(-1)]), ("dp",))
    grad_taps, grad_beta = flat[: grad_taps.size].reshape(grad_taps.shape), flat[grad_taps.size :]
    rows = width // lax.axis_size("dp")
    grad_beta = lax.dynamic_slice_in_dim(grad_beta.reshape(width, heads), lax.axis_index("dp") * rows, rows, 0)
    units = mlp_in.shape[3]
    grad_expand = jnp.stack([part[:, :units] for part in jnp.split(early, 2, axis=1)]).astype(F32)
    grad_project = jnp.stack(jnp.split(spread(grad_project, 0), 3, axis=1)).astype(F32)
    return (
        grad_tokens,
        grad_project[None],
        grad_beta[None],
        grad_taps[None],
        grad_head_gain[None],
        grad_merge[None],
        grad_expand[None],
        grad_contract[None],
        grad_gains[None],
    )


def solution(mesh):
    return jax.shard_map(
        per_device,
        mesh=mesh,
        in_specs=(
            P("dp", None, None),
            P("dp", None),
            P("dp", None, None),
            P("section", None, None, "head"),
            P("section", None, "head"),
            P("section", None, None, "head"),
            P("section", None),
            P("section", "head", None),
            P("section", None, None, "head"),
            P("section", "head", None),
            P("section", None, None),
        ),
        out_specs=(
            P("dp", "head", "section"),
            P("section", None, "dp", "head"),
            P("section", "dp", "head"),
            P("section", None, None, "head"),
            P("section", None),
            P("section", "head", "dp"),
            P("section", None, "dp", "head"),
            P("section", "head", "dp"),
            P("section", None, None),
        ),
        check_vma=False,
    )
```

```python
import functools

import jax
import jax.numpy as jnp
from jax import lax
from jax.experimental import pallas as pl
from jax.experimental.pallas import tpu as pltpu
from jax.sharding import PartitionSpec as P

HEAD_DIM = 128
CONV = 4
TOK_MB = 384
BLOCK = 128
BLOCKS = TOK_MB // BLOCK
EPS = 1e-06
OUT_FLOOR = 0.0001
F32 = jnp.float32
BF16 = jnp.bfloat16
BASE = 4
LANES = 128
TILE = 256
QUARTERS = 4
ATTEND_KEPT = 9
ROW_COPIES = 16
KEEP_GRANT, PASS_GRANT, EXPAND_BACK_GRANT, ATTEND_BACK_GRANT = 50, 47, 50, 50


def mm(left, right):
    return lax.dot_general(
        left.astype(BF16), right.astype(BF16), (((1,), (0,)), ((), ())), preferred_element_type=F32
    )


def mm_t(left, right):
    return lax.dot_general(
        left.astype(BF16), right.astype(BF16), (((1,), (1,)), ((), ())), preferred_element_type=F32
    )


def t_mm(left, right):
    return lax.dot_general(
        left.astype(BF16), right.astype(BF16), (((0,), (0,)), ((), ())), preferred_element_type=F32
    )


def rows_of(b):
    return slice(b * BLOCK, (b + 1) * BLOCK)


def tiles_of(size, tile=TILE):
    return [slice(start, min(start + tile, size)) for start in range(0, size, tile)]


def quarters(size):
    return tiles_of(size, size // QUARTERS)


def relative_order(count):
    order, bit = [0], count // 2
    while bit:
        order = order + [k ^ bit for k in order]
        bit //= 2
    return order


def place_of(me_ref, difference, share):
    return pl.ds(pl.multiple_of((me_ref[0] ^ difference) * share, 16), share)


def stream(x, taps, masks):
    pre = taps[0:1] * x
    for tap in range(1, CONV):
        pre = pre + taps[tap : tap + 1] * (pltpu.roll(x, tap, 0) * masks[tap - 1])
    gate = jax.nn.sigmoid(pre)
    return pre, gate, pre * gate


def unit_inverses(systems):
    size = systems[0].shape[0]
    row = lax.broadcasted_iota(jnp.int32, (size, size), 0)
    col = lax.broadcasted_iota(jnp.int32, (size, size), 1)
    eye = (row == col).astype(F32)
    near = (row // BASE == col // BASE).astype(F32)
    first = [-a * near for a in systems]
    total = [eye + n for n in first]
    second = [mm(n, n) for n in first]
    third = [mm(n, s) for n, s in zip(first, second)]
    total = [t + s + r for t, s, r in zip(total, second, third)]
    step = BASE
    while step < size:
        span = 2 * step
        off = ((row // span == col // span) & (row // step != col // step)).astype(F32)
        inner = [mm(a * off, t) for a, t in zip(systems, total)]
        outer = [mm(t, i) for t, i in zip(total, inner)]
        total = [t - o for t, o in zip(total, outer)]
        step = span
    return total


def block_masks(seg_col_ref, seg_row_ref):
    row = lax.broadcasted_iota(jnp.int32, (BLOCK, BLOCK), 0)
    col = lax.broadcasted_iota(jnp.int32, (BLOCK, BLOCK), 1)
    strict, lower = {}, {}
    for b in range(BLOCKS):
        for c in range(b + 1):
            same = seg_col_ref[rows_of(b), :] == seg_row_ref[:, rows_of(c)]
            strict[b, c] = same & (col < row) if b == c else same
            lower[b, c] = same & (col <= row) if b == c else same
    return strict, lower


class Fetch:

    def __init__(self, pairs, sems, ahead):
        self.copies = [pltpu.make_async_copy(src, dst, sems.at[i]) for i, (src, dst) in enumerate(pairs)]
        self.ahead = ahead
        self.started = 0
        self.start_to(ahead)

    def start_to(self, place):
        while self.started < min(place, len(self.copies)):
            self.copies[self.started].start()
            self.started += 1

    def wait(self, place):
        self.copies[place].wait()
        self.start_to(place + 1 + self.ahead)

    def wait_group(self, group):
        for place in range(QUARTERS):
            self.wait(QUARTERS * group + place)


def load_rows(me_ref, shards, rows_ref, count, sems):
    share = TOK_MB // count
    if len(shards) == count:
        for k in range(count):
            rows_ref[k * share : (k + 1) * share, :] = shards[k][...]
        return
    copies = [
        pltpu.make_async_copy(
            shards[0].at[place_of(me_ref, difference, share), :],
            rows_ref.at[k * share : (k + 1) * share, :],
            sems.at[k],
        )
        for k, difference in enumerate(relative_order(count))
    ]
    for copy in copies:
        copy.start()
    for copy in copies:
        copy.wait()


class Push:

    def __init__(self, sems):
        self.sems = sems
        self.copies = []

    def start(self, source, target):
        copy = pltpu.make_async_copy(source, target, self.sems.at[len(self.copies)])
        copy.start()
        self.copies.append(copy)

    def wait(self):
        for copy in self.copies:
            copy.wait()


def attend_kernel(heads, count, save, held, me_ref, seg_col_ref, seg_row_ref, masks_ref, taps_ref, gain_ref, *refs):
    *refs, row_sems = refs
    shards, refs = refs[:held], refs[held:]
    project_hbm, beta_hbm, merge_hbm = refs[:3]
    partials, refs = refs[3 : 3 + count], refs[3 + count :]
    targets, refs = (refs[:ATTEND_KEPT], refs[ATTEND_KEPT:]) if save else ([], refs)
    kept_refs, refs = refs[:ATTEND_KEPT], refs[ATTEND_KEPT:]
    rows_ref, qkv_ref, logit_ref, mixed_ref, system_ref, attend_ref, inverse_ref, fresh_ref, out_ref = kept_refs
    mixed_abs, project_ref, beta_ref, merge_ref, sems, push_sems = refs
    push = Push(push_sems)

    def ready(*places):
        if save:
            for place in places:
                push.start(kept_refs[place], targets[place])

    order = relative_order(count)
    share = TOK_MB // count
    fetch = Fetch(
        [(project_hbm.at[0, j], project_ref.at[j]) for j in range(3)]
        + [(beta_hbm, beta_ref), (merge_hbm.at[0], merge_ref)],
        sems,
        5,
    )
    load_rows(me_ref, shards, rows_ref, count, row_sems)
    rows = rows_ref[...]
    ready(0)

    def spread(ref, value, *lead):
        for k, difference in enumerate(order):
            ref[(*lead, place_of(me_ref, difference, share), slice(None))] = value[k * share : (k + 1) * share]

    for j in range(3):
        fetch.wait(j)
        for cols in tiles_of(heads * HEAD_DIM):
            value = mm(rows, project_ref[j, :, cols])
            for k, difference in enumerate(order):
                qkv_ref[j, place_of(me_ref, difference, share), cols] = value[k * share : (k + 1) * share]
    fetch.wait(3)
    spread(logit_ref, mm(rows, beta_ref[...]))
    ready(1, 2)

    masks = [masks_ref[i] for i in range(CONV - 1)]
    strict, lower = block_masks(seg_col_ref, seg_row_ref)
    queries, keys, values, betas = [], [], [], []
    for h in range(heads):
        cols = slice(h * HEAD_DIM, (h + 1) * HEAD_DIM)
        taps = [taps_ref[0, j, :, cols] for j in range(3)]
        _, _, query = stream(qkv_ref[0, :, cols], taps[0], masks)
        _, _, key = stream(qkv_ref[1, :, cols], taps[1], masks)
        _, _, value = stream(qkv_ref[2, :, cols], taps[2], masks)
        query = query * lax.rsqrt(jnp.sum(query * query, axis=-1, keepdims=True) + EPS) * HEAD_DIM**-0.5
        key = key * lax.rsqrt(jnp.sum(key * key, axis=-1, keepdims=True) + EPS)
        beta = jax.nn.sigmoid(logit_ref[:, h : h + 1])
        queries.append(query.astype(BF16))
        keys.append(key.astype(BF16))
        values.append(value * beta)
        betas.append(beta)
    attend, system = {}, {}
    for h in range(heads):
        for b in range(BLOCKS):
            for c in range(b + 1):
                inner = mm_t(keys[h][rows_of(b)], keys[h][rows_of(c)])
                system[h, b, c] = jnp.where(strict[b, c], inner * betas[h][rows_of(b)], 0.0)
                scores = mm_t(queries[h][rows_of(b)], keys[h][rows_of(c)])
                attend[h, b, c] = jnp.where(lower[b, c], scores, 0.0).astype(BF16)
                if c < b:
                    system[h, b, c] = system[h, b, c].astype(BF16)
                if save:
                    attend_ref[h, rows_of(b), rows_of(c)] = attend[h, b, c]
                    if c < b:
                        system_ref[h, rows_of(b), rows_of(c)] = system[h, b, c]
    index = [(h, b) for h in range(heads) for b in range(BLOCKS)]
    inverse = dict(zip(index, unit_inverses([system[h, b, b] for h, b in index])))
    for h, b in index:
        inverse[h, b] = inverse[h, b].astype(BF16)
        if save:
            inverse_ref[h, b] = inverse[h, b]
    ready(4, 5, 6)
    fresh = {}
    for b in range(BLOCKS):
        for h in range(heads):
            target = values[h][rows_of(b)]
            for c in range(b):
                target = target - mm(system[h, b, c], fresh[h, c])
            fresh[h, b] = mm(inverse[h, b], target).astype(BF16)
            if save:
                fresh_ref[rows_of(b), h * HEAD_DIM : (h + 1) * HEAD_DIM] = fresh[h, b]
    for h in range(heads):
        cols = slice(h * HEAD_DIM, (h + 1) * HEAD_DIM)
        for b in range(BLOCKS):
            out = mm(attend[h, b, 0], fresh[h, 0])
            for c in range(1, b + 1):
                out = out + mm(attend[h, b, c], fresh[h, c])
            mean = jnp.mean(out * out, axis=-1, keepdims=True)
            if save:
                out_ref[rows_of(b), cols] = out
            mixed_abs[rows_of(b), cols] = (
                out * lax.rsqrt(jnp.maximum(mean, OUT_FLOOR)) * gain_ref[...]
            ).astype(BF16)
    for k, difference in enumerate(order):
        mixed_ref[k * share : (k + 1) * share, :] = mixed_abs[place_of(me_ref, difference, share), :]
    ready(3, 7, 8)
    fetch.wait(4)
    write_partials(partials, merge_ref.shape[1], share, lambda cols: mm(mixed_ref[...], merge_ref[:, cols]))
    push.wait()


def write_partials(partials, width, share, product):
    for cols in tiles_of(width):
        value = product(cols)
        for k, ref in enumerate(partials):
            ref[:, cols] = value[k * share : (k + 1) * share].astype(ref.dtype)


def partial_shapes(count, width):
    share = TOK_MB // count
    return [jax.ShapeDtypeStruct((share, width), F32 if k < count // 2 else BF16) for k in range(count)]


def call(kernel, operands, rows, hbm, out_shape, hbm_shape, scratch_shapes, grant, in_place=False):
    vmem = pl.BlockSpec(memory_space=pltpu.VMEM)
    far = pl.BlockSpec(memory_space=pltpu.HBM)
    blocks = isinstance(rows, list)
    rows = rows if blocks else [rows]
    return pl.pallas_call(
        functools.partial(kernel, len(rows)),
        in_specs=[pl.BlockSpec(memory_space=pltpu.SMEM)]
        + [vmem] * (len(operands) - 1)
        + [vmem if blocks else far] * len(rows)
        + [far] * len(hbm),
        out_specs=[vmem] * len(out_shape) + [far] * len(hbm_shape),
        out_shape=out_shape + hbm_shape,
        input_output_aliases=(
            {len(operands) + len(rows) + len(hbm) - 1: len(out_shape) + len(hbm_shape) - 1} if in_place else {}
        ),
        scratch_shapes=scratch_shapes + [pltpu.SemaphoreType.DMA((ROW_COPIES,))],
        compiler_params=pltpu.CompilerParams(vmem_limit_bytes=grant * 1024 * 1024),
        cost_estimate=pl.CostEstimate(flops=2 * 10**9, bytes_accessed=10**5, transcendentals=0),
    )(*operands, *rows, *hbm)


def as_scratch(shapes):
    return [pltpu.VMEM(shape.shape, shape.dtype) for shape in shapes]


def attend_forward(me, mine, count, rows, taps, gain, project, beta_weight, merge, save):
    masks, seg_col, seg_row = mine
    heads = merge.shape[1] // HEAD_DIM
    width = heads * HEAD_DIM
    model = merge.shape[2]
    kept = [
        jax.ShapeDtypeStruct((TOK_MB, model), BF16),
        jax.ShapeDtypeStruct((3, TOK_MB, width), F32),
        jax.ShapeDtypeStruct((TOK_MB, LANES), F32),
        jax.ShapeDtypeStruct((TOK_MB, width), BF16),
        jax.ShapeDtypeStruct((heads, TOK_MB, TOK_MB), BF16),
        jax.ShapeDtypeStruct((heads, TOK_MB, TOK_MB), BF16),
        jax.ShapeDtypeStruct((heads, BLOCKS, BLOCK, BLOCK), BF16),
        jax.ShapeDtypeStruct((TOK_MB, width), BF16),
        jax.ShapeDtypeStruct((TOK_MB, width), F32),
    ]
    results = call(
        functools.partial(attend_kernel, heads, count, save),
        (me, seg_col, seg_row, masks, taps, gain),
        rows,
        (project, beta_weight, merge),
        partial_shapes(count, model),
        kept if save else [],
        as_scratch(kept)
        + [
            pltpu.VMEM((TOK_MB, width), BF16),
            pltpu.VMEM(project.shape[1:], BF16),
            pltpu.VMEM(beta_weight.shape, BF16),
            pltpu.VMEM(merge.shape[1:], BF16),
            pltpu.SemaphoreType.DMA((5,)),
            pltpu.SemaphoreType.DMA((ATTEND_KEPT,)),
        ],
        KEEP_GRANT if save else PASS_GRANT,
    )
    return results[count:], results[:count]


def expand_kernel(count, save, held, me_ref, *refs):
    *refs, row_sems = refs
    shards, refs = refs[:held], refs[held:]
    share = TOK_MB // count
    if save:
        expand_hbm, *targets = refs[:5]
        rows_ref, hidden_ref, silu_ref, slope_ref, gate_ref, expand_ref, sems, push_sems = refs[5:]
        push = Push(push_sems)
        contract_copies = []
    else:
        expand_hbm, contract_hbm, *partials = refs[: 2 + count]
        rows_ref, hidden_ref, gate_ref, expand_ref, contract_ref, sems = refs[2 + count :]
        contract_copies = [(contract_hbm.at[0, s, :], contract_ref.at[s, :]) for s in quarters(contract_ref.shape[0])]
    tiles = tiles_of(hidden_ref.shape[1])
    fetch = Fetch(
        [(expand_hbm.at[0, j, s, :], expand_ref.at[j, s, :]) for j in range(2) for s in quarters(expand_ref.shape[1])]
        + contract_copies,
        sems,
        QUARTERS,
    )
    load_rows(me_ref, shards, rows_ref, count, row_sems)
    if save:
        push.start(rows_ref, targets[0])
    fetch.wait_group(0)
    for t in tiles:
        gate_ref[:, t] = mm(rows_ref[...], expand_ref[0, :, t])
    fetch.wait_group(1)
    for t in tiles:
        up_in = mm(rows_ref[...], expand_ref[1, :, t])
        gate_in = gate_ref[:, t]
        gate = jax.nn.sigmoid(gate_in)
        silu = gate_in * gate
        hidden_ref[:, t] = (silu * up_in).astype(BF16)
        if save:
            silu_ref[:, t] = silu.astype(BF16)
            slope_ref[:, t] = (up_in * gate * (1.0 + gate_in * (1.0 - gate))).astype(BF16)
    if save:
        for source, target in zip((hidden_ref, silu_ref, slope_ref), targets[1:]):
            push.start(source, target)
        push.wait()
    else:
        fetch.wait_group(2)
        write_partials(partials, rows_ref.shape[1], share, lambda cols: mm(hidden_ref[...], contract_ref[:, cols]))


def expand_forward(me, count, rows, expand, contract, save):
    model, units = expand.shape[2:]
    kept = [jax.ShapeDtypeStruct((TOK_MB, model), BF16)] + [jax.ShapeDtypeStruct((TOK_MB, units), BF16)] * 3
    results = call(
        functools.partial(expand_kernel, count, save),
        (me,),
        rows,
        (expand,) if save else (expand, contract),
        [] if save else partial_shapes(count, model),
        kept if save else [],
        as_scratch(kept if save else kept[:2])
        + [pltpu.VMEM((TOK_MB, units), F32), pltpu.VMEM(expand.shape[1:], BF16)]
        + ([] if save else [pltpu.VMEM(contract.shape[1:], BF16)])
        + [pltpu.SemaphoreType.DMA(((2 if save else 3) * QUARTERS,))]
        + ([pltpu.SemaphoreType.DMA((4,))] if save else []),
        KEEP_GRANT if save else PASS_GRANT,
    )
    return (results, None) if save else (None, results)


def padded(units):
    return -(-units // LANES) * LANES


def expand_back_kernel(count, into, held, me_ref, *refs):
    *refs, row_sems = refs
    shards, refs = refs[:held], refs[held:]
    silu_hbm, slope_hbm, expand_hbm, contract_hbm, *refs = refs
    if into:
        refs = refs[1:]
    partials, refs = refs[:count], refs[count:]
    both_hbm, rows_ref, silu_ref, slope_ref, both_ref, expand_ref, contract_ref, sems, push_sems = refs
    push = Push(push_sems)
    share = TOK_MB // count
    units = silu_ref.shape[1]
    second = padded(units)
    spans = tiles_of(rows_ref.shape[1], 2 * TILE)
    fetch = Fetch(
        [(contract_hbm.at[0, s, :], contract_ref.at[s, :]) for s in quarters(contract_ref.shape[0])]
        + [(slope_hbm, slope_ref), (silu_hbm, silu_ref)]
        + [(expand_hbm.at[0, j, s, :], expand_ref.at[j, s, :]) for s in spans for j in range(2)],
        sems,
        QUARTERS + 2,
    )
    load_rows(me_ref, shards, rows_ref, count, row_sems)
    if second > units:
        both_ref[...] = jnp.zeros(both_ref.shape, BF16)
    fetch.wait_group(0)
    fetch.wait(QUARTERS)
    fetch.wait(QUARTERS + 1)
    for t in tiles_of(units):
        grad_hidden = mm_t(rows_ref[...], contract_ref[t, :])
        both_ref[:, t] = (grad_hidden * slope_ref[:, t].astype(F32)).astype(BF16)
        both_ref[:, second + t.start : second + t.stop] = (
            grad_hidden * silu_ref[:, t].astype(F32)
        ).astype(BF16)
    push.start(both_ref, both_hbm.at[into * TOK_MB : (into + 1) * TOK_MB, :])
    for i, span in enumerate(spans):
        for j in range(2):
            fetch.wait(QUARTERS + 2 + 2 * i + j)
        for s in tiles_of(span.stop - span.start):
            s = slice(span.start + s.start, span.start + s.stop)
            value = mm_t(both_ref[:, :units], expand_ref[0, s, :])
            value = value + mm_t(both_ref[:, second : second + units], expand_ref[1, s, :])
            for k, ref in enumerate(partials):
                ref[:, s] = value[k * share : (k + 1) * share].astype(ref.dtype)
    push.wait()


def expand_backward(me, count, rows, silu, slope, expand, contract, into, micro, joint):
    model, units = expand.shape[2:]
    both = jax.ShapeDtypeStruct((TOK_MB, 2 * padded(units)), BF16)
    results = call(
        functools.partial(expand_back_kernel, count, into),
        (me,),
        rows,
        (silu, slope, expand, contract) + ((joint,) if into else ()),
        partial_shapes(count, model),
        [jax.ShapeDtypeStruct((micro * TOK_MB, both.shape[1]), BF16)],
        [pltpu.VMEM((TOK_MB, model), BF16)]
        + as_scratch([silu, slope, both])
        + [
            pltpu.VMEM(expand.shape[1:], BF16),
            pltpu.VMEM(contract.shape[1:], BF16),
            pltpu.SemaphoreType.DMA((QUARTERS + 2 + 2 * len(tiles_of(model, 2 * TILE)),)),
            pltpu.SemaphoreType.DMA((1,)),
        ],
        EXPAND_BACK_GRANT,
        into > 0,
    )
    return results[count], results[:count]


def stream_back(grad, x, pre, gate, taps, masks, taps_out, j, cols):
    grad_pre = grad * gate * (1.0 + pre * (1.0 - gate))
    grad_x = taps[0:1] * grad_pre
    taps_out[j, 0:1, cols] = jnp.sum(grad_pre * x, axis=0, keepdims=True)
    for tap in range(1, CONV):
        masked = grad_pre * masks[tap - 1]
        grad_x = grad_x + taps[tap : tap + 1] * pltpu.roll(masked, TOK_MB - tap, 0)
        taps_out[j, tap : tap + 1, cols] = jnp.sum(masked * pltpu.roll(x, tap, 0), axis=0, keepdims=True)
    return grad_x


def attend_back_kernel(heads, count, held, me_ref, seg_col_ref, seg_row_ref, masks_ref, taps_ref, gain_ref, *refs):
    *refs, row_sems = refs
    shards, refs = refs[:held], refs[held:]
    sources, refs = refs[: ATTEND_KEPT - 2], refs[ATTEND_KEPT - 2 :]
    project_hbm, beta_hbm, merge_hbm = refs[:3]
    partials, refs = refs[3 : 3 + count], refs[3 + count :]
    grad_taps_ref, grad_gain_ref, grad_qkv_hbm, grad_logit_hbm = refs[:4]
    kept_refs, refs = refs[4 : 2 + ATTEND_KEPT], refs[2 + ATTEND_KEPT :]
    qkv_ref, logit_ref, system_ref, attend_ref, inverse_ref, fresh_ref, out_ref = kept_refs
    rows_ref, grad_mixed_ref, grad_abs_ref, logit_abs_ref, grad_qkv_ref, grad_logit_ref, *refs = refs
    project_ref, beta_ref, merge_ref, sems, push_sems = refs
    push = Push(push_sems)
    order = relative_order(count)
    share = TOK_MB // count
    model = rows_ref.shape[1]
    width = heads * HEAD_DIM
    fetch = Fetch(
        [(merge_hbm.at[0], merge_ref)]
        + list(zip(sources, kept_refs))
        + [(beta_hbm, beta_ref)]
        + [(project_hbm.at[0, j], project_ref.at[j]) for j in range(3)],
        sems,
        ATTEND_KEPT,
    )
    load_rows(me_ref, shards, rows_ref, count, row_sems)
    fetch.wait(0)
    for cols in tiles_of(heads * HEAD_DIM):
        value = mm_t(rows_ref[...], merge_ref[cols, :])
        for k, difference in enumerate(order):
            grad_mixed_ref[place_of(me_ref, difference, share), cols] = value[k * share : (k + 1) * share]

    for place in range(1, ATTEND_KEPT - 1):
        fetch.wait(place)
    masks = [masks_ref[i] for i in range(CONV - 1)]
    strict, lower = block_masks(seg_col_ref, seg_row_ref)
    lane = lax.broadcasted_iota(jnp.int32, (TOK_MB, LANES), 1)
    everyone = range(heads)
    columns = [slice(h * HEAD_DIM, (h + 1) * HEAD_DIM) for h in everyone]
    grad_gain = jnp.zeros((8, HEAD_DIM), F32)
    grad_outs, queries, keys, values, betas, convs = [], [], [], [], [], []
    for h in everyone:
        cols = columns[h]
        taps = [taps_ref[0, j, :, cols] for j in range(3)]
        _, _, conv_q = stream(qkv_ref[0, :, cols], taps[0], masks)
        _, _, conv_k = stream(qkv_ref[1, :, cols], taps[1], masks)
        scale_q = lax.rsqrt(jnp.sum(conv_q * conv_q, axis=-1, keepdims=True) + EPS)
        scale_k = lax.rsqrt(jnp.sum(conv_k * conv_k, axis=-1, keepdims=True) + EPS)
        queries.append((conv_q * (scale_q * HEAD_DIM**-0.5)).astype(BF16))
        keys.append((conv_k * scale_k).astype(BF16))
        betas.append(jax.nn.sigmoid(logit_ref[:, h : h + 1]))
        out = out_ref[:, cols]
        grad_mixed = grad_mixed_ref[:, cols]
        mean = jnp.mean(out * out, axis=-1, keepdims=True)
        scale = lax.rsqrt(jnp.maximum(mean, OUT_FLOOR))
        unit = out * scale
        grad_gain = grad_gain + jnp.sum((grad_mixed * unit).reshape(TOK_MB // 8, 8, HEAD_DIM), axis=0)
        grad_unit = grad_mixed * gain_ref[...]
        through = jnp.where(mean > OUT_FLOOR, 1.0, jnp.where(mean == OUT_FLOOR, 0.5, 0.0))
        grad_out = scale * (
            grad_unit - unit * (through * jnp.mean(grad_unit * unit, axis=-1, keepdims=True))
        )
        grad_outs.append(grad_out.astype(BF16))
    grad_gain_ref[...] = grad_gain
    fresh = {(h, b): fresh_ref[rows_of(b), columns[h]] for h in everyone for b in range(BLOCKS)}
    d_out = {(h, b): grad_outs[h][rows_of(b)] for h in everyone for b in range(BLOCKS)}
    key_blocks = {(h, b): keys[h][rows_of(b)] for h in everyone for b in range(BLOCKS)}
    d_fresh, d_target, d_target_b = {}, {}, {}
    for c in range(BLOCKS):
        for h in everyone:
            total = t_mm(attend_ref[h, rows_of(c), rows_of(c)], d_out[h, c])
            for b in range(c + 1, BLOCKS):
                total = total + t_mm(attend_ref[h, rows_of(b), rows_of(c)], d_out[h, b])
            d_fresh[h, c] = total
    for b in reversed(range(BLOCKS)):
        for h in everyone:
            d_target[h, b] = t_mm(inverse_ref[h, b], d_fresh[h, b])
            d_target_b[h, b] = d_target[h, b].astype(BF16)
        for h in everyone:
            for c in range(b):
                d_fresh[h, c] = d_fresh[h, c] - t_mm(system_ref[h, rows_of(b), rows_of(c)], d_target_b[h, b])
    grad_query, inner, grad_key = {}, {}, {}
    for b in range(BLOCKS):
        for c in range(b + 1):
            for h in everyone:
                d_attend = jnp.where(lower[b, c], mm_t(d_out[h, b], fresh[h, c]), 0.0).astype(BF16)
                d_system = jnp.where(strict[b, c], -mm_t(d_target_b[h, b], fresh[h, c]), 0.0)
                for store, place, part in (
                    (grad_query, b, mm(d_attend, key_blocks[h, c])),
                    (inner, b, mm(d_system, key_blocks[h, c])),
                    (grad_key, c, t_mm(d_attend, queries[h][rows_of(b)])
                     + t_mm(d_system * betas[h][rows_of(b)], key_blocks[h, b])),
                ):
                    store[h, place] = store[h, place] + part if (h, place) in store else part

    def whole(store, h):
        return jnp.concatenate([store[h, b] for b in range(BLOCKS)], axis=0)

    grad_logits = jnp.zeros((TOK_MB, LANES), F32)
    for h in everyone:
        cols = columns[h]
        beta = betas[h]
        taps = [taps_ref[0, j, :, cols] for j in range(3)]
        inputs = [qkv_ref[j, :, cols] for j in range(3)]
        pre_q, gate_q, conv_q = stream(inputs[0], taps[0], masks)
        pre_k, gate_k, conv_k = stream(inputs[1], taps[1], masks)
        pre_v, gate_v, value = stream(inputs[2], taps[2], masks)
        scale_q = lax.rsqrt(jnp.sum(conv_q * conv_q, axis=-1, keepdims=True) + EPS)
        scale_k = lax.rsqrt(jnp.sum(conv_k * conv_k, axis=-1, keepdims=True) + EPS)
        unit_q, key = conv_q * scale_q, conv_k * scale_k
        within = whole(inner, h)
        target = whole(d_target, h)
        grad_q = whole(grad_query, h)
        grad_k = whole(grad_key, h) + beta * within
        grad_beta = jnp.sum(within * key + target * value, axis=-1, keepdims=True)
        grad_logits = jnp.where(lane == h, grad_beta * beta * (1.0 - beta), grad_logits)
        grad_conv_q = (HEAD_DIM**-0.5 * scale_q) * (
            grad_q - unit_q * jnp.sum(grad_q * unit_q, axis=-1, keepdims=True)
        )
        grad_conv_k = scale_k * (grad_k - key * jnp.sum(grad_k * key, axis=-1, keepdims=True))
        for j, (grad, pre, gate) in enumerate(
            ((grad_conv_q, pre_q, gate_q), (grad_conv_k, pre_k, gate_k), (beta * target, pre_v, gate_v))
        ):
            grad_x = stream_back(grad, inputs[j], pre, gate, taps[j], masks, grad_taps_ref, j, cols)
            grad_abs_ref[j, :, cols] = grad_x.astype(BF16)
    logit_abs_ref[...] = grad_logits.astype(BF16)
    for k, difference in enumerate(order):
        here = slice(k * share, (k + 1) * share)
        there = place_of(me_ref, difference, share)
        grad_logit_ref[here, :] = logit_abs_ref[there, :]
        for j in range(3):
            grad_qkv_ref[here, j * width : (j + 1) * width] = grad_abs_ref[j, there, :]
    push.start(grad_qkv_ref, grad_qkv_hbm)
    push.start(grad_logit_ref, grad_logit_hbm)
    for place in range(ATTEND_KEPT - 1, ATTEND_KEPT + 3):
        fetch.wait(place)
    for span in tiles_of(model):
        value = mm_t(grad_logit_ref[...], beta_ref[span, :])
        for j in range(3):
            value = value + mm_t(grad_qkv_ref[:, j * width : (j + 1) * width], project_ref[j, span, :])
        for k, ref in enumerate(partials):
            ref[:, span] = value[k * share : (k + 1) * share].astype(ref.dtype)
    push.wait()


def attend_backward(me, mine, count, rows, kept, taps, gain, project, beta_weight, merge):
    masks, seg_col, seg_row = mine
    heads = merge.shape[1] // HEAD_DIM
    width = heads * HEAD_DIM
    model = merge.shape[2]
    kept = kept[1:3] + kept[4:]
    grads = [jax.ShapeDtypeStruct((TOK_MB, 3 * width), BF16), jax.ShapeDtypeStruct((TOK_MB, LANES), BF16)]
    results = call(
        functools.partial(attend_back_kernel, heads, count),
        (me, seg_col, seg_row, masks, taps, gain),
        rows,
        (*kept, project, beta_weight, merge),
        partial_shapes(count, model)
        + [
            jax.ShapeDtypeStruct((3, CONV, width), F32),
            jax.ShapeDtypeStruct((8, HEAD_DIM), F32),
        ],
        grads,
        as_scratch(kept)
        + [
            pltpu.VMEM((TOK_MB, model), BF16),
            pltpu.VMEM((TOK_MB, width), F32),
            pltpu.VMEM((3, TOK_MB, width), BF16),
            pltpu.VMEM((TOK_MB, LANES), BF16),
        ]
        + as_scratch(grads)
        + [
            pltpu.VMEM(project.shape[1:], BF16),
            pltpu.VMEM(beta_weight.shape, BF16),
            pltpu.VMEM(merge.shape[1:], BF16),
            pltpu.SemaphoreType.DMA((ATTEND_KEPT + 3,)),
            pltpu.SemaphoreType.DMA((2,)),
        ],
        ATTEND_BACK_GRANT,
    )
    return results[count + 2 :] + results[count : count + 2], results[:count]


def small_call(kernel, operands, out_shape):
    vmem = pl.BlockSpec(memory_space=pltpu.VMEM)
    return pl.pallas_call(
        kernel,
        in_specs=[vmem] * len(operands),
        out_specs=[vmem] * len(out_shape),
        out_shape=out_shape,
        compiler_params=pltpu.CompilerParams(vmem_limit_bytes=16 * 1024 * 1024),
        cost_estimate=pl.CostEstimate(flops=10**9, bytes_accessed=10**5, transcendentals=0),
    )(*operands)


def total_of(refs):
    total = refs[0][...].astype(F32)
    for ref in refs[1:]:
        total = total + ref[...].astype(F32)
    return total


def norm_kernel(gain_ref, *refs):
    *terms, total_ref, normed_ref = refs
    total = total_of(terms)
    scale = lax.rsqrt(jnp.mean(total * total, axis=-1, keepdims=True) + EPS)
    total_ref[...] = total
    normed_ref[...] = (total * scale * gain_ref[...]).astype(BF16)


def norm_of_sum(gain, *terms):
    shape = terms[0].shape
    return small_call(
        norm_kernel, (gain, *terms), [jax.ShapeDtypeStruct(shape, F32), jax.ShapeDtypeStruct(shape, BF16)]
    )


def first_norm_kernel(m, me_ref, gain_ref, tokens_hbm, normed_ref, own_ref, rows_ref, sem):
    copy = pltpu.make_async_copy(tokens_hbm.at[m], rows_ref, sem)
    copy.start()
    copy.wait()
    share = own_ref.shape[0]
    own_ref[...] = rows_ref[place_of(me_ref, 0, share), :]
    for rows in tiles_of(TOK_MB, BLOCK):
        x = rows_ref[rows, :].astype(F32)
        scale = lax.rsqrt(jnp.mean(x * x, axis=-1, keepdims=True) + EPS)
        normed_ref[rows, :] = (x * scale * gain_ref[...]).astype(BF16)


def first_norm(me, gain, tokens, m, share):
    vmem = pl.BlockSpec(memory_space=pltpu.VMEM)
    width = tokens.shape[2]
    return pl.pallas_call(
        functools.partial(first_norm_kernel, m),
        in_specs=[pl.BlockSpec(memory_space=pltpu.SMEM), vmem, pl.BlockSpec(memory_space=pltpu.HBM)],
        out_specs=[vmem, vmem],
        out_shape=[jax.ShapeDtypeStruct((TOK_MB, width), BF16), jax.ShapeDtypeStruct((share, width), BF16)],
        scratch_shapes=[pltpu.VMEM((TOK_MB, width), BF16), pltpu.SemaphoreType.DMA],
        compiler_params=pltpu.CompilerParams(vmem_limit_bytes=16 * 1024 * 1024),
        cost_estimate=pl.CostEstimate(flops=10**9, bytes_accessed=10**5, transcendentals=0),
    )(me, gain, tokens)


def norm_back_kernel(gain_ref, base_ref, x_ref, *refs):
    *terms, grad_ref, narrow_ref, gain_out = refs
    grad_normed = total_of(terms)
    x = x_ref[...].astype(F32)
    scale = lax.rsqrt(jnp.mean(x * x, axis=-1, keepdims=True) + EPS)
    unit = x * scale
    grad_scaled = grad_normed * gain_ref[...]
    grad = base_ref[...].astype(F32) + scale * (
        grad_scaled - unit * jnp.mean(grad_scaled * unit, axis=-1, keepdims=True)
    )
    grad_ref[...] = grad
    narrow_ref[...] = grad.astype(BF16)
    rows, width = x.shape
    gain_out[...] = jnp.sum((grad_normed * unit).reshape(rows // 8, 8, width), axis=0)


def norm_backward(gain, base, x, *terms):
    shape = x.shape
    return small_call(
        norm_back_kernel,
        (gain, base, x, *terms),
        [
            jax.ShapeDtypeStruct(shape, F32),
            jax.ShapeDtypeStruct(shape, BF16),
            jax.ShapeDtypeStruct((8, shape[1]), F32),
        ],
    )


def tap_masks(segment):
    masks = []
    for tap in range(1, CONV):
        earlier = jnp.concatenate([jnp.full((tap,), -1, jnp.int32), segment[: TOK_MB - tap]], axis=0)
        masks.append(jnp.broadcast_to((earlier == segment).astype(F32)[:, None], (TOK_MB, HEAD_DIM)))
    return jnp.stack(masks)


def narrow(values):
    return values.astype(BF16)


def product(left, right):
    return jnp.dot(left, right, preferred_element_type=F32)


def product_left(left, right):
    return lax.dot_general(left, right, (((0,), (0,)), ((), ())), preferred_element_type=F32)


def product_right(left, right):
    return lax.dot_general(left, right, (((1,), (1,)), ((), ())), preferred_element_type=F32)


def segment_ids(lengths, count):
    ends = jnp.cumsum(lengths)
    places = jnp.arange(count, dtype=jnp.int32)
    return jnp.sum((places[:, None] >= ends[None, :]).astype(jnp.int32), axis=1, dtype=jnp.int32)


def flipped(values, axis, bit):
    return lax.ppermute(values, axis, [(i, i ^ bit) for i in range(lax.axis_size(axis))])


def shifted(values, axis, distance):
    devices = range(lax.axis_size(axis))
    return lax.ppermute(values, axis, [(i, i + distance) for i in devices if i + distance in devices])


def bits_of(axis):
    size = lax.axis_size(axis)
    bits = [1 << k for k in range(size.bit_length() - 1)]
    assert 1 << len(bits) == size
    return bits


def summed(values, axes):
    for axis in axes:
        for bit in bits_of(axis):
            values = values + flipped(values, axis, bit)
    return values


class Order:

    def __init__(self):
        self.last = None

    def flipped(self, values, bit):
        if bit > 1:
            if self.last is not None:
                values, _ = lax.optimization_barrier((values, self.last))
            self.last = flipped(values, "head", bit)
            return self.last
        return flipped(values, "head", bit)


def gather_far(shard, order):
    parts = [shard]
    for bit in reversed(bits_of("head")[1:]):
        parts = parts + [order.flipped(part, bit) for part in parts]
    return parts


def gather_near(parts):
    return parts + [flipped(part, "head", 1) for part in parts]


def gather(shard, order):
    return gather_near(gather_far(shard, order))


def total(terms):
    return sum(term.astype(F32) for term in terms)


def scatter_near(parts):
    half = len(parts) // 2
    return [[part, flipped(other, "head", 1)] for part, other in zip(parts[:half], parts[half:])]


def scatter_far(parts, order):
    for bit in bits_of("head")[1:]:
        half = len(parts) // 2
        arrived = [order.flipped(narrow(total(terms)), bit) for terms in parts[half:]]
        parts = [terms + [other] for terms, other in zip(parts[:half], arrived)]
    return parts[0]


def after(values, earlier):
    return lax.optimization_barrier((values, earlier))[0]


def together(*values):
    return lax.optimization_barrier(values)


def in_turn(kernel, order, shards=None, rows=None, finish=None):
    if rows is None:
        fars = [gather_far(shard, order) for shard in shards]
    kept, sums, near = [], [], None
    for m in range(len(rows or fars)):
        parts = gather_near(fars[m]) if rows is None else rows[m]
        if near is not None:
            half = len(near) // 2
            sent_on = [[total(terms)] for terms in near[half:]]
            parts, sent_on = together(parts, sent_on)
            near = near[:half] + sent_on
            sums.append(scatter_far(near, order))
        keep, partials = kernel(m, parts)
        if sums:
            partials = after(partials, sums[-1][-1])
        if rows is None and m + 1 < len(fars):
            fars[m + 1], keep, partials = together(fars[m + 1], keep, partials)
        kept.append(keep)
        if finish is not None and m + 1 == len(rows or fars):
            kept = finish(kept)
            partials = after(partials, kept)
        if partials is not None:
            near = scatter_near(partials)
    if near is not None:
        sums.append(scatter_far(near, order))
    return kept, sums


def in_order(sums, finish):
    results = []
    for m, (*terms, far) in enumerate(sums):
        if results:
            far, results[-1] = together(far, results[-1])
        results.append(finish(m, *terms, far))
    return results


def sent(distance, sums, finish):
    arrived = []
    for m, (*terms, far) in enumerate(sums):
        if arrived:
            far = after(far, arrived[-1])
        arrived.append(shifted(finish(m, *terms, far), "section", distance))
    return arrived


def swapped(shards):
    count = lax.axis_size("dp")
    me = lax.axis_index("dp")
    values = jnp.stack(shards)
    wide = values.shape[-1] // count
    arrived = []
    for pair in range(count):
        block = lax.dynamic_slice_in_dim(values, (me ^ pair) * wide, wide, 2)
        arrived.append(flipped(block, "dp", pair) if pair else block)
    return arrived


def in_dp_order(arrived):
    me = lax.axis_index("dp")
    count = len(arrived)
    arrived = jnp.stack(arrived)
    ordered = [lax.dynamic_index_in_dim(arrived, me ^ q, 0, keepdims=False) for q in range(count)]
    return jnp.stack(ordered, axis=1)


def per_device(
    tokens,
    lengths,
    cotangent,
    attn_in,
    beta_weight,
    conv_weight,
    o_gain,
    attn_out,
    mlp_in,
    mlp_out,
    norm_gains,
):
    section = lax.axis_index("section")
    sections = lax.axis_size("section")
    member = lax.axis_index("head")
    micro = tokens.shape[0]
    width = tokens.shape[2]
    heads = beta_weight.shape[2]
    share = TOK_MB // lax.axis_size("head")
    me = member[None]
    beta_wide = jnp.pad(beta_weight[0], ((0, 0), (0, LANES - heads)))
    gains = norm_gains[0]
    every = range(micro)
    segments = [segment_ids(lengths[m], TOK_MB) for m in every]
    masks = [(tap_masks(s), s[:, None], s[None, :]) for s in segments]
    order = Order()
    groups = lax.axis_size("head")
    cotangent_own = [
        lax.dynamic_slice(cotangent, (m, member * share, 0), (1, share, width))[0] for m in every
    ]
    gain_in, gain_mid = gains[0:1], gains[1:2]

    def forward_turn(inputs, save, shards=None, rows=None):
        kept, sums = in_turn(
            lambda m, rows: attend_forward(
                me, masks[m], groups, rows, conv_weight, o_gain, attn_in, beta_wide, attn_out, save
            ),
            order,
            shards,
            rows,
        )
        middles = in_order(sums, lambda m, *terms: norm_of_sum(gain_mid, inputs[m], *terms))
        kept_mid, sums = in_turn(
            lambda m, rows: expand_forward(me, groups, rows, mlp_in, mlp_out, save),
            order,
            [values[1] for values in middles],
        )
        if save:
            return kept, [values[0] for values in middles], kept_mid
        return sent(1, sums, lambda m, *terms: narrow(total([middles[m][0], *terms])))

    def backward_expand(incoming, slopes, shards=None, rows=None, finish=None):
        joint = [None]

        def kernel(m, rows):
            joint[0], partials = expand_backward(
                me, groups, rows, *slopes[m], mlp_in, mlp_out, m, micro, joint[0]
            )
            return joint[0], partials

        grads, sums = in_turn(kernel, order, shards, rows, finish)
        return grads, in_order(sums, lambda m, *terms: norm_backward(gain_mid, incoming[m], middles[m], *terms))

    def backward_attend(grad_middles):
        return in_turn(
            lambda m, rows: attend_backward(
                me, masks[m], groups, rows, kept[m], conv_weight, o_gain, attn_in, beta_wide, attn_out
            ),
            order,
            [values[1] for values in grad_middles],
        )

    def all_rows(values):
        return jnp.concatenate(values, axis=0)

    last = sections - 1
    normed, tokens_own = zip(*(first_norm(me, gain_in, tokens, m, share) for m in every))
    inputs, normed_own = tokens_own, None
    for turn in range(last):
        arrived = forward_turn(inputs, False, normed_own, normed)
        inputs = [jnp.where(section == 0, tokens_own[m], arrived[m]) for m in every]
        normed_own = [norm_of_sum(gain_in, value)[1] for value in inputs]
        normed = None
    kept, middles, kept_mid = forward_turn(inputs, True, normed_own, normed)

    hidden_rows = [lax.all_gather(values[1], "dp", axis=0, tiled=True) for values in kept_mid]
    mixed_rows = [lax.all_gather(values[3], "dp", axis=0, tiled=True) for values in kept]

    slopes = [values[2:] for values in kept_mid]
    incoming = cotangent_own
    rows = [cotangent[m] for m in every]
    for turn in range(last):
        _, grad_middles = backward_expand(incoming, slopes, incoming, rows)
        _, sums = backward_attend(grad_middles)
        arrived = sent(
            -1, sums, lambda m, *terms: norm_backward(gain_in, grad_middles[m][0], inputs[m], *terms)[1]
        )
        incoming = [jnp.where(section == last, cotangent_own[m], arrived[m]) for m in every]
        rows = None
    normed_mid = all_rows([values[0] for values in kept_mid])


    def expand_terms(grads):
        nonlocal hidden_rows, mixed_rows
        both, hidden_rows, mixed_rows = together(grads[-1], hidden_rows, mixed_rows)
        columns = swapped(after(incoming, both))
        return together(narrow(product_left(normed_mid, both)), columns)

    (expands, columns_out), grad_middles = backward_expand(incoming, slopes, incoming, rows, expand_terms)
    grads, sums = backward_attend(grad_middles)
    finals = [norm_backward(gain_in, grad_middles[m][0], inputs[m], *sums[m]) for m in every]
    gain_one, gain_two = (
        sum(jnp.sum(values[2], axis=0) for values in group) for group in (finals, grad_middles)
    )
    rows_out = jnp.stack([values[0] for values in finals])
    half = width // sections
    moved = shifted(narrow(rows_out[:, :, half:]), "section", 1).astype(F32)
    grad_tokens = jnp.where(section == 0, rows_out[:, :, :half], moved)

    def spread(value, axis):
        return lax.psum_scatter(value, "dp", scatter_dimension=axis, tiled=True)

    early = spread(expands, 0)
    normed = all_rows([values[0] for values in kept])
    grad_project = narrow(product_left(normed, all_rows([grad[0] for grad in grads])))
    grad_beta = product_left(normed, all_rows([grad[1] for grad in grads]))[:, :heads]
    grad_taps, grad_head_gain = (sum(grad[place] for grad in grads) for place in (2, 3))
    grad_head_gain = jnp.sum(grad_head_gain, axis=0)

    grad_project, early, middles_out = together(grad_project, early, [values[1] for values in grad_middles])
    grad_project, columns_mid = together(grad_project, swapped(middles_out))
    columns = [
        part.reshape(-1, part.shape[-1])
        for arrived in (columns_out, columns_mid)
        for part in jnp.concatenate(gather(in_dp_order(arrived), order), axis=2)
    ]
    grad_contract = sum(product_left(left, right) for left, right in zip(hidden_rows, columns[:micro]))
    grad_merge = sum(product_left(left, right) for left, right in zip(mixed_rows, columns[micro:]))
    flat = jnp.concatenate([gain_one, gain_two, grad_head_gain])
    flat = summed(flat, ("dp", "head"))
    grad_gains, grad_head_gain = flat[: 2 * width].reshape(2, width), flat[2 * width :]
    flat = summed(jnp.concatenate([grad_taps.reshape(-1), grad_beta.reshape(-1)]), ("dp",))
    grad_taps, grad_beta = flat[: grad_taps.size].reshape(grad_taps.shape), flat[grad_taps.size :]
    rows = width // lax.axis_size("dp")
    grad_beta = lax.dynamic_slice_in_dim(grad_beta.reshape(width, heads), lax.axis_index("dp") * rows, rows, 0)
    units = mlp_in.shape[3]
    grad_expand = jnp.stack([part[:, :units] for part in jnp.split(early, 2, axis=1)]).astype(F32)
    grad_project = jnp.stack(jnp.split(spread(grad_project, 0), 3, axis=1)).astype(F32)
    return (
        grad_tokens,
        grad_project[None],
        grad_beta[None],
        grad_taps[None],
        grad_head_gain[None],
        grad_merge[None],
        grad_expand[None],
        grad_contract[None],
        grad_gains[None],
    )


def solution(mesh):
    return jax.shard_map(
        per_device,
        mesh=mesh,
        in_specs=(
            P("dp", None, None),
            P("dp", None),
            P("dp", None, None),
            P("section", None, None, "head"),
            P("section", None, "head"),
            P("section", None, None, "head"),
            P("section", None),
            P("section", "head", None),
            P("section", None, None, "head"),
            P("section", "head", None),
            P("section", None, None),
        ),
        out_specs=(
            P("dp", "head", "section"),
            P("section", None, "dp", "head"),
            P("section", "dp", "head"),
            P("section", None, None, "head"),
            P("section", None),
            P("section", "head", "dp"),
            P("section", None, "dp", "head"),
            P("section", "head", "dp"),
            P("section", None, None),
        ),
        check_vma=False,
    )
```
